32 devices in a mesh: row: 8 (over z, x), col: 4 (over y, core).
Axes of the slice: x: 2, y: 2, z: 4, core: 2. Of those that a mesh axis runs over, the one named last changes fastest.
Arguments:
- front: float32 [12, 8, 24, 4, 128, 128], P(None, 'row', None, 'col'), may hold values from -6 to 6
- child_tiles: float32 [512, 128, 128], P(('row', 'col')), may hold values from -6 to 6
- tile_dest: int32 [512, 1], P(('row', 'col')), may hold values from 0 to 31; in each aligned block of 16 rows (0 to 15, 16 to 31, ...) no two rows name the same one
- tile_slot: int32 [512], P(('row', 'col')), may hold values from 0 to 287
- tile_count: int32 [32], P(('row', 'col')), may hold values from 12 to 16, as said below
- diag_inverses: float32 [2, 256, 256], replicated, as said below
Outputs:
- factored: float32 [12, 8, 24, 4, 128, 128], P(None, 'row', None, 'col')
The draws below stay inside these ranges and needn't reach their ends.
Inputs may be any that keep to these rules, and one draw needn't show every extreme that they name: Among the 16 slots of one device, no two name the same device in tile_dest, live or not; every device is named by some slot. `tile_count`: some device has all 16 slots live. `diag_inverses`: each matrix is upper triangular with a positive diagonal; it is given as it is and need not match any diagonal block of the front.
All inputs are finite; a program needn't handle non-finite values.
Results may differ from the reference program's by a relative error of at most 0.000068.
Values sent between devices are 32-bit elements; how exact they have to be, the bound alone decides.
No kernel may reach another device: no remote copies, remote signals or barrier semaphores. Data moves between devices by JAX's collectives and lax.ppermute only.
A program may use at most 128 MiB of HBM per device.

```python
import math
import jax
import jax.numpy as jnp
import numpy as np
from jax import lax

N = 12288
TILE = 128
PANEL = 256
RT = 12
CT = 24
KT = 16
N_ROW = 8
N_COL = 4
DEVICES = 32


def draw_tile_count(key, part):
    first_key, second_key = jax.random.split(jax.random.fold_in(key, 11))
    counts = jax.random.randint(first_key, (DEVICES,), KT - KT // 4, KT + 1).astype(jnp.int32)
    where_full = jax.random.randint(second_key, (), 0, DEVICES)
    full_mask = jnp.arange(DEVICES, dtype=jnp.int32) == where_full
    return jnp.where(full_mask, jnp.int32(KT), counts).astype(jnp.int32)


def draw_diag_inverses(key, part):
    first_key, second_key = jax.random.split(jax.random.fold_in(key, 23))
    upper_part = jnp.clip(jax.random.normal(first_key, (2, PANEL, PANEL), jnp.float32), -4.0, 4.0)
    upper_part = upper_part * (0.25 / math.sqrt(PANEL))
    diagonal = jnp.exp(jax.random.uniform(second_key, (2, PANEL), jnp.float32, math.log(0.08), math.log(0.3)))
    eye_table = jnp.eye(PANEL, dtype=jnp.float32)
    return (jnp.triu(upper_part, 1) + diagonal[:, :, None] * eye_table[None]).astype(jnp.float32)


def touch_ends(result, own_key, smallest, top_value):
    longest = result.shape.index(max(result.shape))
    spots = []
    for shift in (0, 1):
        where = [jax.random.randint(jax.random.fold_in(own_key, axis), (), 0, length) for axis, length in enumerate(result.shape)]
        where[longest] = (where[longest] + shift) % result.shape[longest]
        spots.append(tuple(where))
    return result.at[spots[0]].set(smallest).at[spots[1]].set(top_value)


def levels(stream_key, dims, shards, low, largest):
    def one(dim, blocks):
        steps = jax.random.uniform(jax.random.fold_in(jax.random.fold_in(stream_key, 6), dim), (blocks,), jnp.float32, low / len(shards), largest / len(shards))
        return jnp.repeat(jnp.exp(steps), dims[dim] // blocks).reshape((-1,) + (1,) * (len(dims) - dim - 1))

    gain = one(*shards[0])
    for cut in shards[1:]:
        gain = gain * one(*cut)
    return gain


def assign_block(own_key, own, number, rows, number_of, top, limit, skew):
    ranking = jax.random.permutation(own_key, number_of)
    crowded, usual = load_shares(number_of, rows * top, limit, skew, True), load_shares(number_of, rows * top, limit, skew, False)
    places = jnp.arange(number_of)

    def named(lengths, rotation):
        used = int((lengths > 0).sum())
        fixed = max(1, used // 4)
        moved = fixed + (places - fixed + rotation * (used - fixed)) % max(1, number_of - fixed)
        return jnp.zeros((number_of,), jnp.int32).at[ranking[jnp.where(places < fixed, places, moved)]].set(jnp.asarray(lengths, jnp.int32))

    lengths = jnp.where(number % 4 == 0, named(crowded, number // 4), named(usual, number - number // 4 - 1))
    mixed = jax.random.permutation(jax.random.fold_in(own, 3), number_of)
    donor, taker = mixed[0:number_of // 2 * 2:2], mixed[1:number_of // 2 * 2:2]
    room = jnp.minimum(lengths[donor] - 1, limit - lengths[taker]) // 2
    room = jnp.where((donor == ranking[0]) | (taker == ranking[0]) | (lengths[taker] == 0), 0, jnp.maximum(room, 0))
    moved = jax.random.randint(jax.random.fold_in(own, 4), (number_of // 2,), 0, 1 << 20) % (room + 1)
    lengths = lengths.at[donor].add(-moved).at[taker].add(moved)
    members = jnp.searchsorted(jnp.cumsum(lengths), jnp.arange(rows * top), side="right").astype(jnp.int32)
    grid = members.reshape(top, rows).T
    grid = grid[jax.random.permutation(jax.random.fold_in(own, 1), rows)]
    rotation = jax.random.randint(jax.random.fold_in(own, 2), (rows, 1), 0, top)
    return jnp.take_along_axis(grid, (jnp.arange(top)[None, :] + rotation) % top, axis=1)


def load_shares(count, total, limit, lean, full):
    portions = [(1 << 20) // math.isqrt(grade ** lean) + 1 for grade in range(1, count + 1)]
    largest = limit if full else min(limit, max(-(-total // count), total * portions[0] // sum(portions)))
    least = 1 if total - largest >= count - 1 else 0
    given, rest = [largest] + [least] * (count - 1), total - largest - least * (count - 1)
    while rest > 0:
        free = [i for i in range(1, count) if given[i] < largest] or [i for i in range(1, count) if given[i] < limit]
        whole, left = sum([portions[i] for i in free]), rest
        for i in free:
            addition = min(limit - given[i], max(1, left * portions[i] // whole), rest)
            given[i] = given[i] + addition
            rest = rest - addition
    return np.array(given)


def gaussian(own_key, dims, spread, limit, cuts=(), held_as=jnp.bfloat16):
    values = spread * jax.random.normal(own_key, dims, jnp.float32)
    if cuts:
        values = values * levels(own_key, dims, cuts, -0.22, 0.18)
    return jnp.clip(values, -limit, limit).astype(held_as)


def setup_inputs(seed: int = 0) -> dict:
    streams_of = jax.random.split(jax.random.key(seed), 7)
    front = gaussian(streams_of[0], (RT, N_ROW, CT, N_COL, TILE, TILE), 1.0, 6.0, ((1, 8), (3, 4)), jnp.float32)
    child_tiles = gaussian(streams_of[1], (DEVICES * KT, TILE, TILE), 1.0, 6.0, ((0, 32),), jnp.float32)
    tile_dest_keys = jax.random.split(jax.random.fold_in(streams_of[2], 1), (DEVICES * KT) // KT)
    tile_dest_turns = jax.random.permutation(jax.random.fold_in(streams_of[2], 3), (DEVICES * KT) // KT)
    tile_dest = jax.vmap(lambda own, number: assign_block(jax.random.fold_in(streams_of[2], 2), own, number, KT, DEVICES, 1, 1, 2))(tile_dest_keys, tile_dest_turns).reshape((DEVICES * KT, 1))
    tile_slot = touch_ends(jax.random.randint(streams_of[3], (DEVICES * KT,), 0, RT * CT), jax.random.fold_in(streams_of[3], 1), 0, (RT * CT) - 1).astype(jnp.int32)
    tile_count = draw_tile_count(jax.random.fold_in(streams_of[6], 71), 0)
    diag_inverses = draw_diag_inverses(jax.random.fold_in(streams_of[6], 71), 0)
    return {"front": front, "child_tiles": child_tiles, "tile_dest": tile_dest, "tile_slot": tile_slot, "tile_count": tile_count, "diag_inverses": diag_inverses}


def to_matrix(tiles):
    return tiles.transpose(0, 1, 4, 2, 3, 5).reshape(N, N)


def to_tiles(matrix):
    return matrix.reshape(RT, N_ROW, TILE, CT, N_COL, TILE).transpose(0, 1, 3, 4, 2, 5)


def reference(front, child_tiles, tile_dest, tile_slot, tile_count, diag_inverses):
    high = lax.Precision.HIGHEST
    live = (jnp.arange(KT, dtype=jnp.int32)[None, :] < tile_count[:, None]).reshape(-1)
    dest = tile_dest[:, 0]
    row_dev = dest // N_COL
    col_dev = dest % N_COL
    tile_a = tile_slot // CT
    tile_b = tile_slot % CT
    added = jnp.where(live[:, None, None], child_tiles, jnp.zeros_like(child_tiles))
    assembled = front.at[tile_a, row_dev, tile_b, col_dev].add(added)
    first = to_matrix(assembled)
    index = jnp.arange(N, dtype=jnp.int32)
    panel_one = jnp.dot(first[:, :PANEL], diag_inverses[0], precision=high)
    keep_one = index >= PANEL
    second = first - jnp.where(keep_one[:, None] & keep_one[None, :], jnp.dot(panel_one, panel_one.T, precision=high), jnp.zeros_like(first))
    panel_two = jnp.dot(second[:, PANEL:2 * PANEL], diag_inverses[1], precision=high)
    panel_two = jnp.where(keep_one[:, None], panel_two, jnp.zeros_like(panel_two))
    keep_two = index >= 2 * PANEL
    third = second - jnp.where(keep_two[:, None] & keep_two[None, :], jnp.dot(panel_two, panel_two.T, precision=high), jnp.zeros_like(second))
    factored = third.at[:, :PANEL].set(panel_one).at[:, PANEL:2 * PANEL].set(panel_two)
    return to_tiles(factored)
```

```python
import functools

import jax
import jax.numpy as jnp
from jax import lax
from jax.experimental import pallas as pl
from jax.experimental.pallas import tpu as pltpu
from jax.sharding import PartitionSpec as P

TILE = 128
PANEL = 256
CHUNKS = 3
VMEM = 56 * 1024 * 1024
NT = (((1,), (1,)), ((), ()))
NN = (((1,), (0,)), ((), ()))


def halves(value):
    high = value.astype(jnp.bfloat16)
    low = (value - high.astype(jnp.float32)).astype(jnp.bfloat16)
    return high, low


def product(left, right, dims):
    dot = functools.partial(
        lax.dot_general, dimension_numbers=dims, preferred_element_type=jnp.float32
    )
    return dot(left[0], right[0]) + (dot(left[0], right[1]) + dot(left[1], right[0]))


def columns_kernel(row_of, col_of, front_ref, incoming_ref, out_ref, tile_ref, sem):
    out_ref[...] = front_ref[:, 0, 0, 0]

    @pl.loop(0, incoming_ref.shape[0])
    def _(s):
        @pl.when(col_of[s] == 0)
        def _():
            copy = pltpu.make_async_copy(incoming_ref.at[s], tile_ref, sem)
            copy.start()
            copy.wait()
            out_ref[row_of[s]] = out_ref[row_of[s]] + tile_ref[...]


def assemble_columns(front, incoming, row_of, col_of):
    rows = front.shape[0]
    return pl.pallas_call(
        columns_kernel,
        grid_spec=pltpu.PrefetchScalarGridSpec(
            num_scalar_prefetch=2,
            grid=(1,),
            in_specs=[
                pl.BlockSpec((rows, 1, 1, 1, TILE, TILE), lambda i, *_: (0, 0, 0, 0, 0, 0)),
                pl.BlockSpec(memory_space=pl.ANY),
            ],
            out_specs=pl.BlockSpec((rows, TILE, TILE), lambda i, *_: (0, 0, 0)),
            scratch_shapes=[pltpu.VMEM((TILE, TILE), jnp.float32), pltpu.SemaphoreType.DMA],
        ),
        out_shape=jax.ShapeDtypeStruct((rows, TILE, TILE), jnp.float32),
        compiler_params=pltpu.CompilerParams(vmem_limit_bytes=VMEM),
        name="panel_columns",
    )(row_of, col_of, front, incoming)


def row_panels_kernel(
    place, tiles_ref, lead_ref, diag_ref,
    high_ref, low_ref, mine_ref, small_high_ref, small_low_ref,
):
    step = pl.program_id(0)
    my_row, my_col = place[0], place[1]
    group = tiles_ref.shape[1]
    height = group * TILE

    @pl.when(step == 0)
    def _():
        inverse_one = halves(diag_ref[0])
        lead = jnp.concatenate(
            [jnp.concatenate([lead_ref[i, 0], lead_ref[i, 1]], axis=1) for i in range(2)], axis=0
        )
        lead = halves(product(halves(lead), inverse_one, NN))
        inverse_two = halves(diag_ref[1])
        for index, pair in enumerate((inverse_one, lead, inverse_two)):
            small_high_ref[index] = pair[0]
            small_low_ref[index] = pair[1]

    small = [(small_high_ref[i], small_low_ref[i]) for i in range(3)]
    columns = [tiles_ref[c].reshape(height, TILE) for c in range(4)]
    tile_row = lax.broadcasted_iota(jnp.int32, (height, PANEL), 0) // TILE
    first = jnp.logical_and(step == 0, tile_row == 0)
    above_one = jnp.logical_and(first, my_row < 2)
    above_two = jnp.logical_and(first, my_row < 4)
    one = product(halves(jnp.concatenate(columns[:2], axis=1)), small[0], NN)
    masked = jnp.where(above_one, 0.0, one)
    one_pair = halves(masked)
    field = jnp.concatenate(columns[2:], axis=1) - product(one_pair, small[1], NT)
    two = product(halves(field), small[2], NN)
    two = jnp.where(above_one, 0.0, two)
    two_pair = halves(jnp.where(above_two, 0.0, two))
    high_ref[:, :PANEL] = one_pair[0]
    low_ref[:, :PANEL] = one_pair[1]
    high_ref[:, PANEL:] = two_pair[0]
    low_ref[:, PANEL:] = two_pair[1]
    pieces = (one[:, :TILE], one[:, TILE:], two[:, :TILE], two[:, TILE:])
    for c in range(4):

        @pl.when(my_col == c)
        def _():
            mine_ref[...] = pieces[c].reshape(group, TILE, TILE)


def row_panels(tiles, lead, diag, place):
    rows = tiles.shape[1]
    group = rows // CHUNKS
    height = group * TILE
    flat = jax.ShapeDtypeStruct((rows * TILE, 2 * PANEL), jnp.bfloat16)
    small = jax.ShapeDtypeStruct((3, PANEL, PANEL), jnp.bfloat16)
    whole = lambda shape: pl.BlockSpec(shape, lambda i, *_: (0,) * len(shape))
    return pl.pallas_call(
        row_panels_kernel,
        grid_spec=pltpu.PrefetchScalarGridSpec(
            num_scalar_prefetch=1,
            grid=(CHUNKS,),
            in_specs=[
                pl.BlockSpec((4, group, TILE, TILE), lambda i, *_: (0, i, 0, 0)),
                whole((2, 2, TILE, TILE)),
                whole((2, PANEL, PANEL)),
            ],
            out_specs=[
                pl.BlockSpec((height, 2 * PANEL), lambda i, *_: (i, 0)),
                pl.BlockSpec((height, 2 * PANEL), lambda i, *_: (i, 0)),
                pl.BlockSpec((group, TILE, TILE), lambda i, *_: (i, 0, 0)),
                whole((3, PANEL, PANEL)),
                whole((3, PANEL, PANEL)),
            ],
        ),
        out_shape=[
            flat, flat, jax.ShapeDtypeStruct((rows, TILE, TILE), jnp.float32), small, small
        ],
        compiler_params=pltpu.CompilerParams(vmem_limit_bytes=VMEM),
        name="row_panels",
    )(place, tiles, lead, diag)


def trailing_kernel(
    first, row_of, col_of, front_ref, gathered_ref, high_ref, low_ref, small_high_ref,
    small_low_ref, incoming_ref, mine_ref, *rest,
):
    out_ref = rest[-1]
    pair = first + pl.program_id(0)
    rows = out_ref.shape[0]
    small = [(small_high_ref[i], small_low_ref[i]) for i in range(3)]

    def raw(start):
        return jnp.concatenate(
            [
                jnp.concatenate([gathered_ref[4 * h + c, 0] for c in (start, start + 1)], axis=1)
                for h in range(2)
            ],
            axis=0,
        )

    one = halves(product(halves(raw(0)), small[0], NN))
    field = raw(2) - product(one, small[1], NT)
    two = halves(product(halves(field), small[2], NN))
    right = tuple(jnp.concatenate([a, b], axis=1) for a, b in zip(one, two))
    group = rows // 3
    height = group * TILE

    @pl.loop(0, 3)
    def _(g):
        span = pl.ds(pl.multiple_of(g * height, height), height)
        update = product((high_ref[span], low_ref[span]), right, NT)
        for j in range(2):
            part = update[:, j * TILE : (j + 1) * TILE].reshape(group, TILE, TILE)
            out_ref[pl.ds(g * group, group), 0, j, 0] = (
                front_ref[pl.ds(g * group, group), 0, j, 0] - part
            )

    @pl.loop(0, incoming_ref.shape[0])
    def _(s):
        @pl.when(col_of[s] // 2 == pair)
        def _():
            a, j = row_of[s], col_of[s] % 2
            out_ref[a, 0, j, 0] = out_ref[a, 0, j, 0] + incoming_ref[s]

    if first == 0:

        @pl.when(pair == 0)
        def _():
            out_ref[:, 0, 0, 0] = mine_ref[...]


def trailing(front, gathered, panels, incoming, row_of, col_of, chunk, before):
    rows, cols = front.shape[0], front.shape[2]
    high, low, mine, small_high, small_low = panels
    pairs = cols // 2 // CHUNKS
    first = chunk * pairs
    halves_here = gathered.shape[0] // 8
    whole = lambda a: pl.BlockSpec(a.shape, lambda i, *_: (0,) * a.ndim)
    strip = pl.BlockSpec((rows, 1, 2, 1, TILE, TILE), lambda i, *_: (0, 0, first + i, 0, 0, 0))
    operands = [front, gathered, high, low, small_high, small_low, incoming, mine]
    in_specs = [
        strip,
        pl.BlockSpec((8, 1, TILE, TILE), lambda i, *_: (i % halves_here, i // halves_here, 0, 0)),
        *[whole(a) for a in operands[2:]],
    ]
    aliases = {}
    if before is not None:
        operands.append(before)
        in_specs.append(pl.BlockSpec(memory_space=pl.ANY))
        aliases = {len(operands) + 1: 0}
    height = rows * TILE
    return pl.pallas_call(
        functools.partial(trailing_kernel, first),
        grid_spec=pltpu.PrefetchScalarGridSpec(
            num_scalar_prefetch=2, grid=(pairs,), in_specs=in_specs, out_specs=strip
        ),
        out_shape=jax.ShapeDtypeStruct(front.shape, jnp.float32),
        input_output_aliases=aliases,
        compiler_params=pltpu.CompilerParams(vmem_limit_bytes=VMEM),
        cost_estimate=pl.CostEstimate(
            flops=pairs * 2 * height * 2 * TILE * 2 * PANEL * 3,
            bytes_accessed=pairs * 2 * height * 2 * TILE * 4,
            transcendentals=0,
        ),
        name="trailing",
    )(row_of, col_of, *operands)


def body(front, child_tiles, tile_dest, tile_slot, tile_count, diag_inverses):
    n_row = lax.axis_size("row")
    n_col = lax.axis_size("col")
    my_row = lax.axis_index("row")
    my_col = lax.axis_index("col")
    me = my_row * n_col + my_col
    rows_here, cols_here = (front.shape[0], front.shape[2])
    slots = child_tiles.shape[0]
    devices = n_row * n_col
    assert n_col == 4 and n_row % 8 == 0 and rows_here % CHUNKS == 0

    numbers = jnp.arange(slots, dtype=jnp.int32)
    live = numbers < tile_count[0]
    dest = tile_dest[:, 0]
    hits = (dest[None, :] == jnp.arange(devices, dtype=jnp.int32)[:, None]) & live[None, :]
    picked = jnp.sum(hits.astype(jnp.int32) * numbers[None, :], axis=1)
    outgoing = jnp.take(child_tiles, picked, axis=0)
    area = rows_here * cols_here
    notes = jnp.where(live, dest * area + tile_slot, -1)
    all_notes = lax.all_gather(notes, ("row", "col"), axis=0, tiled=False)
    incoming = lax.all_to_all(outgoing, ("row", "col"), split_axis=0, concat_axis=0, tiled=True)
    to_me = (all_notes >= 0) & (all_notes // area == me)
    slot_in = jnp.sum(jnp.where(to_me, all_notes % area + 1, 0), axis=1) - 1
    row_of = jnp.where(slot_in >= 0, slot_in // cols_here, 0)
    col_of = jnp.where(slot_in >= 0, slot_in % cols_here, -1)

    mine = assemble_columns(front, incoming, row_of, col_of)

    pairs = [
        (r * n_col + c, ((r // n_col) * n_col + c) * n_col + r % n_col)
        for r in range(n_row)
        for c in range(n_col)
    ]
    group = rows_here // CHUNKS
    gathered = []
    for chunk in range(CHUNKS):
        moved = lax.ppermute(mine[chunk * group : (chunk + 1) * group], ("row", "col"), pairs)
        gathered.append(lax.all_gather(moved, "row", axis=0, tiled=False))
        if chunk == 0:
            lead_rows = jnp.arange(2)[:, None] == my_row - 2
            lead_cols = jnp.arange(2)[None, :] == my_col
            lead = jnp.where((lead_rows & lead_cols)[:, :, None, None], mine[0][None, None], 0.0)
            lead = lax.psum(lead, ("row", "col"))
            tiles = lax.all_gather(mine, "col", axis=0, tiled=False)
    place = jnp.stack([my_row, my_col]).astype(jnp.int32)
    panels = row_panels(tiles, lead, diag_inverses, place)

    out = None
    for chunk in range(CHUNKS):
        out = trailing(front, gathered[chunk], panels, incoming, row_of, col_of, chunk, out)
    return out


def solution(mesh):
    return jax.shard_map(
        body,
        mesh=mesh,
        in_specs=(
            P(None, "row", None, "col", None, None),
            P(("row", "col"), None, None),
            P(("row", "col"), None),
            P(("row", "col")),
            P(("row", "col")),
            P(),
        ),
        out_specs=P(None, "row", None, "col", None, None),
        check_vma=False,
    )
```

```python
import functools

import jax
import jax.numpy as jnp
from jax import lax
from jax.experimental import pallas as pl
from jax.experimental.pallas import tpu as pltpu
from jax.sharding import PartitionSpec as P

TILE = 128
PANEL = 256
WIDTH = 2 * PANEL
NOTE = 8
VMEM = 56 * 1024 * 1024
NT = (((1,), (1,)), ((), ()))
NN = (((1,), (0,)), ((), ()))
BOTH = ("row", "col")


def halves(value):
    high = value.astype(jnp.bfloat16)
    low = (value - high.astype(jnp.float32)).astype(jnp.bfloat16)
    return high, low


def product(left, right, dims):
    dot = functools.partial(
        lax.dot_general, dimension_numbers=dims, preferred_element_type=jnp.float32
    )
    return dot(left[0], right[0]) + (dot(left[0], right[1]) + dot(left[1], right[0]))


def whole_spec(array):
    rank = len(array.shape)
    return pl.BlockSpec(array.shape, lambda *_: (0,) * rank)


def columns_kernel(
    place, row_of, col_of, front_ref, incoming_ref, out_ref, lead_ref, *rest
):
    *parts, tile_ref, sem = rest
    my_row, my_col = place[0], place[1]
    out_ref[...] = front_ref[:, 0, 0, 0]

    @pl.loop(0, incoming_ref.shape[0])
    def _(s):
        @pl.when(col_of[s] == 0)
        def _():
            copy = pltpu.make_async_copy(incoming_ref.at[s, pl.ds(0, TILE)], tile_ref, sem)
            copy.start()
            copy.wait()
            out_ref[row_of[s]] = out_ref[row_of[s]] + tile_ref[...]

    lead_ref[...] = jnp.zeros_like(lead_ref)
    for r in range(2):
        for c in range(2):

            @pl.when(jnp.logical_and(my_row == 2 + r, my_col == c))
            def _():
                lead_ref[r, c] = out_ref[0]

    count = len(parts)
    for j, part_ref in enumerate(parts):
        group = part_ref.shape[0]
        part_ref[...] = out_ref[pl.ds(lax.rem(my_col + j, count) * group, group)]


def assemble_columns(front, incoming, place, row_of, col_of, parts):
    rows = front.shape[0]
    shapes = [(rows, TILE, TILE), (2, 2, TILE, TILE)] + [(rows // parts, TILE, TILE)] * parts
    out_shape = [jax.ShapeDtypeStruct(shape, jnp.float32) for shape in shapes]
    return pl.pallas_call(
        columns_kernel,
        grid_spec=pltpu.PrefetchScalarGridSpec(
            num_scalar_prefetch=3,
            grid=(1,),
            in_specs=[
                pl.BlockSpec((rows, 1, 1, 1, TILE, TILE), lambda i, *_: (0, 0, 0, 0, 0, 0)),
                pl.BlockSpec(memory_space=pl.ANY),
            ],
            out_specs=[whole_spec(a) for a in out_shape],
            scratch_shapes=[pltpu.VMEM((TILE, TILE), jnp.float32), pltpu.SemaphoreType.DMA],
        ),
        out_shape=out_shape,
        compiler_params=pltpu.CompilerParams(vmem_limit_bytes=VMEM),
        name="panel_columns",
    )(place, row_of, col_of, front, incoming)


def row_panels_kernel(
    place, t0, t1, t2, t3, lead_ref, diag_ref,
    pair_ref, mine_ref, small_high_ref, small_low_ref, tiles_ref,
):
    step = pl.program_id(0)
    my_row, my_col = place[0], place[1]
    group = t0.shape[0]
    height = group * TILE

    @pl.when(step == 0)
    def _():
        inverse_one = halves(diag_ref[0])
        lead = jnp.concatenate(
            [jnp.concatenate([lead_ref[i, 0], lead_ref[i, 1]], axis=1) for i in range(2)], axis=0
        )
        lead = halves(product(halves(lead), inverse_one, NN))
        inverse_two = halves(diag_ref[1])
        for index, pair in enumerate((inverse_one, lead, inverse_two)):
            small_high_ref[index] = pair[0]
            small_low_ref[index] = pair[1]

    for i, tile_ref in enumerate((t0, t1, t2, t3)):
        tiles_ref[jnp.bitwise_xor(my_col, i)] = tile_ref[...]
    small = [(small_high_ref[i], small_low_ref[i]) for i in range(3)]
    columns = [tiles_ref[c].reshape(height, TILE) for c in range(4)]
    tile_row = lax.broadcasted_iota(jnp.int32, (height, PANEL), 0) // TILE
    first = jnp.logical_and(step == 0, tile_row == 0)
    above_one = jnp.logical_and(first, my_row < 2)
    above_two = jnp.logical_and(first, my_row < 4)
    one = product(halves(jnp.concatenate(columns[:2], axis=1)), small[0], NN)
    one_pair = halves(jnp.where(above_one, 0.0, one))
    field = jnp.concatenate(columns[2:], axis=1) - product(one_pair, small[1], NT)
    two = jnp.where(above_one, 0.0, product(halves(field), small[2], NN))
    two_pair = halves(jnp.where(above_two, 0.0, two))
    for i in range(2):
        pair_ref[:, i * WIDTH : i * WIDTH + PANEL] = one_pair[i]
        pair_ref[:, i * WIDTH + PANEL : (i + 1) * WIDTH] = two_pair[i]
    pieces = (one[:, :TILE], one[:, TILE:], two[:, :TILE], two[:, TILE:])
    for c in range(4):

        @pl.when(my_col == c)
        def _():
            mine_ref[...] = pieces[c].reshape(group, TILE, TILE)


def row_panels(tiles, lead, diag, place):
    rows = tiles[0].shape[0]
    group = rows // 3
    height = group * TILE
    out_shape = [
        jax.ShapeDtypeStruct((rows * TILE, 2 * WIDTH), jnp.bfloat16),
        jax.ShapeDtypeStruct((rows, TILE, TILE), jnp.float32),
        jax.ShapeDtypeStruct((3, PANEL, PANEL), jnp.bfloat16),
        jax.ShapeDtypeStruct((3, PANEL, PANEL), jnp.bfloat16),
    ]
    strip = pl.BlockSpec((group, TILE, TILE), lambda i, *_: (i, 0, 0))
    return pl.pallas_call(
        row_panels_kernel,
        grid_spec=pltpu.PrefetchScalarGridSpec(
            num_scalar_prefetch=1,
            grid=(3,),
            in_specs=[strip] * 4 + [whole_spec(lead), whole_spec(diag)],
            out_specs=[
                pl.BlockSpec((height, 2 * WIDTH), lambda i, *_: (i, 0)),
                strip,
                whole_spec(out_shape[2]),
                whole_spec(out_shape[3]),
            ],
            scratch_shapes=[pltpu.VMEM((4, group, TILE, TILE), jnp.float32)],
        ),
        out_shape=out_shape,
        compiler_params=pltpu.CompilerParams(vmem_limit_bytes=VMEM),
        name="row_panels",
    )(place, *tiles, lead, diag)


def trailing_kernel(
    n_pieces, columns, places, order, starts, front_one, front_two, pair_ref, small_high_ref,
    small_low_ref, incoming_ref, mine_ref, *rest,
):
    piece_refs = rest[:n_pieces]
    out_ref, right_high, right_low, buffer, sems = rest[-5:]
    step, steps = pl.program_id(0), pl.num_programs(0)
    group = piece_refs[0].shape[1]
    count = n_pieces * group
    rows = front_one.shape[0]
    slot = lax.rem(step, 2)

    def copy_of(at_step, j):
        at_slot = lax.rem(at_step, 2)
        index = jnp.minimum(2 * at_step, count - 2) + j
        return pltpu.make_async_copy(
            buffer.at[at_slot, j], out_ref.at[:, 0, columns[index], 0], sems.at[at_slot, j]
        )

    def each_copy(at_step, act):
        for j in range(2):
            if count % 2 and j == 0:
                pl.when(at_step < steps - 1)(lambda: act(copy_of(at_step, 0)))
            else:
                act(copy_of(at_step, j))

    @pl.when(step == 0)
    def _():
        small = [(small_high_ref[i], small_low_ref[i]) for i in range(3)]
        for p, piece in enumerate(piece_refs):
            columns_here = [piece[places[4 * p + c]].reshape(group * TILE, TILE) for c in range(4)]
            one = product(halves(jnp.concatenate(columns_here[:2], axis=1)), small[0], NN)
            field = jnp.concatenate(columns_here[2:], axis=1)
            field = field - product(halves(one), small[1], NT)
            two = product(halves(field), small[2], NN)
            for i, panel in enumerate((one, two)):
                high, low = halves(panel.T)
                span = slice(p * group * TILE, (p + 1) * group * TILE)
                right_high[i * PANEL : (i + 1) * PANEL, span] = high
                right_low[i * PANEL : (i + 1) * PANEL, span] = low

    @pl.when(step >= 2)
    def _():
        each_copy(step - 2, lambda copy: copy.wait())

    start = jnp.minimum(2 * step, count - 2)
    lanes = pl.ds(pl.multiple_of(start * TILE, TILE), 2 * TILE)
    right = (right_high[:, lanes], right_low[:, lanes])
    update = product((pair_ref[:, :WIDTH], pair_ref[:, WIDTH:]), right, NN)
    for j, front_ref in enumerate((front_one, front_two)):
        part = update[:, j * TILE : (j + 1) * TILE].reshape(rows, TILE, TILE)
        buffer[slot, j] = front_ref[:, 0, 0, 0] - part
        b = columns[start + j]

        @pl.when(b == 0)
        def _():
            buffer[slot, j] = mine_ref[...]

        @pl.when(b > 0)
        def _():
            @pl.loop(starts[b], starts[b + 1])
            def _(i):
                s, a = order[2 * i], order[2 * i + 1]
                buffer[slot, j, a] = buffer[slot, j, a] + incoming_ref[s, :TILE]

    each_copy(step, lambda copy: copy.start())

    @pl.when(step == steps - 1)
    def _():
        @pl.when(step >= 1)
        def _():
            each_copy(step - 1, lambda copy: copy.wait())

        each_copy(step, lambda copy: copy.wait())


def trailing(front, pieces, columns, places, panels, incoming, order, starts, before):
    rows = front.shape[0]
    pair, mine, small_high, small_low = panels
    group = pieces[0].shape[1]
    count = len(pieces) * group
    steps = (count + 1) // 2

    def strip(j):
        def index(i, columns, *_):
            return (0, 0, columns[jnp.minimum(2 * i, count - 2) + j], 0, 0, 0)

        return pl.BlockSpec((rows, 1, 1, 1, TILE, TILE), index)

    operands = [pair, small_high, small_low, incoming, mine, *pieces]
    in_specs = [strip(0), strip(1), *[whole_spec(a) for a in operands]]
    operands = [front, front, *operands]
    aliases = {}
    if before is not None:
        operands.append(before)
        in_specs.append(pl.BlockSpec(memory_space=pl.ANY))
        aliases = {len(operands) + 3: 0}
    height = rows * TILE
    return pl.pallas_call(
        functools.partial(trailing_kernel, len(pieces)),
        grid_spec=pltpu.PrefetchScalarGridSpec(
            num_scalar_prefetch=4,
            grid=(steps,),
            in_specs=in_specs,
            out_specs=pl.BlockSpec(memory_space=pl.ANY),
            scratch_shapes=[
                pltpu.VMEM((WIDTH, count * TILE), jnp.bfloat16),
                pltpu.VMEM((WIDTH, count * TILE), jnp.bfloat16),
                pltpu.VMEM((2, 2, rows, TILE, TILE), jnp.float32),
                pltpu.SemaphoreType.DMA((2, 2)),
            ],
        ),
        out_shape=jax.ShapeDtypeStruct(front.shape, jnp.float32),
        input_output_aliases=aliases,
        compiler_params=pltpu.CompilerParams(vmem_limit_bytes=VMEM),
        cost_estimate=pl.CostEstimate(
            flops=count * 2 * height * TILE * WIDTH * 3,
            bytes_accessed=count * 2 * height * TILE * 4,
            transcendentals=0,
        ),
        name="trailing",
    )(columns, places, order, starts, *operands)


def spread_lead(lead, n_row, n_col):
    lead = lead + lax.ppermute(
        lead, BOTH, [(r * n_col + c, r * n_col + 1 - c) for r in (2, 3) for c in (0, 1)]
    )
    lead = lead + lax.ppermute(
        lead, BOTH, [(r * n_col + c, (5 - r) * n_col + c) for r in (2, 3) for c in (0, 1)]
    )
    lead = lead + lax.ppermute(
        lead, BOTH, [(r * n_col + c, r * n_col + c + 2) for r in (2, 3) for c in (0, 1)]
    )
    below = lax.ppermute(lead, "row", [(2, 0), (3, 1)])
    for r in range(4, n_row, 2):
        lead = lead + lax.ppermute(lead, "row", [(r - 2, r), (r - 1, r + 1)])
    return lead + below


def body(front, child_tiles, tile_dest, tile_slot, tile_count, diag_inverses):
    n_row = lax.axis_size("row")
    n_col = lax.axis_size("col")
    my_row = lax.axis_index("row").astype(jnp.int32)
    my_col = lax.axis_index("col").astype(jnp.int32)
    rows_here, cols_here = (front.shape[0], front.shape[2])
    slots = child_tiles.shape[0]
    devices = n_row * n_col
    assert n_col == 4 and n_row % 4 == 0 and rows_here % 3 == 0
    place = jnp.stack([my_row, my_col])

    numbers = jnp.arange(slots, dtype=jnp.int32)
    live = numbers < tile_count[0]
    dest = tile_dest[:, 0]
    hits = (dest[None, :] == jnp.arange(devices, dtype=jnp.int32)[:, None]) & live[None, :]
    picked = jnp.sum(jnp.where(hits, numbers[None, :], 0), axis=1)
    slot_out = jnp.sum(jnp.where(hits, tile_slot[None, :] + 1, 0), axis=1) - 1
    notes = jnp.broadcast_to(
        slot_out.astype(jnp.float32)[:, None, None], (devices, NOTE, TILE)
    )
    outgoing = jnp.concatenate([jnp.take(child_tiles, picked, axis=0), notes], axis=1)
    incoming = lax.all_to_all(outgoing, BOTH, split_axis=0, concat_axis=0, tiled=True)
    slot_in = incoming[:, TILE, 0].astype(jnp.int32)
    row_of = jnp.where(slot_in >= 0, slot_in // cols_here, 0)
    col_of = jnp.where(slot_in >= 0, slot_in % cols_here, -1)
    sources = jnp.arange(devices, dtype=jnp.int32)
    key = jnp.where(slot_in >= 0, col_of, cols_here) * devices + sources
    rank = jnp.sum((key[None, :] < key[:, None]).astype(jnp.int32), axis=1)
    at = rank[None, :] == sources[:, None]
    order = jnp.stack(
        [jnp.sum(jnp.where(at, v[None, :], 0), axis=1) for v in (sources, row_of)], axis=1
    ).reshape(-1)
    edges = jnp.arange(cols_here + 1, dtype=jnp.int32) * devices
    starts = jnp.sum((key[None, :] < edges[:, None]).astype(jnp.int32), axis=1)

    ring = rows_here % n_col == 0
    mine, lead, *parts = assemble_columns(
        front, incoming, place, row_of, col_of, n_col if ring else 1
    )

    sets = n_row // n_col
    if ring:
        arrived = []
        for j, part in enumerate(parts):
            pairs = [
                (r * n_col + c, ((r // n_col) * n_col + (c + j) % n_col) * n_col + r % n_col)
                for r in range(n_row)
                for c in range(n_col)
            ]
            arrived.append(lax.ppermute(part, BOTH, pairs))
        piece = jnp.stack(arrived)
        circle = list(range(0, n_row, 2)) + list(range(n_row - 1, 0, -2))
        spot = jnp.asarray([circle.index(r) for r in range(n_row)], jnp.int32)[my_row]
        up = [(circle[i], circle[(i + 1) % n_row]) for i in range(n_row)]
        down = [(b, a) for a, b in up]
        rounds = [[(piece, 0)]]
        ahead = behind = piece
        for step in range(1, n_row // 2):
            ahead = lax.ppermute(ahead, "row", up)
            behind = lax.ppermute(behind, "row", down)
            rounds.append([(ahead, -step), (behind, step)])
        last = jnp.concatenate(
            [lax.ppermute(ahead[:2], "row", up), lax.ppermute(behind[2:], "row", down)]
        )
        rounds.append([(last, n_row // 2)])
        rounds = [rounds[0] + rounds[1]] + rounds[2:]

        def described(shift):
            origin = jnp.asarray(circle, jnp.int32)[(spot + shift + n_row) % n_row]
            part, group = origin % n_col, rows_here // n_col
            row = part * group + jnp.arange(group, dtype=jnp.int32)
            places = (part - jnp.arange(n_col, dtype=jnp.int32) + n_col) % n_col
            return row * sets + origin // n_col, places

    else:
        pairs = [
            (r * n_col + c, ((r // n_col) * n_col + c) * n_col + r % n_col)
            for r in range(n_row)
            for c in range(n_col)
        ]
        moved = lax.all_gather(lax.ppermute(mine, BOTH, pairs), "row", axis=0, tiled=False)
        rounds = [[(moved[h * n_col : (h + 1) * n_col], h)] for h in range(sets)]

        def described(h):
            row = jnp.arange(rows_here, dtype=jnp.int32)
            return row * sets + h, jnp.arange(n_col, dtype=jnp.int32)

    lead = spread_lead(lead, n_row, n_col)
    near = lax.ppermute(mine, "col", [(c, c ^ 1) for c in range(n_col)])
    far = lax.ppermute(mine, "col", [(c, c ^ 2) for c in range(n_col)])
    other = lax.ppermute(far, "col", [(c, c ^ 1) for c in range(n_col)])
    panels = row_panels([mine, near, far, other], lead, diag_inverses, place)

    out = None
    for entries in rounds:
        described_here = [described(shift) for _, shift in entries]
        columns = jnp.concatenate([d[0] for d in described_here])
        places = jnp.concatenate([d[1] for d in described_here])
        pieces = [p for p, _ in entries]
        out = trailing(front, pieces, columns, places, panels, incoming, order, starts, out)
    return out


def solution(mesh):
    return jax.shard_map(
        body,
        mesh=mesh,
        in_specs=(
            P(None, "row", None, "col", None, None),
            P(BOTH, None, None),
            P(BOTH, None),
            P(BOTH),
            P(BOTH),
            P(),
        ),
        out_specs=P(None, "row", None, "col", None, None),
        check_vma=False,
    )
```

```python
import functools

import jax
import jax.numpy as jnp
from jax import lax
from jax.experimental import pallas as pl
from jax.experimental.pallas import tpu as pltpu
from jax.sharding import PartitionSpec as P

TILE = 128
PANEL = 256
WIDTH = 2 * PANEL
NOTE = 8
VMEM = 48 * 1024 * 1024
NT = (((1,), (1,)), ((), ()))
NN = (((1,), (0,)), ((), ()))
BOTH = ("row", "col")


def halves(value):
    high = value.astype(jnp.bfloat16)
    low = (value - high.astype(jnp.float32)).astype(jnp.bfloat16)
    return high, low


def product(left, right, dims):
    dot = functools.partial(
        lax.dot_general, dimension_numbers=dims, preferred_element_type=jnp.float32
    )
    return dot(left[0], right[0]) + (dot(left[0], right[1]) + dot(left[1], right[0]))


def whole_spec(array):
    rank = len(array.shape)
    return pl.BlockSpec(array.shape, lambda *_: (0,) * rank)


def columns_kernel(place, slot_in, front_ref, incoming_ref, out_ref, *rest):
    *parts, tile_ref, sem = rest
    cols = place[2]
    out_ref[...] = front_ref[:, 0, 0, 0]

    @pl.loop(0, incoming_ref.shape[0])
    def _(s):
        slot = slot_in[s]

        @pl.when(jnp.logical_and(slot >= 0, lax.rem(slot, cols) == 0))
        def _():
            copy = pltpu.make_async_copy(incoming_ref.at[s, pl.ds(0, TILE)], tile_ref, sem)
            copy.start()
            copy.wait()
            row = lax.div(slot, cols)
            out_ref[row] = out_ref[row] + tile_ref[...]

    count = len(parts)
    for j, part_ref in enumerate(parts):
        group = part_ref.shape[0]
        part_ref[...] = out_ref[pl.ds(lax.rem(place[1] + j, count) * group, group)]


def assemble_columns(front, incoming, place, slot_in, parts):
    rows = front.shape[0]
    shapes = [(rows, TILE, TILE)] + [(rows // parts, TILE, TILE)] * parts
    out_shape = [jax.ShapeDtypeStruct(shape, jnp.float32) for shape in shapes]
    return pl.pallas_call(
        columns_kernel,
        grid_spec=pltpu.PrefetchScalarGridSpec(
            num_scalar_prefetch=2,
            grid=(1,),
            in_specs=[
                pl.BlockSpec((rows, 1, 1, 1, TILE, TILE), lambda i, *_: (0, 0, 0, 0, 0, 0)),
                pl.BlockSpec(memory_space=pl.ANY),
            ],
            out_specs=[whole_spec(a) for a in out_shape],
            scratch_shapes=[pltpu.VMEM((TILE, TILE), jnp.float32), pltpu.SemaphoreType.DMA],
        ),
        out_shape=out_shape,
        compiler_params=pltpu.CompilerParams(vmem_limit_bytes=VMEM),
        name="panel_columns",
    )(place, slot_in, front, incoming)


def row_panels_kernel(
    place, tiles_ref, lead_ref, diag_ref, pair_ref, out_ref, small_high_ref, small_low_ref
):
    step = pl.program_id(0)
    my_row, my_col = place[0], place[1]
    group = tiles_ref.shape[1]
    height = group * TILE

    @pl.when(step == 0)
    def _():
        inverse_one = halves(diag_ref[0])
        lead = jnp.concatenate(
            [jnp.concatenate([lead_ref[i, 0], lead_ref[i, 1]], axis=1) for i in range(2)], axis=0
        )
        lead = halves(product(halves(lead), inverse_one, NN))
        inverse_two = halves(diag_ref[1])
        for index, pair in enumerate((inverse_one, lead, inverse_two)):
            small_high_ref[index] = pair[0]
            small_low_ref[index] = pair[1]

    small = [(small_high_ref[i], small_low_ref[i]) for i in range(3)]
    columns = [tiles_ref[c].reshape(height, TILE) for c in range(4)]
    tile_row = lax.broadcasted_iota(jnp.int32, (height, PANEL), 0) // TILE
    first = jnp.logical_and(step == 0, tile_row == 0)
    above_one = jnp.logical_and(first, my_row < 2)
    above_two = jnp.logical_and(first, my_row < 4)
    one = product(halves(jnp.concatenate(columns[:2], axis=1)), small[0], NN)
    one_pair = halves(jnp.where(above_one, 0.0, one))
    field = jnp.concatenate(columns[2:], axis=1) - product(one_pair, small[1], NT)
    two = jnp.where(above_one, 0.0, product(halves(field), small[2], NN))
    two_pair = halves(jnp.where(above_two, 0.0, two))
    for i in range(2):
        pair_ref[:, i * WIDTH : i * WIDTH + PANEL] = one_pair[i]
        pair_ref[:, i * WIDTH + PANEL : (i + 1) * WIDTH] = two_pair[i]
    pieces = (one[:, :TILE], one[:, TILE:], two[:, :TILE], two[:, TILE:])
    for c in range(4):

        @pl.when(my_col == c)
        def _():
            out_ref[:, 0, 0, 0] = pieces[c].reshape(group, TILE, TILE)


def row_panels(tiles, lead, diag, place, front):
    rows = tiles.shape[1]
    group = rows // 3
    height = group * TILE
    out_shape = [
        jax.ShapeDtypeStruct((rows * TILE, 2 * WIDTH), jnp.bfloat16),
        jax.ShapeDtypeStruct(front.shape, jnp.float32),
        jax.ShapeDtypeStruct((3, PANEL, PANEL), jnp.bfloat16),
        jax.ShapeDtypeStruct((3, PANEL, PANEL), jnp.bfloat16),
    ]
    return pl.pallas_call(
        row_panels_kernel,
        grid_spec=pltpu.PrefetchScalarGridSpec(
            num_scalar_prefetch=1,
            grid=(3,),
            in_specs=[
                pl.BlockSpec((4, group, TILE, TILE), lambda i, *_: (0, i, 0, 0)),
                whole_spec(lead),
                whole_spec(diag),
            ],
            out_specs=[
                pl.BlockSpec((height, 2 * WIDTH), lambda i, *_: (i, 0)),
                pl.BlockSpec((group, 1, 1, 1, TILE, TILE), lambda i, *_: (i, 0, 0, 0, 0, 0)),
                whole_spec(out_shape[2]),
                whole_spec(out_shape[3]),
            ],
        ),
        out_shape=out_shape,
        compiler_params=pltpu.CompilerParams(vmem_limit_bytes=VMEM),
        name="row_panels",
    )(place, tiles, lead, diag)


def trailing_kernel(
    n_pieces, columns, places, order, starts, front_one, front_two, pair_ref, small_high_ref,
    small_low_ref, incoming_ref, *rest,
):
    piece_refs = rest[:n_pieces]
    out_ref, right_ref, buffer, sems, child_ref, child_sems = rest[-6:]
    step, steps = pl.program_id(0), pl.num_programs(0)
    group = piece_refs[0].shape[1]
    count = n_pieces * group
    rows = front_one.shape[0]
    slot = lax.rem(step, 2)

    def columns_of(at_step):
        for j in range(2):
            index = jnp.minimum(2 * at_step, count - 2) + j
            wanted = columns[index] > 0
            if count % 2 and j == 0:
                wanted = jnp.logical_and(wanted, at_step < steps - 1)
            yield j, columns[index], wanted

    def each_copy(at_step, act):
        at_slot = lax.rem(at_step, 2)
        for j, b, wanted in columns_of(at_step):

            @pl.when(wanted)
            def _():
                act(
                    pltpu.make_async_copy(
                        buffer.at[at_slot, j], out_ref.at[:, 0, b, 0], sems.at[at_slot, j]
                    )
                )

    def child_copy(s):
        return pltpu.make_async_copy(
            incoming_ref.at[s, pl.ds(0, TILE)], child_ref.at[s], child_sems.at[s]
        )

    @pl.when(step == 0)
    def _():
        for t in range(count):
            b = columns[t]

            @pl.when(b > 0)
            def _():
                @pl.loop(starts[b], starts[b + 1])
                def _(i):
                    child_copy(order[2 * i]).start()

        small = [(small_high_ref[i], small_low_ref[i]) for i in range(3)]
        for p, piece in enumerate(piece_refs):
            columns_here = [piece[places[4 * p + c]].reshape(group * TILE, TILE) for c in range(4)]
            one = product(halves(jnp.concatenate(columns_here[:2], axis=1)), small[0], NN)
            field = jnp.concatenate(columns_here[2:], axis=1)
            field = field - product(halves(one), small[1], NT)
            two = product(halves(field), small[2], NN)
            span = slice(p * group * TILE, (p + 1) * group * TILE)
            for i, panel in enumerate((one, two)):
                for k, half in enumerate(halves(panel.T)):
                    top = 2 * k * WIDTH + i * PANEL
                    right_ref[top : top + PANEL, span] = half
                    if k == 0:
                        right_ref[top + WIDTH : top + WIDTH + PANEL, span] = half

    @pl.when(step >= 2)
    def _():
        each_copy(step - 2, lambda copy: copy.wait())

    start = jnp.minimum(2 * step, count - 2)
    lanes = pl.ds(pl.multiple_of(start * TILE, TILE), 2 * TILE)
    block = rows // 3
    for m in range(3):
        left = pair_ref[m * block * TILE : (m + 1) * block * TILE]
        left = jnp.concatenate([left, left[:, :WIDTH]], axis=1)
        update = jnp.dot(left, right_ref[:, lanes], preferred_element_type=jnp.float32)
        span = slice(m * block, (m + 1) * block)
        for j, front_ref in enumerate((front_one, front_two)):
            part = update[:, j * TILE : (j + 1) * TILE].reshape(block, TILE, TILE)
            buffer[slot, j, span] = front_ref[span, 0, 0, 0] - part

    for j, b, wanted in columns_of(step):

        @pl.when(wanted)
        def _():
            @pl.loop(starts[b], starts[b + 1])
            def _(i):
                s, a = order[2 * i], order[2 * i + 1]
                child_copy(s).wait()
                buffer[slot, j, a] = buffer[slot, j, a] + child_ref[s]

    each_copy(step, lambda copy: copy.start())

    @pl.when(step == steps - 1)
    def _():
        if count > 2:
            each_copy(step - 1, lambda copy: copy.wait())
        each_copy(step, lambda copy: copy.wait())


def trailing(front, pieces, columns, places, panels, incoming, order, starts):
    rows = front.shape[0]
    pair, out, small_high, small_low = panels
    group = pieces[0].shape[1]
    count = len(pieces) * group
    steps = (count + 1) // 2

    def strip(j):
        def index(i, columns, *_):
            return (0, 0, columns[jnp.minimum(2 * i, count - 2) + j], 0, 0, 0)

        return pl.BlockSpec((rows, 1, 1, 1, TILE, TILE), index)

    anywhere = pl.BlockSpec(memory_space=pl.ANY)
    operands = [front, front, pair, small_high, small_low, incoming, *pieces, out]
    in_specs = [strip(0), strip(1), *[whole_spec(a) for a in operands[2:5]], anywhere]
    in_specs += [*[whole_spec(a) for a in pieces], anywhere]
    height = rows * TILE
    devices = incoming.shape[0]
    return pl.pallas_call(
        functools.partial(trailing_kernel, len(pieces)),
        grid_spec=pltpu.PrefetchScalarGridSpec(
            num_scalar_prefetch=4,
            grid=(steps,),
            in_specs=in_specs,
            out_specs=anywhere,
            scratch_shapes=[
                pltpu.VMEM((3 * WIDTH, count * TILE), jnp.bfloat16),
                pltpu.VMEM((2, 2, rows, TILE, TILE), jnp.float32),
                pltpu.SemaphoreType.DMA((2, 2)),
                pltpu.VMEM((devices, TILE, TILE), jnp.float32),
                pltpu.SemaphoreType.DMA((devices,)),
            ],
        ),
        out_shape=jax.ShapeDtypeStruct(front.shape, jnp.float32),
        input_output_aliases={len(operands) + 3: 0},
        compiler_params=pltpu.CompilerParams(vmem_limit_bytes=VMEM),
        cost_estimate=pl.CostEstimate(
            flops=count * 2 * height * TILE * WIDTH * 3,
            bytes_accessed=count * 2 * height * TILE * 4,
            transcendentals=0,
        ),
        name="trailing",
    )(columns, places, order, starts, *operands)


def body(front, child_tiles, tile_dest, tile_slot, tile_count, diag_inverses):
    n_row = lax.axis_size("row")
    n_col = lax.axis_size("col")
    my_row = lax.axis_index("row").astype(jnp.int32)
    my_col = lax.axis_index("col").astype(jnp.int32)
    rows_here, cols_here = (front.shape[0], front.shape[2])
    slots = child_tiles.shape[0]
    devices = n_row * n_col
    assert n_col == 4 and n_row % 4 == 0 and rows_here % 3 == 0
    place = jnp.stack([my_row, my_col, jnp.int32(cols_here)])

    numbers = jnp.arange(slots, dtype=jnp.int32)
    live = numbers < tile_count[0]
    dest = tile_dest[:, 0]
    hits = (dest[None, :] == jnp.arange(devices, dtype=jnp.int32)[:, None]) & live[None, :]
    picked = jnp.sum(jnp.where(hits, numbers[None, :], 0), axis=1)
    slot_out = jnp.sum(jnp.where(hits, tile_slot[None, :] + 1, 0), axis=1) - 1
    notes = jnp.broadcast_to(
        slot_out.astype(jnp.float32)[:, None, None], (devices, NOTE, TILE)
    )
    taken = jnp.take(child_tiles, picked, axis=0)
    outgoing = jnp.concatenate([taken, notes], axis=1)
    incoming = lax.all_to_all(outgoing, BOTH, split_axis=0, concat_axis=0, tiled=True)
    slot_in = lax.optimization_barrier(incoming[:, TILE, 0].astype(jnp.int32))

    me = my_row * n_col + my_col
    lead = []
    for owner in [r * n_col + c for r in (2, 3) for c in (0, 1)]:
        own = jnp.where(me == owner, front[0, 0, 0, 0], 0.0)
        lead.append(own + jnp.where(slot_out[owner] == 0, taken[owner], 0.0))
    lead = lax.psum(jnp.stack(lead).reshape(2, 2, TILE, TILE), BOTH)

    row_of = jnp.where(slot_in >= 0, slot_in // cols_here, 0)
    col_of = jnp.where(slot_in >= 0, slot_in % cols_here, -1)
    sources = jnp.arange(devices, dtype=jnp.int32)
    key = jnp.where(slot_in >= 0, col_of, cols_here) * devices + sources
    rank = jnp.sum((key[None, :] < key[:, None]).astype(jnp.int32), axis=1)
    at = rank[None, :] == sources[:, None]
    order = jnp.stack(
        [jnp.sum(jnp.where(at, v[None, :], 0), axis=1) for v in (sources, row_of)], axis=1
    ).reshape(-1)
    edges = jnp.arange(cols_here + 1, dtype=jnp.int32) * devices
    starts = jnp.sum((key[None, :] < edges[:, None]).astype(jnp.int32), axis=1)

    ring = rows_here % n_col == 0
    mine, *parts = assemble_columns(front, incoming, place, slot_in, n_col if ring else 1)
    tiles = lax.all_gather(mine, "col", axis=0, tiled=False)

    sets = n_row // n_col
    if ring:
        arrived = []
        for j, part in enumerate(parts):
            pairs = [
                (r * n_col + c, ((r // n_col) * n_col + (c + j) % n_col) * n_col + r % n_col)
                for r in range(n_row)
                for c in range(n_col)
            ]
            arrived.append(lax.ppermute(part, BOTH, pairs))
        piece = jnp.stack(arrived)
        circle = list(range(0, n_row, 2)) + list(range(n_row - 1, 0, -2))
        spot = jnp.asarray([circle.index(r) for r in range(n_row)], jnp.int32)[my_row]
        up = [(circle[i], circle[(i + 1) % n_row]) for i in range(n_row)]
        down = [(b, a) for a, b in up]
        rounds = [[(piece, 0)]]
        ahead = behind = piece
        for step in range(1, n_row // 2):
            ahead = lax.ppermute(ahead, "row", up)
            behind = lax.ppermute(behind, "row", down)
            rounds.append([(ahead, -step), (behind, step)])
        last = jnp.concatenate(
            [lax.ppermute(ahead[:2], "row", up), lax.ppermute(behind[2:], "row", down)]
        )
        rounds.append([(last, n_row // 2)])
        rounds = [rounds[0] + rounds[1]] + rounds[2:]

        def described(shift):
            origin = jnp.asarray(circle, jnp.int32)[(spot + shift + n_row) % n_row]
            part, group = origin % n_col, rows_here // n_col
            row = part * group + jnp.arange(group, dtype=jnp.int32)
            places = (part - jnp.arange(n_col, dtype=jnp.int32) + n_col) % n_col
            return row * sets + origin // n_col, places

    else:
        pairs = [
            (r * n_col + c, ((r // n_col) * n_col + c) * n_col + r % n_col)
            for r in range(n_row)
            for c in range(n_col)
        ]
        moved = lax.all_gather(lax.ppermute(mine, BOTH, pairs), "row", axis=0, tiled=False)
        rounds = [[(moved[h * n_col : (h + 1) * n_col], h)] for h in range(sets)]

        def described(h):
            row = jnp.arange(rows_here, dtype=jnp.int32)
            return row * sets + h, jnp.arange(n_col, dtype=jnp.int32)

    panels = row_panels(tiles, lead, diag_inverses, place, front)
    for entries in rounds:
        described_here = [described(shift) for _, shift in entries]
        columns = jnp.concatenate([d[0] for d in described_here])
        places = jnp.concatenate([d[1] for d in described_here])
        pieces = [p for p, _ in entries]
        out = trailing(front, pieces, columns, places, panels, incoming, order, starts)
        panels = [panels[0], out, *panels[2:]]
    return panels[1]


def solution(mesh):
    return jax.shard_map(
        body,
        mesh=mesh,
        in_specs=(
            P(None, "row", None, "col", None, None),
            P(BOTH, None, None),
            P(BOTH, None),
            P(BOTH),
            P(BOTH),
            P(),
        ),
        out_specs=P(None, "row", None, "col", None, None),
        check_vma=False,
    )
```

```python
import functools

import jax
import jax.numpy as jnp
from jax import lax
from jax.experimental import pallas as pl
from jax.experimental.pallas import tpu as pltpu
from jax.sharding import PartitionSpec as P

TILE = 128
PANEL = 256
WIDTH = 2 * PANEL
NOTE = 8
VMEM = 30 * 1024 * 1024
BOTH = ("row", "col")


def halves(value):
    high = value.astype(jnp.bfloat16)
    low = (value - high.astype(jnp.float32)).astype(jnp.bfloat16)
    return high, low


def deep(value):
    high, low = halves(value)
    return jnp.concatenate([high, low, high], axis=1)


def stacked(value):
    high, low = halves(value)
    return jnp.concatenate([high, high, low], axis=0)


def dot(left, right):
    return jnp.dot(left, right, preferred_element_type=jnp.float32)


def two_panels(columns, small_ref, mask):
    one = mask(0, dot(deep(jnp.concatenate(columns[:2], axis=1)), small_ref[0]))
    field = jnp.concatenate(columns[2:], axis=1) - dot(deep(mask(1, one)), small_ref[1])
    return one, mask(1, dot(deep(field), small_ref[2]))


def whole_spec(array):
    rank = len(array.shape)
    return pl.BlockSpec(array.shape, lambda *_: (0,) * rank)


def columns_kernel(place, slot_in, front_ref, incoming_ref, out_ref, *rest):
    *parts, tile_ref, sem = rest
    cols = place[2]
    out_ref[...] = front_ref[:, 0, 0, 0]

    @pl.loop(0, incoming_ref.shape[0])
    def _(s):
        slot = slot_in[s]

        @pl.when(jnp.logical_and(slot >= 0, lax.rem(slot, cols) == 0))
        def _():
            copy = pltpu.make_async_copy(incoming_ref.at[s, pl.ds(0, TILE)], tile_ref, sem)
            copy.start()
            copy.wait()
            row = lax.div(slot, cols)
            out_ref[row] = out_ref[row] + tile_ref[...]

    count = len(parts)
    for j, part_ref in enumerate(parts):
        group = part_ref.shape[0]
        part_ref[...] = out_ref[pl.ds(lax.rem(place[1] + j, count) * group, group)]


def assemble_columns(front, incoming, place, slot_in, parts):
    rows = front.shape[0]
    shapes = [(rows, TILE, TILE)] + [(rows // parts, TILE, TILE)] * parts
    out_shape = [jax.ShapeDtypeStruct(shape, jnp.float32) for shape in shapes]
    return pl.pallas_call(
        columns_kernel,
        grid_spec=pltpu.PrefetchScalarGridSpec(
            num_scalar_prefetch=2,
            grid=(1,),
            in_specs=[
                pl.BlockSpec((rows, 1, 1, 1, TILE, TILE), lambda i, *_: (0, 0, 0, 0, 0, 0)),
                pl.BlockSpec(memory_space=pl.ANY),
            ],
            out_specs=[whole_spec(a) for a in out_shape],
            scratch_shapes=[pltpu.VMEM((TILE, TILE), jnp.float32), pltpu.SemaphoreType.DMA],
        ),
        out_shape=out_shape,
        compiler_params=pltpu.CompilerParams(vmem_limit_bytes=VMEM),
        name="panel_columns",
    )(place, slot_in, front, incoming)


def row_panels_kernel(
    place, t0, t1, t2, t3, lead_ref, diag_ref, pair_ref, out_ref, small_ref, tiles_ref
):
    step = pl.program_id(0)
    my_row, my_col = place[0], place[1]
    group = t0.shape[0]
    height = group * TILE

    @pl.when(step == 0)
    def _():
        small_ref[0] = stacked(diag_ref[0])
        lead = jnp.concatenate(
            [jnp.concatenate([lead_ref[i, 0], lead_ref[i, 1]], axis=1) for i in range(2)], axis=0
        )
        small_ref[1] = stacked(dot(deep(lead), small_ref[0]).T)
        small_ref[2] = stacked(diag_ref[1])

    for i, tile_ref in enumerate((t0, t1, t2, t3)):
        tiles_ref[jnp.bitwise_xor(my_col, i)] = tile_ref[...]
    columns = [tiles_ref[c].reshape(height, TILE) for c in range(4)]
    tile_row = lax.broadcasted_iota(jnp.int32, (height, PANEL), 0) // TILE
    first = jnp.logical_and(step == 0, tile_row == 0)

    def mask(panels_above, value):
        above = jnp.logical_and(first, my_row < 2 * panels_above)
        return jnp.where(above, 0.0, value) if panels_above else value

    one, two = two_panels(columns, small_ref, mask)
    pair_ref[:, :PANEL], pair_ref[:, WIDTH : WIDTH + PANEL] = halves(mask(1, one))
    pair_ref[:, PANEL:WIDTH], pair_ref[:, WIDTH + PANEL :] = halves(mask(2, two))
    pieces = (one[:, :TILE], one[:, TILE:], two[:, :TILE], two[:, TILE:])
    for c in range(4):

        @pl.when(my_col == c)
        def _():
            out_ref[:, 0, 0, 0] = pieces[c].reshape(group, TILE, TILE)


def row_panels(tiles, lead, diag, place, front):
    rows = front.shape[0]
    group = rows // 3
    height = group * TILE
    out_shape = [
        jax.ShapeDtypeStruct((rows * TILE, 2 * WIDTH), jnp.bfloat16),
        jax.ShapeDtypeStruct(front.shape, jnp.float32),
        jax.ShapeDtypeStruct((3, 3 * PANEL, PANEL), jnp.bfloat16),
    ]
    strip = pl.BlockSpec((group, TILE, TILE), lambda i, *_: (i, 0, 0))
    return pl.pallas_call(
        row_panels_kernel,
        grid_spec=pltpu.PrefetchScalarGridSpec(
            num_scalar_prefetch=1,
            grid=(3,),
            in_specs=[strip] * 4 + [whole_spec(lead), whole_spec(diag)],
            out_specs=[
                pl.BlockSpec((height, 2 * WIDTH), lambda i, *_: (i, 0)),
                pl.BlockSpec((group, 1, 1, 1, TILE, TILE), lambda i, *_: (i, 0, 0, 0, 0, 0)),
                whole_spec(out_shape[2]),
            ],
            scratch_shapes=[pltpu.VMEM((4, group, TILE, TILE), jnp.float32)],
        ),
        out_shape=out_shape,
        compiler_params=pltpu.CompilerParams(vmem_limit_bytes=VMEM),
        name="row_panels",
    )(place, *tiles, lead, diag)


def trailing_kernel(n_pieces, columns, places, order, starts, pair_ref, small_ref, *rest):
    piece_refs = rest[:n_pieces]
    front_ref, incoming_ref, _, out_ref, right_ref, taken, given, child_ref = rest[n_pieces:-3]
    take_sems, give_sems, child_sems = rest[-3:]
    group = piece_refs[0].shape[1]
    count = n_pieces * group
    steps = (count + 1) // 2
    rows = front_ref.shape[0]

    def columns_of(step):
        for j in range(2):
            index = jnp.minimum(2 * step, count - 2) + j
            wanted = columns[index] > 0
            if count % 2 and j == 0:
                wanted = jnp.logical_and(wanted, step < steps - 1)
            yield j, columns[index], wanted

    def each_take(step, act):
        slot = lax.rem(step, 2)
        for j, b, wanted in columns_of(step):

            @pl.when(wanted)
            def _():
                act(
                    pltpu.make_async_copy(
                        front_ref.at[:, 0, b, 0], taken.at[slot, j], take_sems.at[slot, j]
                    )
                )

    def each_give(step, act):
        slot = lax.rem(step, 2)
        for j, b, wanted in columns_of(step):

            @pl.when(wanted)
            def _():
                act(
                    pltpu.make_async_copy(
                        given.at[slot, j], out_ref.at[:, 0, b, 0], give_sems.at[slot, j]
                    )
                )

    def each_child(step, act):
        for j, b, wanted in columns_of(step):

            @pl.when(wanted)
            def _():
                @pl.loop(starts[b], starts[b + 1])
                def _(i):
                    s = order[2 * i]
                    copy = pltpu.make_async_copy(
                        incoming_ref.at[s, pl.ds(0, TILE)], child_ref.at[s], child_sems.at[s]
                    )
                    act(copy, j, s, order[2 * i + 1])

    for step in range(min(steps, 2)):
        each_take(step, lambda copy: copy.start())
    for step in range(steps):
        each_child(step, lambda copy, *_: copy.start())

    tile_columns = [
        jnp.concatenate(
            [
                piece[places[4 * p + c]].reshape(group * TILE, TILE)
                for p, piece in enumerate(piece_refs)
            ],
            axis=0,
        )
        for c in range(4)
    ]
    for i, panel in enumerate(two_panels(tile_columns, small_ref, lambda _, value: value)):
        high, low = halves(panel.T)
        for k, half in enumerate((high, high, low)):
            right_ref[k * WIDTH + i * PANEL : k * WIDTH + (i + 1) * PANEL] = half

    @pl.loop(0, steps)
    def _(step):
        slot = lax.rem(step, 2)
        each_take(step, lambda copy: copy.wait())

        @pl.when(step >= 2)
        def _():
            each_give(step - 2, lambda copy: copy.wait())

        start = jnp.minimum(2 * step, count - 2)
        lanes = pl.ds(pl.multiple_of(start * TILE, TILE), 2 * TILE)
        block = rows // 3
        for m in range(3):
            left = pair_ref[m * block * TILE : (m + 1) * block * TILE]
            update = dot(jnp.concatenate([left, left[:, :WIDTH]], axis=1), right_ref[:, lanes])
            span = slice(m * block, (m + 1) * block)
            for j in range(2):
                part = update[:, j * TILE : (j + 1) * TILE].reshape(block, TILE, TILE)
                given[slot, j, span] = taken[slot, j, span] - part

        def add(copy, j, s, a):
            copy.wait()
            given[slot, j, a] = given[slot, j, a] + child_ref[s]

        each_child(step, add)
        each_give(step, lambda copy: copy.start())

        @pl.when(step + 2 < steps)
        def _():
            each_take(step + 2, lambda copy: copy.start())

    for step in range(max(steps - 2, 0), steps):
        each_give(step, lambda copy: copy.wait())


def trailing(front, pieces, columns, places, panels, incoming, order, starts):
    rows = front.shape[0]
    pair, out, small = panels
    group = pieces[0].shape[1]
    count = len(pieces) * group
    scalars = [columns, places, order, starts]
    held = [pair, small, *pieces]
    distant = [front, incoming, out]
    spec = lambda space, n: [pl.BlockSpec(memory_space=space)] * n
    height = rows * TILE
    devices = incoming.shape[0]
    return pl.pallas_call(
        functools.partial(trailing_kernel, len(pieces)),
        in_specs=spec(pltpu.SMEM, 4) + spec(pltpu.VMEM, len(held)) + spec(pl.ANY, 3),
        out_specs=pl.BlockSpec(memory_space=pl.ANY),
        scratch_shapes=[
            pltpu.VMEM((3 * WIDTH, count * TILE), jnp.bfloat16),
            pltpu.VMEM((2, 2, rows, TILE, TILE), jnp.float32),
            pltpu.VMEM((2, 2, rows, TILE, TILE), jnp.float32),
            pltpu.VMEM((devices, TILE, TILE), jnp.float32),
            pltpu.SemaphoreType.DMA((2, 2)),
            pltpu.SemaphoreType.DMA((2, 2)),
            pltpu.SemaphoreType.DMA((devices,)),
        ],
        out_shape=jax.ShapeDtypeStruct(front.shape, jnp.float32),
        input_output_aliases={len(held) + 6: 0},
        compiler_params=pltpu.CompilerParams(vmem_limit_bytes=VMEM),
        cost_estimate=pl.CostEstimate(
            flops=count * 2 * height * TILE * WIDTH * 3,
            bytes_accessed=count * 2 * height * TILE * 4,
            transcendentals=0,
        ),
        name="trailing",
    )(*scalars, *held, *distant)


def body(front, child_tiles, tile_dest, tile_slot, tile_count, diag_inverses):
    n_row = lax.axis_size("row")
    n_col = lax.axis_size("col")
    my_row = lax.axis_index("row").astype(jnp.int32)
    my_col = lax.axis_index("col").astype(jnp.int32)
    rows_here, cols_here = (front.shape[0], front.shape[2])
    slots = child_tiles.shape[0]
    devices = n_row * n_col
    assert n_col == 4 and n_row % 4 == 0 and rows_here % 3 == 0
    place = jnp.stack([my_row, my_col, jnp.int32(cols_here)])

    numbers = jnp.arange(slots, dtype=jnp.int32)
    live = numbers < tile_count[0]
    dest = tile_dest[:, 0]
    hits = (dest[None, :] == jnp.arange(devices, dtype=jnp.int32)[:, None]) & live[None, :]
    picked = jnp.sum(jnp.where(hits, numbers[None, :], 0), axis=1)
    slot_out = jnp.sum(jnp.where(hits, tile_slot[None, :] + 1, 0), axis=1) - 1
    notes = jnp.broadcast_to(
        slot_out.astype(jnp.float32)[:, None, None], (devices, NOTE, TILE)
    )
    outgoing = jnp.concatenate([jnp.take(child_tiles, picked, axis=0), notes], axis=1)
    incoming = lax.all_to_all(outgoing, BOTH, split_axis=0, concat_axis=0, tiled=True)
    slot_in = lax.optimization_barrier(incoming[:, TILE, 0].astype(jnp.int32))

    row_of = jnp.where(slot_in >= 0, slot_in // cols_here, 0)
    col_of = jnp.where(slot_in >= 0, slot_in % cols_here, -1)
    sources = jnp.arange(devices, dtype=jnp.int32)
    key = jnp.where(slot_in >= 0, col_of, cols_here) * devices + sources
    rank = jnp.sum((key[None, :] < key[:, None]).astype(jnp.int32), axis=1)
    at = rank[None, :] == sources[:, None]
    order = jnp.stack(
        [jnp.sum(jnp.where(at, v[None, :], 0), axis=1) for v in (sources, row_of)], axis=1
    ).reshape(-1)
    edges = jnp.arange(cols_here + 1, dtype=jnp.int32) * devices
    starts = jnp.sum((key[None, :] < edges[:, None]).astype(jnp.int32), axis=1)

    ring = rows_here % n_col == 0
    mine, *parts = assemble_columns(front, incoming, place, slot_in, n_col if ring else 1)

    sets = n_row // n_col
    if ring:
        arrived = []
        for j, part in enumerate(parts):
            pairs = [
                (r * n_col + c, ((r // n_col) * n_col + (c + j) % n_col) * n_col + r % n_col)
                for r in range(n_row)
                for c in range(n_col)
            ]
            arrived.append(lax.ppermute(part, BOTH, pairs))
        piece = jnp.stack(arrived)
        circle = list(range(0, n_row, 2)) + list(range(n_row - 1, 0, -2))
        spot = jnp.asarray([circle.index(r) for r in range(n_row)], jnp.int32)[my_row]
        up = [(circle[i], circle[(i + 1) % n_row]) for i in range(n_row)]
        down = [(b, a) for a, b in up]
        rounds = [[(piece, 0)]]
        ahead = behind = piece
        for step in range(1, n_row // 2):
            ahead = lax.ppermute(ahead, "row", up)
            behind = lax.ppermute(behind, "row", down)
            rounds.append([(ahead, -step), (behind, step)])
        last = jnp.concatenate(
            [lax.ppermute(ahead[:2], "row", up), lax.ppermute(behind[2:], "row", down)]
        )
        rounds.append([(last, n_row // 2)])
        rounds = [rounds[0] + rounds[1]] + rounds[2:]

        def described(shift):
            origin = jnp.asarray(circle, jnp.int32)[(spot + shift + n_row) % n_row]
            part, group = origin % n_col, rows_here // n_col
            row = part * group + jnp.arange(group, dtype=jnp.int32)
            places = (part - jnp.arange(n_col, dtype=jnp.int32) + n_col) % n_col
            return row * sets + origin // n_col, places

    else:
        pairs = [
            (r * n_col + c, ((r // n_col) * n_col + c) * n_col + r % n_col)
            for r in range(n_row)
            for c in range(n_col)
        ]
        moved = lax.all_gather(lax.ppermute(mine, BOTH, pairs), "row", axis=0, tiled=False)
        rounds = [[(moved[h * n_col : (h + 1) * n_col], h)] for h in range(sets)]

        def described(h):
            row = jnp.arange(rows_here, dtype=jnp.int32)
            return row * sets + h, jnp.arange(n_col, dtype=jnp.int32)

    owners = [r * n_col + c for r in (2, 3) for c in (0, 1)]
    slices = lax.all_to_all(
        mine[0].reshape(devices, TILE // devices, TILE), BOTH, split_axis=0, concat_axis=0, tiled=True
    )
    own = jnp.stack([slices[owner] for owner in owners])
    own = jnp.broadcast_to(own[None], (devices,) + own.shape)
    lead = lax.all_to_all(own, BOTH, split_axis=0, concat_axis=0, tiled=True)
    lead = lead.transpose(1, 0, 2, 3).reshape(2, 2, TILE, TILE)

    near = lax.ppermute(mine, "col", [(c, c ^ 1) for c in range(n_col)])
    far = lax.ppermute(mine, "col", [(c, c ^ 2) for c in range(n_col)])
    other = lax.ppermute(far, "col", [(c, c ^ 1) for c in range(n_col)])
    panels = row_panels([mine, near, far, other], lead, diag_inverses, place, front)

    for entries in rounds:
        described_here = [described(shift) for _, shift in entries]
        columns = jnp.concatenate([d[0] for d in described_here])
        places = jnp.concatenate([d[1] for d in described_here])
        pieces = [p for p, _ in entries]
        out = trailing(front, pieces, columns, places, panels, incoming, order, starts)
        panels = [panels[0], out, panels[2]]
    return panels[1]


def solution(mesh):
    return jax.shard_map(
        body,
        mesh=mesh,
        in_specs=(
            P(None, "row", None, "col", None, None),
            P(BOTH, None, None),
            P(BOTH, None),
            P(BOTH),
            P(BOTH),
            P(),
        ),
        out_specs=P(None, "row", None, "col", None, None),
        check_vma=False,
    )
```

```python
import functools

import jax
import jax.numpy as jnp
from jax import lax
from jax.experimental import pallas as pl
from jax.experimental.pallas import tpu as pltpu
from jax.sharding import PartitionSpec as P

TILE = 128
PANEL = 256
WIDTH = 2 * PANEL
NOTE = 8
VMEM = 30 * 1024 * 1024
BOTH = ("row", "col")


def halves(value):
    high = value.astype(jnp.bfloat16)
    low = (value - high.astype(jnp.float32)).astype(jnp.bfloat16)
    return high, low


def deep(value):
    high, low = halves(value)
    return jnp.concatenate([high, low, high], axis=1)


def stacked(value):
    high, low = halves(value)
    return jnp.concatenate([high, high, low], axis=0)


def dot(left, right):
    return jnp.dot(left, right, preferred_element_type=jnp.float32)


def two_panels(columns, small_ref, mask):
    one = mask(0, dot(deep(jnp.concatenate(columns[:2], axis=1)), small_ref[0]))
    field = jnp.concatenate(columns[2:], axis=1) - dot(deep(mask(1, one)), small_ref[1])
    return one, mask(1, dot(deep(field), small_ref[2]))


def whole_spec(array):
    rank = len(array.shape)
    return pl.BlockSpec(array.shape, lambda *_: (0,) * rank)


def pack_kernel(dest, slot, count, child_ref, out_ref, notes_ref, sems, notes_sem):
    slots = child_ref.shape[0]

    def copy(k):
        return pltpu.make_async_copy(
            child_ref.at[k], out_ref.at[dest[k], pl.ds(0, TILE)], sems.at[k]
        )

    notes_ref[...] = jnp.full_like(notes_ref, -1.0)
    live = jnp.minimum(count[0], slots)

    @pl.loop(0, live)
    def _(k):
        copy(k).start()
        notes_ref[dest[k]] = jnp.full(notes_ref.shape[1:], slot[k].astype(jnp.float32))

    notes = pltpu.make_async_copy(notes_ref, out_ref.at[:, pl.ds(TILE, NOTE)], notes_sem)
    notes.start()
    notes.wait()

    @pl.loop(0, live)
    def _(k):
        copy(k).wait()


def pack(child_tiles, dest, slot, count, devices):
    slots = child_tiles.shape[0]
    hbm = pl.BlockSpec(memory_space=pltpu.HBM)
    return pl.pallas_call(
        pack_kernel,
        in_specs=[pl.BlockSpec(memory_space=pltpu.SMEM)] * 3 + [hbm],
        out_specs=hbm,
        scratch_shapes=[
            pltpu.VMEM((devices, NOTE, TILE), jnp.float32),
            pltpu.SemaphoreType.DMA((slots,)),
            pltpu.SemaphoreType.DMA,
        ],
        out_shape=jax.ShapeDtypeStruct((devices, TILE + NOTE, TILE), jnp.float32),
        name="pack",
    )(dest, slot, count, child_tiles)


def columns_kernel(place, slot_in, front_ref, incoming_ref, out_ref, *rest):
    *parts, tile_ref, sem = rest
    cols = place[2]
    out_ref[...] = front_ref[:, 0, 0, 0]

    @pl.loop(0, incoming_ref.shape[0])
    def _(s):
        slot = slot_in[s]

        @pl.when(jnp.logical_and(slot >= 0, lax.rem(slot, cols) == 0))
        def _():
            copy = pltpu.make_async_copy(incoming_ref.at[s, pl.ds(0, TILE)], tile_ref, sem)
            copy.start()
            copy.wait()
            row = lax.div(slot, cols)
            out_ref[row] = out_ref[row] + tile_ref[...]

    count = len(parts)
    for j, part_ref in enumerate(parts):
        group = part_ref.shape[0]
        part_ref[...] = out_ref[pl.ds(lax.rem(place[1] + j, count) * group, group)]


def assemble_columns(front, incoming, place, slot_in, parts):
    rows = front.shape[0]
    shapes = [(rows, TILE, TILE)] + [(rows // parts, TILE, TILE)] * parts
    out_shape = [jax.ShapeDtypeStruct(shape, jnp.float32) for shape in shapes]
    return pl.pallas_call(
        columns_kernel,
        grid_spec=pltpu.PrefetchScalarGridSpec(
            num_scalar_prefetch=2,
            grid=(1,),
            in_specs=[
                pl.BlockSpec((rows, 1, 1, 1, TILE, TILE), lambda i, *_: (0, 0, 0, 0, 0, 0)),
                pl.BlockSpec(memory_space=pltpu.HBM),
            ],
            out_specs=[whole_spec(a) for a in out_shape],
            scratch_shapes=[pltpu.VMEM((TILE, TILE), jnp.float32), pltpu.SemaphoreType.DMA],
        ),
        out_shape=out_shape,
        compiler_params=pltpu.CompilerParams(vmem_limit_bytes=VMEM),
        name="panel_columns",
    )(place, slot_in, front, incoming)


def row_panels_kernel(
    place, t0, t1, t2, t3, lead_ref, diag_ref, pair_ref, out_ref, small_ref, tiles_ref
):
    step = pl.program_id(0)
    my_row, my_col = place[0], place[1]
    group = t0.shape[0]
    height = group * TILE

    @pl.when(step == 0)
    def _():
        small_ref[0] = stacked(diag_ref[0])
        lead = jnp.concatenate(
            [jnp.concatenate([lead_ref[i, 0], lead_ref[i, 1]], axis=1) for i in range(2)], axis=0
        )
        small_ref[1] = stacked(dot(deep(lead), small_ref[0]).T)
        small_ref[2] = stacked(diag_ref[1])

    for i, tile_ref in enumerate((t0, t1, t2, t3)):
        tiles_ref[jnp.bitwise_xor(my_col, i)] = tile_ref[...]
    columns = [tiles_ref[c].reshape(height, TILE) for c in range(4)]
    tile_row = lax.broadcasted_iota(jnp.int32, (height, PANEL), 0) // TILE
    first = jnp.logical_and(step == 0, tile_row == 0)

    def mask(panels_above, value):
        above = jnp.logical_and(first, my_row < 2 * panels_above)
        return jnp.where(above, 0.0, value) if panels_above else value

    one, two = two_panels(columns, small_ref, mask)
    pair_ref[:, :PANEL], pair_ref[:, WIDTH : WIDTH + PANEL] = halves(mask(1, one))
    pair_ref[:, PANEL:WIDTH], pair_ref[:, WIDTH + PANEL :] = halves(mask(2, two))
    pieces = (one[:, :TILE], one[:, TILE:], two[:, :TILE], two[:, TILE:])
    for c in range(4):

        @pl.when(my_col == c)
        def _():
            out_ref[:, 0, 0, 0] = pieces[c].reshape(group, TILE, TILE)


def row_panels(tiles, lead, diag, place, front):
    rows = front.shape[0]
    group = rows // 3
    height = group * TILE
    out_shape = [
        jax.ShapeDtypeStruct((rows * TILE, 2 * WIDTH), jnp.bfloat16),
        jax.ShapeDtypeStruct(front.shape, jnp.float32),
        jax.ShapeDtypeStruct((3, 3 * PANEL, PANEL), jnp.bfloat16),
    ]
    strip = pl.BlockSpec((group, TILE, TILE), lambda i, *_: (i, 0, 0))
    return pl.pallas_call(
        row_panels_kernel,
        grid_spec=pltpu.PrefetchScalarGridSpec(
            num_scalar_prefetch=1,
            grid=(3,),
            in_specs=[strip] * 4 + [whole_spec(lead), whole_spec(diag)],
            out_specs=[
                pl.BlockSpec((height, 2 * WIDTH), lambda i, *_: (i, 0)),
                pl.BlockSpec((group, 1, 1, 1, TILE, TILE), lambda i, *_: (i, 0, 0, 0, 0, 0)),
                whole_spec(out_shape[2]),
            ],
            scratch_shapes=[pltpu.VMEM((4, group, TILE, TILE), jnp.float32)],
        ),
        out_shape=out_shape,
        compiler_params=pltpu.CompilerParams(vmem_limit_bytes=VMEM),
        name="row_panels",
    )(place, *tiles, lead, diag)


def trailing_kernel(n_pieces, columns, places, order, starts, pair_ref, small_ref, *rest):
    piece_refs = rest[:n_pieces]
    front_ref, incoming_ref, _, out_ref, right_ref, taken, given, child_ref = rest[n_pieces:-3]
    take_sems, give_sems, child_sems = rest[-3:]
    group = piece_refs[0].shape[1]
    count = n_pieces * group
    steps = (count + 1) // 2
    rows = front_ref.shape[0]

    def columns_of(step):
        for j in range(2):
            index = jnp.minimum(2 * step, count - 2) + j
            wanted = columns[index] > 0
            if count % 2 and j == 0:
                wanted = jnp.logical_and(wanted, step < steps - 1)
            yield j, columns[index], wanted

    def each_take(step, act):
        slot = lax.rem(step, 2)
        for j, b, wanted in columns_of(step):

            @pl.when(wanted)
            def _():
                act(
                    pltpu.make_async_copy(
                        front_ref.at[:, 0, b, 0], taken.at[slot, j], take_sems.at[slot, j]
                    )
                )

    def each_give(step, act):
        slot = lax.rem(step, 2)
        for j, b, wanted in columns_of(step):

            @pl.when(wanted)
            def _():
                act(
                    pltpu.make_async_copy(
                        given.at[slot, j], out_ref.at[:, 0, b, 0], give_sems.at[slot, j]
                    )
                )

    def each_child(step, act):
        for j, b, wanted in columns_of(step):

            @pl.when(wanted)
            def _():
                @pl.loop(starts[b], starts[b + 1])
                def _(i):
                    s = order[2 * i]
                    copy = pltpu.make_async_copy(
                        incoming_ref.at[s, pl.ds(0, TILE)], child_ref.at[s], child_sems.at[s]
                    )
                    act(copy, j, s, order[2 * i + 1])

    for step in range(min(steps, 2)):
        each_take(step, lambda copy: copy.start())
    for step in range(steps):
        each_child(step, lambda copy, *_: copy.start())

    tile_columns = [
        jnp.concatenate(
            [
                piece[places[4 * p + c]].reshape(group * TILE, TILE)
                for p, piece in enumerate(piece_refs)
            ],
            axis=0,
        )
        for c in range(4)
    ]
    for i, panel in enumerate(two_panels(tile_columns, small_ref, lambda _, value: value)):
        high, low = halves(panel.T)
        for k, half in enumerate((high, high, low)):
            right_ref[k * WIDTH + i * PANEL : k * WIDTH + (i + 1) * PANEL] = half

    @pl.loop(0, steps)
    def _(step):
        slot = lax.rem(step, 2)
        each_take(step, lambda copy: copy.wait())

        @pl.when(step >= 2)
        def _():
            each_give(step - 2, lambda copy: copy.wait())

        start = jnp.minimum(2 * step, count - 2)
        lanes = pl.ds(pl.multiple_of(start * TILE, TILE), 2 * TILE)
        block = rows // 3
        for m in range(3):
            left = pair_ref[m * block * TILE : (m + 1) * block * TILE]
            update = dot(jnp.concatenate([left, left[:, :WIDTH]], axis=1), right_ref[:, lanes])
            span = slice(m * block, (m + 1) * block)
            for j in range(2):
                part = update[:, j * TILE : (j + 1) * TILE].reshape(block, TILE, TILE)
                given[slot, j, span] = taken[slot, j, span] - part

        def add(copy, j, s, a):
            copy.wait()
            given[slot, j, a] = given[slot, j, a] + child_ref[s]

        each_child(step, add)
        each_give(step, lambda copy: copy.start())

        @pl.when(step + 2 < steps)
        def _():
            each_take(step + 2, lambda copy: copy.start())

    for step in range(max(steps - 2, 0), steps):
        each_give(step, lambda copy: copy.wait())


def trailing(front, pieces, columns, places, panels, incoming, order, starts):
    rows = front.shape[0]
    pair, out, small = panels
    group = pieces[0].shape[1]
    count = len(pieces) * group
    scalars = [columns, places, order, starts]
    held = [pair, small, *pieces]
    distant = [front, incoming, out]
    spec = lambda space, n: [pl.BlockSpec(memory_space=space)] * n
    height = rows * TILE
    devices = incoming.shape[0]
    return pl.pallas_call(
        functools.partial(trailing_kernel, len(pieces)),
        in_specs=spec(pltpu.SMEM, 4) + spec(pltpu.VMEM, len(held)) + spec(pltpu.HBM, 3),
        out_specs=pl.BlockSpec(memory_space=pltpu.HBM),
        scratch_shapes=[
            pltpu.VMEM((3 * WIDTH, count * TILE), jnp.bfloat16),
            pltpu.VMEM((2, 2, rows, TILE, TILE), jnp.float32),
            pltpu.VMEM((2, 2, rows, TILE, TILE), jnp.float32),
            pltpu.VMEM((devices, TILE, TILE), jnp.float32),
            pltpu.SemaphoreType.DMA((2, 2)),
            pltpu.SemaphoreType.DMA((2, 2)),
            pltpu.SemaphoreType.DMA((devices,)),
        ],
        out_shape=jax.ShapeDtypeStruct(front.shape, jnp.float32),
        input_output_aliases={len(held) + 6: 0},
        compiler_params=pltpu.CompilerParams(vmem_limit_bytes=VMEM),
        cost_estimate=pl.CostEstimate(
            flops=8 * count * 2 * height * TILE * WIDTH,
            bytes_accessed=count * 2 * height * TILE * 4,
            transcendentals=0,
        ),
        name="trailing",
    )(*scalars, *held, *distant)


def body(front, child_tiles, tile_dest, tile_slot, tile_count, diag_inverses):
    n_row = lax.axis_size("row")
    n_col = lax.axis_size("col")
    my_row = lax.axis_index("row").astype(jnp.int32)
    my_col = lax.axis_index("col").astype(jnp.int32)
    rows_here, cols_here = (front.shape[0], front.shape[2])
    devices = n_row * n_col
    assert n_col == 4 and n_row % 4 == 0 and rows_here % 3 == 0
    place = jnp.stack([my_row, my_col, jnp.int32(cols_here)])

    outgoing = pack(child_tiles, tile_dest[:, 0], tile_slot, tile_count, devices)
    incoming = lax.all_to_all(outgoing, BOTH, split_axis=0, concat_axis=0, tiled=True)
    slot_in = lax.optimization_barrier(incoming[:, TILE, 0].astype(jnp.int32))

    row_of = jnp.where(slot_in >= 0, slot_in // cols_here, 0)
    col_of = jnp.where(slot_in >= 0, slot_in % cols_here, -1)
    sources = jnp.arange(devices, dtype=jnp.int32)
    key = jnp.where(slot_in >= 0, col_of, cols_here) * devices + sources
    rank = jnp.sum((key[None, :] < key[:, None]).astype(jnp.int32), axis=1)
    at = rank[None, :] == sources[:, None]
    order = jnp.stack(
        [jnp.sum(jnp.where(at, v[None, :], 0), axis=1) for v in (sources, row_of)], axis=1
    ).reshape(-1)
    edges = jnp.arange(cols_here + 1, dtype=jnp.int32) * devices
    starts = jnp.sum((key[None, :] < edges[:, None]).astype(jnp.int32), axis=1)

    ring = rows_here % n_col == 0
    mine, *parts = assemble_columns(front, incoming, place, slot_in, n_col if ring else 1)

    owners = [r * n_col + c for r in (2, 3) for c in (0, 1)]
    slices = lax.all_to_all(
        mine[0].reshape(devices, TILE // devices, TILE), BOTH, split_axis=0, concat_axis=0, tiled=True
    )
    own = jnp.stack([slices[owner] for owner in owners])

    def hand_on(own):
        lead = lax.all_to_all(own, BOTH, split_axis=0, concat_axis=0, tiled=True)
        return lead.transpose(1, 0, 2, 3).reshape(2, 2, TILE, TILE)

    own = jnp.broadcast_to(own[None], (devices,) + own.shape)
    near = lax.ppermute(mine, "col", [(c, c ^ 1) for c in range(n_col)])
    far = lax.ppermute(mine, "col", [(c, c ^ 2) for c in range(n_col)])
    other = lax.ppermute(far, "col", [(c, c ^ 1) for c in range(n_col)])
    others = [near, far, other]
    sets = n_row // n_col
    if ring:
        arrived = []
        for j, part in enumerate(parts):
            pairs = [
                (r * n_col + c, ((r // n_col) * n_col + (c + j) % n_col) * n_col + r % n_col)
                for r in range(n_row)
                for c in range(n_col)
            ]
            arrived.append(lax.ppermute(part, BOTH, pairs))
        arrived, own = lax.optimization_barrier((arrived, own))
        piece = jnp.stack(arrived)
        circle = list(range(0, n_row, 2)) + list(range(n_row - 1, 0, -2))
        spot = jnp.asarray([circle.index(r) for r in range(n_row)], jnp.int32)[my_row]
        up = [(circle[i], circle[(i + 1) % n_row]) for i in range(n_row)]
        down = [(b, a) for a, b in up]
        rounds = [[(piece, 0)]]
        ahead = behind = piece
        for step in range(1, n_row // 2):
            ahead = lax.ppermute(ahead, "row", up)
            behind = lax.ppermute(behind, "row", down)
            if step == 1:
                ahead, behind, lead, others = lax.optimization_barrier(
                    (ahead, behind, hand_on(own), others)
                )
            rounds.append([(ahead, -step), (behind, step)])
        last = jnp.concatenate(
            [lax.ppermute(ahead[:2], "row", up), lax.ppermute(behind[2:], "row", down)]
        )
        rounds.append([(last, n_row // 2)])
        rounds = [rounds[0] + rounds[1]] + rounds[2:]

        def described(shift):
            origin = jnp.asarray(circle, jnp.int32)[(spot + shift + n_row) % n_row]
            part, group = origin % n_col, rows_here // n_col
            row = part * group + jnp.arange(group, dtype=jnp.int32)
            places = (part - jnp.arange(n_col, dtype=jnp.int32) + n_col) % n_col
            return row * sets + origin // n_col, places

    else:
        pairs = [
            (r * n_col + c, ((r // n_col) * n_col + c) * n_col + r % n_col)
            for r in range(n_row)
            for c in range(n_col)
        ]
        moved = lax.all_gather(lax.ppermute(mine, BOTH, pairs), "row", axis=0, tiled=False)
        rounds = [[(moved[h * n_col : (h + 1) * n_col], h)] for h in range(sets)]
        lead = hand_on(own)

        def described(h):
            row = jnp.arange(rows_here, dtype=jnp.int32)
            return row * sets + h, jnp.arange(n_col, dtype=jnp.int32)

    panels = row_panels([mine, *others], lead, diag_inverses, place, front)

    for entries in rounds:
        described_here = [described(shift) for _, shift in entries]
        columns = jnp.concatenate([d[0] for d in described_here])
        places = jnp.concatenate([d[1] for d in described_here])
        pieces = [p for p, _ in entries]
        out = trailing(front, pieces, columns, places, panels, incoming, order, starts)
        panels = [panels[0], out, panels[2]]
    return panels[1]


def solution(mesh):
    return jax.shard_map(
        body,
        mesh=mesh,
        in_specs=(
            P(None, "row", None, "col", None, None),
            P(BOTH, None, None),
            P(BOTH, None),
            P(BOTH),
            P(BOTH),
            P(),
        ),
        out_specs=P(None, "row", None, "col", None, None),
        check_vma=False,
    )
```

```python
import functools

import jax
import jax.numpy as jnp
from jax import lax
from jax.experimental import pallas as pl
from jax.experimental.pallas import tpu as pltpu
from jax.sharding import PartitionSpec as P

TILE = 128
PANEL = 256
WIDTH = 2 * PANEL
NOTE = 8
VMEM = 30 * 1024 * 1024
BOTH = ("row", "col")


def halves(value):
    high = value.astype(jnp.bfloat16)
    low = (value - high.astype(jnp.float32)).astype(jnp.bfloat16)
    return high, low


def deep(value):
    high, low = halves(value)
    return jnp.concatenate([high, low, high], axis=1)


def stacked(value):
    high, low = halves(value)
    return jnp.concatenate([high, high, low], axis=0)


def dot(left, right):
    return jnp.dot(left, right, preferred_element_type=jnp.float32)


def two_panels(columns, small_ref, mask):
    one = mask(0, dot(deep(jnp.concatenate(columns[:2], axis=1)), small_ref[0]))
    field = jnp.concatenate(columns[2:], axis=1) - dot(deep(mask(1, one)), small_ref[1])
    return one, mask(1, dot(deep(field), small_ref[2]))


def two_panels_across(columns, small_ref):
    one = dot(small_ref[0], stacked(jnp.concatenate(columns[:2], axis=0)))
    field = jnp.concatenate(columns[2:], axis=0) - dot(small_ref[1], stacked(one))
    return one, dot(small_ref[2], stacked(field))


def whole_spec(array):
    rank = len(array.shape)
    return pl.BlockSpec(array.shape, lambda *_: (0,) * rank)


def pack_kernel(dest, slot, count, child_ref, out_ref, notes_ref, sems, notes_sem):
    slots = child_ref.shape[0]

    def copy(k):
        return pltpu.make_async_copy(
            child_ref.at[k], out_ref.at[dest[k], pl.ds(0, TILE)], sems.at[k]
        )

    notes_ref[...] = jnp.full_like(notes_ref, -1.0)
    live = jnp.minimum(count[0], slots)

    @pl.loop(0, live)
    def _(k):
        copy(k).start()
        notes_ref[dest[k]] = jnp.full(notes_ref.shape[1:], slot[k].astype(jnp.float32))

    notes = pltpu.make_async_copy(notes_ref, out_ref.at[:, pl.ds(TILE, NOTE)], notes_sem)
    notes.start()
    notes.wait()

    @pl.loop(0, live)
    def _(k):
        copy(k).wait()


def pack(child_tiles, dest, slot, count, devices):
    slots = child_tiles.shape[0]
    hbm = pl.BlockSpec(memory_space=pltpu.HBM)
    return pl.pallas_call(
        pack_kernel,
        in_specs=[pl.BlockSpec(memory_space=pltpu.SMEM)] * 3
        + [pl.BlockSpec(memory_space=pltpu.VMEM)],
        out_specs=hbm,
        scratch_shapes=[
            pltpu.VMEM((devices, NOTE, TILE), jnp.float32),
            pltpu.SemaphoreType.DMA((slots,)),
            pltpu.SemaphoreType.DMA,
        ],
        out_shape=jax.ShapeDtypeStruct((devices, TILE + NOTE, TILE), jnp.float32),
        name="pack",
    )(dest, slot, count, child_tiles)


def columns_kernel(place, slot_in, front_ref, incoming_ref, out_ref, *rest):
    *parts, tile_ref, sem = rest
    cols = place[2]
    strip = pltpu.make_async_copy(front_ref.at[:, 0, 0, 0], out_ref, sem)
    strip.start()
    strip.wait()

    @pl.loop(0, incoming_ref.shape[0])
    def _(s):
        slot = slot_in[s]

        @pl.when(jnp.logical_and(slot >= 0, lax.rem(slot, cols) == 0))
        def _():
            copy = pltpu.make_async_copy(incoming_ref.at[s, pl.ds(0, TILE)], tile_ref, sem)
            copy.start()
            copy.wait()
            row = lax.div(slot, cols)
            out_ref[row] = out_ref[row] + tile_ref[...]

    count = len(parts)
    for j, part_ref in enumerate(parts):
        group = part_ref.shape[0]
        for t in range(group):
            part_ref[t] = out_ref[lax.rem(place[1] + j, count) * group + t].T


def assemble_columns(front, incoming, place, slot_in, parts):
    rows = front.shape[0]
    shapes = [(rows, TILE, TILE)] + [(rows // parts, TILE, TILE)] * parts
    out_shape = [jax.ShapeDtypeStruct(shape, jnp.float32) for shape in shapes]
    return pl.pallas_call(
        columns_kernel,
        grid_spec=pltpu.PrefetchScalarGridSpec(
            num_scalar_prefetch=2,
            grid=(1,),
            in_specs=[
                pl.BlockSpec(memory_space=pltpu.HBM),
                pl.BlockSpec(memory_space=pltpu.HBM),
            ],
            out_specs=[whole_spec(a) for a in out_shape],
            scratch_shapes=[pltpu.VMEM((TILE, TILE), jnp.float32), pltpu.SemaphoreType.DMA],
        ),
        out_shape=out_shape,
        compiler_params=pltpu.CompilerParams(vmem_limit_bytes=VMEM),
        name="panel_columns",
    )(place, slot_in, front, incoming)


def row_panels_kernel(
    place, t0, t1, t2, t3, lead_ref, diag_ref, pair_ref, out_ref, across_ref, small_ref, tiles_ref
):
    step = pl.program_id(0)
    my_row, my_col = place[0], place[1]
    group = t0.shape[0]
    height = group * TILE

    @pl.when(step == 0)
    def _():
        small_ref[0] = stacked(diag_ref[0])
        lead = jnp.concatenate(
            [jnp.concatenate([lead_ref[i, 0], lead_ref[i, 1]], axis=1) for i in range(2)], axis=0
        )
        lead = dot(deep(lead), small_ref[0])
        small_ref[1] = stacked(lead.T)
        small_ref[2] = stacked(diag_ref[1])
        across_ref[0] = deep(diag_ref[0].T)
        across_ref[1] = deep(lead)
        across_ref[2] = deep(diag_ref[1].T)

    for i, tile_ref in enumerate((t0, t1, t2, t3)):
        tiles_ref[jnp.bitwise_xor(my_col, i)] = tile_ref[...]
    columns = [tiles_ref[c].reshape(height, TILE) for c in range(4)]
    tile_row = lax.broadcasted_iota(jnp.int32, (height, PANEL), 0) // TILE
    first = jnp.logical_and(step == 0, tile_row == 0)

    def mask(panels_above, value):
        above = jnp.logical_and(first, my_row < 2 * panels_above)
        return jnp.where(above, 0.0, value) if panels_above else value

    one, two = two_panels(columns, small_ref, mask)
    pair_ref[:, :PANEL], pair_ref[:, WIDTH : WIDTH + PANEL] = halves(mask(1, one))
    pair_ref[:, PANEL:WIDTH], pair_ref[:, WIDTH + PANEL :] = halves(mask(2, two))
    pieces = (one[:, :TILE], one[:, TILE:], two[:, :TILE], two[:, TILE:])
    for c in range(4):

        @pl.when(my_col == c)
        def _():
            out_ref[:, 0, 0, 0] = pieces[c].reshape(group, TILE, TILE)


def row_panels(mine, others, lead, diag, place, front):
    rows = front.shape[0]
    group = rows // 3
    height = group * TILE
    out_shape = [
        jax.ShapeDtypeStruct((rows * TILE, 2 * WIDTH), jnp.bfloat16),
        jax.ShapeDtypeStruct(front.shape, jnp.float32),
        jax.ShapeDtypeStruct((3, PANEL, 3 * PANEL), jnp.bfloat16),
    ]
    strip = pl.BlockSpec((group, TILE, TILE), lambda i, *_: (i, 0, 0))
    return pl.pallas_call(
        row_panels_kernel,
        grid_spec=pltpu.PrefetchScalarGridSpec(
            num_scalar_prefetch=1,
            grid=(3,),
            in_specs=[strip] * 4 + [whole_spec(lead), whole_spec(diag)],
            out_specs=[
                pl.BlockSpec((height, 2 * WIDTH), lambda i, *_: (i, 0)),
                pl.BlockSpec((group, 1, 1, 1, TILE, TILE), lambda i, *_: (i, 0, 0, 0, 0, 0)),
                whole_spec(out_shape[2]),
            ],
            scratch_shapes=[
                pltpu.VMEM((3, 3 * PANEL, PANEL), jnp.bfloat16),
                pltpu.VMEM((4, group, TILE, TILE), jnp.float32),
            ],
        ),
        out_shape=out_shape,
        compiler_params=pltpu.CompilerParams(vmem_limit_bytes=VMEM),
        name="row_panels",
    )(place, mine, *others, lead, diag)


def trailing_kernel(n_pieces, columns, places, order, starts, pair_ref, small_ref, *rest):
    piece_refs = rest[:n_pieces]
    front_ref, incoming_ref, _, out_ref, right_ref, taken, given, child_ref = rest[n_pieces:-3]
    take_sems, give_sems, child_sems = rest[-3:]
    group = piece_refs[0].shape[1]
    count = n_pieces * group
    steps = (count + 1) // 2
    rows = front_ref.shape[0]

    def columns_of(step):
        for j in range(2):
            index = jnp.minimum(2 * step, count - 2) + j
            wanted = columns[index] > 0
            if count % 2 and j == 0:
                wanted = jnp.logical_and(wanted, step < steps - 1)
            yield j, columns[index], wanted

    def each_take(step, act):
        slot = lax.rem(step, 2)
        for j, b, wanted in columns_of(step):

            @pl.when(wanted)
            def _():
                act(
                    pltpu.make_async_copy(
                        front_ref.at[:, 0, b, 0], taken.at[slot, j], take_sems.at[slot, j]
                    )
                )

    def each_give(step, act):
        slot = lax.rem(step, 2)
        for j, b, wanted in columns_of(step):

            @pl.when(wanted)
            def _():
                act(
                    pltpu.make_async_copy(
                        given.at[slot, j], out_ref.at[:, 0, b, 0], give_sems.at[slot, j]
                    )
                )

    def each_child(step, act):
        for j, b, wanted in columns_of(step):

            @pl.when(wanted)
            def _():
                @pl.loop(starts[b], starts[b + 1])
                def _(i):
                    s = order[2 * i]
                    copy = pltpu.make_async_copy(
                        incoming_ref.at[s, pl.ds(0, TILE)], child_ref.at[s], child_sems.at[s]
                    )
                    act(copy, j, s, order[2 * i + 1])

    for step in range(min(steps, 2)):
        each_take(step, lambda copy: copy.start())
    for step in range(steps):
        each_child(step, lambda copy, *_: copy.start())

    tile_columns = [
        jnp.concatenate(
            [
                piece[places[4 * p + c], t]
                for p, piece in enumerate(piece_refs)
                for t in range(group)
            ],
            axis=1,
        )
        for c in range(4)
    ]
    for i, panel in enumerate(two_panels_across(tile_columns, small_ref)):
        high, low = halves(panel)
        for k, half in enumerate((high, high, low)):
            right_ref[k * WIDTH + i * PANEL : k * WIDTH + (i + 1) * PANEL] = half

    @pl.loop(0, steps)
    def _(step):
        slot = lax.rem(step, 2)
        each_take(step, lambda copy: copy.wait())

        @pl.when(step >= 2)
        def _():
            each_give(step - 2, lambda copy: copy.wait())

        start = jnp.minimum(2 * step, count - 2)
        lanes = pl.ds(pl.multiple_of(start * TILE, TILE), 2 * TILE)
        block = rows // 3
        for m in range(3):
            left = pair_ref[m * block * TILE : (m + 1) * block * TILE]
            update = dot(jnp.concatenate([left, left[:, :WIDTH]], axis=1), right_ref[:, lanes])
            span = slice(m * block, (m + 1) * block)
            for j in range(2):
                part = update[:, j * TILE : (j + 1) * TILE].reshape(block, TILE, TILE)
                given[slot, j, span] = taken[slot, j, span] - part

        def add(copy, j, s, a):
            copy.wait()
            given[slot, j, a] = given[slot, j, a] + child_ref[s]

        each_child(step, add)
        each_give(step, lambda copy: copy.start())

        @pl.when(step + 2 < steps)
        def _():
            each_take(step + 2, lambda copy: copy.start())

    for step in range(max(steps - 2, 0), steps):
        each_give(step, lambda copy: copy.wait())


def trailing(front, pieces, columns, places, panels, incoming, order, starts):
    rows = front.shape[0]
    pair, out, small = panels
    group = pieces[0].shape[1]
    count = len(pieces) * group
    scalars = [columns, places, order, starts]
    held = [pair, small, *pieces]
    distant = [front, incoming, out]
    spec = lambda space, n: [pl.BlockSpec(memory_space=space)] * n
    height = rows * TILE
    devices = incoming.shape[0]
    return pl.pallas_call(
        functools.partial(trailing_kernel, len(pieces)),
        in_specs=spec(pltpu.SMEM, 4) + spec(pltpu.VMEM, len(held)) + spec(pltpu.HBM, 3),
        out_specs=pl.BlockSpec(memory_space=pltpu.HBM),
        scratch_shapes=[
            pltpu.VMEM((3 * WIDTH, count * TILE), jnp.bfloat16),
            pltpu.VMEM((2, 2, rows, TILE, TILE), jnp.float32),
            pltpu.VMEM((2, 2, rows, TILE, TILE), jnp.float32),
            pltpu.VMEM((devices, TILE, TILE), jnp.float32),
            pltpu.SemaphoreType.DMA((2, 2)),
            pltpu.SemaphoreType.DMA((2, 2)),
            pltpu.SemaphoreType.DMA((devices,)),
        ],
        out_shape=jax.ShapeDtypeStruct(front.shape, jnp.float32),
        input_output_aliases={len(held) + 6: 0},
        compiler_params=pltpu.CompilerParams(vmem_limit_bytes=VMEM),
        cost_estimate=pl.CostEstimate(
            flops=8 * count * 2 * height * TILE * WIDTH,
            bytes_accessed=count * 2 * height * TILE * 4,
            transcendentals=0,
        ),
        name="trailing",
    )(*scalars, *held, *distant)


def body(front, child_tiles, tile_dest, tile_slot, tile_count, diag_inverses):
    n_row = lax.axis_size("row")
    n_col = lax.axis_size("col")
    my_row = lax.axis_index("row").astype(jnp.int32)
    my_col = lax.axis_index("col").astype(jnp.int32)
    rows_here, cols_here = (front.shape[0], front.shape[2])
    devices = n_row * n_col
    assert n_col == 4 and n_row % 4 == 0 and rows_here % 3 == 0
    place = jnp.stack([my_row, my_col, jnp.int32(cols_here)])

    outgoing = pack(child_tiles, tile_dest[:, 0], tile_slot, tile_count, devices)
    incoming = lax.all_to_all(outgoing, BOTH, split_axis=0, concat_axis=0, tiled=True)
    slot_in = lax.optimization_barrier(incoming[:, TILE, 0].astype(jnp.int32))

    row_of = jnp.where(slot_in >= 0, slot_in // cols_here, 0)
    col_of = jnp.where(slot_in >= 0, slot_in % cols_here, -1)
    sources = jnp.arange(devices, dtype=jnp.int32)
    key = jnp.where(slot_in >= 0, col_of, cols_here) * devices + sources
    rank = jnp.sum((key[None, :] < key[:, None]).astype(jnp.int32), axis=1)
    at = rank[None, :] == sources[:, None]
    order = jnp.stack(
        [jnp.sum(jnp.where(at, v[None, :], 0), axis=1) for v in (sources, row_of)], axis=1
    ).reshape(-1)
    edges = jnp.arange(cols_here + 1, dtype=jnp.int32) * devices
    starts = jnp.sum((key[None, :] < edges[:, None]).astype(jnp.int32), axis=1)

    ring = rows_here % n_col == 0
    mine, *parts = assemble_columns(front, incoming, place, slot_in, n_col if ring else 1)

    owners = [r * n_col + c for r in (2, 3) for c in (0, 1)]
    slices = mine[0].reshape(devices, TILE // devices, TILE)
    slices = lax.all_to_all(slices, BOTH, split_axis=0, concat_axis=0, tiled=True)
    own = jnp.stack([slices[owner] for owner in owners])

    def hand_on(own):
        lead = lax.all_to_all(own, BOTH, split_axis=0, concat_axis=0, tiled=True)
        return lead.transpose(1, 0, 2, 3).reshape(2, 2, TILE, TILE)

    own = jnp.broadcast_to(own[None], (devices,) + own.shape)

    def exchange(mine):
        near = lax.ppermute(mine, "col", [(c, c ^ 1) for c in range(n_col)])
        far = lax.ppermute(mine, "col", [(c, c ^ 2) for c in range(n_col)])
        return [near, far, lax.ppermute(far, "col", [(c, c ^ 1) for c in range(n_col)])]

    sets = n_row // n_col
    if ring:
        arrived = []
        for j, part in enumerate(parts):
            pairs = [
                (r * n_col + c, ((r // n_col) * n_col + (c + j) % n_col) * n_col + r % n_col)
                for r in range(n_row)
                for c in range(n_col)
            ]
            arrived.append(lax.ppermute(part, BOTH, pairs))
        arrived, own, mine = lax.optimization_barrier((arrived, own, mine))
        piece = jnp.stack(arrived)
        circle = list(range(0, n_row, 2)) + list(range(n_row - 1, 0, -2))
        spot = jnp.asarray([circle.index(r) for r in range(n_row)], jnp.int32)[my_row]
        up = [(circle[i], circle[(i + 1) % n_row]) for i in range(n_row)]
        down = [(b, a) for a, b in up]
        rounds = [[(piece, 0)]]
        panels = row_panels(mine, exchange(mine), hand_on(own), diag_inverses, place, front)
        ahead = behind = piece
        for step in range(1, n_row // 2):
            ahead = lax.ppermute(ahead, "row", up)
            behind = lax.ppermute(behind, "row", down)
            if step == 2:
                ahead, behind, panels = lax.optimization_barrier((ahead, behind, panels))
            rounds.append([(ahead, -step), (behind, step)])
        last = jnp.concatenate(
            [lax.ppermute(ahead[:2], "row", up), lax.ppermute(behind[2:], "row", down)]
        )
        rounds.append([(last, n_row // 2)])
        rounds = [rounds[0] + rounds[1]] + rounds[2:]

        def described(shift):
            origin = jnp.asarray(circle, jnp.int32)[(spot + shift + n_row) % n_row]
            part, group = origin % n_col, rows_here // n_col
            row = part * group + jnp.arange(group, dtype=jnp.int32)
            places = (part - jnp.arange(n_col, dtype=jnp.int32) + n_col) % n_col
            return row * sets + origin // n_col, places

    else:
        pairs = [
            (r * n_col + c, ((r // n_col) * n_col + c) * n_col + r % n_col)
            for r in range(n_row)
            for c in range(n_col)
        ]
        moved = lax.all_gather(lax.ppermute(parts[0], BOTH, pairs), "row", axis=0, tiled=False)
        rounds = [[(moved[h * n_col : (h + 1) * n_col], h)] for h in range(sets)]
        panels = row_panels(mine, exchange(mine), hand_on(own), diag_inverses, place, front)

        def described(h):
            row = jnp.arange(rows_here, dtype=jnp.int32)
            return row * sets + h, jnp.arange(n_col, dtype=jnp.int32)

    for entries in rounds:
        described_here = [described(shift) for _, shift in entries]
        columns = jnp.concatenate([d[0] for d in described_here])
        places = jnp.concatenate([d[1] for d in described_here])
        pieces = [p for p, _ in entries]
        out = trailing(front, pieces, columns, places, panels, incoming, order, starts)
        panels = [panels[0], out, panels[2]]
    return panels[1]


def solution(mesh):
    return jax.shard_map(
        body,
        mesh=mesh,
        in_specs=(
            P(None, "row", None, "col", None, None),
            P(BOTH, None, None),
            P(BOTH, None),
            P(BOTH),
            P(BOTH),
            P(),
        ),
        out_specs=P(None, "row", None, "col", None, None),
        check_vma=False,
    )
```

```python
import functools

import jax
import jax.numpy as jnp
import numpy as np
from jax import lax
from jax.experimental import pallas as pl
from jax.experimental.pallas import tpu as pltpu
from jax.sharding import PartitionSpec as P

TILE = 128
PANEL = 256
WIDTH = 2 * PANEL
NOTE = 8
VMEM = 46 * 1024 * 1024
BOTH = ("row", "col")


def halves(value):
    high = value.astype(jnp.bfloat16)
    low = (value - high.astype(jnp.float32)).astype(jnp.bfloat16)
    return high, low


def deep(value):
    high, low = halves(value)
    return jnp.concatenate([high, low, high], axis=1)


def stacked(value):
    high, low = halves(value)
    return jnp.concatenate([high, high, low], axis=0)


def dot(left, right):
    return jnp.dot(left, right, preferred_element_type=jnp.float32)


def two_panels(columns, small_ref, mask):
    one = mask(0, dot(deep(jnp.concatenate(columns[:2], axis=1)), small_ref[0]))
    field = jnp.concatenate(columns[2:], axis=1) - dot(deep(mask(1, one)), small_ref[1])
    return one, mask(1, dot(deep(field), small_ref[2]))


def two_panels_across(columns, small_ref):
    one = dot(small_ref[0], stacked(jnp.concatenate(columns[:2], axis=0)))
    field = jnp.concatenate(columns[2:], axis=0) - dot(small_ref[1], stacked(one))
    return one, dot(small_ref[2], stacked(field))


def whole_spec(array):
    rank = len(array.shape)
    return pl.BlockSpec(array.shape, lambda *_: (0,) * rank)


def lead_slices(devices):
    height = max(8, 4 * TILE // devices)
    return 4 * TILE // height, height


def pack_kernel(
    owners, place, dest, slot, count, child_ref, front_ref, out_ref, notes_ref, lead_ref,
    tile_ref, sems, notes_sem, lead_sem,
):
    slots = child_ref.shape[0]
    n_slices, height, _ = lead_ref.shape
    each = n_slices // 4

    def copy(k):
        return pltpu.make_async_copy(
            child_ref.at[k], out_ref.at[dest[k], pl.ds(0, TILE)], sems.at[k]
        )

    notes_ref[...] = jnp.full_like(notes_ref, -1.0)
    lead_ref[...] = jnp.zeros_like(lead_ref)
    live = jnp.minimum(count[0], slots)

    @pl.loop(0, live)
    def _(k):
        copy(k).start()
        notes_ref[dest[k]] = jnp.full(notes_ref.shape[1:], slot[k].astype(jnp.float32))

    notes = pltpu.make_async_copy(notes_ref, out_ref.at[:, pl.ds(TILE, NOTE)], notes_sem)
    notes.start()

    for i, owner in enumerate(owners):
        span = pl.ds(i * each, each)

        @pl.when(place[3] == owner)
        def _():
            own = pltpu.make_async_copy(front_ref.at[0, 0, 0, 0], tile_ref, lead_sem)
            own.start()
            own.wait()
            lead_ref[span] = tile_ref[...].reshape(each, height, TILE)

        @pl.loop(0, live)
        def _(k):
            @pl.when(jnp.logical_and(slot[k] == 0, dest[k] == owner))
            def _():
                lead_ref[span] = lead_ref[span] + child_ref[k].reshape(each, height, TILE)

    lead = pltpu.make_async_copy(
        lead_ref, out_ref.at[pl.ds(0, n_slices), pl.ds(TILE + NOTE, height)], lead_sem
    )
    lead.start()
    notes.wait()
    lead.wait()

    @pl.loop(0, live)
    def _(k):
        copy(k).wait()


def pack(child_tiles, front, place, dest, slot, count, devices, owners):
    slots = child_tiles.shape[0]
    n_slices, height = lead_slices(devices)
    hbm = pl.BlockSpec(memory_space=pltpu.HBM)
    return pl.pallas_call(
        functools.partial(pack_kernel, owners),
        in_specs=[pl.BlockSpec(memory_space=pltpu.SMEM)] * 4
        + [pl.BlockSpec(memory_space=pltpu.VMEM), hbm],
        out_specs=hbm,
        scratch_shapes=[
            pltpu.VMEM((devices, NOTE, TILE), jnp.float32),
            pltpu.VMEM((n_slices, height, TILE), jnp.float32),
            pltpu.VMEM((TILE, TILE), jnp.float32),
            pltpu.SemaphoreType.DMA((slots,)),
            pltpu.SemaphoreType.DMA,
            pltpu.SemaphoreType.DMA,
        ],
        out_shape=jax.ShapeDtypeStruct((devices, TILE + NOTE + height, TILE), jnp.float32),
        compiler_params=pltpu.CompilerParams(vmem_limit_bytes=VMEM),
        name="pack",
    )(place, dest, slot, count, child_tiles, front)


def columns_kernel(place, slot_in, front_ref, incoming_ref, out_ref, own_ref, *rest):
    *parts, tile_ref, slices_ref, sem, slices_sem = rest
    cols = place[2]
    height = own_ref.shape[1]
    strip = pltpu.make_async_copy(front_ref.at[:, 0, 0, 0], out_ref, sem)
    strip.start()
    slices = pltpu.make_async_copy(
        incoming_ref.at[:, pl.ds(TILE + NOTE, height)], slices_ref, slices_sem
    )
    slices.start()
    strip.wait()

    @pl.loop(0, incoming_ref.shape[0])
    def _(s):
        slot = slot_in[s]

        @pl.when(jnp.logical_and(slot >= 0, lax.rem(slot, cols) == 0))
        def _():
            copy = pltpu.make_async_copy(incoming_ref.at[s, pl.ds(0, TILE)], tile_ref, sem)
            copy.start()
            copy.wait()
            row = lax.div(slot, cols)
            out_ref[row] = out_ref[row] + tile_ref[...]

    count = len(parts)
    for j, part_ref in enumerate(parts):
        group = part_ref.shape[0]
        for t in range(group):
            part_ref[t] = out_ref[lax.rem(place[1] + j, count) * group + t].T

    slices.wait()
    own_ref[...] = jnp.broadcast_to(jnp.sum(slices_ref[...], axis=0)[None], own_ref.shape)


def assemble_columns(front, incoming, place, slot_in, parts):
    rows, devices = front.shape[0], incoming.shape[0]
    _, height = lead_slices(devices)
    shapes = [(rows, TILE, TILE), (devices, height, TILE)]
    shapes += [(rows // parts, TILE, TILE)] * parts
    out_shape = [jax.ShapeDtypeStruct(shape, jnp.float32) for shape in shapes]
    return pl.pallas_call(
        columns_kernel,
        grid_spec=pltpu.PrefetchScalarGridSpec(
            num_scalar_prefetch=2,
            grid=(1,),
            in_specs=[pl.BlockSpec(memory_space=pltpu.HBM)] * 2,
            out_specs=[whole_spec(a) for a in out_shape],
            scratch_shapes=[
                pltpu.VMEM((TILE, TILE), jnp.float32),
                pltpu.VMEM((devices, height, TILE), jnp.float32),
                pltpu.SemaphoreType.DMA,
                pltpu.SemaphoreType.DMA,
            ],
        ),
        out_shape=out_shape,
        compiler_params=pltpu.CompilerParams(vmem_limit_bytes=VMEM),
        name="panel_columns",
    )(place, slot_in, front, incoming)


def row_panels_kernel(
    place, slot_in, t0, t1, t2, t3, lead_ref, diag_ref, pair_ref, out_ref, across_ref, order,
    starts, small_ref, tiles_ref, cursor,
):
    step = pl.program_id(0)
    cols = starts.shape[0] - 1
    my_row, my_col = place[0], place[1]
    group = t0.shape[0]
    height = group * TILE

    @pl.when(step == 0)
    def _():
        small_ref[0] = stacked(diag_ref[0])
        lead = jnp.concatenate(
            [jnp.concatenate([lead_ref[i, 0], lead_ref[i, 1]], axis=1) for i in range(2)], axis=0
        )
        lead = dot(deep(lead), small_ref[0])
        small_ref[1] = stacked(lead.T)
        small_ref[2] = stacked(diag_ref[1])
        across_ref[0] = deep(diag_ref[0].T)
        across_ref[1] = deep(lead)
        across_ref[2] = deep(diag_ref[1].T)

        @pl.loop(0, cols + 1)
        def _(b):
            starts[b] = 0

        @pl.loop(0, slot_in.shape[0])
        def _(s):
            @pl.when(slot_in[s] >= 0)
            def _():
                b = lax.rem(slot_in[s], cols)
                starts[b + 1] = starts[b + 1] + 1

        @pl.loop(0, cols)
        def _(b):
            cursor[b] = starts[b]
            starts[b + 1] = starts[b + 1] + starts[b]

        @pl.loop(0, slot_in.shape[0])
        def _(s):
            @pl.when(slot_in[s] >= 0)
            def _():
                b = lax.rem(slot_in[s], cols)
                i = cursor[b]
                order[2 * i] = s
                order[2 * i + 1] = lax.div(slot_in[s], cols)
                cursor[b] = i + 1


    for i, tile_ref in enumerate((t0, t1, t2, t3)):
        tiles_ref[jnp.bitwise_xor(my_col, i)] = tile_ref[...]
    columns = [tiles_ref[c].reshape(height, TILE) for c in range(4)]
    tile_row = lax.broadcasted_iota(jnp.int32, (height, PANEL), 0) // TILE
    first = jnp.logical_and(step == 0, tile_row == 0)

    def mask(panels_above, value):
        above = jnp.logical_and(first, my_row < 2 * panels_above)
        return jnp.where(above, 0.0, value) if panels_above else value

    one, two = two_panels(columns, small_ref, mask)
    for i, panel in enumerate((mask(1, one), mask(2, two))):
        high, low = halves(panel)
        for k, half in enumerate((high, low, high)):
            pair_ref[:, k * WIDTH + i * PANEL : k * WIDTH + (i + 1) * PANEL] = half
    pieces = (one[:, :TILE], one[:, TILE:], two[:, :TILE], two[:, TILE:])
    for c in range(4):

        @pl.when(my_col == c)
        def _():
            out_ref[:, 0, 0, 0] = pieces[c].reshape(group, TILE, TILE)


def row_panels(mine, others, lead, diag, place, slot_in, front):
    rows = front.shape[0]
    cols = front.shape[2]
    group = rows // 3
    height = group * TILE
    out_shape = [
        jax.ShapeDtypeStruct((rows * TILE, 3 * WIDTH), jnp.bfloat16),
        jax.ShapeDtypeStruct(front.shape, jnp.float32),
        jax.ShapeDtypeStruct((3, PANEL, 3 * PANEL), jnp.bfloat16),
        jax.ShapeDtypeStruct((2 * slot_in.shape[0],), jnp.int32),
        jax.ShapeDtypeStruct((cols + 1,), jnp.int32),
    ]
    strip = pl.BlockSpec((group, TILE, TILE), lambda i, *_: (i, 0, 0))
    return pl.pallas_call(
        row_panels_kernel,
        grid_spec=pltpu.PrefetchScalarGridSpec(
            num_scalar_prefetch=2,
            grid=(3,),
            in_specs=[strip] * 4 + [whole_spec(lead), whole_spec(diag)],
            out_specs=[
                pl.BlockSpec((height, 3 * WIDTH), lambda i, *_: (i, 0)),
                pl.BlockSpec((group, 1, 1, 1, TILE, TILE), lambda i, *_: (i, 0, 0, 0, 0, 0)),
                whole_spec(out_shape[2]),
                pl.BlockSpec(memory_space=pltpu.SMEM),
                pl.BlockSpec(memory_space=pltpu.SMEM),
            ],
            scratch_shapes=[
                pltpu.VMEM((3, 3 * PANEL, PANEL), jnp.bfloat16),
                pltpu.VMEM((4, group, TILE, TILE), jnp.float32),
                pltpu.SMEM((cols,), jnp.int32),
            ],
        ),
        out_shape=out_shape,
        compiler_params=pltpu.CompilerParams(vmem_limit_bytes=VMEM),
        name="row_panels",
    )(place, slot_in, mine, *others, lead, diag)


def trailing_kernel(
    first, n_pieces, place, columns_table, places_table, order, starts, pair_ref, small_ref, *rest
):
    piece_refs = rest[:n_pieces]
    front_ref, incoming_ref, _, out_ref, right_ref, taken, given, child_ref = rest[n_pieces:-3]
    take_sems, give_sems, child_sems = rest[-3:]
    group = piece_refs[0].shape[1]
    count = n_pieces * group
    steps = (count + 1) // 2
    rows, cols = front_ref.shape[0], front_ref.shape[2]
    columns_base = place[0] * cols + first * group
    places_base = (place[0] * (cols // group) + first) * 4

    def columns_of(step):
        for j in range(2):
            index = jnp.minimum(2 * step, count - 2) + j
            b = columns_table[columns_base + index]
            wanted = b > 0
            if count % 2 and j == 0:
                wanted = jnp.logical_and(wanted, step < steps - 1)
            yield j, b, wanted

    def each_take(step, act):
        slot = lax.rem(step, 2)
        for j, b, wanted in columns_of(step):

            @pl.when(wanted)
            def _():
                act(
                    pltpu.make_async_copy(
                        front_ref.at[:, 0, b, 0], taken.at[slot, j], take_sems.at[slot, j]
                    )
                )

    def each_give(step, act):
        slot = lax.rem(step, 2)
        for j, b, wanted in columns_of(step):

            @pl.when(wanted)
            def _():
                act(
                    pltpu.make_async_copy(
                        given.at[slot, j], out_ref.at[:, 0, b, 0], give_sems.at[slot, j]
                    )
                )

    def each_child(step, act):
        for j, b, wanted in columns_of(step):

            @pl.when(wanted)
            def _():
                @pl.loop(starts[b], starts[b + 1])
                def _(i):
                    s = order[2 * i]
                    copy = pltpu.make_async_copy(
                        incoming_ref.at[s, pl.ds(0, TILE)], child_ref.at[s], child_sems.at[s]
                    )
                    act(copy, j, s, order[2 * i + 1])

    for step in range(min(steps, 2)):
        each_take(step, lambda copy: copy.start())
    for step in range(steps):
        each_child(step, lambda copy, *_: copy.start())

    tile_columns = [
        jnp.concatenate(
            [
                piece[places_table[places_base + 4 * p + c], t]
                for p, piece in enumerate(piece_refs)
                for t in range(group)
            ],
            axis=1,
        )
        for c in range(4)
    ]
    for i, panel in enumerate(two_panels_across(tile_columns, small_ref)):
        high, low = halves(panel)
        for k, half in enumerate((high, high, low)):
            right_ref[k * WIDTH + i * PANEL : k * WIDTH + (i + 1) * PANEL] = half

    @pl.loop(0, steps)
    def _(step):
        slot = lax.rem(step, 2)
        each_take(step, lambda copy: copy.wait())

        @pl.when(step >= 2)
        def _():
            each_give(step - 2, lambda copy: copy.wait())

        start = jnp.minimum(2 * step, count - 2)
        lanes = pl.ds(pl.multiple_of(start * TILE, TILE), 2 * TILE)
        update = dot(pair_ref[...], right_ref[:, lanes])
        for j in range(2):
            part = update[:, j * TILE : (j + 1) * TILE].reshape(rows, TILE, TILE)
            given[slot, j] = taken[slot, j] - part

        def add(copy, j, s, a):
            copy.wait()
            given[slot, j, a] = given[slot, j, a] + child_ref[s]

        each_child(step, add)
        each_give(step, lambda copy: copy.start())

        @pl.when(step + 2 < steps)
        def _():
            each_take(step + 2, lambda copy: copy.start())

    for step in range(max(steps - 2, 0), steps):
        each_give(step, lambda copy: copy.wait())


def trailing(front, pieces, first, place, tables, panels, incoming):
    rows = front.shape[0]
    pair, out, small, order, starts = panels
    group = pieces[0].shape[1]
    count = len(pieces) * group
    scalars = [place, *tables, order, starts]
    held = [pair, small, *pieces]
    distant = [front, incoming, out]
    spec = lambda space, n: [pl.BlockSpec(memory_space=space)] * n
    height = rows * TILE
    devices = incoming.shape[0]
    return pl.pallas_call(
        functools.partial(trailing_kernel, first, len(pieces)),
        in_specs=spec(pltpu.SMEM, 5) + spec(pltpu.VMEM, len(held)) + spec(pltpu.HBM, 3),
        out_specs=pl.BlockSpec(memory_space=pltpu.HBM),
        scratch_shapes=[
            pltpu.VMEM((3 * WIDTH, count * TILE), jnp.bfloat16),
            pltpu.VMEM((2, 2, rows, TILE, TILE), jnp.float32),
            pltpu.VMEM((2, 2, rows, TILE, TILE), jnp.float32),
            pltpu.VMEM((devices, TILE, TILE), jnp.float32),
            pltpu.SemaphoreType.DMA((2, 2)),
            pltpu.SemaphoreType.DMA((2, 2)),
            pltpu.SemaphoreType.DMA((devices,)),
        ],
        out_shape=jax.ShapeDtypeStruct(front.shape, jnp.float32),
        input_output_aliases={len(held) + 7: 0},
        compiler_params=pltpu.CompilerParams(vmem_limit_bytes=VMEM),
        cost_estimate=pl.CostEstimate(
            flops=8 * count * 2 * height * TILE * WIDTH,
            bytes_accessed=count * 2 * height * TILE * 4,
            transcendentals=0,
        ),
        name="trailing",
    )(*scalars, *held, *distant)


def body(front, child_tiles, tile_dest, tile_slot, tile_count, diag_inverses):
    n_row = lax.axis_size("row")
    n_col = lax.axis_size("col")
    my_row = lax.axis_index("row").astype(jnp.int32)
    my_col = lax.axis_index("col").astype(jnp.int32)
    rows_here, cols_here = (front.shape[0], front.shape[2])
    devices = n_row * n_col
    assert n_col == 4 and n_row % 4 == 0 and rows_here % 3 == 0
    owners = [r * n_col + c for r in (2, 3) for c in (0, 1)]
    place = jnp.stack([my_row, my_col, jnp.int32(cols_here), my_row * n_col + my_col])

    outgoing = pack(
        child_tiles, front, place, tile_dest[:, 0], tile_slot, tile_count, devices, owners
    )
    incoming = lax.all_to_all(outgoing, BOTH, split_axis=0, concat_axis=0, tiled=True)
    slot_in = lax.optimization_barrier(incoming[:, TILE, 0].astype(jnp.int32))

    ring = rows_here % n_col == 0
    mine, own, *parts = assemble_columns(front, incoming, place, slot_in, n_col if ring else 1)

    def hand_on(own):
        lead = lax.all_to_all(own, BOTH, split_axis=0, concat_axis=0, tiled=True)
        return lead[: lead_slices(devices)[0]].reshape(2, 2, TILE, TILE)

    def exchange(mine):
        near = lax.ppermute(mine, "col", [(c, c ^ 1) for c in range(n_col)])
        far = lax.ppermute(mine, "col", [(c, c ^ 2) for c in range(n_col)])
        return [near, far, lax.ppermute(far, "col", [(c, c ^ 1) for c in range(n_col)])]

    def own_panels(mine, own):
        tiles = exchange(mine)
        return row_panels(mine, tiles, hand_on(own), diag_inverses, place, slot_in, front)

    sets = n_row // n_col
    if ring:
        arrived = []
        for j, part in enumerate(parts):
            pairs = [
                (r * n_col + c, ((r // n_col) * n_col + (c + j) % n_col) * n_col + r % n_col)
                for r in range(n_row)
                for c in range(n_col)
            ]
            arrived.append(lax.ppermute(part, BOTH, pairs))
        arrived, own, mine = lax.optimization_barrier((arrived, own, mine))
        piece = jnp.stack(arrived)
        circle = list(range(0, n_row, 2)) + list(range(n_row - 1, 0, -2))
        up = [(circle[i], circle[(i + 1) % n_row]) for i in range(n_row)]
        down = [(b, a) for a, b in up]
        rounds = [[(piece, 0)]]
        panels = own_panels(mine, own)
        ahead = behind = piece
        for step in range(1, n_row // 2):
            ahead = lax.ppermute(ahead, "row", up)
            behind = lax.ppermute(behind, "row", down)
            if step == 2:
                ahead, behind, panels = lax.optimization_barrier((ahead, behind, panels))
            rounds.append([(ahead, -step), (behind, step)])
        last = jnp.concatenate(
            [lax.ppermute(ahead[:2], "row", up), lax.ppermute(behind[2:], "row", down)]
        )
        rounds.append([(last, n_row // 2)])
        rounds = [rounds[0] + rounds[1]] + rounds[2:]

        def described(row, shift):
            origin = circle[(circle.index(row) + shift) % n_row]
            part, group = origin % n_col, rows_here // n_col
            columns = [(part * group + t) * sets + origin // n_col for t in range(group)]
            return columns, [(part - c) % n_col for c in range(n_col)]

    else:
        pairs = [
            (r * n_col + c, ((r // n_col) * n_col + c) * n_col + r % n_col)
            for r in range(n_row)
            for c in range(n_col)
        ]
        moved = lax.all_gather(lax.ppermute(parts[0], BOTH, pairs), "row", axis=0, tiled=False)
        rounds = [[(moved[h * n_col : (h + 1) * n_col], h)] for h in range(sets)]
        panels = own_panels(mine, own)

        def described(row, h):
            return [a * sets + h for a in range(rows_here)], list(range(n_col))

    shifts = [shift for entries in rounds for _, shift in entries]
    tables = [
        jnp.asarray(
            np.concatenate([described(row, shift)[k] for row in range(n_row) for shift in shifts]),
            jnp.int32,
        )
        for k in range(2)
    ]
    first = 0
    for entries in rounds:
        pieces = [piece for piece, _ in entries]
        out = trailing(front, pieces, first, place, tables, panels, incoming)
        panels = [panels[0], out, *panels[2:]]
        first += len(pieces)
    return panels[1]


def solution(mesh):
    return jax.shard_map(
        body,
        mesh=mesh,
        in_specs=(
            P(None, "row", None, "col", None, None),
            P(BOTH, None, None),
            P(BOTH, None),
            P(BOTH),
            P(BOTH),
            P(),
        ),
        out_specs=P(None, "row", None, "col", None, None),
        check_vma=False,
    )
```

```python
import functools

import jax
import jax.numpy as jnp
import numpy as np
from jax import lax
from jax.experimental import pallas as pl
from jax.experimental.pallas import tpu as pltpu
from jax.sharding import PartitionSpec as P

TILE = 128
PANEL = 256
WIDTH = 2 * PANEL
NOTE = 8
VMEM = 46 * 1024 * 1024
BOTH = ("row", "col")


def halves(value):
    high = value.astype(jnp.bfloat16)
    low = (value - high.astype(jnp.float32)).astype(jnp.bfloat16)
    return high, low


def deep(value):
    high, low = halves(value)
    return jnp.concatenate([high, low, high], axis=1)


def stacked(value):
    high, low = halves(value)
    return jnp.concatenate([high, high, low], axis=0)


def dot(left, right):
    return jnp.dot(left, right, preferred_element_type=jnp.float32)


def two_panels(columns, small_ref, mask):
    one = mask(0, dot(deep(jnp.concatenate(columns[:2], axis=1)), small_ref[0]))
    field = jnp.concatenate(columns[2:], axis=1) - dot(deep(mask(1, one)), small_ref[1])
    return one, mask(1, dot(deep(field), small_ref[2]))


def two_panels_across(columns, small_ref):
    one = dot(small_ref[0], stacked(jnp.concatenate(columns[:2], axis=0)))
    field = jnp.concatenate(columns[2:], axis=0) - dot(small_ref[1], stacked(one))
    return one, dot(small_ref[2], stacked(field))


def whole_spec(array):
    rank = len(array.shape)
    return pl.BlockSpec(array.shape, lambda *_: (0,) * rank)


def lead_slices(devices):
    height = max(8, 4 * TILE // devices)
    return 4 * TILE // height, height


def notes_kernel(
    owners, place, dest, slot, count, child_ref, front_ref, out_ref, tile_ref, sem
):
    slots = dest.shape[0]
    height = out_ref.shape[1] - NOTE
    each = TILE // height
    live = jnp.minimum(count[0], slots)
    out_ref[:, :NOTE] = jnp.full((out_ref.shape[0], NOTE, TILE), -1.0, jnp.float32)
    out_ref[:, NOTE:] = jnp.zeros((out_ref.shape[0], height, TILE), jnp.float32)

    @pl.loop(0, live)
    def _(k):
        out_ref[dest[k], :NOTE] = jnp.full((NOTE, TILE), slot[k].astype(jnp.float32))

    def add(i, tile):
        copy = pltpu.make_async_copy(tile, tile_ref, sem)
        copy.start()
        copy.wait()
        span = pl.ds(i * each, each)
        out_ref[span, NOTE:] = out_ref[span, NOTE:] + tile_ref[...].reshape(each, height, TILE)

    for i, owner in enumerate(owners):
        pl.when(place[3] == owner)(functools.partial(add, i, front_ref.at[0, 0, 0, 0]))

    @pl.loop(0, live)
    def _(k):
        for i, owner in enumerate(owners):
            wanted = jnp.logical_and(slot[k] == 0, dest[k] == owner)
            pl.when(wanted)(functools.partial(add, i, child_ref.at[k]))


def make_notes(child_tiles, front, place, dest, slot, count, devices, owners):
    _, height = lead_slices(devices)
    hbm = pl.BlockSpec(memory_space=pltpu.HBM)
    return pl.pallas_call(
        functools.partial(notes_kernel, owners),
        in_specs=[pl.BlockSpec(memory_space=pltpu.SMEM)] * 4 + [hbm, hbm],
        out_specs=pl.BlockSpec(memory_space=pltpu.VMEM),
        scratch_shapes=[pltpu.VMEM((TILE, TILE), jnp.float32), pltpu.SemaphoreType.DMA],
        out_shape=jax.ShapeDtypeStruct((devices, NOTE + height, TILE), jnp.float32),
        compiler_params=pltpu.CompilerParams(vmem_limit_bytes=VMEM),
        name="notes",
    )(place, dest, slot, count, child_tiles, front)


def pack_kernel(dest, count, child_ref, out_ref, sems):
    slots = child_ref.shape[0]
    live = jnp.minimum(count[0], slots)

    def copy(k):
        return pltpu.make_async_copy(child_ref.at[k], out_ref.at[dest[k]], sems.at[k])

    @pl.loop(0, live)
    def _(k):
        copy(k).start()

    @pl.loop(0, live)
    def _(k):
        copy(k).wait()


def pack(child_tiles, dest, count, devices):
    slots = child_tiles.shape[0]
    return pl.pallas_call(
        pack_kernel,
        in_specs=[pl.BlockSpec(memory_space=pltpu.SMEM)] * 2
        + [pl.BlockSpec(memory_space=pltpu.VMEM)],
        out_specs=pl.BlockSpec(memory_space=pltpu.HBM),
        scratch_shapes=[pltpu.SemaphoreType.DMA((slots,))],
        out_shape=jax.ShapeDtypeStruct((devices, TILE, TILE), jnp.float32),
        compiler_params=pltpu.CompilerParams(vmem_limit_bytes=VMEM),
        name="pack",
    )(dest, count, child_tiles)


def columns_kernel(place, slot_in, front_ref, incoming_ref, out_ref, *rest):
    *parts, tile_ref, sem = rest
    cols = place[2]
    strip = pltpu.make_async_copy(front_ref.at[:, 0, 0, 0], out_ref, sem)
    strip.start()
    strip.wait()

    @pl.loop(0, incoming_ref.shape[0])
    def _(s):
        slot = slot_in[s]

        @pl.when(jnp.logical_and(slot >= 0, lax.rem(slot, cols) == 0))
        def _():
            copy = pltpu.make_async_copy(incoming_ref.at[s], tile_ref, sem)
            copy.start()
            copy.wait()
            row = lax.div(slot, cols)
            out_ref[row] = out_ref[row] + tile_ref[...]

    count = len(parts)
    for j, part_ref in enumerate(parts):
        group = part_ref.shape[0]
        for t in range(group):
            part_ref[t] = out_ref[lax.rem(place[1] + j, count) * group + t].T


def assemble_columns(front, incoming, place, slot_in, parts):
    rows = front.shape[0]
    shapes = [(rows, TILE, TILE)] + [(rows // parts, TILE, TILE)] * parts
    out_shape = [jax.ShapeDtypeStruct(shape, jnp.float32) for shape in shapes]
    return pl.pallas_call(
        columns_kernel,
        grid_spec=pltpu.PrefetchScalarGridSpec(
            num_scalar_prefetch=2,
            grid=(1,),
            in_specs=[pl.BlockSpec(memory_space=pltpu.HBM)] * 2,
            out_specs=[whole_spec(a) for a in out_shape],
            scratch_shapes=[
                pltpu.VMEM((TILE, TILE), jnp.float32),
                pltpu.SemaphoreType.DMA,
            ],
        ),
        out_shape=out_shape,
        compiler_params=pltpu.CompilerParams(vmem_limit_bytes=VMEM),
        name="panel_columns",
    )(place, slot_in, front, incoming)


def row_panels_kernel(
    place, slot_in, t0, t1, t2, t3, lead_ref, diag_ref, pair_ref, out_ref, across_ref, order,
    starts, small_ref, tiles_ref, cursor,
):
    step = pl.program_id(0)
    cols = starts.shape[0] - 1
    my_row, my_col = place[0], place[1]
    group = t0.shape[0]
    height = group * TILE

    @pl.when(step == 0)
    def _():
        small_ref[0] = stacked(diag_ref[0])
        lead = jnp.concatenate(
            [jnp.concatenate([lead_ref[i, 0], lead_ref[i, 1]], axis=1) for i in range(2)], axis=0
        )
        lead = dot(deep(lead), small_ref[0])
        small_ref[1] = stacked(lead.T)
        small_ref[2] = stacked(diag_ref[1])
        across_ref[0] = deep(diag_ref[0].T)
        across_ref[1] = deep(lead)
        across_ref[2] = deep(diag_ref[1].T)

        @pl.loop(0, cols + 1)
        def _(b):
            starts[b] = 0

        @pl.loop(0, slot_in.shape[0])
        def _(s):
            @pl.when(slot_in[s] >= 0)
            def _():
                b = lax.rem(slot_in[s], cols)
                starts[b + 1] = starts[b + 1] + 1

        @pl.loop(0, cols)
        def _(b):
            cursor[b] = starts[b]
            starts[b + 1] = starts[b + 1] + starts[b]

        @pl.loop(0, slot_in.shape[0])
        def _(s):
            @pl.when(slot_in[s] >= 0)
            def _():
                b = lax.rem(slot_in[s], cols)
                i = cursor[b]
                order[2 * i] = s
                order[2 * i + 1] = lax.div(slot_in[s], cols)
                cursor[b] = i + 1


    for i, tile_ref in enumerate((t0, t1, t2, t3)):
        tiles_ref[jnp.bitwise_xor(my_col, i)] = tile_ref[...]
    columns = [tiles_ref[c].reshape(height, TILE) for c in range(4)]
    tile_row = lax.broadcasted_iota(jnp.int32, (height, PANEL), 0) // TILE
    first = jnp.logical_and(step == 0, tile_row == 0)

    def mask(panels_above, value):
        above = jnp.logical_and(first, my_row < 2 * panels_above)
        return jnp.where(above, 0.0, value) if panels_above else value

    one, two = two_panels(columns, small_ref, mask)
    for i, panel in enumerate((mask(1, one), mask(2, two))):
        for k, half in enumerate(halves(panel)):
            pair_ref[:, k * WIDTH + i * PANEL : k * WIDTH + (i + 1) * PANEL] = half
    pieces = (one[:, :TILE], one[:, TILE:], two[:, :TILE], two[:, TILE:])
    for c in range(4):

        @pl.when(my_col == c)
        def _():
            out_ref[:, 0, 0, 0] = pieces[c].reshape(group, TILE, TILE)


def row_panels(mine, others, lead, diag, place, slot_in, front):
    rows = front.shape[0]
    cols = front.shape[2]
    group = rows // 3
    height = group * TILE
    out_shape = [
        jax.ShapeDtypeStruct((rows * TILE, 2 * WIDTH), jnp.bfloat16),
        jax.ShapeDtypeStruct(front.shape, jnp.float32),
        jax.ShapeDtypeStruct((3, PANEL, 3 * PANEL), jnp.bfloat16),
        jax.ShapeDtypeStruct((2 * slot_in.shape[0],), jnp.int32),
        jax.ShapeDtypeStruct((cols + 1,), jnp.int32),
    ]
    strip = pl.BlockSpec((group, TILE, TILE), lambda i, *_: (i, 0, 0))
    return pl.pallas_call(
        row_panels_kernel,
        grid_spec=pltpu.PrefetchScalarGridSpec(
            num_scalar_prefetch=2,
            grid=(3,),
            in_specs=[strip] * 4 + [whole_spec(lead), whole_spec(diag)],
            out_specs=[
                pl.BlockSpec((height, 2 * WIDTH), lambda i, *_: (i, 0)),
                pl.BlockSpec((group, 1, 1, 1, TILE, TILE), lambda i, *_: (i, 0, 0, 0, 0, 0)),
                whole_spec(out_shape[2]),
                pl.BlockSpec(memory_space=pltpu.SMEM),
                pl.BlockSpec(memory_space=pltpu.SMEM),
            ],
            scratch_shapes=[
                pltpu.VMEM((3, 3 * PANEL, PANEL), jnp.bfloat16),
                pltpu.VMEM((4, group, TILE, TILE), jnp.float32),
                pltpu.SMEM((cols,), jnp.int32),
            ],
        ),
        out_shape=out_shape,
        compiler_params=pltpu.CompilerParams(vmem_limit_bytes=VMEM),
        name="row_panels",
    )(place, slot_in, mine, *others, lead, diag)


def trailing_kernel(
    first, n_pieces, place, columns_table, places_table, order, starts, pair_ref, small_ref, *rest
):
    piece_refs = rest[:n_pieces]
    front_ref, incoming_ref, _, out_ref, right_ref, taken, given, child_ref = rest[n_pieces:-3]
    take_sems, give_sems, child_sems = rest[-3:]
    group = piece_refs[0].shape[1]
    count = n_pieces * group
    steps = (count + 1) // 2
    rows, cols = front_ref.shape[0], front_ref.shape[2]
    columns_base = place[0] * cols + first * group
    places_base = (place[0] * (cols // group) + first) * 4

    def columns_of(step):
        for j in range(2):
            index = jnp.minimum(2 * step, count - 2) + j
            b = columns_table[columns_base + index]
            wanted = b > 0
            if count % 2 and j == 0:
                wanted = jnp.logical_and(wanted, step < steps - 1)
            yield j, b, wanted

    def each_take(step, act):
        slot = lax.rem(step, 2)
        for j, b, wanted in columns_of(step):

            @pl.when(wanted)
            def _():
                act(
                    pltpu.make_async_copy(
                        front_ref.at[:, 0, b, 0], taken.at[slot, j], take_sems.at[slot, j]
                    )
                )

    def each_give(step, act):
        slot = lax.rem(step, 2)
        for j, b, wanted in columns_of(step):

            @pl.when(wanted)
            def _():
                act(
                    pltpu.make_async_copy(
                        given.at[slot, j], out_ref.at[:, 0, b, 0], give_sems.at[slot, j]
                    )
                )

    def each_child(step, act):
        for j, b, wanted in columns_of(step):

            @pl.when(wanted)
            def _():
                @pl.loop(starts[b], starts[b + 1])
                def _(i):
                    s = order[2 * i]
                    copy = pltpu.make_async_copy(
                        incoming_ref.at[s], child_ref.at[s], child_sems.at[s]
                    )
                    act(copy, j, s, order[2 * i + 1])

    for step in range(min(steps, 2)):
        each_take(step, lambda copy: copy.start())
    for step in range(steps):
        each_child(step, lambda copy, *_: copy.start())

    tile_columns = [
        jnp.concatenate(
            [
                piece[places_table[places_base + 4 * p + c], t]
                for p, piece in enumerate(piece_refs)
                for t in range(group)
            ],
            axis=1,
        )
        for c in range(4)
    ]
    for i, panel in enumerate(two_panels_across(tile_columns, small_ref)):
        high, low = halves(panel)
        for k, half in enumerate((high, high, low)):
            right_ref[k * WIDTH + i * PANEL : k * WIDTH + (i + 1) * PANEL] = half

    @pl.loop(0, steps)
    def _(step):
        slot = lax.rem(step, 2)
        each_take(step, lambda copy: copy.wait())

        @pl.when(step >= 2)
        def _():
            each_give(step - 2, lambda copy: copy.wait())

        start = jnp.minimum(2 * step, count - 2)
        lanes = pl.ds(pl.multiple_of(start * TILE, TILE), 2 * TILE)
        block = rows // 3
        for m in range(3):
            left = pair_ref[m * block * TILE : (m + 1) * block * TILE]
            update = dot(jnp.concatenate([left, left[:, :WIDTH]], axis=1), right_ref[:, lanes])
            span = slice(m * block, (m + 1) * block)
            for j in range(2):
                part = update[:, j * TILE : (j + 1) * TILE].reshape(block, TILE, TILE)
                given[slot, j, span] = taken[slot, j, span] - part

        def add(copy, j, s, a):
            copy.wait()
            given[slot, j, a] = given[slot, j, a] + child_ref[s]

        each_child(step, add)
        each_give(step, lambda copy: copy.start())

        @pl.when(step + 2 < steps)
        def _():
            each_take(step + 2, lambda copy: copy.start())

    for step in range(max(steps - 2, 0), steps):
        each_give(step, lambda copy: copy.wait())


def trailing(front, pieces, first, place, tables, panels, incoming):
    rows = front.shape[0]
    pair, out, small, order, starts = panels
    group = pieces[0].shape[1]
    count = len(pieces) * group
    scalars = [place, *tables, order, starts]
    held = [pair, small, *pieces]
    distant = [front, incoming, out]
    spec = lambda space, n: [pl.BlockSpec(memory_space=space)] * n
    height = rows * TILE
    devices = incoming.shape[0]
    return pl.pallas_call(
        functools.partial(trailing_kernel, first, len(pieces)),
        in_specs=spec(pltpu.SMEM, 5) + spec(pltpu.VMEM, len(held)) + spec(pltpu.HBM, 3),
        out_specs=pl.BlockSpec(memory_space=pltpu.HBM),
        scratch_shapes=[
            pltpu.VMEM((3 * WIDTH, count * TILE), jnp.bfloat16),
            pltpu.VMEM((2, 2, rows, TILE, TILE), jnp.float32),
            pltpu.VMEM((2, 2, rows, TILE, TILE), jnp.float32),
            pltpu.VMEM((devices, TILE, TILE), jnp.float32),
            pltpu.SemaphoreType.DMA((2, 2)),
            pltpu.SemaphoreType.DMA((2, 2)),
            pltpu.SemaphoreType.DMA((devices,)),
        ],
        out_shape=jax.ShapeDtypeStruct(front.shape, jnp.float32),
        input_output_aliases={len(held) + 7: 0},
        compiler_params=pltpu.CompilerParams(vmem_limit_bytes=VMEM),
        cost_estimate=pl.CostEstimate(
            flops=8 * count * 2 * height * TILE * WIDTH,
            bytes_accessed=count * 2 * height * TILE * 4,
            transcendentals=0,
        ),
        name="trailing",
    )(*scalars, *held, *distant)


def body(front, child_tiles, tile_dest, tile_slot, tile_count, diag_inverses):
    n_row = lax.axis_size("row")
    n_col = lax.axis_size("col")
    my_row = lax.axis_index("row").astype(jnp.int32)
    my_col = lax.axis_index("col").astype(jnp.int32)
    rows_here, cols_here = (front.shape[0], front.shape[2])
    devices = n_row * n_col
    assert n_col == 4 and n_row % 4 == 0 and rows_here % 3 == 0
    owners = [r * n_col + c for r in (2, 3) for c in (0, 1)]
    place = jnp.stack([my_row, my_col, jnp.int32(cols_here), my_row * n_col + my_col])

    dest = tile_dest[:, 0]
    notes = make_notes(child_tiles, front, place, dest, tile_slot, tile_count, devices, owners)
    notes = lax.all_to_all(notes, BOTH, split_axis=0, concat_axis=0, tiled=True)
    slot_in = notes[:, 0, 0].astype(jnp.int32)
    lead = jnp.broadcast_to(jnp.sum(notes[:, NOTE:], axis=0)[None], notes[:, NOTE:].shape)
    lead = lax.all_to_all(lead, BOTH, split_axis=0, concat_axis=0, tiled=True)
    lead = lead[: lead_slices(devices)[0]].reshape(2, 2, TILE, TILE)

    outgoing = pack(child_tiles, dest, tile_count, devices)
    outgoing, slot_in = lax.optimization_barrier((outgoing, slot_in))
    incoming = lax.all_to_all(outgoing, BOTH, split_axis=0, concat_axis=0, tiled=True)
    incoming, lead = lax.optimization_barrier((incoming, lead))

    ring = rows_here % n_col == 0
    mine, *parts = assemble_columns(front, incoming, place, slot_in, n_col if ring else 1)

    def exchange(mine):
        near = lax.ppermute(mine, "col", [(c, c ^ 1) for c in range(n_col)])
        far = lax.ppermute(mine, "col", [(c, c ^ 2) for c in range(n_col)])
        return [near, far, lax.ppermute(far, "col", [(c, c ^ 1) for c in range(n_col)])]

    def own_panels(mine):
        return row_panels(mine, exchange(mine), lead, diag_inverses, place, slot_in, front)

    sets = n_row // n_col
    if ring:
        arrived = []
        for j, part in enumerate(parts):
            pairs = [
                (r * n_col + c, ((r // n_col) * n_col + (c + j) % n_col) * n_col + r % n_col)
                for r in range(n_row)
                for c in range(n_col)
            ]
            arrived.append(lax.ppermute(part, BOTH, pairs))
        arrived, mine = lax.optimization_barrier((arrived, mine))
        piece = jnp.stack(arrived)
        circle = list(range(0, n_row, 2)) + list(range(n_row - 1, 0, -2))
        up = [(circle[i], circle[(i + 1) % n_row]) for i in range(n_row)]
        down = [(b, a) for a, b in up]
        rounds = [[(piece, 0)]]
        panels = own_panels(mine)
        ahead = behind = piece
        for step in range(1, n_row // 2):
            ahead = lax.ppermute(ahead, "row", up)
            behind = lax.ppermute(behind, "row", down)
            if step == 2:
                ahead, behind, panels = lax.optimization_barrier((ahead, behind, panels))
            rounds.append([(ahead, -step), (behind, step)])
        last = jnp.concatenate(
            [lax.ppermute(ahead[:2], "row", up), lax.ppermute(behind[2:], "row", down)]
        )
        rounds.append([(last, n_row // 2)])
        rounds = [rounds[0] + rounds[1]] + rounds[2:]

        def described(row, shift):
            origin = circle[(circle.index(row) + shift) % n_row]
            part, group = origin % n_col, rows_here // n_col
            columns = [(part * group + t) * sets + origin // n_col for t in range(group)]
            return columns, [(part - c) % n_col for c in range(n_col)]

    else:
        pairs = [
            (r * n_col + c, ((r // n_col) * n_col + c) * n_col + r % n_col)
            for r in range(n_row)
            for c in range(n_col)
        ]
        moved = lax.all_gather(lax.ppermute(parts[0], BOTH, pairs), "row", axis=0, tiled=False)
        rounds = [[(moved[h * n_col : (h + 1) * n_col], h)] for h in range(sets)]
        panels = own_panels(mine)

        def described(row, h):
            return [a * sets + h for a in range(rows_here)], list(range(n_col))

    shifts = [shift for entries in rounds for _, shift in entries]
    tables = [
        jnp.asarray(
            np.concatenate([described(row, shift)[k] for row in range(n_row) for shift in shifts]),
            jnp.int32,
        )
        for k in range(2)
    ]
    first = 0
    for entries in rounds:
        pieces = [piece for piece, _ in entries]
        out = trailing(front, pieces, first, place, tables, panels, incoming)
        panels = [panels[0], out, *panels[2:]]
        first += len(pieces)
    return panels[1]


def solution(mesh):
    return jax.shard_map(
        body,
        mesh=mesh,
        in_specs=(
            P(None, "row", None, "col", None, None),
            P(BOTH, None, None),
            P(BOTH, None),
            P(BOTH),
            P(BOTH),
            P(),
        ),
        out_specs=P(None, "row", None, "col", None, None),
        check_vma=False,
    )
```

```python
import functools

import jax
import jax.numpy as jnp
import numpy as np
from jax import lax
from jax.experimental import pallas as pl
from jax.experimental.pallas import tpu as pltpu
from jax.sharding import PartitionSpec as P

TILE = 128
PANEL = 256
WIDTH = 2 * PANEL
NOTE = 8
VMEM = 46 * 1024 * 1024
BOTH = ("row", "col")


def halves(value):
    high = value.astype(jnp.bfloat16)
    low = (value - high.astype(jnp.float32)).astype(jnp.bfloat16)
    return high, low


def deep(value):
    high, low = halves(value)
    return jnp.concatenate([high, low, high], axis=1)


def stacked(value):
    high, low = halves(value)
    return jnp.concatenate([high, high, low], axis=0)


def dot(left, right):
    return jnp.dot(left, right, preferred_element_type=jnp.float32)


def two_panels(columns, small_ref, mask):
    one = mask(0, dot(deep(jnp.concatenate(columns[:2], axis=1)), small_ref[0]))
    field = jnp.concatenate(columns[2:], axis=1) - dot(deep(mask(1, one)), small_ref[1])
    return one, mask(1, dot(deep(field), small_ref[2]))


def two_panels_across(columns, small_ref):
    one = dot(small_ref[0], stacked(jnp.concatenate(columns[:2], axis=0)))
    field = jnp.concatenate(columns[2:], axis=0) - dot(small_ref[1], stacked(one))
    return one, dot(small_ref[2], stacked(field))


def whole_spec(array):
    rank = len(array.shape)
    return pl.BlockSpec(array.shape, lambda *_: (0,) * rank)


def pack_kernel(dest, slot, count, child_ref, out_ref, notes_ref, sems, notes_sem):
    slots = child_ref.shape[0]
    live = jnp.minimum(count[0], slots)

    def copy(k):
        return pltpu.make_async_copy(
            child_ref.at[k], out_ref.at[dest[k], pl.ds(0, TILE)], sems.at[k]
        )

    notes_ref[...] = jnp.full_like(notes_ref, -1.0)

    @pl.loop(0, live)
    def _(k):
        copy(k).start()
        notes_ref[dest[k]] = jnp.full(notes_ref.shape[1:], slot[k].astype(jnp.float32))

    notes = pltpu.make_async_copy(notes_ref, out_ref.at[:, pl.ds(TILE, NOTE)], notes_sem)
    notes.start()
    notes.wait()

    @pl.loop(0, live)
    def _(k):
        copy(k).wait()


def pack(child_tiles, dest, slot, count, devices):
    slots = child_tiles.shape[0]
    return pl.pallas_call(
        pack_kernel,
        in_specs=[pl.BlockSpec(memory_space=pltpu.SMEM)] * 3
        + [pl.BlockSpec(memory_space=pltpu.VMEM)],
        out_specs=pl.BlockSpec(memory_space=pltpu.HBM),
        scratch_shapes=[
            pltpu.VMEM((devices, NOTE, TILE), jnp.float32),
            pltpu.SemaphoreType.DMA((slots,)),
            pltpu.SemaphoreType.DMA,
        ],
        out_shape=jax.ShapeDtypeStruct((devices, TILE + NOTE, TILE), jnp.float32),
        compiler_params=pltpu.CompilerParams(vmem_limit_bytes=VMEM),
        name="pack",
    )(dest, slot, count, child_tiles)


def columns_kernel(place, slot_in, front_ref, incoming_ref, out_ref, top_ref, *rest):
    *parts, tile_ref, sem = rest
    cols = place[2]
    strip = pltpu.make_async_copy(front_ref.at[:, 0, 0, 0], out_ref, sem)
    strip.start()
    strip.wait()

    @pl.loop(0, incoming_ref.shape[0])
    def _(s):
        slot = slot_in[s]

        @pl.when(jnp.logical_and(slot >= 0, lax.rem(slot, cols) == 0))
        def _():
            copy = pltpu.make_async_copy(incoming_ref.at[s, pl.ds(0, TILE)], tile_ref, sem)
            copy.start()
            copy.wait()
            row = lax.div(slot, cols)
            out_ref[row] = out_ref[row] + tile_ref[...]

    top_ref[...] = out_ref[0]
    count = len(parts)
    for j, part_ref in enumerate(parts):
        group = part_ref.shape[0]
        for t in range(group):
            part_ref[t] = out_ref[lax.rem(place[1] + j, count) * group + t].T


def assemble_columns(front, incoming, place, slot_in, parts):
    rows = front.shape[0]
    shapes = [(rows, TILE, TILE), (TILE, TILE)] + [(rows // parts, TILE, TILE)] * parts
    out_shape = [jax.ShapeDtypeStruct(shape, jnp.float32) for shape in shapes]
    return pl.pallas_call(
        columns_kernel,
        grid_spec=pltpu.PrefetchScalarGridSpec(
            num_scalar_prefetch=2,
            grid=(1,),
            in_specs=[pl.BlockSpec(memory_space=pltpu.HBM)] * 2,
            out_specs=[whole_spec(a) for a in out_shape],
            scratch_shapes=[
                pltpu.VMEM((TILE, TILE), jnp.float32),
                pltpu.SemaphoreType.DMA,
            ],
        ),
        out_shape=out_shape,
        compiler_params=pltpu.CompilerParams(vmem_limit_bytes=VMEM),
        name="panel_columns",
    )(place, slot_in, front, incoming)


def row_panels_kernel(
    place, slot_in, t0, t1, t2, t3, lead_ref, diag_ref, pair_ref, out_ref, across_ref, order,
    starts, small_ref, tiles_ref, cursor,
):
    step = pl.program_id(0)
    cols = starts.shape[0] - 1
    my_row, my_col = place[0], place[1]
    group = t0.shape[0]
    height = group * TILE

    @pl.when(step == 0)
    def _():
        small_ref[0] = stacked(diag_ref[0])
        lead = jnp.concatenate(
            [jnp.concatenate([lead_ref[i, 0], lead_ref[i, 1]], axis=1) for i in range(2)], axis=0
        )
        lead = dot(deep(lead), small_ref[0])
        small_ref[1] = stacked(lead.T)
        small_ref[2] = stacked(diag_ref[1])
        across_ref[0] = deep(diag_ref[0].T)
        across_ref[1] = deep(lead)
        across_ref[2] = deep(diag_ref[1].T)

        @pl.loop(0, cols + 1)
        def _(b):
            starts[b] = 0

        @pl.loop(0, slot_in.shape[0])
        def _(s):
            @pl.when(slot_in[s] >= 0)
            def _():
                b = lax.rem(slot_in[s], cols)
                starts[b + 1] = starts[b + 1] + 1

        @pl.loop(0, cols)
        def _(b):
            cursor[b] = starts[b]
            starts[b + 1] = starts[b + 1] + starts[b]

        @pl.loop(0, slot_in.shape[0])
        def _(s):
            @pl.when(slot_in[s] >= 0)
            def _():
                b = lax.rem(slot_in[s], cols)
                i = cursor[b]
                order[2 * i] = s
                order[2 * i + 1] = lax.div(slot_in[s], cols)
                cursor[b] = i + 1


    for i, tile_ref in enumerate((t0, t1, t2, t3)):
        tiles_ref[jnp.bitwise_xor(my_col, i)] = tile_ref[...]
    columns = [tiles_ref[c].reshape(height, TILE) for c in range(4)]
    tile_row = lax.broadcasted_iota(jnp.int32, (height, PANEL), 0) // TILE
    first = jnp.logical_and(step == 0, tile_row == 0)

    def mask(panels_above, value):
        above = jnp.logical_and(first, my_row < 2 * panels_above)
        return jnp.where(above, 0.0, value) if panels_above else value

    one, two = two_panels(columns, small_ref, mask)
    for i, panel in enumerate((mask(1, one), mask(2, two))):
        for k, half in enumerate(halves(panel)):
            pair_ref[:, k * WIDTH + i * PANEL : k * WIDTH + (i + 1) * PANEL] = half
    pieces = (one[:, :TILE], one[:, TILE:], two[:, :TILE], two[:, TILE:])
    for c in range(4):

        @pl.when(my_col == c)
        def _():
            out_ref[:, 0, 0, 0] = pieces[c].reshape(group, TILE, TILE)


def row_panels(mine, others, lead, diag, place, slot_in, front):
    rows = front.shape[0]
    cols = front.shape[2]
    group = rows // 3
    height = group * TILE
    out_shape = [
        jax.ShapeDtypeStruct((rows * TILE, 2 * WIDTH), jnp.bfloat16),
        jax.ShapeDtypeStruct(front.shape, jnp.float32),
        jax.ShapeDtypeStruct((3, PANEL, 3 * PANEL), jnp.bfloat16),
        jax.ShapeDtypeStruct((2 * slot_in.shape[0],), jnp.int32),
        jax.ShapeDtypeStruct((cols + 1,), jnp.int32),
    ]
    strip = pl.BlockSpec((group, TILE, TILE), lambda i, *_: (i, 0, 0))
    return pl.pallas_call(
        row_panels_kernel,
        grid_spec=pltpu.PrefetchScalarGridSpec(
            num_scalar_prefetch=2,
            grid=(3,),
            in_specs=[strip] * 4 + [whole_spec(lead), whole_spec(diag)],
            out_specs=[
                pl.BlockSpec((height, 2 * WIDTH), lambda i, *_: (i, 0)),
                pl.BlockSpec((group, 1, 1, 1, TILE, TILE), lambda i, *_: (i, 0, 0, 0, 0, 0)),
                whole_spec(out_shape[2]),
                pl.BlockSpec(memory_space=pltpu.SMEM),
                pl.BlockSpec(memory_space=pltpu.SMEM),
            ],
            scratch_shapes=[
                pltpu.VMEM((3, 3 * PANEL, PANEL), jnp.bfloat16),
                pltpu.VMEM((4, group, TILE, TILE), jnp.float32),
                pltpu.SMEM((cols,), jnp.int32),
            ],
        ),
        out_shape=out_shape,
        compiler_params=pltpu.CompilerParams(vmem_limit_bytes=VMEM),
        name="row_panels",
    )(place, slot_in, mine, *others, lead, diag)


def trailing_kernel(
    first, n_pieces, place, columns_table, places_table, order, starts, pair_ref, small_ref, *rest
):
    piece_refs = rest[:n_pieces]
    front_ref, incoming_ref, _, out_ref, right_ref, taken, given, child_ref = rest[n_pieces:-3]
    take_sems, give_sems, child_sems = rest[-3:]
    group = piece_refs[0].shape[1]
    count = n_pieces * group
    steps = (count + 1) // 2
    rows, cols = front_ref.shape[0], front_ref.shape[2]
    columns_base = place[0] * cols + first * group
    places_base = (place[0] * (cols // group) + first) * 4

    def columns_of(step):
        for j in range(2):
            index = jnp.minimum(2 * step, count - 2) + j
            b = columns_table[columns_base + index]
            wanted = b > 0
            if count % 2 and j == 0:
                wanted = jnp.logical_and(wanted, step < steps - 1)
            yield j, b, wanted

    def each_take(step, act):
        slot = lax.rem(step, 2)
        for j, b, wanted in columns_of(step):

            @pl.when(wanted)
            def _():
                act(
                    pltpu.make_async_copy(
                        front_ref.at[:, 0, b, 0], taken.at[slot, j], take_sems.at[slot, j]
                    )
                )

    def each_give(step, act):
        slot = lax.rem(step, 2)
        for j, b, wanted in columns_of(step):

            @pl.when(wanted)
            def _():
                act(
                    pltpu.make_async_copy(
                        given.at[slot, j], out_ref.at[:, 0, b, 0], give_sems.at[slot, j]
                    )
                )

    def each_child(step, act):
        for j, b, wanted in columns_of(step):

            @pl.when(wanted)
            def _():
                @pl.loop(starts[b], starts[b + 1])
                def _(i):
                    s = order[2 * i]
                    copy = pltpu.make_async_copy(
                        incoming_ref.at[s, pl.ds(0, TILE)], child_ref.at[s], child_sems.at[s]
                    )
                    act(copy, j, s, order[2 * i + 1])

    for step in range(min(steps, 2)):
        each_take(step, lambda copy: copy.start())
    for step in range(steps):
        each_child(step, lambda copy, *_: copy.start())

    tile_columns = [
        jnp.concatenate(
            [
                piece[places_table[places_base + 4 * p + c], t]
                for p, piece in enumerate(piece_refs)
                for t in range(group)
            ],
            axis=1,
        )
        for c in range(4)
    ]
    for i, panel in enumerate(two_panels_across(tile_columns, small_ref)):
        high, low = halves(panel)
        for k, half in enumerate((high, high, low)):
            right_ref[k * WIDTH + i * PANEL : k * WIDTH + (i + 1) * PANEL] = half

    @pl.loop(0, steps)
    def _(step):
        slot = lax.rem(step, 2)
        each_take(step, lambda copy: copy.wait())

        @pl.when(step >= 2)
        def _():
            each_give(step - 2, lambda copy: copy.wait())

        start = jnp.minimum(2 * step, count - 2)
        lanes = pl.ds(pl.multiple_of(start * TILE, TILE), 2 * TILE)
        block = rows // 3
        for m in range(3):
            left = pair_ref[m * block * TILE : (m + 1) * block * TILE]
            update = dot(jnp.concatenate([left, left[:, :WIDTH]], axis=1), right_ref[:, lanes])
            span = slice(m * block, (m + 1) * block)
            for j in range(2):
                part = update[:, j * TILE : (j + 1) * TILE].reshape(block, TILE, TILE)
                given[slot, j, span] = taken[slot, j, span] - part

        def add(copy, j, s, a):
            copy.wait()
            given[slot, j, a] = given[slot, j, a] + child_ref[s]

        each_child(step, add)
        each_give(step, lambda copy: copy.start())

        @pl.when(step + 2 < steps)
        def _():
            each_take(step + 2, lambda copy: copy.start())

    for step in range(max(steps - 2, 0), steps):
        each_give(step, lambda copy: copy.wait())


def trailing(front, pieces, first, place, tables, panels, incoming):
    rows = front.shape[0]
    pair, out, small, order, starts = panels
    group = pieces[0].shape[1]
    count = len(pieces) * group
    scalars = [place, *tables, order, starts]
    held = [pair, small, *pieces]
    distant = [front, incoming, out]
    spec = lambda space, n: [pl.BlockSpec(memory_space=space)] * n
    height = rows * TILE
    devices = incoming.shape[0]
    return pl.pallas_call(
        functools.partial(trailing_kernel, first, len(pieces)),
        in_specs=spec(pltpu.SMEM, 5) + spec(pltpu.VMEM, len(held)) + spec(pltpu.HBM, 3),
        out_specs=pl.BlockSpec(memory_space=pltpu.HBM),
        scratch_shapes=[
            pltpu.VMEM((3 * WIDTH, count * TILE), jnp.bfloat16),
            pltpu.VMEM((2, 2, rows, TILE, TILE), jnp.float32),
            pltpu.VMEM((2, 2, rows, TILE, TILE), jnp.float32),
            pltpu.VMEM((devices, TILE, TILE), jnp.float32),
            pltpu.SemaphoreType.DMA((2, 2)),
            pltpu.SemaphoreType.DMA((2, 2)),
            pltpu.SemaphoreType.DMA((devices,)),
        ],
        out_shape=jax.ShapeDtypeStruct(front.shape, jnp.float32),
        input_output_aliases={len(held) + 7: 0},
        compiler_params=pltpu.CompilerParams(vmem_limit_bytes=VMEM),
        cost_estimate=pl.CostEstimate(
            flops=8 * count * 2 * height * TILE * WIDTH,
            bytes_accessed=count * 2 * height * TILE * 4,
            transcendentals=0,
        ),
        name="trailing",
    )(*scalars, *held, *distant)


def body(front, child_tiles, tile_dest, tile_slot, tile_count, diag_inverses):
    n_row = lax.axis_size("row")
    n_col = lax.axis_size("col")
    my_row = lax.axis_index("row").astype(jnp.int32)
    my_col = lax.axis_index("col").astype(jnp.int32)
    rows_here, cols_here = (front.shape[0], front.shape[2])
    devices = n_row * n_col
    assert n_col == 4 and n_row % 4 == 0 and rows_here % 3 == 0
    owners = [r * n_col + c for r in (2, 3) for c in (0, 1)]
    place = jnp.stack([my_row, my_col, jnp.int32(cols_here), my_row * n_col + my_col])

    outgoing = pack(child_tiles, tile_dest[:, 0], tile_slot, tile_count, devices)
    incoming = lax.all_to_all(outgoing, BOTH, split_axis=0, concat_axis=0, tiled=True)
    slot_in = lax.optimization_barrier(incoming[:, TILE, 0].astype(jnp.int32))

    ring = rows_here % n_col == 0
    mine, top, *parts = assemble_columns(front, incoming, place, slot_in, n_col if ring else 1)

    slices = top.reshape(devices, TILE // devices, TILE)
    slices = lax.all_to_all(slices, BOTH, split_axis=0, concat_axis=0, tiled=True)
    slices = jnp.stack([slices[owner] for owner in owners])
    slices = jnp.broadcast_to(slices[None], (devices,) + slices.shape)

    def hand_on(slices):
        lead = lax.all_to_all(slices, BOTH, split_axis=0, concat_axis=0, tiled=True)
        return lead.transpose(1, 0, 2, 3).reshape(2, 2, TILE, TILE)

    def exchange(mine):
        near = lax.ppermute(mine, "col", [(c, c ^ 1) for c in range(n_col)])
        far = lax.ppermute(mine, "col", [(c, c ^ 2) for c in range(n_col)])
        return [near, far, lax.ppermute(far, "col", [(c, c ^ 1) for c in range(n_col)])]

    def own_panels(mine, lead):
        return row_panels(mine, exchange(mine), lead, diag_inverses, place, slot_in, front)

    sets = n_row // n_col
    if ring:
        arrived = []
        for j, part in enumerate(parts):
            pairs = [
                (r * n_col + c, ((r // n_col) * n_col + (c + j) % n_col) * n_col + r % n_col)
                for r in range(n_row)
                for c in range(n_col)
            ]
            arrived.append(lax.ppermute(part, BOTH, pairs))
        arrived, mine, slices = lax.optimization_barrier((arrived, mine, slices))
        piece = jnp.stack(arrived)
        circle = list(range(0, n_row, 2)) + list(range(n_row - 1, 0, -2))
        up = [(circle[i], circle[(i + 1) % n_row]) for i in range(n_row)]
        down = [(b, a) for a, b in up]
        rounds = [[(piece, 0)]]
        lead = hand_on(slices)
        ahead = behind = piece
        for step in range(1, n_row // 2):
            ahead = lax.ppermute(ahead, "row", up)
            behind = lax.ppermute(behind, "row", down)
            if step == 1:
                ahead, behind, lead = lax.optimization_barrier((ahead, behind, lead))
                panels = own_panels(mine, lead)
            if step == 2:
                ahead, behind, panels = lax.optimization_barrier((ahead, behind, panels))
            rounds.append([(ahead, -step), (behind, step)])
        last = jnp.concatenate(
            [lax.ppermute(ahead[:2], "row", up), lax.ppermute(behind[2:], "row", down)]
        )
        rounds.append([(last, n_row // 2)])
        rounds = [rounds[0] + rounds[1]] + rounds[2:]

        def described(row, shift):
            origin = circle[(circle.index(row) + shift) % n_row]
            part, group = origin % n_col, rows_here // n_col
            columns = [(part * group + t) * sets + origin // n_col for t in range(group)]
            return columns, [(part - c) % n_col for c in range(n_col)]

    else:
        pairs = [
            (r * n_col + c, ((r // n_col) * n_col + c) * n_col + r % n_col)
            for r in range(n_row)
            for c in range(n_col)
        ]
        moved = lax.all_gather(lax.ppermute(parts[0], BOTH, pairs), "row", axis=0, tiled=False)
        rounds = [[(moved[h * n_col : (h + 1) * n_col], h)] for h in range(sets)]
        panels = own_panels(mine, hand_on(slices))

        def described(row, h):
            return [a * sets + h for a in range(rows_here)], list(range(n_col))

    shifts = [shift for entries in rounds for _, shift in entries]
    tables = [
        jnp.asarray(
            np.concatenate([described(row, shift)[k] for row in range(n_row) for shift in shifts]),
            jnp.int32,
        )
        for k in range(2)
    ]
    first = 0
    for entries in rounds:
        pieces = [piece for piece, _ in entries]
        out = trailing(front, pieces, first, place, tables, panels, incoming)
        panels = [panels[0], out, *panels[2:]]
        first += len(pieces)
    return panels[1]


def solution(mesh):
    return jax.shard_map(
        body,
        mesh=mesh,
        in_specs=(
            P(None, "row", None, "col", None, None),
            P(BOTH, None, None),
            P(BOTH, None),
            P(BOTH),
            P(BOTH),
            P(),
        ),
        out_specs=P(None, "row", None, "col", None, None),
        check_vma=False,
    )
```

```python
import functools

import jax
import jax.numpy as jnp
import numpy as np
from jax import lax
from jax.experimental import pallas as pl
from jax.experimental.pallas import tpu as pltpu
from jax.sharding import PartitionSpec as P

TILE = 128
PANEL = 256
WIDTH = 2 * PANEL
NOTE = 8
VMEM = 46 * 1024 * 1024
BOTH = ("row", "col")


def halves(value):
    high = value.astype(jnp.bfloat16)
    low = (value - high.astype(jnp.float32)).astype(jnp.bfloat16)
    return high, low


def deep(value):
    high, low = halves(value)
    return jnp.concatenate([high, low, high], axis=1)


def stacked(value):
    high, low = halves(value)
    return jnp.concatenate([high, high, low], axis=0)


def dot(left, right):
    return jnp.dot(left, right, preferred_element_type=jnp.float32)


def two_panels(columns, small_ref, mask):
    one = mask(0, dot(deep(jnp.concatenate(columns[:2], axis=1)), small_ref[0]))
    field = jnp.concatenate(columns[2:], axis=1) - dot(deep(mask(1, one)), small_ref[1])
    return one, mask(1, dot(deep(field), small_ref[2]))


def two_panels_across(columns, small_ref):
    one = dot(small_ref[0], stacked(jnp.concatenate(columns[:2], axis=0)))
    field = jnp.concatenate(columns[2:], axis=0) - dot(small_ref[1], stacked(one))
    return one, dot(small_ref[2], stacked(field))


def whole_spec(array):
    rank = len(array.shape)
    return pl.BlockSpec(array.shape, lambda *_: (0,) * rank)


def pack_kernel(owners, me, dest, slot, count, child_ref, top_ref, out_ref, lead_ref):
    out_ref[:, TILE:] = jnp.full((out_ref.shape[0], NOTE, TILE), -1.0, jnp.float32)
    for i, owner in enumerate(owners):
        lead_ref[i] = jnp.where(me[0] == owner, top_ref[...], 0.0)

    @pl.loop(0, jnp.minimum(count[0], child_ref.shape[0]))
    def _(k):
        out_ref[dest[k], :TILE] = child_ref[k]
        out_ref[dest[k], TILE:] = jnp.full((NOTE, TILE), slot[k].astype(jnp.float32))
        for i, owner in enumerate(owners):

            @pl.when(jnp.logical_and(slot[k] == 0, dest[k] == owner))
            def _():
                lead_ref[i] = lead_ref[i] + child_ref[k]


def pack(child_tiles, top, me, dest, slot, count, devices, owners):
    shapes = [(devices, TILE + NOTE, TILE), (len(owners), TILE, TILE)]
    spec = lambda space, n: [pl.BlockSpec(memory_space=space)] * n
    return pl.pallas_call(
        functools.partial(pack_kernel, owners),
        in_specs=spec(pltpu.SMEM, 4) + spec(pltpu.VMEM, 2),
        out_specs=spec(pltpu.VMEM, 2),
        out_shape=[jax.ShapeDtypeStruct(shape, jnp.float32) for shape in shapes],
        compiler_params=pltpu.CompilerParams(vmem_limit_bytes=VMEM),
        name="pack",
    )(me, dest, slot, count, child_tiles, top)


def columns_kernel(place, slot_in, front_ref, incoming_ref, out_ref, *rest):
    *parts, tile_ref, sem = rest
    cols = place[2]
    strip = pltpu.make_async_copy(front_ref.at[:, 0, 0, 0], out_ref, sem)
    strip.start()
    strip.wait()

    @pl.loop(0, incoming_ref.shape[0])
    def _(s):
        slot = slot_in[s]

        @pl.when(jnp.logical_and(slot >= 0, lax.rem(slot, cols) == 0))
        def _():
            copy = pltpu.make_async_copy(incoming_ref.at[s, pl.ds(0, TILE)], tile_ref, sem)
            copy.start()
            copy.wait()
            row = lax.div(slot, cols)
            out_ref[row] = out_ref[row] + tile_ref[...]

    count = len(parts)
    for j, part_ref in enumerate(parts):
        group = part_ref.shape[0]
        for t in range(group):
            part_ref[t] = out_ref[lax.rem(place[1] + j, count) * group + t].T


def assemble_columns(front, incoming, place, slot_in, parts):
    rows = front.shape[0]
    shapes = [(rows, TILE, TILE)] + [(rows // parts, TILE, TILE)] * parts
    out_shape = [jax.ShapeDtypeStruct(shape, jnp.float32) for shape in shapes]
    return pl.pallas_call(
        columns_kernel,
        grid_spec=pltpu.PrefetchScalarGridSpec(
            num_scalar_prefetch=2,
            grid=(1,),
            in_specs=[pl.BlockSpec(memory_space=pltpu.HBM)] * 2,
            out_specs=[whole_spec(a) for a in out_shape],
            scratch_shapes=[
                pltpu.VMEM((TILE, TILE), jnp.float32),
                pltpu.SemaphoreType.DMA,
            ],
        ),
        out_shape=out_shape,
        compiler_params=pltpu.CompilerParams(vmem_limit_bytes=VMEM),
        name="panel_columns",
    )(place, slot_in, front, incoming)


def row_panels_kernel(
    place, slot_in, tiles_ref, lead_ref, diag_ref, pair_ref, out_ref, across_ref, order, starts,
    small_ref, cursor,
):
    step = pl.program_id(0)
    cols = starts.shape[0] - 1
    my_row, my_col = place[0], place[1]
    group = tiles_ref.shape[1]
    height = group * TILE

    @pl.when(step == 0)
    def _():
        small_ref[0] = stacked(diag_ref[0])
        lead = jnp.concatenate(
            [jnp.concatenate([lead_ref[i], lead_ref[i + 1]], axis=1) for i in (0, 2)], axis=0
        )
        lead = dot(deep(lead), small_ref[0])
        small_ref[1] = stacked(lead.T)
        small_ref[2] = stacked(diag_ref[1])
        across_ref[0] = deep(diag_ref[0].T)
        across_ref[1] = deep(lead)
        across_ref[2] = deep(diag_ref[1].T)

        @pl.loop(0, cols + 1)
        def _(b):
            starts[b] = 0

        @pl.loop(0, slot_in.shape[0])
        def _(s):
            @pl.when(slot_in[s] >= 0)
            def _():
                b = lax.rem(slot_in[s], cols)
                starts[b + 1] = starts[b + 1] + 1

        @pl.loop(0, cols)
        def _(b):
            cursor[b] = starts[b]
            starts[b + 1] = starts[b + 1] + starts[b]

        @pl.loop(0, slot_in.shape[0])
        def _(s):
            @pl.when(slot_in[s] >= 0)
            def _():
                b = lax.rem(slot_in[s], cols)
                i = cursor[b]
                order[2 * i] = s
                order[2 * i + 1] = lax.div(slot_in[s], cols)
                cursor[b] = i + 1


    columns = [tiles_ref[c].reshape(height, TILE) for c in range(4)]
    tile_row = lax.broadcasted_iota(jnp.int32, (height, PANEL), 0) // TILE
    first = jnp.logical_and(step == 0, tile_row == 0)

    def mask(panels_above, value):
        above = jnp.logical_and(first, my_row < 2 * panels_above)
        return jnp.where(above, 0.0, value) if panels_above else value

    one, two = two_panels(columns, small_ref, mask)
    for i, panel in enumerate((mask(1, one), mask(2, two))):
        for k, half in enumerate(halves(panel)):
            pair_ref[:, k * WIDTH + i * PANEL : k * WIDTH + (i + 1) * PANEL] = half
    pieces = (one[:, :TILE], one[:, TILE:], two[:, :TILE], two[:, TILE:])
    for c in range(4):

        @pl.when(my_col == c)
        def _():
            out_ref[:, 0, 0, 0] = pieces[c].reshape(group, TILE, TILE)


def row_panels(tiles, lead, diag, place, slot_in, front):
    rows = front.shape[0]
    cols = front.shape[2]
    group = rows // 3
    height = group * TILE
    out_shape = [
        jax.ShapeDtypeStruct((rows * TILE, 2 * WIDTH), jnp.bfloat16),
        jax.ShapeDtypeStruct(front.shape, jnp.float32),
        jax.ShapeDtypeStruct((3, PANEL, 3 * PANEL), jnp.bfloat16),
        jax.ShapeDtypeStruct((2 * slot_in.shape[0],), jnp.int32),
        jax.ShapeDtypeStruct((cols + 1,), jnp.int32),
    ]
    return pl.pallas_call(
        row_panels_kernel,
        grid_spec=pltpu.PrefetchScalarGridSpec(
            num_scalar_prefetch=2,
            grid=(3,),
            in_specs=[
                pl.BlockSpec((4, group, TILE, TILE), lambda i, *_: (0, i, 0, 0)),
                whole_spec(lead),
                whole_spec(diag),
            ],
            out_specs=[
                pl.BlockSpec((height, 2 * WIDTH), lambda i, *_: (i, 0)),
                pl.BlockSpec((group, 1, 1, 1, TILE, TILE), lambda i, *_: (i, 0, 0, 0, 0, 0)),
                whole_spec(out_shape[2]),
                pl.BlockSpec(memory_space=pltpu.SMEM),
                pl.BlockSpec(memory_space=pltpu.SMEM),
            ],
            scratch_shapes=[
                pltpu.VMEM((3, 3 * PANEL, PANEL), jnp.bfloat16),
                pltpu.SMEM((cols,), jnp.int32),
            ],
        ),
        out_shape=out_shape,
        compiler_params=pltpu.CompilerParams(vmem_limit_bytes=VMEM),
        name="row_panels",
    )(place, slot_in, tiles, lead, diag)


def trailing_kernel(
    first, n_held, halved, place, columns_table, places_table, order, starts, pair_ref, small_ref, *rest
):
    piece_refs = rest[:n_held]
    front_ref, incoming_ref, _, out_ref, right_ref, taken, given, child_ref, *rest = rest[n_held:]
    take_sems, give_sems, child_sems, *joined = rest
    if halved:
        joined[0][:2] = piece_refs[0][...]
        joined[0][2:] = piece_refs[1][...]
        piece_refs = joined
    n_pieces = len(piece_refs)
    group = piece_refs[0].shape[1]
    count = n_pieces * group
    steps = (count + 1) // 2
    rows, cols = front_ref.shape[0], front_ref.shape[2]
    columns_base = place[0] * cols + first * group
    places_base = (place[0] * (cols // group) + first) * 4

    def columns_of(step):
        for j in range(2):
            index = jnp.minimum(2 * step, count - 2) + j
            b = columns_table[columns_base + index]
            wanted = b > 0
            if count % 2 and j == 0:
                wanted = jnp.logical_and(wanted, step < steps - 1)
            yield j, b, wanted

    def each_take(step, act):
        slot = lax.rem(step, 2)
        for j, b, wanted in columns_of(step):

            @pl.when(wanted)
            def _():
                act(
                    pltpu.make_async_copy(
                        front_ref.at[:, 0, b, 0], taken.at[slot, j], take_sems.at[slot, j]
                    )
                )

    def each_give(step, act):
        slot = lax.rem(step, 2)
        for j, b, wanted in columns_of(step):

            @pl.when(wanted)
            def _():
                act(
                    pltpu.make_async_copy(
                        given.at[slot, j], out_ref.at[:, 0, b, 0], give_sems.at[slot, j]
                    )
                )

    def each_child(step, act):
        for j, b, wanted in columns_of(step):

            @pl.when(wanted)
            def _():
                @pl.loop(starts[b], starts[b + 1])
                def _(i):
                    s = order[2 * i]
                    copy = pltpu.make_async_copy(
                        incoming_ref.at[s, pl.ds(0, TILE)], child_ref.at[s], child_sems.at[s]
                    )
                    act(copy, j, s, order[2 * i + 1])

    for step in range(min(steps, 2)):
        each_take(step, lambda copy: copy.start())
    for step in range(steps):
        each_child(step, lambda copy, *_: copy.start())

    tile_columns = [
        jnp.concatenate(
            [
                piece[places_table[places_base + 4 * p + c], t]
                for p, piece in enumerate(piece_refs)
                for t in range(group)
            ],
            axis=1,
        )
        for c in range(4)
    ]
    for i, panel in enumerate(two_panels_across(tile_columns, small_ref)):
        high, low = halves(panel)
        for k, half in enumerate((high, high, low)):
            right_ref[k * WIDTH + i * PANEL : k * WIDTH + (i + 1) * PANEL] = half

    @pl.loop(0, steps)
    def _(step):
        slot = lax.rem(step, 2)
        each_take(step, lambda copy: copy.wait())

        @pl.when(step >= 2)
        def _():
            each_give(step - 2, lambda copy: copy.wait())

        start = jnp.minimum(2 * step, count - 2)
        lanes = pl.ds(pl.multiple_of(start * TILE, TILE), 2 * TILE)
        block = rows // 3
        for m in range(3):
            left = pair_ref[m * block * TILE : (m + 1) * block * TILE]
            update = dot(jnp.concatenate([left, left[:, :WIDTH]], axis=1), right_ref[:, lanes])
            span = slice(m * block, (m + 1) * block)
            for j in range(2):
                part = update[:, j * TILE : (j + 1) * TILE].reshape(block, TILE, TILE)
                given[slot, j, span] = taken[slot, j, span] - part

        def add(copy, j, s, a):
            copy.wait()
            given[slot, j, a] = given[slot, j, a] + child_ref[s]

        each_child(step, add)
        each_give(step, lambda copy: copy.start())

        @pl.when(step + 2 < steps)
        def _():
            each_take(step + 2, lambda copy: copy.start())

    for step in range(max(steps - 2, 0), steps):
        each_give(step, lambda copy: copy.wait())


def trailing(front, pieces, first, place, tables, panels, incoming):
    rows = front.shape[0]
    pair, out, small, order, starts = panels
    group = pieces[0].shape[1]
    halved = pieces[0].shape[0] == 2
    count = group if halved else len(pieces) * group
    scalars = [place, *tables, order, starts]
    held = [pair, small, *pieces]
    distant = [front, incoming, out]
    spec = lambda space, n: [pl.BlockSpec(memory_space=space)] * n
    height = rows * TILE
    devices = incoming.shape[0]
    return pl.pallas_call(
        functools.partial(trailing_kernel, first, len(pieces), halved),
        in_specs=spec(pltpu.SMEM, 5) + spec(pltpu.VMEM, len(held)) + spec(pltpu.HBM, 3),
        out_specs=pl.BlockSpec(memory_space=pltpu.HBM),
        scratch_shapes=[
            pltpu.VMEM((3 * WIDTH, count * TILE), jnp.bfloat16),
            pltpu.VMEM((2, 2, rows, TILE, TILE), jnp.float32),
            pltpu.VMEM((2, 2, rows, TILE, TILE), jnp.float32),
            pltpu.VMEM((devices, TILE, TILE), jnp.float32),
            pltpu.SemaphoreType.DMA((2, 2)),
            pltpu.SemaphoreType.DMA((2, 2)),
            pltpu.SemaphoreType.DMA((devices,)),
        ]
        + [pltpu.VMEM((4, group, TILE, TILE), jnp.float32)] * halved,
        out_shape=jax.ShapeDtypeStruct(front.shape, jnp.float32),
        input_output_aliases={len(held) + 7: 0},
        compiler_params=pltpu.CompilerParams(vmem_limit_bytes=VMEM),
        cost_estimate=pl.CostEstimate(
            flops=8 * count * 2 * height * TILE * WIDTH,
            bytes_accessed=count * 2 * height * TILE * 4,
            transcendentals=0,
        ),
        name="trailing",
    )(*scalars, *held, *distant)


def body(front, child_tiles, tile_dest, tile_slot, tile_count, diag_inverses):
    n_row = lax.axis_size("row")
    n_col = lax.axis_size("col")
    my_row = lax.axis_index("row").astype(jnp.int32)
    my_col = lax.axis_index("col").astype(jnp.int32)
    rows_here, cols_here = (front.shape[0], front.shape[2])
    devices = n_row * n_col
    assert n_col == 4 and n_row % 4 == 0 and rows_here % 3 == 0
    owners = [r * n_col + c for r in (2, 3) for c in (0, 1)]
    place = jnp.stack([my_row, my_col, jnp.int32(cols_here), my_row * n_col + my_col])

    outgoing, lead = pack(
        child_tiles, front[0, 0, 0, 0], place[3:], tile_dest[:, 0], tile_slot, tile_count,
        devices, owners,
    )
    lead = lax.optimization_barrier(lax.psum(lead, "col"))
    lead = lax.psum(lead, "row")
    incoming = lax.all_to_all(outgoing, BOTH, split_axis=0, concat_axis=0, tiled=True)
    slot_in = lax.optimization_barrier(incoming[:, TILE, 0].astype(jnp.int32))

    ring = rows_here % n_col == 0
    mine, *parts = assemble_columns(front, incoming, place, slot_in, n_col if ring else 1)
    tiles = lax.all_gather(mine, "col", axis=0, tiled=False)
    panels = row_panels(tiles, lead, diag_inverses, place, slot_in, front)

    sets = n_row // n_col
    if ring:
        arrived = []
        for j, part in enumerate(parts):
            pairs = [
                (r * n_col + c, ((r // n_col) * n_col + (c + j) % n_col) * n_col + r % n_col)
                for r in range(n_row)
                for c in range(n_col)
            ]
            arrived.append(lax.ppermute(part, BOTH, pairs))
        piece = jnp.stack(arrived)
        circle = list(range(0, n_row, 2)) + list(range(n_row - 1, 0, -2))
        up = [(circle[i], circle[(i + 1) % n_row]) for i in range(n_row)]
        down = [(b, a) for a, b in up]
        rounds = [[(piece, 0)]]
        ahead = behind = piece
        for step in range(1, n_row // 2):
            ahead = lax.ppermute(ahead, "row", up)
            behind = lax.ppermute(behind, "row", down)
            if step == 2:
                ahead, behind, panels = lax.optimization_barrier((ahead, behind, panels))
            rounds.append([(ahead, -step), (behind, step)])
        last = [lax.ppermute(ahead[:2], "row", up), lax.ppermute(behind[2:], "row", down)]
        whole = [entry for entries in rounds for entry in entries]
        rounds = [whole[:2], whole[2:4], whole[4:5], *rounds[3:], [(last, n_row // 2)]]

        def described(row, shift):
            origin = circle[(circle.index(row) + shift) % n_row]
            part, group = origin % n_col, rows_here // n_col
            columns = [(part * group + t) * sets + origin // n_col for t in range(group)]
            return columns, [(part - c) % n_col for c in range(n_col)]

    else:
        pairs = [
            (r * n_col + c, ((r // n_col) * n_col + c) * n_col + r % n_col)
            for r in range(n_row)
            for c in range(n_col)
        ]
        moved = lax.all_gather(lax.ppermute(parts[0], BOTH, pairs), "row", axis=0, tiled=False)
        rounds = [[(moved[h * n_col : (h + 1) * n_col], h)] for h in range(sets)]

        def described(row, h):
            return [a * sets + h for a in range(rows_here)], list(range(n_col))

    shifts = [shift for entries in rounds for _, shift in entries]
    tables = [
        jnp.asarray(
            np.concatenate([described(row, shift)[k] for row in range(n_row) for shift in shifts]),
            jnp.int32,
        )
        for k in range(2)
    ]
    first = 0
    for entries in rounds:
        pieces = [piece for piece, _ in entries]
        pieces = pieces[0] if isinstance(pieces[0], list) else pieces
        out = trailing(front, pieces, first, place, tables, panels, incoming)
        panels = [panels[0], out, *panels[2:]]
        first += len(entries)
    return panels[1]


def solution(mesh):
    return jax.shard_map(
        body,
        mesh=mesh,
        in_specs=(
            P(None, "row", None, "col", None, None),
            P(BOTH, None, None),
            P(BOTH, None),
            P(BOTH),
            P(BOTH),
            P(),
        ),
        out_specs=P(None, "row", None, "col", None, None),
        check_vma=False,
    )
```

```python
import functools

import jax
import jax.numpy as jnp
import numpy as np
from jax import lax
from jax.experimental import pallas as pl
from jax.experimental.pallas import tpu as pltpu
from jax.sharding import PartitionSpec as P

TILE = 128
PANEL = 256
WIDTH = 2 * PANEL
NOTE = 8
VMEM = 46 * 1024 * 1024
BOTH = ("row", "col")


def halves(value):
    high = value.astype(jnp.bfloat16)
    low = (value - high.astype(jnp.float32)).astype(jnp.bfloat16)
    return high, low


def deep(value):
    high, low = halves(value)
    return jnp.concatenate([high, low, high], axis=1)


def stacked(value):
    high, low = halves(value)
    return jnp.concatenate([high, high, low], axis=0)


def dot(left, right):
    return jnp.dot(left, right, preferred_element_type=jnp.float32)


def two_panels(columns, small_ref, mask):
    one = mask(0, dot(deep(jnp.concatenate(columns[:2], axis=1)), small_ref[0]))
    field = jnp.concatenate(columns[2:], axis=1) - dot(deep(mask(1, one)), small_ref[1])
    return one, mask(1, dot(deep(field), small_ref[2]))


def two_panels_across(columns, small_ref):
    one = dot(small_ref[0], stacked(jnp.concatenate(columns[:2], axis=0)))
    field = jnp.concatenate(columns[2:], axis=0) - dot(small_ref[1], stacked(one))
    return one, dot(small_ref[2], stacked(field))


def whole_spec(array):
    rank = len(array.shape)
    return pl.BlockSpec(array.shape, lambda *_: (0,) * rank)


def lead_slices(devices):
    height = max(8, 4 * TILE // devices)
    return 4 * TILE // height, height


def pack_kernel(
    owners, place, dest, slot, count, child_ref, front_ref, out_ref, held_ref, notes_ref,
    lead_ref, tile_ref, in_sems, out_sems, sem,
):
    n_slices, height, _ = lead_ref.shape
    each = n_slices // 4
    live = jnp.minimum(count[0], child_ref.shape[0])

    def arrive(k):
        return pltpu.make_async_copy(child_ref.at[k], held_ref.at[k], in_sems.at[k])

    def leave(k):
        return pltpu.make_async_copy(
            held_ref.at[k], out_ref.at[dest[k], pl.ds(0, TILE)], out_sems.at[k]
        )

    @pl.loop(0, live)
    def _(k):
        arrive(k).start()

    notes_ref[...] = jnp.full_like(notes_ref, -1.0)
    lead_ref[...] = jnp.zeros_like(lead_ref)
    for i, owner in enumerate(owners):

        @pl.when(place[3] == owner)
        def _():
            own = pltpu.make_async_copy(front_ref.at[0, 0, 0, 0], tile_ref, sem)
            own.start()
            own.wait()
            lead_ref[i * each : (i + 1) * each] = tile_ref[...].reshape(each, height, TILE)

    @pl.loop(0, live)
    def _(k):
        notes_ref[dest[k]] = jnp.full(notes_ref.shape[1:], slot[k].astype(jnp.float32))
        arrive(k).wait()
        leave(k).start()
        for i, owner in enumerate(owners):

            @pl.when(jnp.logical_and(slot[k] == 0, dest[k] == owner))
            def _():
                span = pl.ds(i * each, each)
                lead_ref[span] = lead_ref[span] + held_ref[k].reshape(each, height, TILE)

    notes = pltpu.make_async_copy(notes_ref, out_ref.at[:, pl.ds(TILE, NOTE)], sem)
    notes.start()
    notes.wait()
    lead = pltpu.make_async_copy(
        lead_ref, out_ref.at[pl.ds(0, n_slices), pl.ds(TILE + NOTE, height)], sem
    )
    lead.start()
    lead.wait()

    @pl.loop(0, live)
    def _(k):
        leave(k).wait()


def pack(child_tiles, front, place, dest, slot, count, devices, owners):
    slots = child_tiles.shape[0]
    n_slices, height = lead_slices(devices)
    hbm = pl.BlockSpec(memory_space=pltpu.HBM)
    return pl.pallas_call(
        functools.partial(pack_kernel, owners),
        in_specs=[pl.BlockSpec(memory_space=pltpu.SMEM)] * 4 + [hbm, hbm],
        out_specs=hbm,
        scratch_shapes=[
            pltpu.VMEM((slots, TILE, TILE), jnp.float32),
            pltpu.VMEM((devices, NOTE, TILE), jnp.float32),
            pltpu.VMEM((n_slices, height, TILE), jnp.float32),
            pltpu.VMEM((TILE, TILE), jnp.float32),
            pltpu.SemaphoreType.DMA((slots,)),
            pltpu.SemaphoreType.DMA((slots,)),
            pltpu.SemaphoreType.DMA,
        ],
        out_shape=jax.ShapeDtypeStruct((devices, TILE + NOTE + height, TILE), jnp.float32),
        compiler_params=pltpu.CompilerParams(vmem_limit_bytes=62 * 1024 * 1024),
        name="pack",
    )(place, dest, slot, count, child_tiles, front)


def columns_kernel(place, slot_in, front_ref, incoming_ref, out_ref, own_ref, *rest):
    *parts, tile_ref, slices_ref, sem, slices_sem = rest
    cols = place[2]
    height = own_ref.shape[1]
    strip = pltpu.make_async_copy(front_ref.at[:, 0, 0, 0], out_ref, sem)
    strip.start()
    slices = pltpu.make_async_copy(
        incoming_ref.at[:, pl.ds(TILE + NOTE, height)], slices_ref, slices_sem
    )
    slices.start()
    strip.wait()

    @pl.loop(0, incoming_ref.shape[0])
    def _(s):
        slot = slot_in[s]

        @pl.when(jnp.logical_and(slot >= 0, lax.rem(slot, cols) == 0))
        def _():
            copy = pltpu.make_async_copy(incoming_ref.at[s, pl.ds(0, TILE)], tile_ref, sem)
            copy.start()
            copy.wait()
            row = lax.div(slot, cols)
            out_ref[row] = out_ref[row] + tile_ref[...]

    count = len(parts)
    for j, part_ref in enumerate(parts):
        group = part_ref.shape[0]
        for t in range(group):
            part_ref[t] = out_ref[lax.rem(place[1] + j, count) * group + t].T

    slices.wait()
    own_ref[...] = jnp.broadcast_to(jnp.sum(slices_ref[...], axis=0)[None], own_ref.shape)


def assemble_columns(front, incoming, place, slot_in, parts):
    rows, devices = front.shape[0], incoming.shape[0]
    _, height = lead_slices(devices)
    shapes = [(rows, TILE, TILE), (devices, height, TILE)]
    shapes += [(rows // parts, TILE, TILE)] * parts
    out_shape = [jax.ShapeDtypeStruct(shape, jnp.float32) for shape in shapes]
    return pl.pallas_call(
        columns_kernel,
        grid_spec=pltpu.PrefetchScalarGridSpec(
            num_scalar_prefetch=2,
            grid=(1,),
            in_specs=[pl.BlockSpec(memory_space=pltpu.HBM)] * 2,
            out_specs=[whole_spec(a) for a in out_shape],
            scratch_shapes=[
                pltpu.VMEM((TILE, TILE), jnp.float32),
                pltpu.VMEM((devices, height, TILE), jnp.float32),
                pltpu.SemaphoreType.DMA,
                pltpu.SemaphoreType.DMA,
            ],
        ),
        out_shape=out_shape,
        compiler_params=pltpu.CompilerParams(vmem_limit_bytes=VMEM),
        name="panel_columns",
    )(place, slot_in, front, incoming)


def row_panels_kernel(
    place, slot_in, t0, t1, t2, t3, lead_ref, diag_ref, pair_ref, out_ref, across_ref, order,
    starts, small_ref, tiles_ref, cursor,
):
    step = pl.program_id(0)
    cols = starts.shape[0] - 1
    my_row, my_col = place[0], place[1]
    group = t0.shape[0]
    height = group * TILE

    @pl.when(step == 0)
    def _():
        small_ref[0] = stacked(diag_ref[0])
        lead = jnp.concatenate(
            [jnp.concatenate([lead_ref[i, 0], lead_ref[i, 1]], axis=1) for i in range(2)], axis=0
        )
        lead = dot(deep(lead), small_ref[0])
        small_ref[1] = stacked(lead.T)
        small_ref[2] = stacked(diag_ref[1])
        across_ref[0] = deep(diag_ref[0].T)
        across_ref[1] = deep(lead)
        across_ref[2] = deep(diag_ref[1].T)

        @pl.loop(0, cols + 1)
        def _(b):
            starts[b] = 0

        @pl.loop(0, slot_in.shape[0])
        def _(s):
            @pl.when(slot_in[s] >= 0)
            def _():
                b = lax.rem(slot_in[s], cols)
                starts[b + 1] = starts[b + 1] + 1

        @pl.loop(0, cols)
        def _(b):
            cursor[b] = starts[b]
            starts[b + 1] = starts[b + 1] + starts[b]

        @pl.loop(0, slot_in.shape[0])
        def _(s):
            @pl.when(slot_in[s] >= 0)
            def _():
                b = lax.rem(slot_in[s], cols)
                i = cursor[b]
                order[2 * i] = s
                order[2 * i + 1] = lax.div(slot_in[s], cols)
                cursor[b] = i + 1


    for i, tile_ref in enumerate((t0, t1, t2, t3)):
        tiles_ref[jnp.bitwise_xor(my_col, i)] = tile_ref[...]
    columns = [tiles_ref[c].reshape(height, TILE) for c in range(4)]
    tile_row = lax.broadcasted_iota(jnp.int32, (height, PANEL), 0) // TILE
    first = jnp.logical_and(step == 0, tile_row == 0)

    def mask(panels_above, value):
        above = jnp.logical_and(first, my_row < 2 * panels_above)
        return jnp.where(above, 0.0, value) if panels_above else value

    one, two = two_panels(columns, small_ref, mask)
    for i, panel in enumerate((mask(1, one), mask(2, two))):
        high, low = halves(panel)
        for k, half in enumerate((high, low, high)):
            pair_ref[:, k * WIDTH + i * PANEL : k * WIDTH + (i + 1) * PANEL] = half
    pieces = (one[:, :TILE], one[:, TILE:], two[:, :TILE], two[:, TILE:])
    for c in range(4):

        @pl.when(my_col == c)
        def _():
            out_ref[:, 0, 0, 0] = pieces[c].reshape(group, TILE, TILE)


def row_panels(mine, others, lead, diag, place, slot_in, front):
    rows = front.shape[0]
    cols = front.shape[2]
    group = rows // 3
    height = group * TILE
    out_shape = [
        jax.ShapeDtypeStruct((rows * TILE, 3 * WIDTH), jnp.bfloat16),
        jax.ShapeDtypeStruct(front.shape, jnp.float32),
        jax.ShapeDtypeStruct((3, PANEL, 3 * PANEL), jnp.bfloat16),
        jax.ShapeDtypeStruct((2 * slot_in.shape[0],), jnp.int32),
        jax.ShapeDtypeStruct((cols + 1,), jnp.int32),
    ]
    strip = pl.BlockSpec((group, TILE, TILE), lambda i, *_: (i, 0, 0))
    return pl.pallas_call(
        row_panels_kernel,
        grid_spec=pltpu.PrefetchScalarGridSpec(
            num_scalar_prefetch=2,
            grid=(3,),
            in_specs=[strip] * 4 + [whole_spec(lead), whole_spec(diag)],
            out_specs=[
                pl.BlockSpec((height, 3 * WIDTH), lambda i, *_: (i, 0)),
                pl.BlockSpec((group, 1, 1, 1, TILE, TILE), lambda i, *_: (i, 0, 0, 0, 0, 0)),
                whole_spec(out_shape[2]),
                pl.BlockSpec(memory_space=pltpu.SMEM),
                pl.BlockSpec(memory_space=pltpu.SMEM),
            ],
            scratch_shapes=[
                pltpu.VMEM((3, 3 * PANEL, PANEL), jnp.bfloat16),
                pltpu.VMEM((4, group, TILE, TILE), jnp.float32),
                pltpu.SMEM((cols,), jnp.int32),
            ],
        ),
        out_shape=out_shape,
        compiler_params=pltpu.CompilerParams(vmem_limit_bytes=VMEM),
        name="row_panels",
    )(place, slot_in, mine, *others, lead, diag)


def trailing_kernel(
    first, n_held, halved, place, columns_table, places_table, order, starts, small_ref, *rest
):
    piece_refs = rest[:n_held]
    pair_hbm, front_ref, incoming_ref, _, out_ref, *rest = rest[n_held:]
    pair_ref, right_ref, taken, given, child_ref, *rest = rest
    pair_sem, take_sems, give_sems, child_sems, *joined = rest
    if halved:
        joined[0][:2] = piece_refs[0][...]
        joined[0][2:] = piece_refs[1][...]
        piece_refs = joined
    group = piece_refs[0].shape[1]
    count = len(piece_refs) * group
    pairs, single = count // 2, count % 2
    rows, cols = front_ref.shape[0], front_ref.shape[2]
    columns_base = place[0] * cols + first * group
    places_base = (place[0] * (cols // group) + first) * 4

    def columns_of(step, width):
        for j in range(width):
            b = columns_table[columns_base + 2 * step + j]
            yield j, b, b > 0

    def each_take(step, width, act):
        slot = lax.rem(step, 2)
        for j, b, wanted in columns_of(step, width):

            @pl.when(wanted)
            def _():
                act(
                    pltpu.make_async_copy(
                        front_ref.at[:, 0, b, 0], taken.at[slot, j], take_sems.at[slot, j]
                    )
                )

    def each_give(step, width, act):
        slot = lax.rem(step, 2)
        for j, b, wanted in columns_of(step, width):

            @pl.when(wanted)
            def _():
                act(
                    pltpu.make_async_copy(
                        given.at[slot, j], out_ref.at[:, 0, b, 0], give_sems.at[slot, j]
                    )
                )

    def each_child(step, width, act):
        for j, b, wanted in columns_of(step, width):

            @pl.when(wanted)
            def _():
                @pl.loop(starts[b], starts[b + 1])
                def _(i):
                    s = order[2 * i]
                    copy = pltpu.make_async_copy(
                        incoming_ref.at[s, pl.ds(0, TILE)], child_ref.at[s], child_sems.at[s]
                    )
                    act(copy, j, s, order[2 * i + 1])

    start, wait = (lambda copy, *_: copy.start()), (lambda copy, *_: copy.wait())
    steps = [(step, 2) for step in range(pairs)] + [(pairs, 1)] * single
    pair_copy = pltpu.make_async_copy(pair_hbm, pair_ref, pair_sem)
    pair_copy.start()
    for step, width in steps[:2]:
        each_take(step, width, start)
    for step, width in steps:
        each_child(step, width, start)

    tile_columns = [
        jnp.concatenate(
            [
                piece[places_table[places_base + 4 * p + c], t]
                for p, piece in enumerate(piece_refs)
                for t in range(group)
            ],
            axis=1,
        )
        for c in range(4)
    ]
    for i, panel in enumerate(two_panels_across(tile_columns, small_ref)):
        high, low = halves(panel)
        for k, half in enumerate((high, high, low)):
            right_ref[k * WIDTH + i * PANEL : k * WIDTH + (i + 1) * PANEL] = half
    pair_copy.wait()

    def update(step, width):
        slot = lax.rem(step, 2)
        each_take(step, width, wait)
        pl.when(step >= 2)(lambda: each_give(step - 2, 2, wait))
        lanes = pl.ds(pl.multiple_of(2 * step * TILE, TILE), width * TILE)
        change = dot(pair_ref[...], right_ref[:, lanes])
        for j in range(width):
            part = change[:, j * TILE : (j + 1) * TILE].reshape(rows, TILE, TILE)
            given[slot, j] = taken[slot, j] - part

        def add(copy, j, s, a):
            copy.wait()
            given[slot, j, a] = given[slot, j, a] + child_ref[s]

        each_child(step, width, add)
        each_give(step, width, start)

    @pl.loop(0, pairs)
    def _(step):
        update(step, 2)
        pl.when(step + 2 < pairs)(lambda: each_take(step + 2, 2, start))
        if single:
            pl.when(step + 2 == pairs)(lambda: each_take(step + 2, 1, start))

    if single:
        update(jnp.int32(pairs), 1)
    for step, width in steps[-2:]:
        each_give(step, width, wait)


def trailing(front, pieces, first, place, tables, panels, incoming):
    rows = front.shape[0]
    pair, out, small, order, starts = panels
    group = pieces[0].shape[1]
    halved = pieces[0].shape[0] == 2
    count = group if halved else len(pieces) * group
    scalars = [place, *tables, order, starts]
    held = [small, *pieces]
    distant = [pair, front, incoming, out]
    spec = lambda space, n: [pl.BlockSpec(memory_space=space)] * n
    height = rows * TILE
    devices = incoming.shape[0]
    return pl.pallas_call(
        functools.partial(trailing_kernel, first, len(pieces), halved),
        in_specs=spec(pltpu.SMEM, 5) + spec(pltpu.VMEM, len(held)) + spec(pltpu.HBM, 4),
        out_specs=pl.BlockSpec(memory_space=pltpu.HBM),
        scratch_shapes=[
            pltpu.VMEM(pair.shape, jnp.bfloat16),
            pltpu.VMEM((3 * WIDTH, count * TILE), jnp.bfloat16),
            pltpu.VMEM((2, 2, rows, TILE, TILE), jnp.float32),
            pltpu.VMEM((2, 2, rows, TILE, TILE), jnp.float32),
            pltpu.VMEM((devices, TILE, TILE), jnp.float32),
            pltpu.SemaphoreType.DMA,
            pltpu.SemaphoreType.DMA((2, 2)),
            pltpu.SemaphoreType.DMA((2, 2)),
            pltpu.SemaphoreType.DMA((devices,)),
        ]
        + [pltpu.VMEM((4, group, TILE, TILE), jnp.float32)] * halved,
        out_shape=jax.ShapeDtypeStruct(front.shape, jnp.float32),
        input_output_aliases={5 + len(held) + 3: 0},
        compiler_params=pltpu.CompilerParams(vmem_limit_bytes=VMEM),
        cost_estimate=pl.CostEstimate(
            flops=8 * count * 2 * height * TILE * WIDTH,
            bytes_accessed=count * 2 * height * TILE * 4,
            transcendentals=0,
        ),
        name="trailing",
    )(*scalars, *held, *distant)


def body(front, child_tiles, tile_dest, tile_slot, tile_count, diag_inverses):
    n_row = lax.axis_size("row")
    n_col = lax.axis_size("col")
    my_row = lax.axis_index("row").astype(jnp.int32)
    my_col = lax.axis_index("col").astype(jnp.int32)
    rows_here, cols_here = (front.shape[0], front.shape[2])
    devices = n_row * n_col
    assert n_col == 4 and n_row % 4 == 0 and rows_here % 3 == 0
    owners = [r * n_col + c for r in (2, 3) for c in (0, 1)]
    place = jnp.stack([my_row, my_col, jnp.int32(cols_here), my_row * n_col + my_col])

    outgoing = pack(
        child_tiles, front, place, tile_dest[:, 0], tile_slot, tile_count, devices, owners
    )
    incoming = lax.all_to_all(outgoing, BOTH, split_axis=0, concat_axis=0, tiled=True)
    slot_in = lax.optimization_barrier(incoming[:, TILE, 0].astype(jnp.int32))

    ring = rows_here % n_col == 0
    mine, own, *parts = assemble_columns(front, incoming, place, slot_in, n_col if ring else 1)
    lead = lax.all_to_all(own, BOTH, split_axis=0, concat_axis=0, tiled=True)
    lead = lead[: lead_slices(devices)[0]].reshape(2, 2, TILE, TILE)

    def exchange(mine):
        near = lax.ppermute(mine, "col", [(c, c ^ 1) for c in range(n_col)])
        far = lax.ppermute(mine, "col", [(c, c ^ 2) for c in range(n_col)])
        return [near, far, lax.ppermute(far, "col", [(c, c ^ 1) for c in range(n_col)])]

    def own_panels(mine, lead):
        return row_panels(mine, exchange(mine), lead, diag_inverses, place, slot_in, front)

    sets = n_row // n_col
    if ring:
        arrived = []
        for j, part in enumerate(parts):
            pairs = [
                (r * n_col + c, ((r // n_col) * n_col + (c + j) % n_col) * n_col + r % n_col)
                for r in range(n_row)
                for c in range(n_col)
            ]
            arrived.append(lax.ppermute(part, BOTH, pairs))
        arrived, mine, lead = lax.optimization_barrier((arrived, mine, lead))
        piece = jnp.stack(arrived)
        circle = list(range(0, n_row, 2)) + list(range(n_row - 1, 0, -2))
        up = [(circle[i], circle[(i + 1) % n_row]) for i in range(n_row)]
        down = [(b, a) for a, b in up]
        rounds = [[(piece, 0)]]
        panels = own_panels(mine, lead)
        ahead = behind = piece
        for step in range(1, n_row // 2):
            ahead = lax.ppermute(ahead, "row", up)
            behind = lax.ppermute(behind, "row", down)
            if step == 2:
                ahead, behind, panels = lax.optimization_barrier((ahead, behind, panels))
            rounds.append([(ahead, -step), (behind, step)])
        last = [lax.ppermute(ahead[:2], "row", up), lax.ppermute(behind[2:], "row", down)]
        whole = [entry for entries in rounds for entry in entries]
        rounds = [whole[:2], whole[2:4], whole[4:5], *rounds[3:], [(last, n_row // 2)]]

        def described(row, shift):
            origin = circle[(circle.index(row) + shift) % n_row]
            part, group = origin % n_col, rows_here // n_col
            columns = [(part * group + t) * sets + origin // n_col for t in range(group)]
            return columns, [(part - c) % n_col for c in range(n_col)]

    else:
        pairs = [
            (r * n_col + c, ((r // n_col) * n_col + c) * n_col + r % n_col)
            for r in range(n_row)
            for c in range(n_col)
        ]
        moved = lax.all_gather(lax.ppermute(parts[0], BOTH, pairs), "row", axis=0, tiled=False)
        rounds = [[(moved[h * n_col : (h + 1) * n_col], h)] for h in range(sets)]
        panels = own_panels(mine, lead)

        def described(row, h):
            return [a * sets + h for a in range(rows_here)], list(range(n_col))

    shifts = [shift for entries in rounds for _, shift in entries]
    tables = [
        jnp.asarray(
            np.concatenate([described(row, shift)[k] for row in range(n_row) for shift in shifts]),
            jnp.int32,
        )
        for k in range(2)
    ]
    first = 0
    for entries in rounds:
        pieces = [piece for piece, _ in entries]
        pieces = pieces[0] if isinstance(pieces[0], list) else pieces
        out = trailing(front, pieces, first, place, tables, panels, incoming)
        panels = [panels[0], out, *panels[2:]]
        first += len(entries)
    return panels[1]


def solution(mesh):
    return jax.shard_map(
        body,
        mesh=mesh,
        in_specs=(
            P(None, "row", None, "col", None, None),
            P(BOTH, None, None),
            P(BOTH, None),
            P(BOTH),
            P(BOTH),
            P(),
        ),
        out_specs=P(None, "row", None, "col", None, None),
        check_vma=False,
    )
```

```python
import functools

import jax
import jax.numpy as jnp
import numpy as np
from jax import lax
from jax.experimental import pallas as pl
from jax.experimental.pallas import tpu as pltpu
from jax.sharding import PartitionSpec as P

TILE = 128
PANEL = 256
WIDTH = 2 * PANEL
NOTE = 8
VMEM = 46 * 1024 * 1024
ALL_VMEM = 63 * 1024 * 1024
PARTS = 3
BOTH = ("row", "col")


def halves(value):
    high = value.astype(jnp.bfloat16)
    low = (value - high.astype(jnp.float32)).astype(jnp.bfloat16)
    return high, low


def deep(value):
    high, low = halves(value)
    return jnp.concatenate([high, low, high], axis=1)


def stacked(value):
    high, low = halves(value)
    return jnp.concatenate([high, high, low], axis=0)


def dot(left, right):
    return jnp.dot(left, right, preferred_element_type=jnp.float32)


def two_panels(columns, small_ref, mask):
    one = mask(0, dot(deep(jnp.concatenate(columns[:2], axis=1)), small_ref[0]))
    field = jnp.concatenate(columns[2:], axis=1) - dot(deep(mask(1, one)), small_ref[1])
    return one, mask(1, dot(deep(field), small_ref[2]))


def two_panels_across(columns, small_ref):
    one = dot(small_ref[0], stacked(jnp.concatenate(columns[:2], axis=0)))
    field = jnp.concatenate(columns[2:], axis=0) - dot(small_ref[1], stacked(one))
    return one, dot(small_ref[2], stacked(field))


def whole_spec(array):
    rank = len(array.shape)
    return pl.BlockSpec(array.shape, lambda *_: (0,) * rank)


def lead_slices(devices):
    height = max(8, 4 * TILE // devices)
    return 4 * TILE // height, height


def pack_kernel(
    owners, place, dest, slot, count, child_ref, front_ref, out_ref, held_ref, notes_ref,
    lead_ref, tile_ref, in_sems, out_sems, sem,
):
    n_slices, height, _ = lead_ref.shape
    each = n_slices // 4
    live = jnp.minimum(count[0], child_ref.shape[0])

    def arrive(k):
        return pltpu.make_async_copy(child_ref.at[k], held_ref.at[k], in_sems.at[k])

    def leave(k):
        return pltpu.make_async_copy(
            held_ref.at[k], out_ref.at[dest[k], pl.ds(0, TILE)], out_sems.at[k]
        )

    @pl.loop(0, live)
    def _(k):
        arrive(k).start()

    notes_ref[...] = jnp.full_like(notes_ref, -1.0)
    lead_ref[...] = jnp.zeros_like(lead_ref)
    for i, owner in enumerate(owners):

        @pl.when(place[3] == owner)
        def _():
            own = pltpu.make_async_copy(front_ref.at[0, 0, 0, 0], tile_ref, sem)
            own.start()
            own.wait()
            lead_ref[i * each : (i + 1) * each] = tile_ref[...].reshape(each, height, TILE)

    @pl.loop(0, live)
    def _(k):
        notes_ref[dest[k]] = jnp.full(notes_ref.shape[1:], slot[k].astype(jnp.float32))
        arrive(k).wait()
        leave(k).start()
        for i, owner in enumerate(owners):

            @pl.when(jnp.logical_and(slot[k] == 0, dest[k] == owner))
            def _():
                span = pl.ds(i * each, each)
                lead_ref[span] = lead_ref[span] + held_ref[k].reshape(each, height, TILE)

    notes = pltpu.make_async_copy(notes_ref, out_ref.at[:, pl.ds(TILE, NOTE)], sem)
    notes.start()
    notes.wait()
    lead = pltpu.make_async_copy(
        lead_ref, out_ref.at[pl.ds(0, n_slices), pl.ds(TILE + NOTE, height)], sem
    )
    lead.start()
    lead.wait()

    @pl.loop(0, live)
    def _(k):
        leave(k).wait()


def pack(child_tiles, front, place, dest, slot, count, devices, owners):
    slots = child_tiles.shape[0]
    n_slices, height = lead_slices(devices)
    hbm = pl.BlockSpec(memory_space=pltpu.HBM)
    return pl.pallas_call(
        functools.partial(pack_kernel, owners),
        in_specs=[pl.BlockSpec(memory_space=pltpu.SMEM)] * 4 + [hbm, hbm],
        out_specs=hbm,
        scratch_shapes=[
            pltpu.VMEM((slots, TILE, TILE), jnp.float32),
            pltpu.VMEM((devices, NOTE, TILE), jnp.float32),
            pltpu.VMEM((n_slices, height, TILE), jnp.float32),
            pltpu.VMEM((TILE, TILE), jnp.float32),
            pltpu.SemaphoreType.DMA((slots,)),
            pltpu.SemaphoreType.DMA((slots,)),
            pltpu.SemaphoreType.DMA,
        ],
        out_shape=jax.ShapeDtypeStruct((devices, TILE + NOTE + height, TILE), jnp.float32),
        compiler_params=pltpu.CompilerParams(vmem_limit_bytes=ALL_VMEM),
        name="pack",
    )(place, dest, slot, count, child_tiles, front)


def columns_kernel(place, slot_in, front_ref, incoming_ref, out_ref, own_ref, *rest):
    *parts, tile_ref, slices_ref, sem, slices_sem, strip_sems = rest
    cols = place[2]
    height = own_ref.shape[1]
    strips = [
        pltpu.make_async_copy(front_ref.at[a, 0, 0, 0], out_ref.at[a], strip_sems.at[a])
        for a in range(out_ref.shape[0])
    ]
    for strip in strips:
        strip.start()
    slices = pltpu.make_async_copy(
        incoming_ref.at[:, pl.ds(TILE + NOTE, height)], slices_ref, slices_sem
    )
    slices.start()
    for strip in strips:
        strip.wait()

    @pl.loop(0, incoming_ref.shape[0])
    def _(s):
        slot = slot_in[s]

        @pl.when(jnp.logical_and(slot >= 0, lax.rem(slot, cols) == 0))
        def _():
            copy = pltpu.make_async_copy(incoming_ref.at[s, pl.ds(0, TILE)], tile_ref, sem)
            copy.start()
            copy.wait()
            row = lax.div(slot, cols)
            out_ref[row] = out_ref[row] + tile_ref[...]

    count = len(parts)
    for j, part_ref in enumerate(parts):
        group = part_ref.shape[0]
        for t in range(group):
            part_ref[t] = out_ref[lax.rem(place[1] + j, count) * group + t].T

    slices.wait()
    own_ref[...] = jnp.broadcast_to(jnp.sum(slices_ref[...], axis=0)[None], own_ref.shape)


def assemble_columns(front, incoming, place, slot_in, parts):
    rows, devices = front.shape[0], incoming.shape[0]
    _, height = lead_slices(devices)
    shapes = [(rows, TILE, TILE), (devices, height, TILE)]
    shapes += [(rows // parts, TILE, TILE)] * parts
    out_shape = [jax.ShapeDtypeStruct(shape, jnp.float32) for shape in shapes]
    return pl.pallas_call(
        columns_kernel,
        grid_spec=pltpu.PrefetchScalarGridSpec(
            num_scalar_prefetch=2,
            grid=(1,),
            in_specs=[pl.BlockSpec(memory_space=pltpu.HBM)] * 2,
            out_specs=[whole_spec(a) for a in out_shape],
            scratch_shapes=[
                pltpu.VMEM((TILE, TILE), jnp.float32),
                pltpu.VMEM((devices, height, TILE), jnp.float32),
                pltpu.SemaphoreType.DMA,
                pltpu.SemaphoreType.DMA,
                pltpu.SemaphoreType.DMA((rows,)),
            ],
        ),
        out_shape=out_shape,
        compiler_params=pltpu.CompilerParams(vmem_limit_bytes=ALL_VMEM),
        name="panel_columns",
    )(place, slot_in, front, incoming)


def panel_rows(source, target, sems, t):
    span = pl.ds(pl.multiple_of(t * TILE, TILE), TILE)
    return pltpu.make_async_copy(source.at[span], target.at[span], sems.at[t])


def row_panels_kernel(
    place, slot_in, t0, t1, t2, t3, lead_ref, diag_ref, pair_hbm, out_ref, across_ref, order,
    starts, small_ref, tiles_ref, cursor, pair_ref, pair_sems,
):
    step = pl.program_id(0)
    cols = starts.shape[0] - 1
    my_row, my_col = place[0], place[1]
    group = t0.shape[0]
    height = group * TILE

    @pl.when(step == 0)
    def _():
        small_ref[0] = stacked(diag_ref[0])
        lead = jnp.concatenate(
            [jnp.concatenate([lead_ref[i, 0], lead_ref[i, 1]], axis=1) for i in range(2)], axis=0
        )
        lead = dot(deep(lead), small_ref[0])
        small_ref[1] = stacked(lead.T)
        small_ref[2] = stacked(diag_ref[1])
        across_ref[0] = deep(diag_ref[0].T)
        across_ref[1] = deep(lead)
        across_ref[2] = deep(diag_ref[1].T)

        @pl.loop(0, cols + 1)
        def _(b):
            starts[b] = 0

        @pl.loop(0, slot_in.shape[0])
        def _(s):
            @pl.when(slot_in[s] >= 0)
            def _():
                b = lax.rem(slot_in[s], cols)
                starts[b + 1] = starts[b + 1] + 1

        @pl.loop(0, cols)
        def _(b):
            cursor[b] = starts[b]
            starts[b + 1] = starts[b + 1] + starts[b]

        @pl.loop(0, slot_in.shape[0])
        def _(s):
            @pl.when(slot_in[s] >= 0)
            def _():
                b = lax.rem(slot_in[s], cols)
                i = cursor[b]
                order[2 * i] = s
                order[2 * i + 1] = lax.div(slot_in[s], cols)
                cursor[b] = i + 1


    for i, tile_ref in enumerate((t0, t1, t2, t3)):
        tiles_ref[jnp.bitwise_xor(my_col, i)] = tile_ref[...]
    columns = [tiles_ref[c].reshape(height, TILE) for c in range(4)]
    tile_row = lax.broadcasted_iota(jnp.int32, (height, PANEL), 0) // TILE
    first = jnp.logical_and(step == 0, tile_row == 0)

    def mask(panels_above, value):
        above = jnp.logical_and(first, my_row < 2 * panels_above)
        return jnp.where(above, 0.0, value) if panels_above else value

    one, two = two_panels(columns, small_ref, mask)
    for i, panel in enumerate((mask(1, one), mask(2, two))):
        high, low = halves(panel)
        for k, half in enumerate((high, low, high)):
            lanes = slice(k * WIDTH + i * PANEL, k * WIDTH + (i + 1) * PANEL)
            pair_ref[pl.ds(pl.multiple_of(step * height, height), height), lanes] = half
    for t in range(group):
        panel_rows(pair_ref, pair_hbm, pair_sems, step * group + t).start()

    @pl.when(step == pl.num_programs(0) - 1)
    def _():
        for t in range(pair_sems.shape[0]):
            panel_rows(pair_ref, pair_hbm, pair_sems, t).wait()

    pieces = (one[:, :TILE], one[:, TILE:], two[:, :TILE], two[:, TILE:])
    for c in range(4):

        @pl.when(my_col == c)
        def _():
            out_ref[:, 0, 0, 0] = pieces[c].reshape(group, TILE, TILE)


def row_panels(mine, others, lead, diag, place, slot_in, front):
    rows = front.shape[0]
    cols = front.shape[2]
    group = rows // 3
    height = group * TILE
    out_shape = [
        jax.ShapeDtypeStruct((rows * TILE, 3 * WIDTH), jnp.bfloat16),
        jax.ShapeDtypeStruct(front.shape, jnp.float32),
        jax.ShapeDtypeStruct((3, PANEL, 3 * PANEL), jnp.bfloat16),
        jax.ShapeDtypeStruct((2 * slot_in.shape[0],), jnp.int32),
        jax.ShapeDtypeStruct((cols + 1,), jnp.int32),
    ]
    strip = pl.BlockSpec((group, TILE, TILE), lambda i, *_: (i, 0, 0))
    return pl.pallas_call(
        row_panels_kernel,
        grid_spec=pltpu.PrefetchScalarGridSpec(
            num_scalar_prefetch=2,
            grid=(3,),
            in_specs=[strip] * 4 + [whole_spec(lead), whole_spec(diag)],
            out_specs=[
                pl.BlockSpec(memory_space=pltpu.HBM),
                pl.BlockSpec((group, 1, 1, 1, TILE, TILE), lambda i, *_: (i, 0, 0, 0, 0, 0)),
                whole_spec(out_shape[2]),
                pl.BlockSpec(memory_space=pltpu.SMEM),
                pl.BlockSpec(memory_space=pltpu.SMEM),
            ],
            scratch_shapes=[
                pltpu.VMEM((3, 3 * PANEL, PANEL), jnp.bfloat16),
                pltpu.VMEM((4, group, TILE, TILE), jnp.float32),
                pltpu.SMEM((cols,), jnp.int32),
                pltpu.VMEM(out_shape[0].shape, jnp.bfloat16),
                pltpu.SemaphoreType.DMA((rows,)),
            ],
        ),
        out_shape=out_shape,
        compiler_params=pltpu.CompilerParams(vmem_limit_bytes=VMEM),
        name="row_panels",
    )(place, slot_in, mine, *others, lead, diag)


def trailing_kernel(
    first, n_held, halved, place, columns_table, places_table, order, starts, small_ref, *rest
):
    piece_refs = rest[:n_held]
    pair_hbm, front_ref, incoming_ref, _, out_ref, *rest = rest[n_held:]
    pair_ref, right_ref, taken, given, child_ref, *rest = rest
    pair_sems, take_sems, give_sems, child_sems, *joined = rest
    if halved:
        joined[0][:2] = piece_refs[0][...]
        joined[0][2:] = piece_refs[1][...]
        piece_refs = joined
    group = piece_refs[0].shape[1]
    count = len(piece_refs) * group
    pairs, single = count // 2, count % 2
    rows, cols = front_ref.shape[0], front_ref.shape[2]
    columns_base = place[0] * cols + first * group
    places_base = (place[0] * (cols // group) + first) * 4

    def columns_of(step, width):
        for j in range(width):
            b = columns_table[columns_base + 2 * step + j]
            yield j, b, b > 0

    def each_take(step, width, act):
        slot = lax.rem(step, 2)
        for j, b, wanted in columns_of(step, width):

            @pl.when(wanted)
            def _():
                for p in range(PARTS):
                    span = pl.ds(p * (rows // PARTS), rows // PARTS)
                    act(
                        pltpu.make_async_copy(
                            front_ref.at[span, 0, b, 0], taken.at[slot, j, span], take_sems.at[slot, j, p]
                        )
                    )

    def each_give(step, width, act):
        slot = lax.rem(step, 2)
        for j, b, wanted in columns_of(step, width):

            @pl.when(wanted)
            def _():
                for p in range(PARTS):
                    span = pl.ds(p * (rows // PARTS), rows // PARTS)
                    act(
                        pltpu.make_async_copy(
                            given.at[slot, j, span], out_ref.at[span, 0, b, 0], give_sems.at[slot, j, p]
                        )
                    )

    def each_child(step, width, act):
        for j, b, wanted in columns_of(step, width):

            @pl.when(wanted)
            def _():
                @pl.loop(starts[b], starts[b + 1])
                def _(i):
                    s = order[2 * i]
                    copy = pltpu.make_async_copy(
                        incoming_ref.at[s, pl.ds(0, TILE)], child_ref.at[s], child_sems.at[s]
                    )
                    act(copy, j, s, order[2 * i + 1])

    start, wait = (lambda copy, *_: copy.start()), (lambda copy, *_: copy.wait())
    steps = [(step, 2) for step in range(pairs)] + [(pairs, 1)] * single
    for t in range(rows):
        panel_rows(pair_hbm, pair_ref, pair_sems, t).start()
    for step, width in steps[:2]:
        each_take(step, width, start)
    for step, width in steps:
        each_child(step, width, start)

    tile_columns = [
        jnp.concatenate(
            [
                piece[places_table[places_base + 4 * p + c], t]
                for p, piece in enumerate(piece_refs)
                for t in range(group)
            ],
            axis=1,
        )
        for c in range(4)
    ]
    for i, panel in enumerate(two_panels_across(tile_columns, small_ref)):
        high, low = halves(panel)
        for k, half in enumerate((high, high, low)):
            right_ref[k * WIDTH + i * PANEL : k * WIDTH + (i + 1) * PANEL] = half
    for t in range(rows):
        panel_rows(pair_hbm, pair_ref, pair_sems, t).wait()

    def update(step, width):
        slot = lax.rem(step, 2)
        each_take(step, width, wait)
        pl.when(step >= 2)(lambda: each_give(step - 2, 2, wait))
        lanes = pl.ds(pl.multiple_of(2 * step * TILE, TILE), width * TILE)
        change = dot(pair_ref[...], right_ref[:, lanes])
        for j in range(width):
            part = change[:, j * TILE : (j + 1) * TILE].reshape(rows, TILE, TILE)
            given[slot, j] = taken[slot, j] - part

        def add(copy, j, s, a):
            copy.wait()
            given[slot, j, a] = given[slot, j, a] + child_ref[s]

        each_child(step, width, add)
        each_give(step, width, start)

    @pl.loop(0, pairs)
    def _(step):
        update(step, 2)
        pl.when(step + 2 < pairs)(lambda: each_take(step + 2, 2, start))
        if single:
            pl.when(step + 2 == pairs)(lambda: each_take(step + 2, 1, start))

    if single:
        update(jnp.int32(pairs), 1)
    for step, width in steps[-2:]:
        each_give(step, width, wait)


def trailing(front, pieces, first, place, tables, panels, incoming):
    rows = front.shape[0]
    pair, out, small, order, starts = panels
    group = pieces[0].shape[1]
    halved = pieces[0].shape[0] == 2
    count = group if halved else len(pieces) * group
    scalars = [place, *tables, order, starts]
    held = [small, *pieces]
    distant = [pair, front, incoming, out]
    spec = lambda space, n: [pl.BlockSpec(memory_space=space)] * n
    height = rows * TILE
    devices = incoming.shape[0]
    return pl.pallas_call(
        functools.partial(trailing_kernel, first, len(pieces), halved),
        in_specs=spec(pltpu.SMEM, 5) + spec(pltpu.VMEM, len(held)) + spec(pltpu.HBM, 4),
        out_specs=pl.BlockSpec(memory_space=pltpu.HBM),
        scratch_shapes=[
            pltpu.VMEM(pair.shape, jnp.bfloat16),
            pltpu.VMEM((3 * WIDTH, count * TILE), jnp.bfloat16),
            pltpu.VMEM((2, 2, rows, TILE, TILE), jnp.float32),
            pltpu.VMEM((2, 2, rows, TILE, TILE), jnp.float32),
            pltpu.VMEM((devices, TILE, TILE), jnp.float32),
            pltpu.SemaphoreType.DMA((rows,)),
            pltpu.SemaphoreType.DMA((2, 2, PARTS)),
            pltpu.SemaphoreType.DMA((2, 2, PARTS)),
            pltpu.SemaphoreType.DMA((devices,)),
        ]
        + [pltpu.VMEM((4, group, TILE, TILE), jnp.float32)] * halved,
        out_shape=jax.ShapeDtypeStruct(front.shape, jnp.float32),
        input_output_aliases={5 + len(held) + 3: 0},
        compiler_params=pltpu.CompilerParams(vmem_limit_bytes=VMEM),
        cost_estimate=pl.CostEstimate(
            flops=8 * count * 2 * height * TILE * WIDTH,
            bytes_accessed=count * 2 * height * TILE * 4,
            transcendentals=0,
        ),
        name="trailing",
    )(*scalars, *held, *distant)


def body(front, child_tiles, tile_dest, tile_slot, tile_count, diag_inverses):
    n_row = lax.axis_size("row")
    n_col = lax.axis_size("col")
    my_row = lax.axis_index("row").astype(jnp.int32)
    my_col = lax.axis_index("col").astype(jnp.int32)
    rows_here, cols_here = (front.shape[0], front.shape[2])
    devices = n_row * n_col
    assert n_col == 4 and n_row % 4 == 0 and rows_here % 3 == 0
    owners = [r * n_col + c for r in (2, 3) for c in (0, 1)]
    place = jnp.stack([my_row, my_col, jnp.int32(cols_here), my_row * n_col + my_col])

    outgoing = pack(
        child_tiles, front, place, tile_dest[:, 0], tile_slot, tile_count, devices, owners
    )
    incoming = lax.all_to_all(outgoing, BOTH, split_axis=0, concat_axis=0, tiled=True)
    slot_in = lax.optimization_barrier(incoming[:, TILE, 0].astype(jnp.int32))

    ring = rows_here % n_col == 0
    mine, own, *parts = assemble_columns(front, incoming, place, slot_in, n_col if ring else 1)
    lead = lax.all_to_all(own, BOTH, split_axis=0, concat_axis=0, tiled=True)
    lead = lead[: lead_slices(devices)[0]].reshape(2, 2, TILE, TILE)

    def exchange(mine):
        near = lax.ppermute(mine, "col", [(c, c ^ 1) for c in range(n_col)])
        far = lax.ppermute(mine, "col", [(c, c ^ 2) for c in range(n_col)])
        return [near, far, lax.ppermute(far, "col", [(c, c ^ 1) for c in range(n_col)])]

    def own_panels(mine, lead):
        return row_panels(mine, exchange(mine), lead, diag_inverses, place, slot_in, front)

    sets = n_row // n_col
    if ring:
        arrived = []
        for j, part in enumerate(parts):
            pairs = [
                (r * n_col + c, ((r // n_col) * n_col + (c + j) % n_col) * n_col + r % n_col)
                for r in range(n_row)
                for c in range(n_col)
            ]
            arrived.append(lax.ppermute(part, BOTH, pairs))
        arrived, mine, lead = lax.optimization_barrier((arrived, mine, lead))
        piece = jnp.stack(arrived)
        circle = list(range(0, n_row, 2)) + list(range(n_row - 1, 0, -2))
        up = [(circle[i], circle[(i + 1) % n_row]) for i in range(n_row)]
        down = [(b, a) for a, b in up]
        rounds = [[(piece, 0)]]
        panels = own_panels(mine, lead)
        ahead = behind = piece
        for step in range(1, n_row // 2):
            ahead = lax.ppermute(ahead, "row", up)
            behind = lax.ppermute(behind, "row", down)
            if step == 2:
                ahead, behind, panels = lax.optimization_barrier((ahead, behind, panels))
            rounds.append([(ahead, -step), (behind, step)])
        last = [lax.ppermute(ahead[:2], "row", up), lax.ppermute(behind[2:], "row", down)]
        whole = [entry for entries in rounds for entry in entries]
        rounds = [whole[:2], whole[2:4], whole[4:5], *rounds[3:], [(last, n_row // 2)]]

        def described(row, shift):
            origin = circle[(circle.index(row) + shift) % n_row]
            part, group = origin % n_col, rows_here // n_col
            columns = [(part * group + t) * sets + origin // n_col for t in range(group)]
            return columns, [(part - c) % n_col for c in range(n_col)]

    else:
        pairs = [
            (r * n_col + c, ((r // n_col) * n_col + c) * n_col + r % n_col)
            for r in range(n_row)
            for c in range(n_col)
        ]
        moved = lax.all_gather(lax.ppermute(parts[0], BOTH, pairs), "row", axis=0, tiled=False)
        rounds = [[(moved[h * n_col : (h + 1) * n_col], h)] for h in range(sets)]
        panels = own_panels(mine, lead)

        def described(row, h):
            return [a * sets + h for a in range(rows_here)], list(range(n_col))

    shifts = [shift for entries in rounds for _, shift in entries]
    tables = [
        jnp.asarray(
            np.concatenate([described(row, shift)[k] for row in range(n_row) for shift in shifts]),
            jnp.int32,
        )
        for k in range(2)
    ]
    first = 0
    for entries in rounds:
        pieces = [piece for piece, _ in entries]
        pieces = pieces[0] if isinstance(pieces[0], list) else pieces
        out = trailing(front, pieces, first, place, tables, panels, incoming)
        panels = [panels[0], out, *panels[2:]]
        first += len(entries)
    return panels[1]


def solution(mesh):
    return jax.shard_map(
        body,
        mesh=mesh,
        in_specs=(
            P(None, "row", None, "col", None, None),
            P(BOTH, None, None),
            P(BOTH, None),
            P(BOTH),
            P(BOTH),
            P(),
        ),
        out_specs=P(None, "row", None, "col", None, None),
        check_vma=False,
    )
```

```python
import functools

import jax
import jax.numpy as jnp
import numpy as np
from jax import lax
from jax.experimental import pallas as pl
from jax.experimental.pallas import tpu as pltpu
from jax.sharding import PartitionSpec as P

TILE = 128
PANEL = 256
WIDTH = 2 * PANEL
NOTE = 8
VMEM = 46 * 1024 * 1024
ALL_VMEM = 63 * 1024 * 1024
BOTH = ("row", "col")


def halves(value):
    high = value.astype(jnp.bfloat16)
    low = (value - high.astype(jnp.float32)).astype(jnp.bfloat16)
    return high, low


def deep(value):
    high, low = halves(value)
    return jnp.concatenate([high, low, high], axis=1)


def stacked(value):
    high, low = halves(value)
    return jnp.concatenate([high, high, low], axis=0)


def dot(left, right):
    return jnp.dot(left, right, preferred_element_type=jnp.float32)


def two_panels(columns, small_ref, mask):
    one = mask(0, dot(deep(jnp.concatenate(columns[:2], axis=1)), small_ref[0]))
    field = jnp.concatenate(columns[2:], axis=1) - dot(deep(mask(1, one)), small_ref[1])
    return one, mask(1, dot(deep(field), small_ref[2]))


def two_panels_across(columns, small_ref):
    one = dot(small_ref[0], stacked(jnp.concatenate(columns[:2], axis=0)))
    field = jnp.concatenate(columns[2:], axis=0) - dot(small_ref[1], stacked(one))
    return one, dot(small_ref[2], stacked(field))


def whole_spec(array):
    rank = len(array.shape)
    return pl.BlockSpec(array.shape, lambda *_: (0,) * rank)


def lead_slices(devices):
    height = max(8, 4 * TILE // devices)
    return 4 * TILE // height, height


def pack_kernel(
    owners, place, dest, slot, count, child_ref, front_ref, out_ref, held_ref, notes_ref,
    lead_ref, tile_ref, in_sems, out_sems, sem,
):
    n_slices, height, _ = lead_ref.shape
    each = n_slices // 4
    live = jnp.minimum(count[0], child_ref.shape[0])

    def arrive(k):
        return pltpu.make_async_copy(child_ref.at[k], held_ref.at[k], in_sems.at[k])

    def leave(k):
        return pltpu.make_async_copy(
            held_ref.at[k], out_ref.at[dest[k], pl.ds(0, TILE)], out_sems.at[k]
        )

    @pl.loop(0, live)
    def _(k):
        arrive(k).start()

    notes_ref[...] = jnp.full_like(notes_ref, -1.0)
    lead_ref[...] = jnp.zeros_like(lead_ref)
    for i, owner in enumerate(owners):

        @pl.when(place[3] == owner)
        def _():
            own = pltpu.make_async_copy(front_ref.at[0, 0, 0, 0], tile_ref, sem)
            own.start()
            own.wait()
            lead_ref[i * each : (i + 1) * each] = tile_ref[...].reshape(each, height, TILE)

    @pl.loop(0, live)
    def _(k):
        notes_ref[dest[k]] = jnp.full(notes_ref.shape[1:], slot[k].astype(jnp.float32))
        arrive(k).wait()
        leave(k).start()
        for i, owner in enumerate(owners):

            @pl.when(jnp.logical_and(slot[k] == 0, dest[k] == owner))
            def _():
                span = pl.ds(i * each, each)
                lead_ref[span] = lead_ref[span] + held_ref[k].reshape(each, height, TILE)

    notes = pltpu.make_async_copy(notes_ref, out_ref.at[:, pl.ds(TILE, NOTE)], sem)
    notes.start()
    notes.wait()
    lead = pltpu.make_async_copy(
        lead_ref, out_ref.at[pl.ds(0, n_slices), pl.ds(TILE + NOTE, height)], sem
    )
    lead.start()
    lead.wait()

    @pl.loop(0, live)
    def _(k):
        leave(k).wait()


def pack(child_tiles, front, place, dest, slot, count, devices, owners):
    slots = child_tiles.shape[0]
    n_slices, height = lead_slices(devices)
    hbm = pl.BlockSpec(memory_space=pltpu.HBM)
    return pl.pallas_call(
        functools.partial(pack_kernel, owners),
        in_specs=[pl.BlockSpec(memory_space=pltpu.SMEM)] * 4 + [hbm, hbm],
        out_specs=hbm,
        scratch_shapes=[
            pltpu.VMEM((slots, TILE, TILE), jnp.float32),
            pltpu.VMEM((devices, NOTE, TILE), jnp.float32),
            pltpu.VMEM((n_slices, height, TILE), jnp.float32),
            pltpu.VMEM((TILE, TILE), jnp.float32),
            pltpu.SemaphoreType.DMA((slots,)),
            pltpu.SemaphoreType.DMA((slots,)),
            pltpu.SemaphoreType.DMA,
        ],
        out_shape=jax.ShapeDtypeStruct((devices, TILE + NOTE + height, TILE), jnp.float32),
        compiler_params=pltpu.CompilerParams(vmem_limit_bytes=ALL_VMEM),
        name="pack",
    )(place, dest, slot, count, child_tiles, front)


def columns_kernel(place, slot_in, front_ref, incoming_ref, out_ref, own_ref, *rest):
    *parts, tile_ref, slices_ref, sem, slices_sem, strip_sems = rest
    cols = place[2]
    height = own_ref.shape[1]
    strips = [
        pltpu.make_async_copy(front_ref.at[a, 0, 0, 0], out_ref.at[a], strip_sems.at[a])
        for a in range(out_ref.shape[0])
    ]
    for strip in strips:
        strip.start()
    slices = pltpu.make_async_copy(
        incoming_ref.at[:, pl.ds(TILE + NOTE, height)], slices_ref, slices_sem
    )
    slices.start()
    for strip in strips:
        strip.wait()

    @pl.loop(0, incoming_ref.shape[0])
    def _(s):
        slot = slot_in[s]

        @pl.when(jnp.logical_and(slot >= 0, lax.rem(slot, cols) == 0))
        def _():
            copy = pltpu.make_async_copy(incoming_ref.at[s, pl.ds(0, TILE)], tile_ref, sem)
            copy.start()
            copy.wait()
            row = lax.div(slot, cols)
            out_ref[row] = out_ref[row] + tile_ref[...]

    count = len(parts)
    for j, part_ref in enumerate(parts):
        group = part_ref.shape[0]
        for t in range(group):
            part_ref[t] = out_ref[lax.rem(place[1] + j, count) * group + t].T

    slices.wait()
    own_ref[...] = jnp.broadcast_to(jnp.sum(slices_ref[...], axis=0)[None], own_ref.shape)


def assemble_columns(front, incoming, place, slot_in, parts):
    rows, devices = front.shape[0], incoming.shape[0]
    _, height = lead_slices(devices)
    shapes = [(rows, TILE, TILE), (devices, height, TILE)]
    shapes += [(rows // parts, TILE, TILE)] * parts
    out_shape = [jax.ShapeDtypeStruct(shape, jnp.float32) for shape in shapes]
    return pl.pallas_call(
        columns_kernel,
        grid_spec=pltpu.PrefetchScalarGridSpec(
            num_scalar_prefetch=2,
            grid=(1,),
            in_specs=[pl.BlockSpec(memory_space=pltpu.HBM)] * 2,
            out_specs=[whole_spec(a) for a in out_shape],
            scratch_shapes=[
                pltpu.VMEM((TILE, TILE), jnp.float32),
                pltpu.VMEM((devices, height, TILE), jnp.float32),
                pltpu.SemaphoreType.DMA,
                pltpu.SemaphoreType.DMA,
                pltpu.SemaphoreType.DMA((rows,)),
            ],
        ),
        out_shape=out_shape,
        compiler_params=pltpu.CompilerParams(vmem_limit_bytes=VMEM),
        name="panel_columns",
    )(place, slot_in, front, incoming)


def panel_rows(source, target, sems, t):
    span = pl.ds(pl.multiple_of(t * TILE, TILE), TILE)
    return pltpu.make_async_copy(source.at[span], target.at[span], sems.at[t])


def row_panels_kernel(
    place, slot_in, t0, t1, t2, t3, lead_ref, diag_ref, pair_hbm, out_ref, across_ref, order,
    starts, small_ref, tiles_ref, cursor, pair_ref, pair_sems,
):
    step = pl.program_id(0)
    cols = starts.shape[0] - 1
    my_row, my_col = place[0], place[1]
    group = t0.shape[0]
    height = group * TILE

    @pl.when(step == 0)
    def _():
        small_ref[0] = stacked(diag_ref[0])
        lead = jnp.concatenate(
            [jnp.concatenate([lead_ref[i, 0], lead_ref[i, 1]], axis=1) for i in range(2)], axis=0
        )
        lead = dot(deep(lead), small_ref[0])
        small_ref[1] = stacked(lead.T)
        small_ref[2] = stacked(diag_ref[1])
        across_ref[0] = deep(diag_ref[0].T)
        across_ref[1] = deep(lead)
        across_ref[2] = deep(diag_ref[1].T)

        @pl.loop(0, cols + 1)
        def _(b):
            starts[b] = 0

        @pl.loop(0, slot_in.shape[0])
        def _(s):
            @pl.when(slot_in[s] >= 0)
            def _():
                b = lax.rem(slot_in[s], cols)
                starts[b + 1] = starts[b + 1] + 1

        @pl.loop(0, cols)
        def _(b):
            cursor[b] = starts[b]
            starts[b + 1] = starts[b + 1] + starts[b]

        @pl.loop(0, slot_in.shape[0])
        def _(s):
            @pl.when(slot_in[s] >= 0)
            def _():
                b = lax.rem(slot_in[s], cols)
                i = cursor[b]
                order[2 * i] = s
                order[2 * i + 1] = lax.div(slot_in[s], cols)
                cursor[b] = i + 1


    for i, tile_ref in enumerate((t0, t1, t2, t3)):
        tiles_ref[jnp.bitwise_xor(my_col, i)] = tile_ref[...]
    columns = [tiles_ref[c].reshape(height, TILE) for c in range(4)]
    tile_row = lax.broadcasted_iota(jnp.int32, (height, PANEL), 0) // TILE
    first = jnp.logical_and(step == 0, tile_row == 0)

    def mask(panels_above, value):
        above = jnp.logical_and(first, my_row < 2 * panels_above)
        return jnp.where(above, 0.0, value) if panels_above else value

    one, two = two_panels(columns, small_ref, mask)
    for i, panel in enumerate((mask(1, one), mask(2, two))):
        high, low = halves(panel)
        for k, half in enumerate((high, low, high)):
            lanes = slice(k * WIDTH + i * PANEL, k * WIDTH + (i + 1) * PANEL)
            pair_ref[pl.ds(pl.multiple_of(step * height, height), height), lanes] = half
    for t in range(group):
        panel_rows(pair_ref, pair_hbm, pair_sems, step * group + t).start()

    @pl.when(step == pl.num_programs(0) - 1)
    def _():
        for t in range(pair_sems.shape[0]):
            panel_rows(pair_ref, pair_hbm, pair_sems, t).wait()

    pieces = (one[:, :TILE], one[:, TILE:], two[:, :TILE], two[:, TILE:])
    for c in range(4):

        @pl.when(my_col == c)
        def _():
            out_ref[:, 0, 0, 0] = pieces[c].reshape(group, TILE, TILE)


def row_panels(mine, others, lead, diag, place, slot_in, front):
    rows, cols = front.shape[0], front.shape[2]
    group = 2 - rows % 2
    height = group * TILE
    out_shape = [
        jax.ShapeDtypeStruct((rows * TILE, 3 * WIDTH), jnp.bfloat16),
        jax.ShapeDtypeStruct(front.shape, jnp.float32),
        jax.ShapeDtypeStruct((3, PANEL, 3 * PANEL), jnp.bfloat16),
        jax.ShapeDtypeStruct((2 * slot_in.shape[0],), jnp.int32),
        jax.ShapeDtypeStruct((cols + 1,), jnp.int32),
    ]
    strip = pl.BlockSpec((group, TILE, TILE), lambda i, *_: (i, 0, 0))
    return pl.pallas_call(
        row_panels_kernel,
        grid_spec=pltpu.PrefetchScalarGridSpec(
            num_scalar_prefetch=2,
            grid=(rows // group,),
            in_specs=[strip] * 4 + [whole_spec(lead), whole_spec(diag)],
            out_specs=[
                pl.BlockSpec(memory_space=pltpu.HBM),
                pl.BlockSpec((group, 1, 1, 1, TILE, TILE), lambda i, *_: (i, 0, 0, 0, 0, 0)),
                whole_spec(out_shape[2]),
                pl.BlockSpec(memory_space=pltpu.SMEM),
                pl.BlockSpec(memory_space=pltpu.SMEM),
            ],
            scratch_shapes=[
                pltpu.VMEM((3, 3 * PANEL, PANEL), jnp.bfloat16),
                pltpu.VMEM((4, group, TILE, TILE), jnp.float32),
                pltpu.SMEM((cols,), jnp.int32),
                pltpu.VMEM(out_shape[0].shape, jnp.bfloat16),
                pltpu.SemaphoreType.DMA((rows,)),
            ],
        ),
        out_shape=out_shape,
        compiler_params=pltpu.CompilerParams(vmem_limit_bytes=VMEM),
        name="row_panels",
    )(place, slot_in, mine, *others, lead, diag)


def trailing_kernel(
    first, n_held, halved, place, columns_table, places_table, order, starts, small_ref, *rest
):
    piece_refs = rest[:n_held]
    pair_hbm, front_ref, incoming_ref, _, out_ref, *rest = rest[n_held:]
    pair_ref, right_ref, taken, given, child_ref, *rest = rest
    pair_sems, take_sems, give_sems, child_sems, *joined = rest
    if halved:
        joined[0][:2] = piece_refs[0][...]
        joined[0][2:] = piece_refs[1][...]
        piece_refs = joined
    group = piece_refs[0].shape[1]
    count = len(piece_refs) * group
    steps = (count + 1) // 2
    rows, cols = front_ref.shape[0], front_ref.shape[2]
    columns_base = place[0] * cols + first * group
    places_base = (place[0] * (cols // group) + first) * 4

    def columns_of(step):
        for j in range(2):
            b = columns_table[columns_base + jnp.minimum(2 * step, count - 2) + j]
            wanted = b > 0
            if count % 2 and j == 0:
                wanted = jnp.logical_and(wanted, step < steps - 1)
            yield j, b, wanted

    def each_take(step, act):
        slot = lax.rem(step, 2)
        for j, b, wanted in columns_of(step):

            @pl.when(wanted)
            def _():
                source = front_ref.at[:, 0, b, 0]
                act(pltpu.make_async_copy(source, taken.at[slot, j], take_sems.at[slot, j]))

    def each_give(step, act):
        slot = lax.rem(step, 2)
        for j, b, wanted in columns_of(step):

            @pl.when(wanted)
            def _():
                target = out_ref.at[:, 0, b, 0]
                act(pltpu.make_async_copy(given.at[slot, j], target, give_sems.at[slot, j]))

    def each_child(step, act):
        for j, b, wanted in columns_of(step):

            @pl.when(wanted)
            def _():
                @pl.loop(starts[b], starts[b + 1])
                def _(i):
                    s = order[2 * i]
                    copy = pltpu.make_async_copy(
                        incoming_ref.at[s, pl.ds(0, TILE)], child_ref.at[s], child_sems.at[s]
                    )
                    act(copy, j, s, order[2 * i + 1])

    start, wait = (lambda copy, *_: copy.start()), (lambda copy, *_: copy.wait())
    for t in range(rows):
        panel_rows(pair_hbm, pair_ref, pair_sems, t).start()
    for step in range(min(steps, 2)):
        each_take(step, start)
    for step in range(steps):
        each_child(step, start)

    tile_columns = [
        jnp.concatenate(
            [
                piece[places_table[places_base + 4 * p + c], t]
                for p, piece in enumerate(piece_refs)
                for t in range(group)
            ],
            axis=1,
        )
        for c in range(4)
    ]
    for i, panel in enumerate(two_panels_across(tile_columns, small_ref)):
        high, low = halves(panel)
        for k, half in enumerate((high, high, low)):
            right_ref[k * WIDTH + i * PANEL : k * WIDTH + (i + 1) * PANEL] = half
    for t in range(rows):
        panel_rows(pair_hbm, pair_ref, pair_sems, t).wait()

    block = rows // 3
    height = block * TILE

    @pl.loop(0, steps)
    def _(step):
        slot = lax.rem(step, 2)
        each_take(step, wait)
        pl.when(step >= 2)(lambda: each_give(step - 2, wait))
        lanes = pl.ds(pl.multiple_of(jnp.minimum(2 * step, count - 2) * TILE, TILE), 2 * TILE)

        @pl.loop(0, 3)
        def _(m):
            left = pair_ref[pl.ds(pl.multiple_of(m * height, height), height)]
            change = dot(left, right_ref[:, lanes])
            span = pl.ds(m * block, block)
            for j in range(2):
                part = change[:, j * TILE : (j + 1) * TILE].reshape(block, TILE, TILE)
                given[slot, j, span] = taken[slot, j, span] - part

        def add(copy, j, s, a):
            copy.wait()
            given[slot, j, a] = given[slot, j, a] + child_ref[s]

        each_child(step, add)
        each_give(step, start)
        pl.when(step + 2 < steps)(lambda: each_take(step + 2, start))

    for step in range(max(steps - 2, 0), steps):
        each_give(step, wait)


def trailing(front, pieces, first, place, tables, panels, incoming):
    rows = front.shape[0]
    pair, out, small, order, starts = panels
    group = pieces[0].shape[1]
    halved = pieces[0].shape[0] == 2
    count = group if halved else len(pieces) * group
    scalars = [place, *tables, order, starts]
    held = [small, *pieces]
    distant = [pair, front, incoming, out]
    spec = lambda space, n: [pl.BlockSpec(memory_space=space)] * n
    height = rows * TILE
    devices = incoming.shape[0]
    return pl.pallas_call(
        functools.partial(trailing_kernel, first, len(pieces), halved),
        in_specs=spec(pltpu.SMEM, 5) + spec(pltpu.VMEM, len(held)) + spec(pltpu.HBM, 4),
        out_specs=pl.BlockSpec(memory_space=pltpu.HBM),
        scratch_shapes=[
            pltpu.VMEM(pair.shape, jnp.bfloat16),
            pltpu.VMEM((3 * WIDTH, count * TILE), jnp.bfloat16),
            pltpu.VMEM((2, 2, rows, TILE, TILE), jnp.float32),
            pltpu.VMEM((2, 2, rows, TILE, TILE), jnp.float32),
            pltpu.VMEM((devices, TILE, TILE), jnp.float32),
            pltpu.SemaphoreType.DMA((rows,)),
            pltpu.SemaphoreType.DMA((2, 2)),
            pltpu.SemaphoreType.DMA((2, 2)),
            pltpu.SemaphoreType.DMA((devices,)),
        ]
        + [pltpu.VMEM((4, group, TILE, TILE), jnp.float32)] * halved,
        out_shape=jax.ShapeDtypeStruct(front.shape, jnp.float32),
        input_output_aliases={5 + len(held) + 3: 0},
        compiler_params=pltpu.CompilerParams(vmem_limit_bytes=VMEM),
        cost_estimate=pl.CostEstimate(
            flops=8 * count * 2 * height * TILE * WIDTH,
            bytes_accessed=count * 2 * height * TILE * 4,
            transcendentals=0,
        ),
        name="trailing",
    )(*scalars, *held, *distant)


def body(front, child_tiles, tile_dest, tile_slot, tile_count, diag_inverses):
    n_row = lax.axis_size("row")
    n_col = lax.axis_size("col")
    my_row = lax.axis_index("row").astype(jnp.int32)
    my_col = lax.axis_index("col").astype(jnp.int32)
    rows_here, cols_here = (front.shape[0], front.shape[2])
    devices = n_row * n_col
    assert n_col == 4 and n_row % 4 == 0 and rows_here % 3 == 0
    owners = [r * n_col + c for r in (2, 3) for c in (0, 1)]
    place = jnp.stack([my_row, my_col, jnp.int32(cols_here), my_row * n_col + my_col])

    outgoing = pack(
        child_tiles, front, place, tile_dest[:, 0], tile_slot, tile_count, devices, owners
    )
    incoming = lax.all_to_all(outgoing, BOTH, split_axis=0, concat_axis=0, tiled=True)
    slot_in = lax.optimization_barrier(incoming[:, TILE, 0].astype(jnp.int32))

    ring = rows_here % n_col == 0
    mine, own, *parts = assemble_columns(front, incoming, place, slot_in, n_col if ring else 1)
    lead = lax.all_to_all(own, BOTH, split_axis=0, concat_axis=0, tiled=True)
    lead = lead[: lead_slices(devices)[0]].reshape(2, 2, TILE, TILE)

    def exchange(mine):
        near = lax.ppermute(mine, "col", [(c, c ^ 1) for c in range(n_col)])
        far = lax.ppermute(mine, "col", [(c, c ^ 2) for c in range(n_col)])
        return [near, far, lax.ppermute(far, "col", [(c, c ^ 1) for c in range(n_col)])]

    def own_panels(mine, lead):
        return row_panels(mine, exchange(mine), lead, diag_inverses, place, slot_in, front)

    sets = n_row // n_col
    if ring:
        arrived = []
        for j, part in enumerate(parts):
            pairs = [
                (r * n_col + c, ((r // n_col) * n_col + (c + j) % n_col) * n_col + r % n_col)
                for r in range(n_row)
                for c in range(n_col)
            ]
            arrived.append(lax.ppermute(part, BOTH, pairs))
        arrived, mine, lead = lax.optimization_barrier((arrived, mine, lead))
        piece = jnp.stack(arrived)
        circle = list(range(0, n_row, 2)) + list(range(n_row - 1, 0, -2))
        up = [(circle[i], circle[(i + 1) % n_row]) for i in range(n_row)]
        down = [(b, a) for a, b in up]
        rounds = [[(piece, 0)]]
        panels = own_panels(mine, lead)
        ahead = behind = piece
        for step in range(1, n_row // 2):
            ahead = lax.ppermute(ahead, "row", up)
            behind = lax.ppermute(behind, "row", down)
            if step == 2:
                ahead, behind, panels = lax.optimization_barrier((ahead, behind, panels))
            rounds.append([(ahead, -step), (behind, step)])
        last = [lax.ppermute(ahead[:2], "row", up), lax.ppermute(behind[2:], "row", down)]
        whole = [entry for entries in rounds for entry in entries]
        rounds = [whole[:2], whole[2:4], whole[4:5], *rounds[3:], [(last, n_row // 2)]]

        def described(row, shift):
            origin = circle[(circle.index(row) + shift) % n_row]
            part, group = origin % n_col, rows_here // n_col
            columns = [(part * group + t) * sets + origin // n_col for t in range(group)]
            return columns, [(part - c) % n_col for c in range(n_col)]

    else:
        pairs = [
            (r * n_col + c, ((r // n_col) * n_col + c) * n_col + r % n_col)
            for r in range(n_row)
            for c in range(n_col)
        ]
        moved = lax.all_gather(lax.ppermute(parts[0], BOTH, pairs), "row", axis=0, tiled=False)
        rounds = [[(moved[h * n_col : (h + 1) * n_col], h)] for h in range(sets)]
        panels = own_panels(mine, lead)

        def described(row, h):
            return [a * sets + h for a in range(rows_here)], list(range(n_col))

    shifts = [shift for entries in rounds for _, shift in entries]
    tables = [
        jnp.asarray(
            np.concatenate([described(row, shift)[k] for row in range(n_row) for shift in shifts]),
            jnp.int32,
        )
        for k in range(2)
    ]
    first = 0
    for entries in rounds:
        pieces = [piece for piece, _ in entries]
        pieces = pieces[0] if isinstance(pieces[0], list) else pieces
        out = trailing(front, pieces, first, place, tables, panels, incoming)
        panels = [panels[0], out, *panels[2:]]
        first += len(entries)
    return panels[1]


def solution(mesh):
    return jax.shard_map(
        body,
        mesh=mesh,
        in_specs=(
            P(None, "row", None, "col", None, None),
            P(BOTH, None, None),
            P(BOTH, None),
            P(BOTH),
            P(BOTH),
            P(),
        ),
        out_specs=P(None, "row", None, "col", None, None),
        check_vma=False,
    )
```

```python
import functools

import jax
import jax.numpy as jnp
import numpy as np
from jax import lax
from jax.experimental import pallas as pl
from jax.experimental.pallas import tpu as pltpu
from jax.sharding import PartitionSpec as P

TILE = 128
PANEL = 256
WIDTH = 2 * PANEL
NOTE = 8
VMEM = 46 * 1024 * 1024
BOTH = ("row", "col")


def halves(value):
    high = value.astype(jnp.bfloat16)
    low = (value - high.astype(jnp.float32)).astype(jnp.bfloat16)
    return high, low


def deep(value):
    high, low = halves(value)
    return jnp.concatenate([high, low, high], axis=1)


def stacked(value):
    high, low = halves(value)
    return jnp.concatenate([high, high, low], axis=0)


def dot(left, right):
    return jnp.dot(left, right, preferred_element_type=jnp.float32)


def two_panels(columns, small_ref, mask):
    one = mask(0, dot(deep(jnp.concatenate(columns[:2], axis=1)), small_ref[0]))
    field = jnp.concatenate(columns[2:], axis=1) - dot(deep(mask(1, one)), small_ref[1])
    return one, mask(1, dot(deep(field), small_ref[2]))


def two_panels_across(columns, small_ref):
    one = dot(small_ref[0], stacked(jnp.concatenate(columns[:2], axis=0)))
    field = jnp.concatenate(columns[2:], axis=0) - dot(small_ref[1], stacked(one))
    return one, dot(small_ref[2], stacked(field))


def whole_spec(array):
    rank = len(array.shape)
    return pl.BlockSpec(array.shape, lambda *_: (0,) * rank)


def lead_slices(devices):
    height = max(8, 4 * TILE // devices)
    return 4 * TILE // height, height


def pack_kernel(
    owners, place, dest, slot, count, child_ref, front_ref, out_ref, held_ref, notes_ref,
    lead_ref, tile_ref, in_sems, out_sems, sem,
):
    n_slices, height, _ = lead_ref.shape
    each = n_slices // 4
    live = jnp.minimum(count[0], child_ref.shape[0])

    def arrive(k):
        return pltpu.make_async_copy(child_ref.at[k], held_ref.at[k], in_sems.at[k])

    def leave(k):
        return pltpu.make_async_copy(
            held_ref.at[k], out_ref.at[dest[k], pl.ds(0, TILE)], out_sems.at[k]
        )

    @pl.loop(0, live)
    def _(k):
        arrive(k).start()

    notes_ref[...] = jnp.full_like(notes_ref, -1.0)
    lead_ref[...] = jnp.zeros_like(lead_ref)
    for i, owner in enumerate(owners):

        @pl.when(place[3] == owner)
        def _():
            own = pltpu.make_async_copy(front_ref.at[0, 0, 0, 0], tile_ref, sem)
            own.start()
            own.wait()
            lead_ref[i * each : (i + 1) * each] = tile_ref[...].reshape(each, height, TILE)

    @pl.loop(0, live)
    def _(k):
        notes_ref[dest[k]] = jnp.full(notes_ref.shape[1:], slot[k].astype(jnp.float32))
        arrive(k).wait()
        leave(k).start()
        for i, owner in enumerate(owners):

            @pl.when(jnp.logical_and(slot[k] == 0, dest[k] == owner))
            def _():
                span = pl.ds(i * each, each)
                lead_ref[span] = lead_ref[span] + held_ref[k].reshape(each, height, TILE)

    notes = pltpu.make_async_copy(notes_ref, out_ref.at[:, pl.ds(TILE, NOTE)], sem)
    notes.start()
    notes.wait()
    lead = pltpu.make_async_copy(
        lead_ref, out_ref.at[pl.ds(0, n_slices), pl.ds(TILE + NOTE, height)], sem
    )
    lead.start()
    lead.wait()

    @pl.loop(0, live)
    def _(k):
        leave(k).wait()


def pack(child_tiles, front, place, dest, slot, count, devices, owners):
    slots = child_tiles.shape[0]
    n_slices, height = lead_slices(devices)
    hbm = pl.BlockSpec(memory_space=pltpu.HBM)
    return pl.pallas_call(
        functools.partial(pack_kernel, owners),
        in_specs=[pl.BlockSpec(memory_space=pltpu.SMEM)] * 4 + [hbm, hbm],
        out_specs=hbm,
        scratch_shapes=[
            pltpu.VMEM((slots, TILE, TILE), jnp.float32),
            pltpu.VMEM((devices, NOTE, TILE), jnp.float32),
            pltpu.VMEM((n_slices, height, TILE), jnp.float32),
            pltpu.VMEM((TILE, TILE), jnp.float32),
            pltpu.SemaphoreType.DMA((slots,)),
            pltpu.SemaphoreType.DMA((slots,)),
            pltpu.SemaphoreType.DMA,
        ],
        out_shape=jax.ShapeDtypeStruct((devices, TILE + NOTE + height, TILE), jnp.float32),
        compiler_params=pltpu.CompilerParams(vmem_limit_bytes=62 * 1024 * 1024),
        name="pack",
    )(place, dest, slot, count, child_tiles, front)


def columns_kernel(place, slot_in, front_ref, incoming_ref, out_ref, own_ref, *rest):
    *parts, tile_ref, slices_ref, sem, slices_sem = rest
    cols = place[2]
    height = own_ref.shape[1]
    strip = pltpu.make_async_copy(front_ref.at[:, 0, 0, 0], out_ref, sem)
    strip.start()
    slices = pltpu.make_async_copy(
        incoming_ref.at[:, pl.ds(TILE + NOTE, height)], slices_ref, slices_sem
    )
    slices.start()
    strip.wait()

    @pl.loop(0, incoming_ref.shape[0])
    def _(s):
        slot = slot_in[s]

        @pl.when(jnp.logical_and(slot >= 0, lax.rem(slot, cols) == 0))
        def _():
            copy = pltpu.make_async_copy(incoming_ref.at[s, pl.ds(0, TILE)], tile_ref, sem)
            copy.start()
            copy.wait()
            row = lax.div(slot, cols)
            out_ref[row] = out_ref[row] + tile_ref[...]

    count = len(parts)
    for j, part_ref in enumerate(parts):
        group = part_ref.shape[0]
        for t in range(group):
            part_ref[t] = out_ref[lax.rem(place[1] + j, count) * group + t].T

    slices.wait()
    own_ref[...] = jnp.broadcast_to(jnp.sum(slices_ref[...], axis=0)[None], own_ref.shape)


def assemble_columns(front, incoming, place, slot_in, parts):
    rows, devices = front.shape[0], incoming.shape[0]
    _, height = lead_slices(devices)
    shapes = [(rows, TILE, TILE), (devices, height, TILE)]
    shapes += [(rows // parts, TILE, TILE)] * parts
    out_shape = [jax.ShapeDtypeStruct(shape, jnp.float32) for shape in shapes]
    return pl.pallas_call(
        columns_kernel,
        grid_spec=pltpu.PrefetchScalarGridSpec(
            num_scalar_prefetch=2,
            grid=(1,),
            in_specs=[pl.BlockSpec(memory_space=pltpu.HBM)] * 2,
            out_specs=[whole_spec(a) for a in out_shape],
            scratch_shapes=[
                pltpu.VMEM((TILE, TILE), jnp.float32),
                pltpu.VMEM((devices, height, TILE), jnp.float32),
                pltpu.SemaphoreType.DMA,
                pltpu.SemaphoreType.DMA,
            ],
        ),
        out_shape=out_shape,
        compiler_params=pltpu.CompilerParams(vmem_limit_bytes=VMEM),
        name="panel_columns",
    )(place, slot_in, front, incoming)


def row_panels_kernel(
    place, slot_in, t0, t1, t2, t3, lead_ref, diag_ref, pair_ref, out_ref, across_ref, order,
    starts, small_ref, tiles_ref, cursor,
):
    step = pl.program_id(0)
    cols = starts.shape[0] - 1
    my_row, my_col = place[0], place[1]
    group = t0.shape[0]
    height = group * TILE

    @pl.when(step == 0)
    def _():
        small_ref[0] = stacked(diag_ref[0])
        lead = jnp.concatenate(
            [jnp.concatenate([lead_ref[i, 0], lead_ref[i, 1]], axis=1) for i in range(2)], axis=0
        )
        lead = dot(deep(lead), small_ref[0])
        small_ref[1] = stacked(lead.T)
        small_ref[2] = stacked(diag_ref[1])
        across_ref[0] = deep(diag_ref[0].T)
        across_ref[1] = deep(lead)
        across_ref[2] = deep(diag_ref[1].T)

        @pl.loop(0, cols + 1)
        def _(b):
            starts[b] = 0

        @pl.loop(0, slot_in.shape[0])
        def _(s):
            @pl.when(slot_in[s] >= 0)
            def _():
                b = lax.rem(slot_in[s], cols)
                starts[b + 1] = starts[b + 1] + 1

        @pl.loop(0, cols)
        def _(b):
            cursor[b] = starts[b]
            starts[b + 1] = starts[b + 1] + starts[b]

        @pl.loop(0, slot_in.shape[0])
        def _(s):
            @pl.when(slot_in[s] >= 0)
            def _():
                b = lax.rem(slot_in[s], cols)
                i = cursor[b]
                order[2 * i] = s
                order[2 * i + 1] = lax.div(slot_in[s], cols)
                cursor[b] = i + 1


    for i, tile_ref in enumerate((t0, t1, t2, t3)):
        tiles_ref[jnp.bitwise_xor(my_col, i)] = tile_ref[...]
    columns = [tiles_ref[c].reshape(height, TILE) for c in range(4)]
    tile_row = lax.broadcasted_iota(jnp.int32, (height, PANEL), 0) // TILE
    first = jnp.logical_and(step == 0, tile_row == 0)

    def mask(panels_above, value):
        above = jnp.logical_and(first, my_row < 2 * panels_above)
        return jnp.where(above, 0.0, value) if panels_above else value

    one, two = two_panels(columns, small_ref, mask)
    for i, panel in enumerate((mask(1, one), mask(2, two))):
        for k, half in enumerate(halves(panel)):
            pair_ref[:, k * WIDTH + i * PANEL : k * WIDTH + (i + 1) * PANEL] = half
    pieces = (one[:, :TILE], one[:, TILE:], two[:, :TILE], two[:, TILE:])
    for c in range(4):

        @pl.when(my_col == c)
        def _():
            out_ref[:, 0, 0, 0] = pieces[c].reshape(group, TILE, TILE)


def row_panels(mine, others, lead, diag, place, slot_in, front):
    rows = front.shape[0]
    cols = front.shape[2]
    group = rows // 3
    height = group * TILE
    out_shape = [
        jax.ShapeDtypeStruct((rows * TILE, 2 * WIDTH), jnp.bfloat16),
        jax.ShapeDtypeStruct(front.shape, jnp.float32),
        jax.ShapeDtypeStruct((3, PANEL, 3 * PANEL), jnp.bfloat16),
        jax.ShapeDtypeStruct((2 * slot_in.shape[0],), jnp.int32),
        jax.ShapeDtypeStruct((cols + 1,), jnp.int32),
    ]
    strip = pl.BlockSpec((group, TILE, TILE), lambda i, *_: (i, 0, 0))
    return pl.pallas_call(
        row_panels_kernel,
        grid_spec=pltpu.PrefetchScalarGridSpec(
            num_scalar_prefetch=2,
            grid=(3,),
            in_specs=[strip] * 4 + [whole_spec(lead), whole_spec(diag)],
            out_specs=[
                pl.BlockSpec((height, 2 * WIDTH), lambda i, *_: (i, 0)),
                pl.BlockSpec((group, 1, 1, 1, TILE, TILE), lambda i, *_: (i, 0, 0, 0, 0, 0)),
                whole_spec(out_shape[2]),
                pl.BlockSpec(memory_space=pltpu.SMEM),
                pl.BlockSpec(memory_space=pltpu.SMEM),
            ],
            scratch_shapes=[
                pltpu.VMEM((3, 3 * PANEL, PANEL), jnp.bfloat16),
                pltpu.VMEM((4, group, TILE, TILE), jnp.float32),
                pltpu.SMEM((cols,), jnp.int32),
            ],
        ),
        out_shape=out_shape,
        compiler_params=pltpu.CompilerParams(vmem_limit_bytes=VMEM),
        name="row_panels",
    )(place, slot_in, mine, *others, lead, diag)


def trailing_kernel(
    first, n_held, halved, place, columns_table, places_table, order, starts, pair_ref, small_ref,
    *rest,
):
    piece_refs = rest[:n_held]
    front_ref, incoming_ref, _, out_ref, right_ref, taken, given, child_ref, *rest = rest[n_held:]
    take_sems, give_sems, child_sems, *joined = rest
    if halved:
        joined[0][:2] = piece_refs[0][...]
        joined[0][2:] = piece_refs[1][...]
        piece_refs = joined
    n_pieces = len(piece_refs)
    group = piece_refs[0].shape[1]
    count = n_pieces * group
    steps = (count + 1) // 2
    rows, cols = front_ref.shape[0], front_ref.shape[2]
    columns_base = place[0] * cols + first * group
    places_base = (place[0] * (cols // group) + first) * 4

    def columns_of(step):
        for j in range(2):
            index = jnp.minimum(2 * step, count - 2) + j
            b = columns_table[columns_base + index]
            wanted = b > 0
            if count % 2 and j == 0:
                wanted = jnp.logical_and(wanted, step < steps - 1)
            yield j, b, wanted

    def each_take(step, act):
        slot = lax.rem(step, 2)
        for j, b, wanted in columns_of(step):

            @pl.when(wanted)
            def _():
                act(
                    pltpu.make_async_copy(
                        front_ref.at[:, 0, b, 0], taken.at[slot, j], take_sems.at[slot, j]
                    )
                )

    def each_give(step, act):
        slot = lax.rem(step, 2)
        for j, b, wanted in columns_of(step):

            @pl.when(wanted)
            def _():
                act(
                    pltpu.make_async_copy(
                        given.at[slot, j], out_ref.at[:, 0, b, 0], give_sems.at[slot, j]
                    )
                )

    def each_child(step, act):
        for j, b, wanted in columns_of(step):

            @pl.when(wanted)
            def _():
                @pl.loop(starts[b], starts[b + 1])
                def _(i):
                    s = order[2 * i]
                    copy = pltpu.make_async_copy(
                        incoming_ref.at[s, pl.ds(0, TILE)], child_ref.at[s], child_sems.at[s]
                    )
                    act(copy, j, s, order[2 * i + 1])

    for step in range(min(steps, 2)):
        each_take(step, lambda copy: copy.start())
    for step in range(steps):
        each_child(step, lambda copy, *_: copy.start())

    tile_columns = [
        jnp.concatenate(
            [
                piece[places_table[places_base + 4 * p + c], t]
                for p, piece in enumerate(piece_refs)
                for t in range(group)
            ],
            axis=1,
        )
        for c in range(4)
    ]
    for i, panel in enumerate(two_panels_across(tile_columns, small_ref)):
        high, low = halves(panel)
        for k, half in enumerate((high, high, low)):
            right_ref[k * WIDTH + i * PANEL : k * WIDTH + (i + 1) * PANEL] = half

    @pl.loop(0, steps)
    def _(step):
        slot = lax.rem(step, 2)
        each_take(step, lambda copy: copy.wait())

        @pl.when(step >= 2)
        def _():
            each_give(step - 2, lambda copy: copy.wait())

        start = jnp.minimum(2 * step, count - 2)
        lanes = pl.ds(pl.multiple_of(start * TILE, TILE), 2 * TILE)
        block = rows // 3
        for m in range(3):
            left = pair_ref[m * block * TILE : (m + 1) * block * TILE]
            update = dot(jnp.concatenate([left, left[:, :WIDTH]], axis=1), right_ref[:, lanes])
            span = slice(m * block, (m + 1) * block)
            for j in range(2):
                part = update[:, j * TILE : (j + 1) * TILE].reshape(block, TILE, TILE)
                given[slot, j, span] = taken[slot, j, span] - part

        def add(copy, j, s, a):
            copy.wait()
            given[slot, j, a] = given[slot, j, a] + child_ref[s]

        each_child(step, add)
        each_give(step, lambda copy: copy.start())

        @pl.when(step + 2 < steps)
        def _():
            each_take(step + 2, lambda copy: copy.start())

    for step in range(max(steps - 2, 0), steps):
        each_give(step, lambda copy: copy.wait())


def trailing(front, pieces, first, place, tables, panels, incoming):
    rows = front.shape[0]
    pair, out, small, order, starts = panels
    group = pieces[0].shape[1]
    halved = pieces[0].shape[0] == 2
    count = group if halved else len(pieces) * group
    scalars = [place, *tables, order, starts]
    held = [pair, small, *pieces]
    distant = [front, incoming, out]
    spec = lambda space, n: [pl.BlockSpec(memory_space=space)] * n
    height = rows * TILE
    devices = incoming.shape[0]
    return pl.pallas_call(
        functools.partial(trailing_kernel, first, len(pieces), halved),
        in_specs=spec(pltpu.SMEM, 5) + spec(pltpu.VMEM, len(held)) + spec(pltpu.HBM, 3),
        out_specs=pl.BlockSpec(memory_space=pltpu.HBM),
        scratch_shapes=[
            pltpu.VMEM((3 * WIDTH, count * TILE), jnp.bfloat16),
            pltpu.VMEM((2, 2, rows, TILE, TILE), jnp.float32),
            pltpu.VMEM((2, 2, rows, TILE, TILE), jnp.float32),
            pltpu.VMEM((devices, TILE, TILE), jnp.float32),
            pltpu.SemaphoreType.DMA((2, 2)),
            pltpu.SemaphoreType.DMA((2, 2)),
            pltpu.SemaphoreType.DMA((devices,)),
        ]
        + [pltpu.VMEM((4, group, TILE, TILE), jnp.float32)] * halved,
        out_shape=jax.ShapeDtypeStruct(front.shape, jnp.float32),
        input_output_aliases={len(held) + 7: 0},
        compiler_params=pltpu.CompilerParams(vmem_limit_bytes=VMEM),
        cost_estimate=pl.CostEstimate(
            flops=8 * count * 2 * height * TILE * WIDTH,
            bytes_accessed=count * 2 * height * TILE * 4,
            transcendentals=0,
        ),
        name="trailing",
    )(*scalars, *held, *distant)


def body(front, child_tiles, tile_dest, tile_slot, tile_count, diag_inverses):
    n_row = lax.axis_size("row")
    n_col = lax.axis_size("col")
    my_row = lax.axis_index("row").astype(jnp.int32)
    my_col = lax.axis_index("col").astype(jnp.int32)
    rows_here, cols_here = (front.shape[0], front.shape[2])
    devices = n_row * n_col
    assert n_col == 4 and n_row % 4 == 0 and rows_here % 3 == 0
    owners = [r * n_col + c for r in (2, 3) for c in (0, 1)]
    place = jnp.stack([my_row, my_col, jnp.int32(cols_here), my_row * n_col + my_col])

    outgoing = pack(
        child_tiles, front, place, tile_dest[:, 0], tile_slot, tile_count, devices, owners
    )
    incoming = lax.all_to_all(outgoing, BOTH, split_axis=0, concat_axis=0, tiled=True)
    slot_in = lax.optimization_barrier(incoming[:, TILE, 0].astype(jnp.int32))

    ring = rows_here % n_col == 0
    mine, own, *parts = assemble_columns(front, incoming, place, slot_in, n_col if ring else 1)
    lead = lax.all_to_all(own, BOTH, split_axis=0, concat_axis=0, tiled=True)
    lead = lead[: lead_slices(devices)[0]].reshape(2, 2, TILE, TILE)

    def exchange(mine):
        near = lax.ppermute(mine, "col", [(c, c ^ 1) for c in range(n_col)])
        far = lax.ppermute(mine, "col", [(c, c ^ 2) for c in range(n_col)])
        return [near, far, lax.ppermute(far, "col", [(c, c ^ 1) for c in range(n_col)])]

    def own_panels(mine, lead):
        return row_panels(mine, exchange(mine), lead, diag_inverses, place, slot_in, front)

    sets = n_row // n_col
    circle = list(range(0, n_row, 2)) + list(range(n_row - 1, 0, -2))
    around = [0] + [sign * step for step in range(1, n_row // 2) for sign in (-1, 1)]
    shifts = around + [n_row // 2] if ring else list(range(sets))

    def described(row, shift):
        if not ring:
            return [a * sets + shift for a in range(rows_here)], list(range(n_col))
        origin = circle[(circle.index(row) + shift) % n_row]
        part, group = origin % n_col, rows_here // n_col
        columns = [(part * group + t) * sets + origin // n_col for t in range(group)]
        return columns, [(part - c) % n_col for c in range(n_col)]

    tables = [
        jnp.asarray(
            np.concatenate([described(row, shift)[k] for row in range(n_row) for shift in shifts]),
            jnp.int32,
        )
        for k in range(2)
    ]

    def updated(entries, panels, first):
        assert [shift for _, shift in entries] == shifts[first : first + len(entries)]
        pieces = [piece for piece, _ in entries]
        pieces = pieces[0] if isinstance(pieces[0], list) else pieces
        out = trailing(front, pieces, first, place, tables, panels, incoming)
        return [panels[0], out, *panels[2:]]

    first = 0
    if ring:
        arrived = []
        for j, part in enumerate(parts):
            pairs = [
                (r * n_col + c, ((r // n_col) * n_col + (c + j) % n_col) * n_col + r % n_col)
                for r in range(n_row)
                for c in range(n_col)
            ]
            arrived.append(lax.ppermute(part, BOTH, pairs))
        arrived[0], mine = lax.optimization_barrier((arrived[0], mine))
        arrived, lead = lax.optimization_barrier((arrived, lead))
        piece = jnp.stack(arrived)
        up = [(circle[i], circle[(i + 1) % n_row]) for i in range(n_row)]
        down = [(b, a) for a, b in up]
        rounds = [[(piece, 0)]]
        panels = own_panels(mine, lead)
        ahead = behind = piece
        for step in range(1, n_row // 2):
            ahead = lax.ppermute(ahead, "row", up)
            behind = lax.ppermute(behind, "row", down)
            if step == 2:
                panels = updated([(piece, 0), rounds[1][0]], panels, 0)
                ahead, behind, panels = lax.optimization_barrier((ahead, behind, panels))
            rounds.append([(ahead, -step), (behind, step)])
        last = [lax.ppermute(ahead[:2], "row", up), lax.ppermute(behind[2:], "row", down)]
        late = [entry for entries in rounds for entry in entries][2:]
        rounds = [late[:2], late[2:3], *rounds[3:], [(last, n_row // 2)]]
        first = 2

    else:
        pairs = [
            (r * n_col + c, ((r // n_col) * n_col + c) * n_col + r % n_col)
            for r in range(n_row)
            for c in range(n_col)
        ]
        moved = lax.all_gather(lax.ppermute(parts[0], BOTH, pairs), "row", axis=0, tiled=False)
        rounds = [[(moved[h * n_col : (h + 1) * n_col], h)] for h in range(sets)]
        panels = own_panels(mine, lead)

    for entries in rounds:
        panels = updated(entries, panels, first)
        first += len(entries)
    return panels[1]


def solution(mesh):
    return jax.shard_map(
        body,
        mesh=mesh,
        in_specs=(
            P(None, "row", None, "col", None, None),
            P(BOTH, None, None),
            P(BOTH, None),
            P(BOTH),
            P(BOTH),
            P(),
        ),
        out_specs=P(None, "row", None, "col", None, None),
        check_vma=False,
    )
```

```python
import functools

import jax
import jax.numpy as jnp
import numpy as np
from jax import lax
from jax.experimental import pallas as pl
from jax.experimental.pallas import tpu as pltpu
from jax.sharding import PartitionSpec as P

TILE = 128
PANEL = 256
WIDTH = 2 * PANEL
NOTE = 8
VMEM = 46 * 1024 * 1024
BOTH = ("row", "col")


def halves(value):
    high = value.astype(jnp.bfloat16)
    low = (value - high.astype(jnp.float32)).astype(jnp.bfloat16)
    return high, low


def deep(value):
    high, low = halves(value)
    return jnp.concatenate([high, low, high], axis=1)


def stacked(value):
    high, low = halves(value)
    return jnp.concatenate([high, high, low], axis=0)


def dot(left, right):
    return jnp.dot(left, right, preferred_element_type=jnp.float32)


def two_panels(columns, small_ref, mask):
    one = mask(0, dot(deep(jnp.concatenate(columns[:2], axis=1)), small_ref[0]))
    field = jnp.concatenate(columns[2:], axis=1) - dot(deep(mask(1, one)), small_ref[1])
    return one, mask(1, dot(deep(field), small_ref[2]))


def two_panels_across(columns, small_ref):
    one = dot(small_ref[0], stacked(jnp.concatenate(columns[:2], axis=0)))
    field = jnp.concatenate(columns[2:], axis=0) - dot(small_ref[1], stacked(one))
    return one, dot(small_ref[2], stacked(field))


def whole_spec(array):
    rank = len(array.shape)
    return pl.BlockSpec(array.shape, lambda *_: (0,) * rank)


def lead_slices(devices):
    height = max(8, 4 * TILE // devices)
    return 4 * TILE // height, height


def pack_kernel(
    owners, place, dest, slot, count, child_ref, front_ref, out_ref, held_ref, notes_ref,
    lead_ref, tile_ref, in_sems, out_sems, sem,
):
    n_slices, height, _ = lead_ref.shape
    each = n_slices // 4
    live = jnp.minimum(count[0], child_ref.shape[0])

    def arrive(k):
        return pltpu.make_async_copy(child_ref.at[k], held_ref.at[k], in_sems.at[k])

    def leave(k):
        return pltpu.make_async_copy(
            held_ref.at[k], out_ref.at[dest[k], pl.ds(0, TILE)], out_sems.at[k]
        )

    @pl.loop(0, live)
    def _(k):
        arrive(k).start()

    notes_ref[...] = jnp.full_like(notes_ref, -1.0)
    lead_ref[...] = jnp.zeros_like(lead_ref)
    for i, owner in enumerate(owners):

        @pl.when(place[3] == owner)
        def _():
            own = pltpu.make_async_copy(front_ref.at[0, 0, 0, 0], tile_ref, sem)
            own.start()
            own.wait()
            lead_ref[i * each : (i + 1) * each] = tile_ref[...].reshape(each, height, TILE)

    @pl.loop(0, live)
    def _(k):
        notes_ref[dest[k]] = jnp.full(notes_ref.shape[1:], slot[k].astype(jnp.float32))
        arrive(k).wait()
        leave(k).start()
        for i, owner in enumerate(owners):

            @pl.when(jnp.logical_and(slot[k] == 0, dest[k] == owner))
            def _():
                span = pl.ds(i * each, each)
                lead_ref[span] = lead_ref[span] + held_ref[k].reshape(each, height, TILE)

    notes = pltpu.make_async_copy(notes_ref, out_ref.at[:, pl.ds(TILE, NOTE)], sem)
    notes.start()
    notes.wait()
    lead = pltpu.make_async_copy(
        lead_ref, out_ref.at[pl.ds(0, n_slices), pl.ds(TILE + NOTE, height)], sem
    )
    lead.start()
    lead.wait()

    @pl.loop(0, live)
    def _(k):
        leave(k).wait()


def pack(child_tiles, front, place, dest, slot, count, devices, owners):
    slots = child_tiles.shape[0]
    n_slices, height = lead_slices(devices)
    hbm = pl.BlockSpec(memory_space=pltpu.HBM)
    return pl.pallas_call(
        functools.partial(pack_kernel, owners),
        in_specs=[pl.BlockSpec(memory_space=pltpu.SMEM)] * 4 + [hbm, hbm],
        out_specs=hbm,
        scratch_shapes=[
            pltpu.VMEM((slots, TILE, TILE), jnp.float32),
            pltpu.VMEM((devices, NOTE, TILE), jnp.float32),
            pltpu.VMEM((n_slices, height, TILE), jnp.float32),
            pltpu.VMEM((TILE, TILE), jnp.float32),
            pltpu.SemaphoreType.DMA((slots,)),
            pltpu.SemaphoreType.DMA((slots,)),
            pltpu.SemaphoreType.DMA,
        ],
        out_shape=jax.ShapeDtypeStruct((devices, TILE + NOTE + height, TILE), jnp.float32),
        compiler_params=pltpu.CompilerParams(vmem_limit_bytes=62 * 1024 * 1024),
        name="pack",
    )(place, dest, slot, count, child_tiles, front)


def columns_kernel(place, slot_in, front_ref, incoming_ref, out_ref, own_ref, *rest):
    *parts, tile_ref, slices_ref, sem, slices_sem = rest
    cols = place[2]
    height = own_ref.shape[1]
    strip = pltpu.make_async_copy(front_ref.at[:, 0, 0, 0], out_ref, sem)
    strip.start()
    slices = pltpu.make_async_copy(
        incoming_ref.at[:, pl.ds(TILE + NOTE, height)], slices_ref, slices_sem
    )
    slices.start()
    strip.wait()

    @pl.loop(0, incoming_ref.shape[0])
    def _(s):
        slot = slot_in[s]

        @pl.when(jnp.logical_and(slot >= 0, lax.rem(slot, cols) == 0))
        def _():
            copy = pltpu.make_async_copy(incoming_ref.at[s, pl.ds(0, TILE)], tile_ref, sem)
            copy.start()
            copy.wait()
            row = lax.div(slot, cols)
            out_ref[row] = out_ref[row] + tile_ref[...]

    count = len(parts)
    for j, part_ref in enumerate(parts):
        group = part_ref.shape[0]
        for t in range(group):
            part_ref[t] = out_ref[lax.rem(place[1] + j, count) * group + t].T

    slices.wait()
    own_ref[...] = jnp.broadcast_to(jnp.sum(slices_ref[...], axis=0)[None], own_ref.shape)


def assemble_columns(front, incoming, place, slot_in, parts):
    rows, devices = front.shape[0], incoming.shape[0]
    _, height = lead_slices(devices)
    shapes = [(rows, TILE, TILE), (devices, height, TILE)]
    shapes += [(rows // parts, TILE, TILE)] * parts
    out_shape = [jax.ShapeDtypeStruct(shape, jnp.float32) for shape in shapes]
    return pl.pallas_call(
        columns_kernel,
        grid_spec=pltpu.PrefetchScalarGridSpec(
            num_scalar_prefetch=2,
            grid=(1,),
            in_specs=[pl.BlockSpec(memory_space=pltpu.HBM)] * 2,
            out_specs=[whole_spec(a) for a in out_shape],
            scratch_shapes=[
                pltpu.VMEM((TILE, TILE), jnp.float32),
                pltpu.VMEM((devices, height, TILE), jnp.float32),
                pltpu.SemaphoreType.DMA,
                pltpu.SemaphoreType.DMA,
            ],
        ),
        out_shape=out_shape,
        compiler_params=pltpu.CompilerParams(vmem_limit_bytes=VMEM),
        name="panel_columns",
    )(place, slot_in, front, incoming)


def row_panels_kernel(
    place, slot_in, t0, t1, t2, t3, lead_ref, diag_ref, pair_ref, out_ref, across_ref, order,
    starts, small_ref, tiles_ref, cursor,
):
    step = pl.program_id(0)
    cols = starts.shape[0] - 1
    my_row, my_col = place[0], place[1]
    group = t0.shape[0]
    height = group * TILE

    @pl.when(step == 0)
    def _():
        small_ref[0] = stacked(diag_ref[0])
        lead = jnp.concatenate(
            [jnp.concatenate([lead_ref[i, 0], lead_ref[i, 1]], axis=1) for i in range(2)], axis=0
        )
        lead = dot(deep(lead), small_ref[0])
        small_ref[1] = stacked(lead.T)
        small_ref[2] = stacked(diag_ref[1])
        across_ref[0] = deep(diag_ref[0].T)
        across_ref[1] = deep(lead)
        across_ref[2] = deep(diag_ref[1].T)

        @pl.loop(0, cols + 1)
        def _(b):
            starts[b] = 0

        @pl.loop(0, slot_in.shape[0])
        def _(s):
            @pl.when(slot_in[s] >= 0)
            def _():
                b = lax.rem(slot_in[s], cols)
                starts[b + 1] = starts[b + 1] + 1

        @pl.loop(0, cols)
        def _(b):
            cursor[b] = starts[b]
            starts[b + 1] = starts[b + 1] + starts[b]

        @pl.loop(0, slot_in.shape[0])
        def _(s):
            @pl.when(slot_in[s] >= 0)
            def _():
                b = lax.rem(slot_in[s], cols)
                i = cursor[b]
                order[2 * i] = s
                order[2 * i + 1] = lax.div(slot_in[s], cols)
                cursor[b] = i + 1


    for i, tile_ref in enumerate((t0, t1, t2, t3)):
        tiles_ref[jnp.bitwise_xor(my_col, i)] = tile_ref[...]
    columns = [tiles_ref[c].reshape(height, TILE) for c in range(4)]
    tile_row = lax.broadcasted_iota(jnp.int32, (height, PANEL), 0) // TILE
    first = jnp.logical_and(step == 0, tile_row == 0)

    def mask(panels_above, value):
        above = jnp.logical_and(first, my_row < 2 * panels_above)
        return jnp.where(above, 0.0, value) if panels_above else value

    one, two = two_panels(columns, small_ref, mask)
    for i, panel in enumerate((mask(1, one), mask(2, two))):
        for k, half in enumerate(halves(panel)):
            pair_ref[:, k * WIDTH + i * PANEL : k * WIDTH + (i + 1) * PANEL] = half
    pieces = (one[:, :TILE], one[:, TILE:], two[:, :TILE], two[:, TILE:])
    for c in range(4):

        @pl.when(my_col == c)
        def _():
            out_ref[:, 0, 0, 0] = pieces[c].reshape(group, TILE, TILE)


def row_panels(mine, others, lead, diag, place, slot_in, front):
    rows = front.shape[0]
    cols = front.shape[2]
    group = rows // 3
    height = group * TILE
    out_shape = [
        jax.ShapeDtypeStruct((rows * TILE, 2 * WIDTH), jnp.bfloat16),
        jax.ShapeDtypeStruct(front.shape, jnp.float32),
        jax.ShapeDtypeStruct((3, PANEL, 3 * PANEL), jnp.bfloat16),
        jax.ShapeDtypeStruct((2 * slot_in.shape[0],), jnp.int32),
        jax.ShapeDtypeStruct((cols + 1,), jnp.int32),
    ]
    strip = pl.BlockSpec((group, TILE, TILE), lambda i, *_: (i, 0, 0))
    return pl.pallas_call(
        row_panels_kernel,
        grid_spec=pltpu.PrefetchScalarGridSpec(
            num_scalar_prefetch=2,
            grid=(3,),
            in_specs=[strip] * 4 + [whole_spec(lead), whole_spec(diag)],
            out_specs=[
                pl.BlockSpec((height, 2 * WIDTH), lambda i, *_: (i, 0)),
                pl.BlockSpec((group, 1, 1, 1, TILE, TILE), lambda i, *_: (i, 0, 0, 0, 0, 0)),
                whole_spec(out_shape[2]),
                pl.BlockSpec(memory_space=pltpu.SMEM),
                pl.BlockSpec(memory_space=pltpu.SMEM),
            ],
            scratch_shapes=[
                pltpu.VMEM((3, 3 * PANEL, PANEL), jnp.bfloat16),
                pltpu.VMEM((4, group, TILE, TILE), jnp.float32),
                pltpu.SMEM((cols,), jnp.int32),
            ],
        ),
        out_shape=out_shape,
        compiler_params=pltpu.CompilerParams(vmem_limit_bytes=VMEM),
        name="row_panels",
    )(place, slot_in, mine, *others, lead, diag)


def trailing_kernel(
    first, n_held, halved, place, columns_table, places_table, order, starts, pair_ref, small_ref,
    *rest,
):
    piece_refs = rest[:n_held]
    front_ref, incoming_ref, _, out_ref, right_ref, taken, given, child_ref, *rest = rest[n_held:]
    take_sems, give_sems, child_sems, *joined = rest
    if halved:
        joined[0][:2] = piece_refs[0][...]
        joined[0][2:] = piece_refs[1][...]
        piece_refs = joined
    n_pieces = len(piece_refs)
    group = piece_refs[0].shape[1]
    count = n_pieces * group
    steps = (count + 1) // 2
    rows, cols = front_ref.shape[0], front_ref.shape[2]
    columns_base = place[0] * cols + first * group
    places_base = (place[0] * (cols // group) + first) * 4

    def columns_of(step):
        for j in range(2):
            index = jnp.minimum(2 * step, count - 2) + j
            b = columns_table[columns_base + index]
            wanted = b > 0
            if count % 2 and j == 0:
                wanted = jnp.logical_and(wanted, step < steps - 1)
            yield j, b, wanted

    def each_take(step, act):
        slot = lax.rem(step, 2)
        for j, b, wanted in columns_of(step):

            @pl.when(wanted)
            def _():
                act(
                    pltpu.make_async_copy(
                        front_ref.at[:, 0, b, 0], taken.at[slot, j], take_sems.at[slot, j]
                    )
                )

    def each_give(step, act):
        slot = lax.rem(step, 2)
        for j, b, wanted in columns_of(step):

            @pl.when(wanted)
            def _():
                act(
                    pltpu.make_async_copy(
                        given.at[slot, j], out_ref.at[:, 0, b, 0], give_sems.at[slot, j]
                    )
                )

    def each_child(step, act):
        for j, b, wanted in columns_of(step):

            @pl.when(wanted)
            def _():
                @pl.loop(starts[b], starts[b + 1])
                def _(i):
                    s = order[2 * i]
                    copy = pltpu.make_async_copy(
                        incoming_ref.at[s, pl.ds(0, TILE)], child_ref.at[s], child_sems.at[s]
                    )
                    act(copy, j, s, order[2 * i + 1])

    for step in range(min(steps, 2)):
        each_take(step, lambda copy: copy.start())
    for step in range(steps):
        each_child(step, lambda copy, *_: copy.start())

    tile_columns = [
        jnp.concatenate(
            [
                piece[places_table[places_base + 4 * p + c], t]
                for p, piece in enumerate(piece_refs)
                for t in range(group)
            ],
            axis=1,
        )
        for c in range(4)
    ]
    for i, panel in enumerate(two_panels_across(tile_columns, small_ref)):
        high, low = halves(panel)
        for k, half in enumerate((high, high, low)):
            right_ref[k * WIDTH + i * PANEL : k * WIDTH + (i + 1) * PANEL] = half

    @pl.loop(0, steps)
    def _(step):
        slot = lax.rem(step, 2)
        each_take(step, lambda copy: copy.wait())

        @pl.when(step >= 2)
        def _():
            each_give(step - 2, lambda copy: copy.wait())

        start = jnp.minimum(2 * step, count - 2)
        lanes = pl.ds(pl.multiple_of(start * TILE, TILE), 2 * TILE)
        block = rows // 3
        for m in range(3):
            left = pair_ref[m * block * TILE : (m + 1) * block * TILE]
            update = dot(jnp.concatenate([left, left[:, :WIDTH]], axis=1), right_ref[:, lanes])
            span = slice(m * block, (m + 1) * block)
            for j in range(2):
                part = update[:, j * TILE : (j + 1) * TILE].reshape(block, TILE, TILE)
                given[slot, j, span] = taken[slot, j, span] - part

        def add(copy, j, s, a):
            copy.wait()
            given[slot, j, a] = given[slot, j, a] + child_ref[s]

        each_child(step, add)
        each_give(step, lambda copy: copy.start())

        @pl.when(step + 2 < steps)
        def _():
            each_take(step + 2, lambda copy: copy.start())

    for step in range(max(steps - 2, 0), steps):
        each_give(step, lambda copy: copy.wait())


def trailing(front, pieces, first, place, tables, panels, incoming):
    rows = front.shape[0]
    pair, out, small, order, starts = panels
    group = pieces[0].shape[1]
    halved = pieces[0].shape[0] == 2
    count = group if halved else len(pieces) * group
    scalars = [place, *tables, order, starts]
    held = [pair, small, *pieces]
    distant = [front, incoming, out]
    spec = lambda space, n: [pl.BlockSpec(memory_space=space)] * n
    height = rows * TILE
    devices = incoming.shape[0]
    return pl.pallas_call(
        functools.partial(trailing_kernel, first, len(pieces), halved),
        in_specs=spec(pltpu.SMEM, 5) + spec(pltpu.VMEM, len(held)) + spec(pltpu.HBM, 3),
        out_specs=pl.BlockSpec(memory_space=pltpu.HBM),
        scratch_shapes=[
            pltpu.VMEM((3 * WIDTH, count * TILE), jnp.bfloat16),
            pltpu.VMEM((2, 2, rows, TILE, TILE), jnp.float32),
            pltpu.VMEM((2, 2, rows, TILE, TILE), jnp.float32),
            pltpu.VMEM((devices, TILE, TILE), jnp.float32),
            pltpu.SemaphoreType.DMA((2, 2)),
            pltpu.SemaphoreType.DMA((2, 2)),
            pltpu.SemaphoreType.DMA((devices,)),
        ]
        + [pltpu.VMEM((4, group, TILE, TILE), jnp.float32)] * halved,
        out_shape=jax.ShapeDtypeStruct(front.shape, jnp.float32),
        input_output_aliases={len(held) + 7: 0},
        compiler_params=pltpu.CompilerParams(vmem_limit_bytes=VMEM),
        cost_estimate=pl.CostEstimate(
            flops=8 * count * 2 * height * TILE * WIDTH,
            bytes_accessed=count * 2 * height * TILE * 4,
            transcendentals=0,
        ),
        name="trailing",
    )(*scalars, *held, *distant)


def body(front, child_tiles, tile_dest, tile_slot, tile_count, diag_inverses):
    n_row = lax.axis_size("row")
    n_col = lax.axis_size("col")
    my_row = lax.axis_index("row").astype(jnp.int32)
    my_col = lax.axis_index("col").astype(jnp.int32)
    rows_here, cols_here = (front.shape[0], front.shape[2])
    devices = n_row * n_col
    assert n_col == 4 and n_row % 4 == 0 and rows_here % 3 == 0
    owners = [r * n_col + c for r in (2, 3) for c in (0, 1)]
    place = jnp.stack([my_row, my_col, jnp.int32(cols_here), my_row * n_col + my_col])

    outgoing = pack(
        child_tiles, front, place, tile_dest[:, 0], tile_slot, tile_count, devices, owners
    )
    incoming = lax.all_to_all(outgoing, BOTH, split_axis=0, concat_axis=0, tiled=True)
    slot_in = lax.optimization_barrier(incoming[:, TILE, 0].astype(jnp.int32))

    ring = rows_here % n_col == 0
    mine, own, *parts = assemble_columns(front, incoming, place, slot_in, n_col if ring else 1)
    lead = lax.all_to_all(own, BOTH, split_axis=0, concat_axis=0, tiled=True)
    lead = lead[: lead_slices(devices)[0]].reshape(2, 2, TILE, TILE)

    def exchange(mine):
        near = lax.ppermute(mine, "col", [(c, c ^ 1) for c in range(n_col)])
        far = lax.ppermute(mine, "col", [(c, c ^ 2) for c in range(n_col)])
        return [near, far, lax.ppermute(far, "col", [(c, c ^ 1) for c in range(n_col)])]

    def own_panels(mine, lead):
        return row_panels(mine, exchange(mine), lead, diag_inverses, place, slot_in, front)

    sets = n_row // n_col
    circle = list(range(0, n_row, 2)) + list(range(n_row - 1, 0, -2))
    around = [0] + [sign * step for step in range(1, n_row // 2) for sign in (-1, 1)]
    shifts = around + [n_row // 2] if ring else list(range(sets))

    def described(row, shift):
        if not ring:
            return [a * sets + shift for a in range(rows_here)], list(range(n_col))
        origin = circle[(circle.index(row) + shift) % n_row]
        part, group = origin % n_col, rows_here // n_col
        columns = [(part * group + t) * sets + origin // n_col for t in range(group)]
        return columns, [(part - c) % n_col for c in range(n_col)]

    tables = [
        jnp.asarray(
            np.concatenate([described(row, shift)[k] for row in range(n_row) for shift in shifts]),
            jnp.int32,
        )
        for k in range(2)
    ]

    def updated(entries, panels, first):
        assert [shift for _, shift in entries] == shifts[first : first + len(entries)]
        pieces = [piece for piece, _ in entries]
        pieces = pieces[0] if isinstance(pieces[0], list) else pieces
        out = trailing(front, pieces, first, place, tables, panels, incoming)
        return [panels[0], out, *panels[2:]]

    first = 0
    if ring:
        arrived = []
        for j, part in enumerate(parts):
            pairs = [
                (r * n_col + c, ((r // n_col) * n_col + (c + j) % n_col) * n_col + r % n_col)
                for r in range(n_row)
                for c in range(n_col)
            ]
            arrived.append(lax.ppermute(part, BOTH, pairs))
        arrived, mine = lax.optimization_barrier((arrived, mine))
        arrived, lead = lax.optimization_barrier((arrived, lead))
        piece = jnp.stack(arrived)
        up = [(circle[i], circle[(i + 1) % n_row]) for i in range(n_row)]
        down = [(b, a) for a, b in up]
        rounds = [[(piece, 0)]]
        panels = own_panels(mine, lead)
        ahead = behind = piece
        for step in range(1, n_row // 2):
            ahead = lax.ppermute(ahead, "row", up)
            behind = lax.ppermute(behind, "row", down)
            if step == 2:
                panels = updated([(piece, 0), rounds[1][0]], panels, 0)
                ahead, behind, panels = lax.optimization_barrier((ahead, behind, panels))
            rounds.append([(ahead, -step), (behind, step)])
        last = [lax.ppermute(ahead[:2], "row", up), lax.ppermute(behind[2:], "row", down)]
        late = [entry for entries in rounds for entry in entries][2:]
        rounds = [late[:2], late[2:3], *rounds[3:], [(last, n_row // 2)]]
        first = 2

    else:
        pairs = [
            (r * n_col + c, ((r // n_col) * n_col + c) * n_col + r % n_col)
            for r in range(n_row)
            for c in range(n_col)
        ]
        moved = lax.all_gather(lax.ppermute(parts[0], BOTH, pairs), "row", axis=0, tiled=False)
        rounds = [[(moved[h * n_col : (h + 1) * n_col], h)] for h in range(sets)]
        panels = own_panels(mine, lead)

    for entries in rounds:
        panels = updated(entries, panels, first)
        first += len(entries)
    return panels[1]


def solution(mesh):
    return jax.shard_map(
        body,
        mesh=mesh,
        in_specs=(
            P(None, "row", None, "col", None, None),
            P(BOTH, None, None),
            P(BOTH, None),
            P(BOTH),
            P(BOTH),
            P(),
        ),
        out_specs=P(None, "row", None, "col", None, None),
        check_vma=False,
    )
```

```python
import functools

import jax
import jax.numpy as jnp
import numpy as np
from jax import lax
from jax.experimental import pallas as pl
from jax.experimental.pallas import tpu as pltpu
from jax.sharding import PartitionSpec as P

TILE = 128
PANEL = 256
WIDTH = 2 * PANEL
NOTE = 8
VMEM = 46 * 1024 * 1024
BOTH = ("row", "col")


def halves(value):
    high = value.astype(jnp.bfloat16)
    low = (value - high.astype(jnp.float32)).astype(jnp.bfloat16)
    return high, low


def deep(value):
    high, low = halves(value)
    return jnp.concatenate([high, low, high], axis=1)


def stacked(value):
    high, low = halves(value)
    return jnp.concatenate([high, high, low], axis=0)


def dot(left, right):
    return jnp.dot(left, right, preferred_element_type=jnp.float32)


def two_panels(columns, small_ref, mask):
    one = mask(0, dot(deep(jnp.concatenate(columns[:2], axis=1)), small_ref[0]))
    field = jnp.concatenate(columns[2:], axis=1) - dot(deep(mask(1, one)), small_ref[1])
    return one, mask(1, dot(deep(field), small_ref[2]))


def two_panels_across(columns, small_ref):
    one = dot(small_ref[0], stacked(jnp.concatenate(columns[:2], axis=0)))
    field = jnp.concatenate(columns[2:], axis=0) - dot(small_ref[1], stacked(one))
    return one, dot(small_ref[2], stacked(field))


def whole_spec(array):
    rank = len(array.shape)
    return pl.BlockSpec(array.shape, lambda *_: (0,) * rank)


def lead_slices(devices):
    height = max(8, 4 * TILE // devices)
    return 4 * TILE // height, height


def pack_kernel(
    owners, place, dest, slot, count, child_ref, front_ref, out_ref, held_ref, notes_ref,
    lead_ref, tile_ref, in_sems, out_sems, sem,
):
    n_slices, height, _ = lead_ref.shape
    each = n_slices // 4
    live = jnp.minimum(count[0], child_ref.shape[0])

    def arrive(k):
        return pltpu.make_async_copy(child_ref.at[k], held_ref.at[k], in_sems.at[k])

    def leave(k):
        return pltpu.make_async_copy(
            held_ref.at[k], out_ref.at[dest[k], pl.ds(0, TILE)], out_sems.at[k]
        )

    @pl.loop(0, live)
    def _(k):
        arrive(k).start()

    notes_ref[...] = jnp.full_like(notes_ref, -1.0)
    lead_ref[...] = jnp.zeros_like(lead_ref)
    for i, owner in enumerate(owners):

        @pl.when(place[3] == owner)
        def _():
            own = pltpu.make_async_copy(front_ref.at[0, 0, 0, 0], tile_ref, sem)
            own.start()
            own.wait()
            lead_ref[i * each : (i + 1) * each] = tile_ref[...].reshape(each, height, TILE)

    @pl.loop(0, live)
    def _(k):
        notes_ref[dest[k]] = jnp.full(notes_ref.shape[1:], slot[k].astype(jnp.float32))
        arrive(k).wait()
        leave(k).start()
        for i, owner in enumerate(owners):

            @pl.when(jnp.logical_and(slot[k] == 0, dest[k] == owner))
            def _():
                span = pl.ds(i * each, each)
                lead_ref[span] = lead_ref[span] + held_ref[k].reshape(each, height, TILE)

    notes = pltpu.make_async_copy(notes_ref, out_ref.at[:, pl.ds(TILE, NOTE)], sem)
    notes.start()
    notes.wait()
    lead = pltpu.make_async_copy(
        lead_ref, out_ref.at[pl.ds(0, n_slices), pl.ds(TILE + NOTE, height)], sem
    )
    lead.start()
    lead.wait()

    @pl.loop(0, live)
    def _(k):
        leave(k).wait()


def pack(child_tiles, front, place, dest, slot, count, devices, owners):
    slots = child_tiles.shape[0]
    n_slices, height = lead_slices(devices)
    hbm = pl.BlockSpec(memory_space=pltpu.HBM)
    return pl.pallas_call(
        functools.partial(pack_kernel, owners),
        in_specs=[pl.BlockSpec(memory_space=pltpu.SMEM)] * 4 + [hbm, hbm],
        out_specs=hbm,
        scratch_shapes=[
            pltpu.VMEM((slots, TILE, TILE), jnp.float32),
            pltpu.VMEM((devices, NOTE, TILE), jnp.float32),
            pltpu.VMEM((n_slices, height, TILE), jnp.float32),
            pltpu.VMEM((TILE, TILE), jnp.float32),
            pltpu.SemaphoreType.DMA((slots,)),
            pltpu.SemaphoreType.DMA((slots,)),
            pltpu.SemaphoreType.DMA,
        ],
        out_shape=jax.ShapeDtypeStruct((devices, TILE + NOTE + height, TILE), jnp.float32),
        compiler_params=pltpu.CompilerParams(vmem_limit_bytes=62 * 1024 * 1024),
        name="pack",
    )(place, dest, slot, count, child_tiles, front)


def columns_kernel(place, slot_in, front_ref, incoming_ref, out_ref, own_ref, *rest):
    *parts, tile_ref, slices_ref, sem, slices_sem = rest
    cols = place[2]
    height = own_ref.shape[1]
    strip = pltpu.make_async_copy(front_ref.at[:, 0, 0, 0], out_ref, sem)
    strip.start()
    slices = pltpu.make_async_copy(
        incoming_ref.at[:, pl.ds(TILE + NOTE, height)], slices_ref, slices_sem
    )
    slices.start()
    strip.wait()

    @pl.loop(0, incoming_ref.shape[0])
    def _(s):
        slot = slot_in[s]

        @pl.when(jnp.logical_and(slot >= 0, lax.rem(slot, cols) == 0))
        def _():
            copy = pltpu.make_async_copy(incoming_ref.at[s, pl.ds(0, TILE)], tile_ref, sem)
            copy.start()
            copy.wait()
            row = lax.div(slot, cols)
            out_ref[row] = out_ref[row] + tile_ref[...]

    count = len(parts)
    for j, part_ref in enumerate(parts):
        group = part_ref.shape[0]
        for t in range(group):
            part_ref[t] = out_ref[lax.rem(place[1] + j, count) * group + t].T

    slices.wait()
    own_ref[...] = jnp.broadcast_to(jnp.sum(slices_ref[...], axis=0)[None], own_ref.shape)


def assemble_columns(front, incoming, place, slot_in, parts):
    rows, devices = front.shape[0], incoming.shape[0]
    _, height = lead_slices(devices)
    shapes = [(rows, TILE, TILE), (devices, height, TILE)]
    shapes += [(rows // parts, TILE, TILE)] * parts
    out_shape = [jax.ShapeDtypeStruct(shape, jnp.float32) for shape in shapes]
    return pl.pallas_call(
        columns_kernel,
        grid_spec=pltpu.PrefetchScalarGridSpec(
            num_scalar_prefetch=2,
            grid=(1,),
            in_specs=[pl.BlockSpec(memory_space=pltpu.HBM)] * 2,
            out_specs=[whole_spec(a) for a in out_shape],
            scratch_shapes=[
                pltpu.VMEM((TILE, TILE), jnp.float32),
                pltpu.VMEM((devices, height, TILE), jnp.float32),
                pltpu.SemaphoreType.DMA,
                pltpu.SemaphoreType.DMA,
            ],
        ),
        out_shape=out_shape,
        compiler_params=pltpu.CompilerParams(vmem_limit_bytes=VMEM),
        name="panel_columns",
    )(place, slot_in, front, incoming)


def row_panels_kernel(
    place, slot_in, t0, t1, t2, t3, lead_ref, diag_ref, pair_ref, out_ref, across_ref, order,
    starts, small_ref, tiles_ref, cursor,
):
    step = pl.program_id(0)
    cols = starts.shape[0] - 1
    my_row, my_col = place[0], place[1]
    group = t0.shape[0]
    height = group * TILE

    @pl.when(step == 0)
    def _():
        small_ref[0] = stacked(diag_ref[0])
        lead = jnp.concatenate(
            [jnp.concatenate([lead_ref[i, 0], lead_ref[i, 1]], axis=1) for i in range(2)], axis=0
        )
        lead = dot(deep(lead), small_ref[0])
        small_ref[1] = stacked(lead.T)
        small_ref[2] = stacked(diag_ref[1])
        across_ref[0] = deep(diag_ref[0].T)
        across_ref[1] = deep(lead)
        across_ref[2] = deep(diag_ref[1].T)

        @pl.loop(0, cols + 1)
        def _(b):
            starts[b] = 0

        @pl.loop(0, slot_in.shape[0])
        def _(s):
            @pl.when(slot_in[s] >= 0)
            def _():
                b = lax.rem(slot_in[s], cols)
                starts[b + 1] = starts[b + 1] + 1

        @pl.loop(0, cols)
        def _(b):
            cursor[b] = starts[b]
            starts[b + 1] = starts[b + 1] + starts[b]

        @pl.loop(0, slot_in.shape[0])
        def _(s):
            @pl.when(slot_in[s] >= 0)
            def _():
                b = lax.rem(slot_in[s], cols)
                i = cursor[b]
                order[2 * i] = s
                order[2 * i + 1] = lax.div(slot_in[s], cols)
                cursor[b] = i + 1


    for i, tile_ref in enumerate((t0, t1, t2, t3)):
        tiles_ref[jnp.bitwise_xor(my_col, i)] = tile_ref[...]
    columns = [tiles_ref[c].reshape(height, TILE) for c in range(4)]
    tile_row = lax.broadcasted_iota(jnp.int32, (height, PANEL), 0) // TILE
    first = jnp.logical_and(step == 0, tile_row == 0)

    def mask(panels_above, value):
        above = jnp.logical_and(first, my_row < 2 * panels_above)
        return jnp.where(above, 0.0, value) if panels_above else value

    one, two = two_panels(columns, small_ref, mask)
    for i, panel in enumerate((mask(1, one), mask(2, two))):
        for k, half in enumerate(halves(panel)):
            pair_ref[:, k * WIDTH + i * PANEL : k * WIDTH + (i + 1) * PANEL] = half
    pieces = (one[:, :TILE], one[:, TILE:], two[:, :TILE], two[:, TILE:])
    for c in range(4):

        @pl.when(my_col == c)
        def _():
            out_ref[:, 0, 0, 0] = pieces[c].reshape(group, TILE, TILE)


def row_panels(mine, others, lead, diag, place, slot_in, front):
    rows = front.shape[0]
    cols = front.shape[2]
    group = rows // 3
    height = group * TILE
    out_shape = [
        jax.ShapeDtypeStruct((rows * TILE, 2 * WIDTH), jnp.bfloat16),
        jax.ShapeDtypeStruct(front.shape, jnp.float32),
        jax.ShapeDtypeStruct((3, PANEL, 3 * PANEL), jnp.bfloat16),
        jax.ShapeDtypeStruct((2 * slot_in.shape[0],), jnp.int32),
        jax.ShapeDtypeStruct((cols + 1,), jnp.int32),
    ]
    strip = pl.BlockSpec((group, TILE, TILE), lambda i, *_: (i, 0, 0))
    return pl.pallas_call(
        row_panels_kernel,
        grid_spec=pltpu.PrefetchScalarGridSpec(
            num_scalar_prefetch=2,
            grid=(3,),
            in_specs=[strip] * 4 + [whole_spec(lead), whole_spec(diag)],
            out_specs=[
                pl.BlockSpec((height, 2 * WIDTH), lambda i, *_: (i, 0)),
                pl.BlockSpec((group, 1, 1, 1, TILE, TILE), lambda i, *_: (i, 0, 0, 0, 0, 0)),
                whole_spec(out_shape[2]),
                pl.BlockSpec(memory_space=pltpu.SMEM),
                pl.BlockSpec(memory_space=pltpu.SMEM),
            ],
            scratch_shapes=[
                pltpu.VMEM((3, 3 * PANEL, PANEL), jnp.bfloat16),
                pltpu.VMEM((4, group, TILE, TILE), jnp.float32),
                pltpu.SMEM((cols,), jnp.int32),
            ],
        ),
        out_shape=out_shape,
        compiler_params=pltpu.CompilerParams(vmem_limit_bytes=VMEM),
        name="row_panels",
    )(place, slot_in, mine, *others, lead, diag)


def trailing_kernel(
    first, n_held, halved, place, columns_table, places_table, order, starts, pair_ref, small_ref,
    *rest,
):
    piece_refs = rest[:n_held]
    front_ref, incoming_ref, _, out_ref, right_ref, taken, given, child_ref, *rest = rest[n_held:]
    take_sems, give_sems, child_sems, *joined = rest
    if halved:
        joined[0][:2] = piece_refs[0][...]
        joined[0][2:] = piece_refs[1][...]
        piece_refs = joined
    n_pieces = len(piece_refs)
    group = piece_refs[0].shape[1]
    count = n_pieces * group
    steps = (count + 1) // 2
    rows, cols = front_ref.shape[0], front_ref.shape[2]
    columns_base = place[0] * cols + first * group
    places_base = (place[0] * (cols // group) + first) * 4

    def columns_of(step):
        for j in range(2):
            index = jnp.minimum(2 * step, count - 2) + j
            b = columns_table[columns_base + index]
            wanted = b > 0
            if count % 2 and j == 0:
                wanted = jnp.logical_and(wanted, step < steps - 1)
            yield j, b, wanted

    def each_take(step, act):
        slot = lax.rem(step, 2)
        for j, b, wanted in columns_of(step):

            @pl.when(wanted)
            def _():
                act(
                    pltpu.make_async_copy(
                        front_ref.at[:, 0, b, 0], taken.at[slot, j], take_sems.at[slot, j]
                    )
                )

    def each_give(step, act):
        slot = lax.rem(step, 2)
        for j, b, wanted in columns_of(step):

            @pl.when(wanted)
            def _():
                act(
                    pltpu.make_async_copy(
                        given.at[slot, j], out_ref.at[:, 0, b, 0], give_sems.at[slot, j]
                    )
                )

    def each_child(step, act):
        for j, b, wanted in columns_of(step):

            @pl.when(wanted)
            def _():
                @pl.loop(starts[b], starts[b + 1])
                def _(i):
                    s = order[2 * i]
                    copy = pltpu.make_async_copy(
                        incoming_ref.at[s, pl.ds(0, TILE)], child_ref.at[s], child_sems.at[s]
                    )
                    act(copy, j, s, order[2 * i + 1])

    for step in range(min(steps, 2)):
        each_take(step, lambda copy: copy.start())
    for step in range(steps):
        each_child(step, lambda copy, *_: copy.start())

    tile_columns = [
        jnp.concatenate(
            [
                piece[places_table[places_base + 4 * p + c], t]
                for p, piece in enumerate(piece_refs)
                for t in range(group)
            ],
            axis=1,
        )
        for c in range(4)
    ]
    for i, panel in enumerate(two_panels_across(tile_columns, small_ref)):
        high, low = halves(panel)
        for k, half in enumerate((high, high, low)):
            right_ref[k * WIDTH + i * PANEL : k * WIDTH + (i + 1) * PANEL] = half

    @pl.loop(0, steps)
    def _(step):
        slot = lax.rem(step, 2)
        each_take(step, lambda copy: copy.wait())

        @pl.when(step >= 2)
        def _():
            each_give(step - 2, lambda copy: copy.wait())

        start = jnp.minimum(2 * step, count - 2)
        lanes = pl.ds(pl.multiple_of(start * TILE, TILE), 2 * TILE)
        block = rows // 3
        for m in range(3):
            left = pair_ref[m * block * TILE : (m + 1) * block * TILE]
            update = dot(jnp.concatenate([left, left[:, :WIDTH]], axis=1), right_ref[:, lanes])
            span = slice(m * block, (m + 1) * block)
            for j in range(2):
                part = update[:, j * TILE : (j + 1) * TILE].reshape(block, TILE, TILE)
                given[slot, j, span] = taken[slot, j, span] - part

        def add(copy, j, s, a):
            copy.wait()
            given[slot, j, a] = given[slot, j, a] + child_ref[s]

        each_child(step, add)
        each_give(step, lambda copy: copy.start())

        @pl.when(step + 2 < steps)
        def _():
            each_take(step + 2, lambda copy: copy.start())

    for step in range(max(steps - 2, 0), steps):
        each_give(step, lambda copy: copy.wait())


def trailing(front, pieces, first, place, tables, panels, incoming):
    rows = front.shape[0]
    pair, out, small, order, starts = panels
    group = pieces[0].shape[1]
    halved = pieces[0].shape[0] == 2
    count = group if halved else len(pieces) * group
    scalars = [place, *tables, order, starts]
    held = [pair, small, *pieces]
    distant = [front, incoming, out]
    spec = lambda space, n: [pl.BlockSpec(memory_space=space)] * n
    height = rows * TILE
    devices = incoming.shape[0]
    return pl.pallas_call(
        functools.partial(trailing_kernel, first, len(pieces), halved),
        in_specs=spec(pltpu.SMEM, 5) + spec(pltpu.VMEM, len(held)) + spec(pltpu.HBM, 3),
        out_specs=pl.BlockSpec(memory_space=pltpu.HBM),
        scratch_shapes=[
            pltpu.VMEM((3 * WIDTH, count * TILE), jnp.bfloat16),
            pltpu.VMEM((2, 2, rows, TILE, TILE), jnp.float32),
            pltpu.VMEM((2, 2, rows, TILE, TILE), jnp.float32),
            pltpu.VMEM((devices, TILE, TILE), jnp.float32),
            pltpu.SemaphoreType.DMA((2, 2)),
            pltpu.SemaphoreType.DMA((2, 2)),
            pltpu.SemaphoreType.DMA((devices,)),
        ]
        + [pltpu.VMEM((4, group, TILE, TILE), jnp.float32)] * halved,
        out_shape=jax.ShapeDtypeStruct(front.shape, jnp.float32),
        input_output_aliases={len(held) + 7: 0},
        compiler_params=pltpu.CompilerParams(vmem_limit_bytes=VMEM),
        cost_estimate=pl.CostEstimate(
            flops=8 * count * 2 * height * TILE * WIDTH,
            bytes_accessed=count * 2 * height * TILE * 4,
            transcendentals=0,
        ),
        name="trailing",
    )(*scalars, *held, *distant)


def body(front, child_tiles, tile_dest, tile_slot, tile_count, diag_inverses):
    n_row = lax.axis_size("row")
    n_col = lax.axis_size("col")
    my_row = lax.axis_index("row").astype(jnp.int32)
    my_col = lax.axis_index("col").astype(jnp.int32)
    rows_here, cols_here = (front.shape[0], front.shape[2])
    devices = n_row * n_col
    assert n_col == 4 and n_row % 4 == 0 and rows_here % 3 == 0
    owners = [r * n_col + c for r in (2, 3) for c in (0, 1)]
    place = jnp.stack([my_row, my_col, jnp.int32(cols_here), my_row * n_col + my_col])

    outgoing = pack(
        child_tiles, front, place, tile_dest[:, 0], tile_slot, tile_count, devices, owners
    )
    incoming = lax.all_to_all(outgoing, BOTH, split_axis=0, concat_axis=0, tiled=True)
    slot_in = lax.optimization_barrier(incoming[:, TILE, 0].astype(jnp.int32))

    ring = rows_here % n_col == 0
    mine, own, *parts = assemble_columns(front, incoming, place, slot_in, n_col if ring else 1)
    lead = lax.all_to_all(own, BOTH, split_axis=0, concat_axis=0, tiled=True)
    lead = lead[: lead_slices(devices)[0]].reshape(2, 2, TILE, TILE)

    def exchange(mine):
        near = lax.ppermute(mine, "col", [(c, c ^ 1) for c in range(n_col)])
        far = lax.ppermute(mine, "col", [(c, c ^ 2) for c in range(n_col)])
        return [near, far, lax.ppermute(far, "col", [(c, c ^ 1) for c in range(n_col)])]

    def own_panels(mine, lead):
        return row_panels(mine, exchange(mine), lead, diag_inverses, place, slot_in, front)

    sets = n_row // n_col
    circle = list(range(0, n_row, 2)) + list(range(n_row - 1, 0, -2))
    around = [0] + [sign * step for step in range(1, n_row // 2) for sign in (-1, 1)]
    shifts = around + [n_row // 2] if ring else list(range(sets))

    def described(row, shift):
        if not ring:
            return [a * sets + shift for a in range(rows_here)], list(range(n_col))
        origin = circle[(circle.index(row) + shift) % n_row]
        part, group = origin % n_col, rows_here // n_col
        columns = [(part * group + t) * sets + origin // n_col for t in range(group)]
        return columns, [(part - c) % n_col for c in range(n_col)]

    tables = [
        jnp.asarray(
            np.concatenate([described(row, shift)[k] for row in range(n_row) for shift in shifts]),
            jnp.int32,
        )
        for k in range(2)
    ]

    def updated(entries, panels, first):
        assert [shift for _, shift in entries] == shifts[first : first + len(entries)]
        pieces = [piece for piece, _ in entries]
        pieces = pieces[0] if isinstance(pieces[0], list) else pieces
        out = trailing(front, pieces, first, place, tables, panels, incoming)
        return [panels[0], out, *panels[2:]]

    first = 0
    if ring:
        arrived = []
        for j, part in enumerate(parts):
            pairs = [
                (r * n_col + c, ((r // n_col) * n_col + (c + j) % n_col) * n_col + r % n_col)
                for r in range(n_row)
                for c in range(n_col)
            ]
            arrived.append(lax.ppermute(part, BOTH, pairs))
        arrived, mine, lead = lax.optimization_barrier((arrived, mine, lead))
        piece = jnp.stack(arrived)
        up = [(circle[i], circle[(i + 1) % n_row]) for i in range(n_row)]
        down = [(b, a) for a, b in up]
        rounds = [[(piece, 0)]]
        panels = own_panels(mine, lead)
        ahead = behind = piece
        for step in range(1, n_row // 2):
            ahead = lax.ppermute(ahead, "row", up)
            behind = lax.ppermute(behind, "row", down)
            if step == 2:
                panels = updated([(piece, 0), rounds[1][0]], panels, 0)
                ahead, behind, panels = lax.optimization_barrier((ahead, behind, panels))
            rounds.append([(ahead, -step), (behind, step)])
        last = [lax.ppermute(ahead[:2], "row", up), lax.ppermute(behind[2:], "row", down)]
        late = [entry for entries in rounds for entry in entries][2:]
        rounds = [late[:2], late[2:3], *rounds[3:], [(last, n_row // 2)]]
        first = 2

    else:
        pairs = [
            (r * n_col + c, ((r // n_col) * n_col + c) * n_col + r % n_col)
            for r in range(n_row)
            for c in range(n_col)
        ]
        moved = lax.all_gather(lax.ppermute(parts[0], BOTH, pairs), "row", axis=0, tiled=False)
        rounds = [[(moved[h * n_col : (h + 1) * n_col], h)] for h in range(sets)]
        panels = own_panels(mine, lead)

    for entries in rounds:
        panels = updated(entries, panels, first)
        first += len(entries)
    return panels[1]


def solution(mesh):
    return jax.shard_map(
        body,
        mesh=mesh,
        in_specs=(
            P(None, "row", None, "col", None, None),
            P(BOTH, None, None),
            P(BOTH, None),
            P(BOTH),
            P(BOTH),
            P(),
        ),
        out_specs=P(None, "row", None, "col", None, None),
        check_vma=False,
    )
```

```python
import functools

import jax
import jax.numpy as jnp
import numpy as np
from jax import lax
from jax.experimental import pallas as pl
from jax.experimental.pallas import tpu as pltpu
from jax.sharding import PartitionSpec as P

TILE = 128
PANEL = 256
WIDTH = 2 * PANEL
NOTE = 8
VMEM = 46 * 1024 * 1024
BOTH = ("row", "col")


def halves(value):
    high = value.astype(jnp.bfloat16)
    low = (value - high.astype(jnp.float32)).astype(jnp.bfloat16)
    return high, low


def deep(value):
    high, low = halves(value)
    return jnp.concatenate([high, low, high], axis=1)


def stacked(value):
    high, low = halves(value)
    return jnp.concatenate([high, high, low], axis=0)


def dot(left, right):
    return jnp.dot(left, right, preferred_element_type=jnp.float32)


def two_panels(columns, small_ref, mask):
    one = mask(0, dot(deep(jnp.concatenate(columns[:2], axis=1)), small_ref[0]))
    field = jnp.concatenate(columns[2:], axis=1) - dot(deep(mask(1, one)), small_ref[1])
    return one, mask(1, dot(deep(field), small_ref[2]))


def two_panels_across(columns, small_ref):
    one = dot(small_ref[0], stacked(jnp.concatenate(columns[:2], axis=0)))
    field = jnp.concatenate(columns[2:], axis=0) - dot(small_ref[1], stacked(one))
    return one, dot(small_ref[2], stacked(field))


def whole_spec(array):
    rank = len(array.shape)
    return pl.BlockSpec(array.shape, lambda *_: (0,) * rank)


def lead_slices(devices):
    height = max(8, 4 * TILE // devices)
    return 4 * TILE // height, height


def pack_kernel(
    owners, place, dest, slot, count, child_ref, front_ref, out_ref, held_ref, notes_ref,
    lead_ref, tile_ref, in_sems, out_sems, sem, lead_sem,
):
    n_slices, height, _ = lead_ref.shape
    each = n_slices // 4
    live = jnp.minimum(count[0], child_ref.shape[0])

    def arrive(k):
        return pltpu.make_async_copy(child_ref.at[k], held_ref.at[k], in_sems.at[k])

    def leave(k):
        return pltpu.make_async_copy(
            held_ref.at[k], out_ref.at[dest[k], pl.ds(0, TILE)], out_sems.at[k]
        )

    own = pltpu.make_async_copy(front_ref.at[0, 0, 0, 0], tile_ref, sem)
    own.start()

    @pl.loop(0, live)
    def _(k):
        arrive(k).start()

    notes_ref[...] = jnp.full_like(notes_ref, -1.0)
    lead_ref[...] = jnp.zeros_like(lead_ref)
    own.wait()
    for i, owner in enumerate(owners):

        @pl.when(place[3] == owner)
        def _():
            lead_ref[i * each : (i + 1) * each] = tile_ref[...].reshape(each, height, TILE)

    @pl.loop(0, live)
    def _(k):
        notes_ref[dest[k]] = jnp.full(notes_ref.shape[1:], slot[k].astype(jnp.float32))
        arrive(k).wait()
        leave(k).start()
        for i, owner in enumerate(owners):

            @pl.when(jnp.logical_and(slot[k] == 0, dest[k] == owner))
            def _():
                span = pl.ds(i * each, each)
                lead_ref[span] = lead_ref[span] + held_ref[k].reshape(each, height, TILE)

    notes = pltpu.make_async_copy(notes_ref, out_ref.at[:, pl.ds(TILE, NOTE)], sem)
    notes.start()
    lead = pltpu.make_async_copy(
        lead_ref, out_ref.at[pl.ds(0, n_slices), pl.ds(TILE + NOTE, height)], lead_sem
    )
    lead.start()
    notes.wait()
    lead.wait()

    @pl.loop(0, live)
    def _(k):
        leave(k).wait()


def pack(child_tiles, front, place, dest, slot, count, devices, owners):
    slots = child_tiles.shape[0]
    n_slices, height = lead_slices(devices)
    hbm = pl.BlockSpec(memory_space=pltpu.HBM)
    return pl.pallas_call(
        functools.partial(pack_kernel, owners),
        in_specs=[pl.BlockSpec(memory_space=pltpu.SMEM)] * 4 + [hbm, hbm],
        out_specs=hbm,
        scratch_shapes=[
            pltpu.VMEM((slots, TILE, TILE), jnp.float32),
            pltpu.VMEM((devices, NOTE, TILE), jnp.float32),
            pltpu.VMEM((n_slices, height, TILE), jnp.float32),
            pltpu.VMEM((TILE, TILE), jnp.float32),
            pltpu.SemaphoreType.DMA((slots,)),
            pltpu.SemaphoreType.DMA((slots,)),
            pltpu.SemaphoreType.DMA,
            pltpu.SemaphoreType.DMA,
        ],
        out_shape=jax.ShapeDtypeStruct((devices, TILE + NOTE + height, TILE), jnp.float32),
        compiler_params=pltpu.CompilerParams(vmem_limit_bytes=62 * 1024 * 1024),
        name="pack",
    )(place, dest, slot, count, child_tiles, front)


def columns_kernel(place, slot_in, front_ref, incoming_ref, out_ref, own_ref, *rest):
    *parts, tile_ref, slices_ref, sem, slices_sem = rest
    cols = place[2]
    height = own_ref.shape[1]
    strip = pltpu.make_async_copy(front_ref.at[:, 0, 0, 0], out_ref, sem)
    strip.start()
    slices = pltpu.make_async_copy(
        incoming_ref.at[:, pl.ds(TILE + NOTE, height)], slices_ref, slices_sem
    )
    slices.start()
    strip.wait()

    @pl.loop(0, incoming_ref.shape[0])
    def _(s):
        slot = slot_in[s]

        @pl.when(jnp.logical_and(slot >= 0, lax.rem(slot, cols) == 0))
        def _():
            copy = pltpu.make_async_copy(incoming_ref.at[s, pl.ds(0, TILE)], tile_ref, sem)
            copy.start()
            copy.wait()
            row = lax.div(slot, cols)
            out_ref[row] = out_ref[row] + tile_ref[...]

    count = len(parts)
    for j, part_ref in enumerate(parts):
        group = part_ref.shape[0]
        for t in range(group):
            part_ref[t] = out_ref[lax.rem(place[1] + j, count) * group + t].T

    slices.wait()
    own_ref[...] = jnp.broadcast_to(jnp.sum(slices_ref[...], axis=0)[None], own_ref.shape)


def assemble_columns(front, incoming, place, slot_in, parts):
    rows, devices = front.shape[0], incoming.shape[0]
    _, height = lead_slices(devices)
    shapes = [(rows, TILE, TILE), (devices, height, TILE)]
    shapes += [(rows // parts, TILE, TILE)] * parts
    out_shape = [jax.ShapeDtypeStruct(shape, jnp.float32) for shape in shapes]
    return pl.pallas_call(
        columns_kernel,
        grid_spec=pltpu.PrefetchScalarGridSpec(
            num_scalar_prefetch=2,
            grid=(1,),
            in_specs=[pl.BlockSpec(memory_space=pltpu.HBM)] * 2,
            out_specs=[whole_spec(a) for a in out_shape],
            scratch_shapes=[
                pltpu.VMEM((TILE, TILE), jnp.float32),
                pltpu.VMEM((devices, height, TILE), jnp.float32),
                pltpu.SemaphoreType.DMA,
                pltpu.SemaphoreType.DMA,
            ],
        ),
        out_shape=out_shape,
        compiler_params=pltpu.CompilerParams(vmem_limit_bytes=VMEM),
        name="panel_columns",
    )(place, slot_in, front, incoming)


def row_panels_kernel(
    place, slot_in, t0, t1, t2, t3, lead_ref, diag_ref, pair_ref, out_ref, across_ref, order,
    starts, small_ref, tiles_ref, cursor,
):
    step = pl.program_id(0)
    cols = starts.shape[0] - 1
    my_row, my_col = place[0], place[1]
    group = t0.shape[0]
    height = group * TILE

    @pl.when(step == 0)
    def _():
        small_ref[0] = stacked(diag_ref[0])
        lead = jnp.concatenate(
            [jnp.concatenate([lead_ref[i, 0], lead_ref[i, 1]], axis=1) for i in range(2)], axis=0
        )
        lead = dot(deep(lead), small_ref[0])
        small_ref[1] = stacked(lead.T)
        small_ref[2] = stacked(diag_ref[1])
        across_ref[0] = deep(diag_ref[0].T)
        across_ref[1] = deep(lead)
        across_ref[2] = deep(diag_ref[1].T)

        @pl.loop(0, cols + 1)
        def _(b):
            starts[b] = 0

        @pl.loop(0, slot_in.shape[0])
        def _(s):
            @pl.when(slot_in[s] >= 0)
            def _():
                b = lax.rem(slot_in[s], cols)
                starts[b + 1] = starts[b + 1] + 1

        @pl.loop(0, cols)
        def _(b):
            cursor[b] = starts[b]
            starts[b + 1] = starts[b + 1] + starts[b]

        @pl.loop(0, slot_in.shape[0])
        def _(s):
            @pl.when(slot_in[s] >= 0)
            def _():
                b = lax.rem(slot_in[s], cols)
                i = cursor[b]
                order[2 * i] = s
                order[2 * i + 1] = lax.div(slot_in[s], cols)
                cursor[b] = i + 1


    for i, tile_ref in enumerate((t0, t1, t2, t3)):
        tiles_ref[jnp.bitwise_xor(my_col, i)] = tile_ref[...]
    columns = [tiles_ref[c].reshape(height, TILE) for c in range(4)]
    tile_row = lax.broadcasted_iota(jnp.int32, (height, PANEL), 0) // TILE
    first = jnp.logical_and(step == 0, tile_row == 0)

    def mask(panels_above, value):
        above = jnp.logical_and(first, my_row < 2 * panels_above)
        return jnp.where(above, 0.0, value) if panels_above else value

    one, two = two_panels(columns, small_ref, mask)
    for i, panel in enumerate((mask(1, one), mask(2, two))):
        for k, half in enumerate(halves(panel)):
            pair_ref[:, k * WIDTH + i * PANEL : k * WIDTH + (i + 1) * PANEL] = half
    pieces = (one[:, :TILE], one[:, TILE:], two[:, :TILE], two[:, TILE:])
    for c in range(4):

        @pl.when(my_col == c)
        def _():
            out_ref[:, 0, 0, 0] = pieces[c].reshape(group, TILE, TILE)


def row_panels(mine, others, lead, diag, place, slot_in, front):
    rows = front.shape[0]
    cols = front.shape[2]
    group = rows // 3
    height = group * TILE
    out_shape = [
        jax.ShapeDtypeStruct((rows * TILE, 2 * WIDTH), jnp.bfloat16),
        jax.ShapeDtypeStruct(front.shape, jnp.float32),
        jax.ShapeDtypeStruct((3, PANEL, 3 * PANEL), jnp.bfloat16),
        jax.ShapeDtypeStruct((2 * slot_in.shape[0],), jnp.int32),
        jax.ShapeDtypeStruct((cols + 1,), jnp.int32),
    ]
    strip = pl.BlockSpec((group, TILE, TILE), lambda i, *_: (i, 0, 0))
    return pl.pallas_call(
        row_panels_kernel,
        grid_spec=pltpu.PrefetchScalarGridSpec(
            num_scalar_prefetch=2,
            grid=(3,),
            in_specs=[strip] * 4 + [whole_spec(lead), whole_spec(diag)],
            out_specs=[
                pl.BlockSpec((height, 2 * WIDTH), lambda i, *_: (i, 0)),
                pl.BlockSpec((group, 1, 1, 1, TILE, TILE), lambda i, *_: (i, 0, 0, 0, 0, 0)),
                whole_spec(out_shape[2]),
                pl.BlockSpec(memory_space=pltpu.SMEM),
                pl.BlockSpec(memory_space=pltpu.SMEM),
            ],
            scratch_shapes=[
                pltpu.VMEM((3, 3 * PANEL, PANEL), jnp.bfloat16),
                pltpu.VMEM((4, group, TILE, TILE), jnp.float32),
                pltpu.SMEM((cols,), jnp.int32),
            ],
        ),
        out_shape=out_shape,
        compiler_params=pltpu.CompilerParams(vmem_limit_bytes=VMEM),
        name="row_panels",
    )(place, slot_in, mine, *others, lead, diag)


def trailing_kernel(
    first, n_held, halved, place, columns_table, places_table, order, starts, pair_ref, small_ref,
    *rest,
):
    piece_refs = rest[:n_held]
    front_ref, incoming_ref, _, out_ref, right_ref, taken, given, child_ref, *rest = rest[n_held:]
    take_sems, give_sems, child_sems, *joined = rest
    if halved:
        joined[0][:2] = piece_refs[0][...]
        joined[0][2:] = piece_refs[1][...]
        piece_refs = joined
    n_pieces = len(piece_refs)
    group = piece_refs[0].shape[1]
    count = n_pieces * group
    steps = (count + 1) // 2
    rows, cols = front_ref.shape[0], front_ref.shape[2]
    columns_base = place[0] * cols + first * group
    places_base = (place[0] * (cols // group) + first) * 4

    def columns_of(step):
        for j in range(2):
            index = jnp.minimum(2 * step, count - 2) + j
            b = columns_table[columns_base + index]
            wanted = b > 0
            if count % 2 and j == 0:
                wanted = jnp.logical_and(wanted, step < steps - 1)
            yield j, b, wanted

    def each_take(step, act):
        slot = lax.rem(step, 2)
        for j, b, wanted in columns_of(step):

            @pl.when(wanted)
            def _():
                act(
                    pltpu.make_async_copy(
                        front_ref.at[:, 0, b, 0], taken.at[slot, j], take_sems.at[slot, j]
                    )
                )

    def each_give(step, act):
        slot = lax.rem(step, 2)
        for j, b, wanted in columns_of(step):

            @pl.when(wanted)
            def _():
                act(
                    pltpu.make_async_copy(
                        given.at[slot, j], out_ref.at[:, 0, b, 0], give_sems.at[slot, j]
                    )
                )

    def each_child(step, act):
        for j, b, wanted in columns_of(step):

            @pl.when(wanted)
            def _():
                @pl.loop(starts[b], starts[b + 1])
                def _(i):
                    s = order[2 * i]
                    copy = pltpu.make_async_copy(
                        incoming_ref.at[s, pl.ds(0, TILE)], child_ref.at[s], child_sems.at[s]
                    )
                    act(copy, j, s, order[2 * i + 1])

    for step in range(min(steps, 2)):
        each_take(step, lambda copy: copy.start())
    for step in range(steps):
        each_child(step, lambda copy, *_: copy.start())

    tile_columns = [
        jnp.concatenate(
            [
                piece[places_table[places_base + 4 * p + c], t]
                for p, piece in enumerate(piece_refs)
                for t in range(group)
            ],
            axis=1,
        )
        for c in range(4)
    ]
    for i, panel in enumerate(two_panels_across(tile_columns, small_ref)):
        high, low = halves(panel)
        for k, half in enumerate((high, high, low)):
            right_ref[k * WIDTH + i * PANEL : k * WIDTH + (i + 1) * PANEL] = half

    @pl.loop(0, steps)
    def _(step):
        slot = lax.rem(step, 2)
        each_take(step, lambda copy: copy.wait())

        @pl.when(step >= 2)
        def _():
            each_give(step - 2, lambda copy: copy.wait())

        start = jnp.minimum(2 * step, count - 2)
        lanes = pl.ds(pl.multiple_of(start * TILE, TILE), 2 * TILE)
        block = rows // 3
        for m in range(3):
            left = pair_ref[m * block * TILE : (m + 1) * block * TILE]
            update = dot(left, right_ref[: 2 * WIDTH, lanes])
            update = update + dot(left[:, :WIDTH], right_ref[2 * WIDTH :, lanes])
            span = slice(m * block, (m + 1) * block)
            for j in range(2):
                part = update[:, j * TILE : (j + 1) * TILE].reshape(block, TILE, TILE)
                given[slot, j, span] = taken[slot, j, span] - part

        def add(copy, j, s, a):
            copy.wait()
            given[slot, j, a] = given[slot, j, a] + child_ref[s]

        each_child(step, add)
        each_give(step, lambda copy: copy.start())

        @pl.when(step + 2 < steps)
        def _():
            each_take(step + 2, lambda copy: copy.start())

    for step in range(max(steps - 2, 0), steps):
        each_give(step, lambda copy: copy.wait())


def trailing(front, pieces, first, place, tables, panels, incoming):
    rows = front.shape[0]
    pair, out, small, order, starts = panels
    group = pieces[0].shape[1]
    halved = pieces[0].shape[0] == 2
    count = group if halved else len(pieces) * group
    scalars = [place, *tables, order, starts]
    held = [pair, small, *pieces]
    distant = [front, incoming, out]
    spec = lambda space, n: [pl.BlockSpec(memory_space=space)] * n
    height = rows * TILE
    devices = incoming.shape[0]
    return pl.pallas_call(
        functools.partial(trailing_kernel, first, len(pieces), halved),
        in_specs=spec(pltpu.SMEM, 5) + spec(pltpu.VMEM, len(held)) + spec(pltpu.HBM, 3),
        out_specs=pl.BlockSpec(memory_space=pltpu.HBM),
        scratch_shapes=[
            pltpu.VMEM((3 * WIDTH, count * TILE), jnp.bfloat16),
            pltpu.VMEM((2, 2, rows, TILE, TILE), jnp.float32),
            pltpu.VMEM((2, 2, rows, TILE, TILE), jnp.float32),
            pltpu.VMEM((devices, TILE, TILE), jnp.float32),
            pltpu.SemaphoreType.DMA((2, 2)),
            pltpu.SemaphoreType.DMA((2, 2)),
            pltpu.SemaphoreType.DMA((devices,)),
        ]
        + [pltpu.VMEM((4, group, TILE, TILE), jnp.float32)] * halved,
        out_shape=jax.ShapeDtypeStruct(front.shape, jnp.float32),
        input_output_aliases={len(held) + 7: 0},
        compiler_params=pltpu.CompilerParams(vmem_limit_bytes=VMEM),
        cost_estimate=pl.CostEstimate(
            flops=8 * count * 2 * height * TILE * WIDTH,
            bytes_accessed=count * 2 * height * TILE * 4,
            transcendentals=0,
        ),
        name="trailing",
    )(*scalars, *held, *distant)


def body(front, child_tiles, tile_dest, tile_slot, tile_count, diag_inverses):
    n_row = lax.axis_size("row")
    n_col = lax.axis_size("col")
    my_row = lax.axis_index("row").astype(jnp.int32)
    my_col = lax.axis_index("col").astype(jnp.int32)
    rows_here, cols_here = (front.shape[0], front.shape[2])
    devices = n_row * n_col
    assert n_col == 4 and n_row % 4 == 0 and rows_here % 3 == 0
    owners = [r * n_col + c for r in (2, 3) for c in (0, 1)]
    place = jnp.stack([my_row, my_col, jnp.int32(cols_here), my_row * n_col + my_col])

    outgoing = pack(
        child_tiles, front, place, tile_dest[:, 0], tile_slot, tile_count, devices, owners
    )
    incoming = lax.all_to_all(outgoing, BOTH, split_axis=0, concat_axis=0, tiled=True)
    slot_in = lax.optimization_barrier(incoming[:, TILE, 0].astype(jnp.int32))

    ring = rows_here % n_col == 0
    mine, own, *parts = assemble_columns(front, incoming, place, slot_in, n_col if ring else 1)
    lead = lax.all_to_all(own, BOTH, split_axis=0, concat_axis=0, tiled=True)
    lead = lead[: lead_slices(devices)[0]].reshape(2, 2, TILE, TILE)

    def exchange(mine):
        near = lax.ppermute(mine, "col", [(c, c ^ 1) for c in range(n_col)])
        far = lax.ppermute(mine, "col", [(c, c ^ 2) for c in range(n_col)])
        return [near, far, lax.ppermute(far, "col", [(c, c ^ 1) for c in range(n_col)])]

    def own_panels(mine, lead):
        return row_panels(mine, exchange(mine), lead, diag_inverses, place, slot_in, front)

    sets = n_row // n_col
    circle = list(range(0, n_row, 2)) + list(range(n_row - 1, 0, -2))
    around = [0] + [sign * step for step in range(1, n_row // 2) for sign in (-1, 1)]
    shifts = around + [n_row // 2] if ring else list(range(sets))

    def described(row, shift):
        if not ring:
            return [a * sets + shift for a in range(rows_here)], list(range(n_col))
        origin = circle[(circle.index(row) + shift) % n_row]
        part, group = origin % n_col, rows_here // n_col
        columns = [(part * group + t) * sets + origin // n_col for t in range(group)]
        return columns, [(part - c) % n_col for c in range(n_col)]

    tables = [
        jnp.asarray(
            np.concatenate([described(row, shift)[k] for row in range(n_row) for shift in shifts]),
            jnp.int32,
        )
        for k in range(2)
    ]

    def updated(entries, panels, first):
        assert [shift for _, shift in entries] == shifts[first : first + len(entries)]
        pieces = [piece for piece, _ in entries]
        pieces = pieces[0] if isinstance(pieces[0], list) else pieces
        out = trailing(front, pieces, first, place, tables, panels, incoming)
        return [panels[0], out, *panels[2:]]

    first = 0
    if ring:
        arrived = []
        for j, part in enumerate(parts):
            pairs = [
                (r * n_col + c, ((r // n_col) * n_col + (c + j) % n_col) * n_col + r % n_col)
                for r in range(n_row)
                for c in range(n_col)
            ]
            arrived.append(lax.ppermute(part, BOTH, pairs))
        arrived, mine, lead = lax.optimization_barrier((arrived, mine, lead))
        piece = jnp.stack(arrived)
        up = [(circle[i], circle[(i + 1) % n_row]) for i in range(n_row)]
        down = [(b, a) for a, b in up]
        rounds = [[(piece, 0)]]
        panels = own_panels(mine, lead)
        ahead = behind = piece
        for step in range(1, n_row // 2):
            ahead = lax.ppermute(ahead, "row", up)
            behind = lax.ppermute(behind, "row", down)
            if step == 2:
                panels = updated(rounds[0], panels, 0)
                ahead, behind, panels = lax.optimization_barrier((ahead, behind, panels))
            rounds.append([(ahead, -step), (behind, step)])
        last = [lax.ppermute(ahead[:2], "row", up), lax.ppermute(behind[2:], "row", down)]
        rounds = [*rounds[1:], [(last, n_row // 2)]]
        first = 1

    else:
        pairs = [
            (r * n_col + c, ((r // n_col) * n_col + c) * n_col + r % n_col)
            for r in range(n_row)
            for c in range(n_col)
        ]
        moved = lax.all_gather(lax.ppermute(parts[0], BOTH, pairs), "row", axis=0, tiled=False)
        rounds = [[(moved[h * n_col : (h + 1) * n_col], h)] for h in range(sets)]
        panels = own_panels(mine, lead)

    for entries in rounds:
        panels = updated(entries, panels, first)
        first += len(entries)
    return panels[1]


def solution(mesh):
    return jax.shard_map(
        body,
        mesh=mesh,
        in_specs=(
            P(None, "row", None, "col", None, None),
            P(BOTH, None, None),
            P(BOTH, None),
            P(BOTH),
            P(BOTH),
            P(),
        ),
        out_specs=P(None, "row", None, "col", None, None),
        check_vma=False,
    )
```

```python
import functools

import jax
import jax.numpy as jnp
import numpy as np
from jax import lax
from jax.experimental import pallas as pl
from jax.experimental.pallas import tpu as pltpu
from jax.sharding import PartitionSpec as P

TILE = 128
PANEL = 256
WIDTH = 2 * PANEL
NOTE = 8
VMEM = 46 * 1024 * 1024
BOTH = ("row", "col")


def halves(value):
    high = value.astype(jnp.bfloat16)
    low = (value - high.astype(jnp.float32)).astype(jnp.bfloat16)
    return high, low


def deep(value):
    high, low = halves(value)
    return jnp.concatenate([high, low, high], axis=1)


def stacked(value):
    high, low = halves(value)
    return jnp.concatenate([high, high, low], axis=0)


def dot(left, right):
    return jnp.dot(left, right, preferred_element_type=jnp.float32)


def two_panels(columns, small_ref, mask):
    one = mask(0, dot(deep(jnp.concatenate(columns[:2], axis=1)), small_ref[0]))
    field = jnp.concatenate(columns[2:], axis=1) - dot(deep(mask(1, one)), small_ref[1])
    return one, mask(1, dot(deep(field), small_ref[2]))


def two_panels_across(columns, small_ref):
    one = dot(small_ref[0], stacked(jnp.concatenate(columns[:2], axis=0)))
    field = jnp.concatenate(columns[2:], axis=0) - dot(small_ref[1], stacked(one))
    return one, dot(small_ref[2], stacked(field))


def whole_spec(array):
    rank = len(array.shape)
    return pl.BlockSpec(array.shape, lambda *_: (0,) * rank)


def lead_slices(devices):
    height = max(8, 4 * TILE // devices)
    return 4 * TILE // height, height


def pack_kernel(
    owners, place, dest, slot, count, child_ref, front_ref, out_ref, held_ref, notes_ref,
    lead_ref, tile_ref, in_sems, out_sems, sem, lead_sem,
):
    n_slices, height, _ = lead_ref.shape
    each = n_slices // 4
    live = jnp.minimum(count[0], child_ref.shape[0])

    def arrive(k):
        return pltpu.make_async_copy(child_ref.at[k], held_ref.at[k], in_sems.at[k])

    def leave(k):
        return pltpu.make_async_copy(
            held_ref.at[k], out_ref.at[dest[k], pl.ds(0, TILE)], out_sems.at[k]
        )

    own = pltpu.make_async_copy(front_ref.at[0, 0, 0, 0], tile_ref, sem)
    own.start()

    @pl.loop(0, live)
    def _(k):
        arrive(k).start()

    notes_ref[...] = jnp.full_like(notes_ref, -1.0)
    lead_ref[...] = jnp.zeros_like(lead_ref)
    own.wait()
    for i, owner in enumerate(owners):

        @pl.when(place[3] == owner)
        def _():
            lead_ref[i * each : (i + 1) * each] = tile_ref[...].reshape(each, height, TILE)

    @pl.loop(0, live)
    def _(k):
        notes_ref[dest[k]] = jnp.full(notes_ref.shape[1:], slot[k].astype(jnp.float32))
        arrive(k).wait()
        leave(k).start()
        for i, owner in enumerate(owners):

            @pl.when(jnp.logical_and(slot[k] == 0, dest[k] == owner))
            def _():
                span = pl.ds(i * each, each)
                lead_ref[span] = lead_ref[span] + held_ref[k].reshape(each, height, TILE)

    notes = pltpu.make_async_copy(notes_ref, out_ref.at[:, pl.ds(TILE, NOTE)], sem)
    notes.start()
    lead = pltpu.make_async_copy(
        lead_ref, out_ref.at[pl.ds(0, n_slices), pl.ds(TILE + NOTE, height)], lead_sem
    )
    lead.start()
    notes.wait()
    lead.wait()

    @pl.loop(0, live)
    def _(k):
        leave(k).wait()


def pack(child_tiles, front, place, dest, slot, count, devices, owners):
    slots = child_tiles.shape[0]
    n_slices, height = lead_slices(devices)
    hbm = pl.BlockSpec(memory_space=pltpu.HBM)
    return pl.pallas_call(
        functools.partial(pack_kernel, owners),
        in_specs=[pl.BlockSpec(memory_space=pltpu.SMEM)] * 4 + [hbm, hbm],
        out_specs=hbm,
        scratch_shapes=[
            pltpu.VMEM((slots, TILE, TILE), jnp.float32),
            pltpu.VMEM((devices, NOTE, TILE), jnp.float32),
            pltpu.VMEM((n_slices, height, TILE), jnp.float32),
            pltpu.VMEM((TILE, TILE), jnp.float32),
            pltpu.SemaphoreType.DMA((slots,)),
            pltpu.SemaphoreType.DMA((slots,)),
            pltpu.SemaphoreType.DMA,
            pltpu.SemaphoreType.DMA,
        ],
        out_shape=jax.ShapeDtypeStruct((devices, TILE + NOTE + height, TILE), jnp.float32),
        compiler_params=pltpu.CompilerParams(vmem_limit_bytes=62 * 1024 * 1024),
        name="pack",
    )(place, dest, slot, count, child_tiles, front)


def columns_kernel(place, slot_in, front_ref, incoming_ref, out_ref, own_ref, *rest):
    *parts, tile_ref, slices_ref, sem, slices_sem = rest
    cols = place[2]
    height = own_ref.shape[1]
    strip = pltpu.make_async_copy(front_ref.at[:, 0, 0, 0], out_ref, sem)
    strip.start()
    slices = pltpu.make_async_copy(
        incoming_ref.at[:, pl.ds(TILE + NOTE, height)], slices_ref, slices_sem
    )
    slices.start()
    strip.wait()

    @pl.loop(0, incoming_ref.shape[0])
    def _(s):
        slot = slot_in[s]

        @pl.when(jnp.logical_and(slot >= 0, lax.rem(slot, cols) == 0))
        def _():
            copy = pltpu.make_async_copy(incoming_ref.at[s, pl.ds(0, TILE)], tile_ref, sem)
            copy.start()
            copy.wait()
            row = lax.div(slot, cols)
            out_ref[row] = out_ref[row] + tile_ref[...]

    count = len(parts)
    for j, part_ref in enumerate(parts):
        group = part_ref.shape[0]
        for t in range(group):
            part_ref[t] = out_ref[lax.rem(place[1] + j, count) * group + t].T

    slices.wait()
    own_ref[...] = jnp.broadcast_to(jnp.sum(slices_ref[...], axis=0)[None], own_ref.shape)


def assemble_columns(front, incoming, place, slot_in, parts):
    rows, devices = front.shape[0], incoming.shape[0]
    _, height = lead_slices(devices)
    shapes = [(rows, TILE, TILE), (devices, height, TILE)]
    shapes += [(rows // parts, TILE, TILE)] * parts
    out_shape = [pltpu.HBM(shape, jnp.float32) for shape in shapes]
    return pl.pallas_call(
        columns_kernel,
        grid_spec=pltpu.PrefetchScalarGridSpec(
            num_scalar_prefetch=2,
            grid=(1,),
            in_specs=[pl.BlockSpec(memory_space=pltpu.HBM)] * 2,
            out_specs=[whole_spec(a) for a in out_shape],
            scratch_shapes=[
                pltpu.VMEM((TILE, TILE), jnp.float32),
                pltpu.VMEM((devices, height, TILE), jnp.float32),
                pltpu.SemaphoreType.DMA,
                pltpu.SemaphoreType.DMA,
            ],
        ),
        out_shape=out_shape,
        compiler_params=pltpu.CompilerParams(vmem_limit_bytes=VMEM),
        name="panel_columns",
    )(place, slot_in, front, incoming)


def row_panels_kernel(
    place, slot_in, t0, t1, t2, t3, lead_ref, diag_ref, pair_ref, out_ref, across_ref, order,
    starts, small_ref, tiles_ref, cursor,
):
    step = pl.program_id(0)
    cols = starts.shape[0] - 1
    my_row, my_col = place[0], place[1]
    group = t0.shape[0]
    height = group * TILE

    @pl.when(step == 0)
    def _():
        small_ref[0] = stacked(diag_ref[0])
        lead = jnp.concatenate(
            [jnp.concatenate([lead_ref[i, 0], lead_ref[i, 1]], axis=1) for i in range(2)], axis=0
        )
        lead = dot(deep(lead), small_ref[0])
        small_ref[1] = stacked(lead.T)
        small_ref[2] = stacked(diag_ref[1])
        across_ref[0] = deep(diag_ref[0].T)
        across_ref[1] = deep(lead)
        across_ref[2] = deep(diag_ref[1].T)

        @pl.loop(0, cols + 1)
        def _(b):
            starts[b] = 0

        @pl.loop(0, slot_in.shape[0])
        def _(s):
            @pl.when(slot_in[s] >= 0)
            def _():
                b = lax.rem(slot_in[s], cols)
                starts[b + 1] = starts[b + 1] + 1

        @pl.loop(0, cols)
        def _(b):
            cursor[b] = starts[b]
            starts[b + 1] = starts[b + 1] + starts[b]

        @pl.loop(0, slot_in.shape[0])
        def _(s):
            @pl.when(slot_in[s] >= 0)
            def _():
                b = lax.rem(slot_in[s], cols)
                i = cursor[b]
                order[2 * i] = s
                order[2 * i + 1] = lax.div(slot_in[s], cols)
                cursor[b] = i + 1


    for i, tile_ref in enumerate((t0, t1, t2, t3)):
        tiles_ref[jnp.bitwise_xor(my_col, i)] = tile_ref[...]
    columns = [tiles_ref[c].reshape(height, TILE) for c in range(4)]
    tile_row = lax.broadcasted_iota(jnp.int32, (height, PANEL), 0) // TILE
    first = jnp.logical_and(step == 0, tile_row == 0)

    def mask(panels_above, value):
        above = jnp.logical_and(first, my_row < 2 * panels_above)
        return jnp.where(above, 0.0, value) if panels_above else value

    one, two = two_panels(columns, small_ref, mask)
    for i, panel in enumerate((mask(1, one), mask(2, two))):
        for k, half in enumerate(halves(panel)):
            pair_ref[:, k * WIDTH + i * PANEL : k * WIDTH + (i + 1) * PANEL] = half
    pieces = (one[:, :TILE], one[:, TILE:], two[:, :TILE], two[:, TILE:])
    for c in range(4):

        @pl.when(my_col == c)
        def _():
            out_ref[:, 0, 0, 0] = pieces[c].reshape(group, TILE, TILE)


def row_panels(mine, others, lead, diag, place, slot_in, front):
    rows = front.shape[0]
    cols = front.shape[2]
    group = rows // 3
    height = group * TILE
    out_shape = [
        pltpu.HBM((rows * TILE, 2 * WIDTH), jnp.bfloat16),
        jax.ShapeDtypeStruct(front.shape, jnp.float32),
        jax.ShapeDtypeStruct((3, PANEL, 3 * PANEL), jnp.bfloat16),
        jax.ShapeDtypeStruct((2 * slot_in.shape[0],), jnp.int32),
        jax.ShapeDtypeStruct((cols + 1,), jnp.int32),
    ]
    strip = pl.BlockSpec((group, TILE, TILE), lambda i, *_: (i, 0, 0))
    return pl.pallas_call(
        row_panels_kernel,
        grid_spec=pltpu.PrefetchScalarGridSpec(
            num_scalar_prefetch=2,
            grid=(3,),
            in_specs=[strip] * 4 + [whole_spec(lead), whole_spec(diag)],
            out_specs=[
                pl.BlockSpec((height, 2 * WIDTH), lambda i, *_: (i, 0)),
                pl.BlockSpec((group, 1, 1, 1, TILE, TILE), lambda i, *_: (i, 0, 0, 0, 0, 0)),
                whole_spec(out_shape[2]),
                pl.BlockSpec(memory_space=pltpu.SMEM),
                pl.BlockSpec(memory_space=pltpu.SMEM),
            ],
            scratch_shapes=[
                pltpu.VMEM((3, 3 * PANEL, PANEL), jnp.bfloat16),
                pltpu.VMEM((4, group, TILE, TILE), jnp.float32),
                pltpu.SMEM((cols,), jnp.int32),
            ],
        ),
        out_shape=out_shape,
        compiler_params=pltpu.CompilerParams(vmem_limit_bytes=VMEM),
        name="row_panels",
    )(place, slot_in, mine, *others, lead, diag)


def trailing_kernel(
    first, n_held, halved, place, columns_table, places_table, order, starts, pair_ref, small_ref,
    *rest,
):
    piece_refs = rest[:n_held]
    front_ref, incoming_ref, _, out_ref, right_ref, taken, given, child_ref, *rest = rest[n_held:]
    take_sems, give_sems, child_sems, *joined = rest
    if halved:
        joined[0][:2] = piece_refs[0][...]
        joined[0][2:] = piece_refs[1][...]
        piece_refs = joined
    n_pieces = len(piece_refs)
    group = piece_refs[0].shape[1]
    count = n_pieces * group
    steps = (count + 1) // 2
    rows, cols = front_ref.shape[0], front_ref.shape[2]
    columns_base = place[0] * cols + first * group
    places_base = (place[0] * (cols // group) + first) * 4

    def columns_of(step):
        for j in range(2):
            index = jnp.minimum(2 * step, count - 2) + j
            b = columns_table[columns_base + index]
            wanted = b > 0
            if count % 2 and j == 0:
                wanted = jnp.logical_and(wanted, step < steps - 1)
            yield j, b, wanted

    def each_take(step, act):
        slot = lax.rem(step, 2)
        for j, b, wanted in columns_of(step):

            @pl.when(wanted)
            def _():
                act(
                    pltpu.make_async_copy(
                        front_ref.at[:, 0, b, 0], taken.at[slot, j], take_sems.at[slot, j]
                    )
                )

    def each_give(step, act):
        slot = lax.rem(step, 2)
        for j, b, wanted in columns_of(step):

            @pl.when(wanted)
            def _():
                act(
                    pltpu.make_async_copy(
                        given.at[slot, j], out_ref.at[:, 0, b, 0], give_sems.at[slot, j]
                    )
                )

    def each_child(step, act):
        for j, b, wanted in columns_of(step):

            @pl.when(wanted)
            def _():
                @pl.loop(starts[b], starts[b + 1])
                def _(i):
                    s = order[2 * i]
                    copy = pltpu.make_async_copy(
                        incoming_ref.at[s, pl.ds(0, TILE)], child_ref.at[s], child_sems.at[s]
                    )
                    act(copy, j, s, order[2 * i + 1])

    for step in range(min(steps, 2)):
        each_take(step, lambda copy: copy.start())
    for step in range(steps):
        each_child(step, lambda copy, *_: copy.start())

    tile_columns = [
        jnp.concatenate(
            [
                piece[places_table[places_base + 4 * p + c], t]
                for p, piece in enumerate(piece_refs)
                for t in range(group)
            ],
            axis=1,
        )
        for c in range(4)
    ]
    for i, panel in enumerate(two_panels_across(tile_columns, small_ref)):
        high, low = halves(panel)
        for k, half in enumerate((high, high, low)):
            right_ref[k * WIDTH + i * PANEL : k * WIDTH + (i + 1) * PANEL] = half

    @pl.loop(0, steps)
    def _(step):
        slot = lax.rem(step, 2)
        each_take(step, lambda copy: copy.wait())

        @pl.when(step >= 2)
        def _():
            each_give(step - 2, lambda copy: copy.wait())

        start = jnp.minimum(2 * step, count - 2)
        lanes = pl.ds(pl.multiple_of(start * TILE, TILE), 2 * TILE)
        update = dot(pair_ref[...], right_ref[: 2 * WIDTH, lanes])
        update = update + dot(pair_ref[:, :WIDTH], right_ref[2 * WIDTH :, lanes])
        for j in range(2):
            part = update[:, j * TILE : (j + 1) * TILE].reshape(rows, TILE, TILE)
            given[slot, j] = taken[slot, j] - part

        def add(copy, j, s, a):
            copy.wait()
            given[slot, j, a] = given[slot, j, a] + child_ref[s]

        each_child(step, add)
        each_give(step, lambda copy: copy.start())

        @pl.when(step + 2 < steps)
        def _():
            each_take(step + 2, lambda copy: copy.start())

    for step in range(max(steps - 2, 0), steps):
        each_give(step, lambda copy: copy.wait())


def trailing(front, pieces, first, place, tables, panels, incoming):
    rows = front.shape[0]
    pair, out, small, order, starts = panels
    group = pieces[0].shape[1]
    halved = pieces[0].shape[0] == 2
    count = group if halved else len(pieces) * group
    scalars = [place, *tables, order, starts]
    held = [pair, small, *pieces]
    distant = [front, incoming, out]
    spec = lambda space, n: [pl.BlockSpec(memory_space=space)] * n
    height = rows * TILE
    devices = incoming.shape[0]
    return pl.pallas_call(
        functools.partial(trailing_kernel, first, len(pieces), halved),
        in_specs=spec(pltpu.SMEM, 5) + spec(pltpu.VMEM, len(held)) + spec(pltpu.HBM, 3),
        out_specs=pl.BlockSpec(memory_space=pltpu.HBM),
        scratch_shapes=[
            pltpu.VMEM((3 * WIDTH, count * TILE), jnp.bfloat16),
            pltpu.VMEM((2, 2, rows, TILE, TILE), jnp.float32),
            pltpu.VMEM((2, 2, rows, TILE, TILE), jnp.float32),
            pltpu.VMEM((devices, TILE, TILE), jnp.float32),
            pltpu.SemaphoreType.DMA((2, 2)),
            pltpu.SemaphoreType.DMA((2, 2)),
            pltpu.SemaphoreType.DMA((devices,)),
        ]
        + [pltpu.VMEM((4, group, TILE, TILE), jnp.float32)] * halved,
        out_shape=jax.ShapeDtypeStruct(front.shape, jnp.float32),
        input_output_aliases={len(held) + 7: 0},
        compiler_params=pltpu.CompilerParams(vmem_limit_bytes=VMEM),
        cost_estimate=pl.CostEstimate(
            flops=8 * count * 2 * height * TILE * WIDTH,
            bytes_accessed=count * 2 * height * TILE * 4,
            transcendentals=0,
        ),
        name="trailing",
    )(*scalars, *held, *distant)


def body(front, child_tiles, tile_dest, tile_slot, tile_count, diag_inverses):
    n_row = lax.axis_size("row")
    n_col = lax.axis_size("col")
    my_row = lax.axis_index("row").astype(jnp.int32)
    my_col = lax.axis_index("col").astype(jnp.int32)
    rows_here, cols_here = (front.shape[0], front.shape[2])
    devices = n_row * n_col
    assert n_col == 4 and n_row % 4 == 0 and rows_here % 3 == 0
    owners = [r * n_col + c for r in (2, 3) for c in (0, 1)]
    place = jnp.stack([my_row, my_col, jnp.int32(cols_here), my_row * n_col + my_col])

    outgoing = pack(
        child_tiles, front, place, tile_dest[:, 0], tile_slot, tile_count, devices, owners
    )
    incoming = lax.all_to_all(outgoing, BOTH, split_axis=0, concat_axis=0, tiled=True)
    slot_in = lax.optimization_barrier(incoming[:, TILE, 0].astype(jnp.int32))

    ring = rows_here % n_col == 0
    mine, own, *parts = assemble_columns(front, incoming, place, slot_in, n_col if ring else 1)
    lead = lax.all_to_all(own, BOTH, split_axis=0, concat_axis=0, tiled=True)
    lead = lead[: lead_slices(devices)[0]].reshape(2, 2, TILE, TILE)

    def exchange(mine):
        near = lax.ppermute(mine, "col", [(c, c ^ 1) for c in range(n_col)])
        far = lax.ppermute(mine, "col", [(c, c ^ 2) for c in range(n_col)])
        return [near, far, lax.ppermute(far, "col", [(c, c ^ 1) for c in range(n_col)])]

    def own_panels(mine, lead):
        return row_panels(mine, exchange(mine), lead, diag_inverses, place, slot_in, front)

    sets = n_row // n_col
    circle = list(range(0, n_row, 2)) + list(range(n_row - 1, 0, -2))
    around = [0] + [sign * step for step in range(1, n_row // 2) for sign in (-1, 1)]
    shifts = around + [n_row // 2] if ring else list(range(sets))

    def described(row, shift):
        if not ring:
            return [a * sets + shift for a in range(rows_here)], list(range(n_col))
        origin = circle[(circle.index(row) + shift) % n_row]
        part, group = origin % n_col, rows_here // n_col
        columns = [(part * group + t) * sets + origin // n_col for t in range(group)]
        return columns, [(part - c) % n_col for c in range(n_col)]

    tables = [
        jnp.asarray(
            np.concatenate([described(row, shift)[k] for row in range(n_row) for shift in shifts]),
            jnp.int32,
        )
        for k in range(2)
    ]

    def updated(entries, panels, first):
        assert [shift for _, shift in entries] == shifts[first : first + len(entries)]
        pieces = [piece for piece, _ in entries]
        pieces = pieces[0] if isinstance(pieces[0], list) else pieces
        out = trailing(front, pieces, first, place, tables, panels, incoming)
        return [panels[0], out, *panels[2:]]

    first = 0
    if ring:
        arrived = []
        for j, part in enumerate(parts):
            pairs = [
                (r * n_col + c, ((r // n_col) * n_col + (c + j) % n_col) * n_col + r % n_col)
                for r in range(n_row)
                for c in range(n_col)
            ]
            arrived.append(lax.ppermute(part, BOTH, pairs))
        arrived, mine, lead = lax.optimization_barrier((arrived, mine, lead))
        piece = jnp.stack(arrived)
        up = [(circle[i], circle[(i + 1) % n_row]) for i in range(n_row)]
        down = [(b, a) for a, b in up]
        rounds = [[(piece, 0)]]
        panels = own_panels(mine, lead)
        ahead = behind = piece
        for step in range(1, n_row // 2):
            ahead = lax.ppermute(ahead, "row", up)
            behind = lax.ppermute(behind, "row", down)
            if step == 2:
                panels = updated([*rounds[0], rounds[1][0]], panels, 0)
                ahead, behind, panels = lax.optimization_barrier((ahead, behind, panels))
            rounds.append([(ahead, -step), (behind, step)])
        last = [lax.ppermute(ahead[:2], "row", up), lax.ppermute(behind[2:], "row", down)]
        late = [entry for entries in rounds for entry in entries][2:]
        rounds = [late[:2], late[2:3], *rounds[3:], [(last, n_row // 2)]]
        first = 2

    else:
        pairs = [
            (r * n_col + c, ((r // n_col) * n_col + c) * n_col + r % n_col)
            for r in range(n_row)
            for c in range(n_col)
        ]
        moved = lax.all_gather(lax.ppermute(parts[0], BOTH, pairs), "row", axis=0, tiled=False)
        rounds = [[(moved[h * n_col : (h + 1) * n_col], h)] for h in range(sets)]
        panels = own_panels(mine, lead)

    for entries in rounds:
        panels = updated(entries, panels, first)
        first += len(entries)
    return panels[1]


def solution(mesh):
    return jax.shard_map(
        body,
        mesh=mesh,
        in_specs=(
            P(None, "row", None, "col", None, None),
            P(BOTH, None, None),
            P(BOTH, None),
            P(BOTH),
            P(BOTH),
            P(),
        ),
        out_specs=P(None, "row", None, "col", None, None),
        check_vma=False,
    )
```

```python
import functools

import jax
import jax.numpy as jnp
import numpy as np
from jax import lax
from jax.experimental import pallas as pl
from jax.experimental.pallas import tpu as pltpu
from jax.sharding import PartitionSpec as P

TILE = 128
PANEL = 256
WIDTH = 2 * PANEL
NOTE = 8
VMEM = 46 * 1024 * 1024
BOTH = ("row", "col")


def halves(value):
    high = value.astype(jnp.bfloat16)
    low = (value - high.astype(jnp.float32)).astype(jnp.bfloat16)
    return high, low


def deep(value):
    high, low = halves(value)
    return jnp.concatenate([high, low, high], axis=1)


def stacked(value):
    high, low = halves(value)
    return jnp.concatenate([high, high, low], axis=0)


def dot(left, right):
    return jnp.dot(left, right, preferred_element_type=jnp.float32)


def two_panels(columns, small_ref, mask):
    one = mask(0, dot(deep(jnp.concatenate(columns[:2], axis=1)), small_ref[0]))
    field = jnp.concatenate(columns[2:], axis=1) - dot(deep(mask(1, one)), small_ref[1])
    return one, mask(1, dot(deep(field), small_ref[2]))


def two_panels_across(columns, small_ref):
    one = dot(small_ref[0], stacked(jnp.concatenate(columns[:2], axis=0)))
    field = jnp.concatenate(columns[2:], axis=0) - dot(small_ref[1], stacked(one))
    return one, dot(small_ref[2], stacked(field))


def whole_spec(array):
    rank = len(array.shape)
    return pl.BlockSpec(array.shape, lambda *_: (0,) * rank)


def lead_slices(devices):
    height = max(8, 4 * TILE // devices)
    return 4 * TILE // height, height


def pack_kernel(
    owners, place, dest, slot, count, child_ref, front_ref, out_ref, held_ref, notes_ref,
    lead_ref, tile_ref, in_sems, out_sems, sem, lead_sem,
):
    n_slices, height, _ = lead_ref.shape
    each = n_slices // 4
    live = jnp.minimum(count[0], child_ref.shape[0])

    def arrive(k):
        return pltpu.make_async_copy(child_ref.at[k], held_ref.at[k], in_sems.at[k])

    def leave(k):
        return pltpu.make_async_copy(
            held_ref.at[k], out_ref.at[dest[k], pl.ds(0, TILE)], out_sems.at[k]
        )

    own = pltpu.make_async_copy(front_ref.at[0, 0, 0, 0], tile_ref, sem)
    own.start()

    @pl.loop(0, live)
    def _(k):
        arrive(k).start()

    notes_ref[...] = jnp.full_like(notes_ref, -1.0)
    lead_ref[...] = jnp.zeros_like(lead_ref)
    own.wait()
    for i, owner in enumerate(owners):

        @pl.when(place[3] == owner)
        def _():
            lead_ref[i * each : (i + 1) * each] = tile_ref[...].reshape(each, height, TILE)

    @pl.loop(0, live)
    def _(k):
        notes_ref[dest[k]] = jnp.full(notes_ref.shape[1:], slot[k].astype(jnp.float32))
        arrive(k).wait()
        leave(k).start()
        for i, owner in enumerate(owners):

            @pl.when(jnp.logical_and(slot[k] == 0, dest[k] == owner))
            def _():
                span = pl.ds(i * each, each)
                lead_ref[span] = lead_ref[span] + held_ref[k].reshape(each, height, TILE)

    notes = pltpu.make_async_copy(notes_ref, out_ref.at[:, pl.ds(TILE, NOTE)], sem)
    notes.start()
    lead = pltpu.make_async_copy(
        lead_ref, out_ref.at[pl.ds(0, n_slices), pl.ds(TILE + NOTE, height)], lead_sem
    )
    lead.start()
    notes.wait()
    lead.wait()

    @pl.loop(0, live)
    def _(k):
        leave(k).wait()


def pack(child_tiles, front, place, dest, slot, count, devices, owners):
    slots = child_tiles.shape[0]
    n_slices, height = lead_slices(devices)
    hbm = pl.BlockSpec(memory_space=pltpu.HBM)
    return pl.pallas_call(
        functools.partial(pack_kernel, owners),
        in_specs=[pl.BlockSpec(memory_space=pltpu.SMEM)] * 4 + [hbm, hbm],
        out_specs=hbm,
        scratch_shapes=[
            pltpu.VMEM((slots, TILE, TILE), jnp.float32),
            pltpu.VMEM((devices, NOTE, TILE), jnp.float32),
            pltpu.VMEM((n_slices, height, TILE), jnp.float32),
            pltpu.VMEM((TILE, TILE), jnp.float32),
            pltpu.SemaphoreType.DMA((slots,)),
            pltpu.SemaphoreType.DMA((slots,)),
            pltpu.SemaphoreType.DMA,
            pltpu.SemaphoreType.DMA,
        ],
        out_shape=jax.ShapeDtypeStruct((devices, TILE + NOTE + height, TILE), jnp.float32),
        compiler_params=pltpu.CompilerParams(vmem_limit_bytes=62 * 1024 * 1024),
        name="pack",
    )(place, dest, slot, count, child_tiles, front)


def columns_kernel(place, slot_in, front_ref, incoming_ref, out_ref, own_ref, *rest):
    *parts, tile_ref, slices_ref, sem, slices_sem = rest
    cols = place[2]
    height = own_ref.shape[1]
    strip = pltpu.make_async_copy(front_ref.at[:, 0, 0, 0], out_ref, sem)
    strip.start()
    slices = pltpu.make_async_copy(
        incoming_ref.at[:, pl.ds(TILE + NOTE, height)], slices_ref, slices_sem
    )
    slices.start()
    strip.wait()

    @pl.loop(0, incoming_ref.shape[0])
    def _(s):
        slot = slot_in[s]

        @pl.when(jnp.logical_and(slot >= 0, lax.rem(slot, cols) == 0))
        def _():
            copy = pltpu.make_async_copy(incoming_ref.at[s, pl.ds(0, TILE)], tile_ref, sem)
            copy.start()
            copy.wait()
            row = lax.div(slot, cols)
            out_ref[row] = out_ref[row] + tile_ref[...]

    count = len(parts)
    for j, part_ref in enumerate(parts):
        group = part_ref.shape[0]
        for t in range(group):
            part_ref[t] = out_ref[lax.rem(place[1] + j, count) * group + t].T

    slices.wait()
    own_ref[...] = jnp.broadcast_to(jnp.sum(slices_ref[...], axis=0)[None], own_ref.shape)


def assemble_columns(front, incoming, place, slot_in, parts):
    rows, devices = front.shape[0], incoming.shape[0]
    _, height = lead_slices(devices)
    shapes = [(rows, TILE, TILE), (devices, height, TILE)]
    shapes += [(rows // parts, TILE, TILE)] * parts
    out_shape = [pltpu.HBM(shape, jnp.float32) for shape in shapes]
    return pl.pallas_call(
        columns_kernel,
        grid_spec=pltpu.PrefetchScalarGridSpec(
            num_scalar_prefetch=2,
            grid=(1,),
            in_specs=[pl.BlockSpec(memory_space=pltpu.HBM)] * 2,
            out_specs=[whole_spec(a) for a in out_shape],
            scratch_shapes=[
                pltpu.VMEM((TILE, TILE), jnp.float32),
                pltpu.VMEM((devices, height, TILE), jnp.float32),
                pltpu.SemaphoreType.DMA,
                pltpu.SemaphoreType.DMA,
            ],
        ),
        out_shape=out_shape,
        compiler_params=pltpu.CompilerParams(vmem_limit_bytes=VMEM),
        name="panel_columns",
    )(place, slot_in, front, incoming)


def square(tiles_ref):
    return jnp.concatenate(
        [jnp.concatenate([tiles_ref[i, 0], tiles_ref[i, 1]], axis=1) for i in range(2)], axis=0
    )


def piece_panels_kernel(rolled, place, t0, t1, t2, t3, lead_ref, diag_ref, out_ref, tiles_ref):
    group = t0.shape[0]
    for i, tile_ref in enumerate((t0, t1, t2, t3)):
        tiles_ref[i] = tile_ref[...]
    lead = dot(deep(square(lead_ref)), stacked(diag_ref[0]))
    small = [deep(diag_ref[0].T), deep(lead), deep(diag_ref[1].T)]
    columns = []
    for c in range(4):
        at = lax.rem(place[0] + 4 - c, 4) if rolled else c
        columns.append(jnp.concatenate([tiles_ref[at, t] for t in range(group)], axis=1))
    for i, panel in enumerate(two_panels_across(columns, small)):
        for j in range(2):
            for t in range(group):
                out_ref[2 * i + j, t] = panel[
                    j * TILE : (j + 1) * TILE, t * TILE : (t + 1) * TILE
                ]


def piece_panels(parts, lead, diag, place, rolled):
    shape = (4, *parts[0].shape)
    return pl.pallas_call(
        functools.partial(piece_panels_kernel, rolled),
        in_specs=[pl.BlockSpec(memory_space=pltpu.SMEM)]
        + [pl.BlockSpec(memory_space=pltpu.VMEM)] * 6,
        out_specs=pl.BlockSpec(memory_space=pltpu.VMEM),
        scratch_shapes=[pltpu.VMEM(shape, jnp.float32)],
        out_shape=jax.ShapeDtypeStruct(shape, jnp.float32),
        compiler_params=pltpu.CompilerParams(vmem_limit_bytes=VMEM),
        name="piece_panels",
    )(place, *parts, lead, diag)


def row_panels_kernel(
    place, slot_in, t0, t1, t2, t3, lead_ref, diag_ref, pair_ref, out_ref, order, starts,
    small_ref, tiles_ref, cursor,
):
    step = pl.program_id(0)
    cols = starts.shape[0] - 1
    my_row, my_col = place[0], place[1]
    group = t0.shape[0]
    height = group * TILE

    @pl.when(step == 0)
    def _():
        small_ref[0] = stacked(diag_ref[0])
        lead = dot(deep(square(lead_ref)), small_ref[0])
        small_ref[1] = stacked(lead.T)
        small_ref[2] = stacked(diag_ref[1])

        @pl.loop(0, cols + 1)
        def _(b):
            starts[b] = 0

        @pl.loop(0, slot_in.shape[0])
        def _(s):
            @pl.when(slot_in[s] >= 0)
            def _():
                b = lax.rem(slot_in[s], cols)
                starts[b + 1] = starts[b + 1] + 1

        @pl.loop(0, cols)
        def _(b):
            cursor[b] = starts[b]
            starts[b + 1] = starts[b + 1] + starts[b]

        @pl.loop(0, slot_in.shape[0])
        def _(s):
            @pl.when(slot_in[s] >= 0)
            def _():
                b = lax.rem(slot_in[s], cols)
                i = cursor[b]
                order[2 * i] = s
                order[2 * i + 1] = lax.div(slot_in[s], cols)
                cursor[b] = i + 1


    for i, tile_ref in enumerate((t0, t1, t2, t3)):
        tiles_ref[jnp.bitwise_xor(my_col, i)] = tile_ref[...]
    columns = [tiles_ref[c].reshape(height, TILE) for c in range(4)]
    tile_row = lax.broadcasted_iota(jnp.int32, (height, PANEL), 0) // TILE
    first = jnp.logical_and(step == 0, tile_row == 0)

    def mask(panels_above, value):
        above = jnp.logical_and(first, my_row < 2 * panels_above)
        return jnp.where(above, 0.0, value) if panels_above else value

    one, two = two_panels(columns, small_ref, mask)
    for i, panel in enumerate((mask(1, one), mask(2, two))):
        for k, half in enumerate(halves(panel)):
            pair_ref[:, k * WIDTH + i * PANEL : k * WIDTH + (i + 1) * PANEL] = half
    pieces = (one[:, :TILE], one[:, TILE:], two[:, :TILE], two[:, TILE:])
    for c in range(4):

        @pl.when(my_col == c)
        def _():
            out_ref[:, 0, 0, 0] = pieces[c].reshape(group, TILE, TILE)


def row_panels(mine, others, lead, diag, place, slot_in, front):
    rows = front.shape[0]
    cols = front.shape[2]
    group = rows // 3
    height = group * TILE
    out_shape = [
        pltpu.HBM((rows * TILE, 2 * WIDTH), jnp.bfloat16),
        jax.ShapeDtypeStruct(front.shape, jnp.float32),
        jax.ShapeDtypeStruct((2 * slot_in.shape[0],), jnp.int32),
        jax.ShapeDtypeStruct((cols + 1,), jnp.int32),
    ]
    strip = pl.BlockSpec((group, TILE, TILE), lambda i, *_: (i, 0, 0))
    return pl.pallas_call(
        row_panels_kernel,
        grid_spec=pltpu.PrefetchScalarGridSpec(
            num_scalar_prefetch=2,
            grid=(3,),
            in_specs=[strip] * 4 + [whole_spec(lead), whole_spec(diag)],
            out_specs=[
                pl.BlockSpec((height, 2 * WIDTH), lambda i, *_: (i, 0)),
                pl.BlockSpec((group, 1, 1, 1, TILE, TILE), lambda i, *_: (i, 0, 0, 0, 0, 0)),
                pl.BlockSpec(memory_space=pltpu.SMEM),
                pl.BlockSpec(memory_space=pltpu.SMEM),
            ],
            scratch_shapes=[
                pltpu.VMEM((3, 3 * PANEL, PANEL), jnp.bfloat16),
                pltpu.VMEM((4, group, TILE, TILE), jnp.float32),
                pltpu.SMEM((cols,), jnp.int32),
            ],
        ),
        out_shape=out_shape,
        compiler_params=pltpu.CompilerParams(vmem_limit_bytes=VMEM),
        name="row_panels",
    )(place, slot_in, mine, *others, lead, diag)


def trailing_kernel(
    first, n_held, halved, place, columns_table, order, starts, pair_ref, *rest
):
    piece_refs = rest[:n_held]
    front_ref, incoming_ref, _, out_ref, right_ref, taken, given, child_ref, *rest = rest[n_held:]
    take_sems, give_sems, child_sems, *joined = rest
    if halved:
        joined[0][:2] = piece_refs[0][...]
        joined[0][2:] = piece_refs[1][...]
        piece_refs = joined
    n_pieces = len(piece_refs)
    group = piece_refs[0].shape[1]
    count = n_pieces * group
    steps = (count + 1) // 2
    rows, cols = front_ref.shape[0], front_ref.shape[2]
    columns_base = place[0] * cols + first * group

    def columns_of(step):
        for j in range(2):
            index = jnp.minimum(2 * step, count - 2) + j
            b = columns_table[columns_base + index]
            wanted = b > 0
            if count % 2 and j == 0:
                wanted = jnp.logical_and(wanted, step < steps - 1)
            yield j, b, wanted

    def each_take(step, act):
        slot = lax.rem(step, 2)
        for j, b, wanted in columns_of(step):

            @pl.when(wanted)
            def _():
                act(
                    pltpu.make_async_copy(
                        front_ref.at[:, 0, b, 0], taken.at[slot, j], take_sems.at[slot, j]
                    )
                )

    def each_give(step, act):
        slot = lax.rem(step, 2)
        for j, b, wanted in columns_of(step):

            @pl.when(wanted)
            def _():
                act(
                    pltpu.make_async_copy(
                        given.at[slot, j], out_ref.at[:, 0, b, 0], give_sems.at[slot, j]
                    )
                )

    def each_child(step, act):
        for j, b, wanted in columns_of(step):

            @pl.when(wanted)
            def _():
                @pl.loop(starts[b], starts[b + 1])
                def _(i):
                    s = order[2 * i]
                    copy = pltpu.make_async_copy(
                        incoming_ref.at[s, pl.ds(0, TILE)], child_ref.at[s], child_sems.at[s]
                    )
                    act(copy, j, s, order[2 * i + 1])

    for step in range(min(steps, 2)):
        each_take(step, lambda copy: copy.start())
    for step in range(steps):
        each_child(step, lambda copy, *_: copy.start())

    for c in range(4):
        tiles = [piece[c, t] for piece in piece_refs for t in range(group)]
        high, low = halves(jnp.concatenate(tiles, axis=1))
        for k, half in enumerate((high, high, low)):
            right_ref[k * WIDTH + c * TILE : k * WIDTH + (c + 1) * TILE] = half

    @pl.loop(0, steps)
    def _(step):
        slot = lax.rem(step, 2)
        each_take(step, lambda copy: copy.wait())

        @pl.when(step >= 2)
        def _():
            each_give(step - 2, lambda copy: copy.wait())

        start = jnp.minimum(2 * step, count - 2)
        lanes = pl.ds(pl.multiple_of(start * TILE, TILE), 2 * TILE)
        update = dot(pair_ref[...], right_ref[: 2 * WIDTH, lanes])
        update = update + dot(pair_ref[:, :WIDTH], right_ref[2 * WIDTH :, lanes])
        for j in range(2):
            part = update[:, j * TILE : (j + 1) * TILE].reshape(rows, TILE, TILE)
            given[slot, j] = taken[slot, j] - part

        def add(copy, j, s, a):
            copy.wait()
            given[slot, j, a] = given[slot, j, a] + child_ref[s]

        each_child(step, add)
        each_give(step, lambda copy: copy.start())

        @pl.when(step + 2 < steps)
        def _():
            each_take(step + 2, lambda copy: copy.start())

    for step in range(max(steps - 2, 0), steps):
        each_give(step, lambda copy: copy.wait())


def trailing(front, pieces, first, place, table, panels, incoming):
    rows = front.shape[0]
    pair, out, order, starts = panels
    group = pieces[0].shape[1]
    halved = pieces[0].shape[0] == 2
    count = group if halved else len(pieces) * group
    scalars = [place, table, order, starts]
    held = [pair, *pieces]
    distant = [front, incoming, out]
    spec = lambda space, n: [pl.BlockSpec(memory_space=space)] * n
    height = rows * TILE
    devices = incoming.shape[0]
    return pl.pallas_call(
        functools.partial(trailing_kernel, first, len(pieces), halved),
        in_specs=spec(pltpu.SMEM, 4) + spec(pltpu.VMEM, len(held)) + spec(pltpu.HBM, 3),
        out_specs=pl.BlockSpec(memory_space=pltpu.HBM),
        scratch_shapes=[
            pltpu.VMEM((3 * WIDTH, count * TILE), jnp.bfloat16),
            pltpu.VMEM((2, 2, rows, TILE, TILE), jnp.float32),
            pltpu.VMEM((2, 2, rows, TILE, TILE), jnp.float32),
            pltpu.VMEM((devices, TILE, TILE), jnp.float32),
            pltpu.SemaphoreType.DMA((2, 2)),
            pltpu.SemaphoreType.DMA((2, 2)),
            pltpu.SemaphoreType.DMA((devices,)),
        ]
        + [pltpu.VMEM((4, group, TILE, TILE), jnp.float32)] * halved,
        out_shape=jax.ShapeDtypeStruct(front.shape, jnp.float32),
        input_output_aliases={len(held) + 6: 0},
        compiler_params=pltpu.CompilerParams(vmem_limit_bytes=VMEM),
        cost_estimate=pl.CostEstimate(
            flops=8 * count * 2 * height * TILE * WIDTH,
            bytes_accessed=count * 2 * height * TILE * 4,
            transcendentals=0,
        ),
        name="trailing",
    )(*scalars, *held, *distant)


def body(front, child_tiles, tile_dest, tile_slot, tile_count, diag_inverses):
    n_row = lax.axis_size("row")
    n_col = lax.axis_size("col")
    my_row = lax.axis_index("row").astype(jnp.int32)
    my_col = lax.axis_index("col").astype(jnp.int32)
    rows_here, cols_here = (front.shape[0], front.shape[2])
    devices = n_row * n_col
    assert n_col == 4 and n_row % 4 == 0 and rows_here % 3 == 0
    owners = [r * n_col + c for r in (2, 3) for c in (0, 1)]
    place = jnp.stack([my_row, my_col, jnp.int32(cols_here), my_row * n_col + my_col])

    outgoing = pack(
        child_tiles, front, place, tile_dest[:, 0], tile_slot, tile_count, devices, owners
    )
    incoming = lax.all_to_all(outgoing, BOTH, split_axis=0, concat_axis=0, tiled=True)
    slot_in = lax.optimization_barrier(incoming[:, TILE, 0].astype(jnp.int32))

    ring = rows_here % n_col == 0
    mine, own, *parts = assemble_columns(front, incoming, place, slot_in, n_col if ring else 1)
    lead = lax.all_to_all(own, BOTH, split_axis=0, concat_axis=0, tiled=True)
    lead = lead[: lead_slices(devices)[0]].reshape(2, 2, TILE, TILE)

    def exchange(mine):
        near = lax.ppermute(mine, "col", [(c, c ^ 1) for c in range(n_col)])
        far = lax.ppermute(mine, "col", [(c, c ^ 2) for c in range(n_col)])
        return [near, far, lax.ppermute(far, "col", [(c, c ^ 1) for c in range(n_col)])]

    def own_panels(mine, lead):
        return row_panels(mine, exchange(mine), lead, diag_inverses, place, slot_in, front)

    sets = n_row // n_col
    circle = list(range(0, n_row, 2)) + list(range(n_row - 1, 0, -2))
    around = [0] + [sign * step for step in range(1, n_row // 2) for sign in (-1, 1)]
    shifts = around + [n_row // 2] if ring else list(range(sets))

    def described(row, shift):
        if not ring:
            return [a * sets + shift for a in range(rows_here)]
        origin = circle[(circle.index(row) + shift) % n_row]
        part, group = origin % n_col, rows_here // n_col
        return [(part * group + t) * sets + origin // n_col for t in range(group)]

    table = np.concatenate([described(row, shift) for row in range(n_row) for shift in shifts])
    table = jnp.asarray(table, jnp.int32)

    def updated(entries, panels, first):
        assert [shift for _, shift in entries] == shifts[first : first + len(entries)]
        pieces = [piece for piece, _ in entries]
        pieces = pieces[0] if isinstance(pieces[0], list) else pieces
        out = trailing(front, pieces, first, place, table, panels, incoming)
        return [panels[0], out, *panels[2:]]

    first = 0
    if ring:
        arrived = []
        for j, part in enumerate(parts):
            pairs = [
                (r * n_col + c, ((r // n_col) * n_col + (c + j) % n_col) * n_col + r % n_col)
                for r in range(n_row)
                for c in range(n_col)
            ]
            arrived.append(lax.ppermute(part, BOTH, pairs))
        arrived, mine, lead = lax.optimization_barrier((arrived, mine, lead))
        piece = piece_panels(arrived, lead, diag_inverses, place, True)
        up = [(circle[i], circle[(i + 1) % n_row]) for i in range(n_row)]
        down = [(b, a) for a, b in up]
        rounds = [[(piece, 0)]]
        panels = own_panels(mine, lead)
        ahead = behind = piece
        for step in range(1, n_row // 2):
            ahead = lax.ppermute(ahead, "row", up)
            behind = lax.ppermute(behind, "row", down)
            if step == 2:
                panels = updated([*rounds[0], rounds[1][0]], panels, 0)
                ahead, behind, panels = lax.optimization_barrier((ahead, behind, panels))
            rounds.append([(ahead, -step), (behind, step)])
        last = [lax.ppermute(ahead[:2], "row", up), lax.ppermute(behind[2:], "row", down)]
        late = [entry for entries in rounds for entry in entries][2:]
        rounds = [late[:2], late[2:3], *rounds[3:], [(last, n_row // 2)]]
        first = 2

    else:
        pairs = [
            (r * n_col + c, ((r // n_col) * n_col + c) * n_col + r % n_col)
            for r in range(n_row)
            for c in range(n_col)
        ]
        moved = lax.all_gather(lax.ppermute(parts[0], BOTH, pairs), "row", axis=0, tiled=False)
        whole = [[moved[h * n_col + c] for c in range(n_col)] for h in range(sets)]
        rounds = [
            [(piece_panels(raw, lead, diag_inverses, place, False), h)]
            for h, raw in enumerate(whole)
        ]
        panels = own_panels(mine, lead)

    for entries in rounds:
        panels = updated(entries, panels, first)
        first += len(entries)
    return panels[1]


def solution(mesh):
    return jax.shard_map(
        body,
        mesh=mesh,
        in_specs=(
            P(None, "row", None, "col", None, None),
            P(BOTH, None, None),
            P(BOTH, None),
            P(BOTH),
            P(BOTH),
            P(),
        ),
        out_specs=P(None, "row", None, "col", None, None),
        check_vma=False,
    )
```

```python
import functools

import jax
import jax.numpy as jnp
import numpy as np
from jax import lax
from jax.experimental import pallas as pl
from jax.experimental.pallas import tpu as pltpu
from jax.sharding import PartitionSpec as P

TILE = 128
PANEL = 256
WIDTH = 2 * PANEL
NOTE = 8
VMEM = 46 * 1024 * 1024
BOTH = ("row", "col")


def halves(value):
    high = value.astype(jnp.bfloat16)
    low = (value - high.astype(jnp.float32)).astype(jnp.bfloat16)
    return high, low


def deep(value):
    high, low = halves(value)
    return jnp.concatenate([high, low, high], axis=1)


def stacked(value):
    high, low = halves(value)
    return jnp.concatenate([high, high, low], axis=0)


def dot(left, right):
    return jnp.dot(left, right, preferred_element_type=jnp.float32)


def two_panels(columns, small_ref, mask):
    one = mask(0, dot(deep(jnp.concatenate(columns[:2], axis=1)), small_ref[0]))
    field = jnp.concatenate(columns[2:], axis=1) - dot(deep(mask(1, one)), small_ref[1])
    return one, mask(1, dot(deep(field), small_ref[2]))


def two_panels_across(columns, small_ref):
    one = dot(small_ref[0], stacked(jnp.concatenate(columns[:2], axis=0)))
    field = jnp.concatenate(columns[2:], axis=0) - dot(small_ref[1], stacked(one))
    return one, dot(small_ref[2], stacked(field))


def whole_spec(array):
    rank = len(array.shape)
    return pl.BlockSpec(array.shape, lambda *_: (0,) * rank)


def lead_slices(devices):
    height = max(8, 4 * TILE // devices)
    return 4 * TILE // height, height


def pack_kernel(
    owners, place, dest, slot, count, child_ref, front_ref, out_ref, held_ref, notes_ref,
    lead_ref, tile_ref, in_sems, out_sems, sem, lead_sem,
):
    n_slices, height, _ = lead_ref.shape
    each = n_slices // 4
    live = jnp.minimum(count[0], child_ref.shape[0])

    def arrive(k):
        return pltpu.make_async_copy(child_ref.at[k], held_ref.at[k], in_sems.at[k])

    def leave(k):
        return pltpu.make_async_copy(
            held_ref.at[k], out_ref.at[dest[k], pl.ds(0, TILE)], out_sems.at[k]
        )

    own = pltpu.make_async_copy(front_ref.at[0, 0, 0, 0], tile_ref, sem)
    own.start()

    @pl.loop(0, live)
    def _(k):
        arrive(k).start()

    notes_ref[...] = jnp.full_like(notes_ref, -1.0)
    lead_ref[...] = jnp.zeros_like(lead_ref)
    own.wait()
    for i, owner in enumerate(owners):

        @pl.when(place[3] == owner)
        def _():
            lead_ref[i * each : (i + 1) * each] = tile_ref[...].reshape(each, height, TILE)

    @pl.loop(0, live)
    def _(k):
        notes_ref[dest[k]] = jnp.full(notes_ref.shape[1:], slot[k].astype(jnp.float32))
        arrive(k).wait()
        leave(k).start()
        for i, owner in enumerate(owners):

            @pl.when(jnp.logical_and(slot[k] == 0, dest[k] == owner))
            def _():
                span = pl.ds(i * each, each)
                lead_ref[span] = lead_ref[span] + held_ref[k].reshape(each, height, TILE)

    notes = pltpu.make_async_copy(notes_ref, out_ref.at[:, pl.ds(TILE, NOTE)], sem)
    notes.start()
    lead = pltpu.make_async_copy(
        lead_ref, out_ref.at[pl.ds(0, n_slices), pl.ds(TILE + NOTE, height)], lead_sem
    )
    lead.start()
    notes.wait()
    lead.wait()

    @pl.loop(0, live)
    def _(k):
        leave(k).wait()


def pack(child_tiles, front, place, dest, slot, count, devices, owners):
    slots = child_tiles.shape[0]
    n_slices, height = lead_slices(devices)
    hbm = pl.BlockSpec(memory_space=pltpu.HBM)
    return pl.pallas_call(
        functools.partial(pack_kernel, owners),
        in_specs=[pl.BlockSpec(memory_space=pltpu.SMEM)] * 4 + [hbm, hbm],
        out_specs=hbm,
        scratch_shapes=[
            pltpu.VMEM((slots, TILE, TILE), jnp.float32),
            pltpu.VMEM((devices, NOTE, TILE), jnp.float32),
            pltpu.VMEM((n_slices, height, TILE), jnp.float32),
            pltpu.VMEM((TILE, TILE), jnp.float32),
            pltpu.SemaphoreType.DMA((slots,)),
            pltpu.SemaphoreType.DMA((slots,)),
            pltpu.SemaphoreType.DMA,
            pltpu.SemaphoreType.DMA,
        ],
        out_shape=jax.ShapeDtypeStruct((devices, TILE + NOTE + height, TILE), jnp.float32),
        compiler_params=pltpu.CompilerParams(vmem_limit_bytes=62 * 1024 * 1024),
        name="pack",
    )(place, dest, slot, count, child_tiles, front)


def columns_kernel(place, slot_in, front_ref, incoming_ref, out_ref, own_ref, *rest):
    *parts, tile_ref, slices_ref, sem, slices_sem = rest
    cols = place[2]
    height = own_ref.shape[1]
    strip = pltpu.make_async_copy(front_ref.at[:, 0, 0, 0], out_ref, sem)
    strip.start()
    slices = pltpu.make_async_copy(
        incoming_ref.at[:, pl.ds(TILE + NOTE, height)], slices_ref, slices_sem
    )
    slices.start()
    strip.wait()

    @pl.loop(0, incoming_ref.shape[0])
    def _(s):
        slot = slot_in[s]

        @pl.when(jnp.logical_and(slot >= 0, lax.rem(slot, cols) == 0))
        def _():
            copy = pltpu.make_async_copy(incoming_ref.at[s, pl.ds(0, TILE)], tile_ref, sem)
            copy.start()
            copy.wait()
            row = lax.div(slot, cols)
            out_ref[row] = out_ref[row] + tile_ref[...]

    count = len(parts)
    for j, part_ref in enumerate(parts):
        group = part_ref.shape[0]
        for t in range(group):
            part_ref[t] = out_ref[lax.rem(place[1] + j, count) * group + t].T

    slices.wait()
    own_ref[...] = jnp.broadcast_to(jnp.sum(slices_ref[...], axis=0)[None], own_ref.shape)


def assemble_columns(front, incoming, place, slot_in, parts):
    rows, devices = front.shape[0], incoming.shape[0]
    _, height = lead_slices(devices)
    shapes = [(rows, TILE, TILE), (devices, height, TILE)]
    shapes += [(rows // parts, TILE, TILE)] * parts
    out_shape = [pltpu.HBM(shape, jnp.float32) for shape in shapes]
    return pl.pallas_call(
        columns_kernel,
        grid_spec=pltpu.PrefetchScalarGridSpec(
            num_scalar_prefetch=2,
            grid=(1,),
            in_specs=[pl.BlockSpec(memory_space=pltpu.HBM)] * 2,
            out_specs=[whole_spec(a) for a in out_shape],
            scratch_shapes=[
                pltpu.VMEM((TILE, TILE), jnp.float32),
                pltpu.VMEM((devices, height, TILE), jnp.float32),
                pltpu.SemaphoreType.DMA,
                pltpu.SemaphoreType.DMA,
            ],
        ),
        out_shape=out_shape,
        compiler_params=pltpu.CompilerParams(vmem_limit_bytes=VMEM),
        name="panel_columns",
    )(place, slot_in, front, incoming)


def square(tiles_ref):
    return jnp.concatenate(
        [jnp.concatenate([tiles_ref[i, 0], tiles_ref[i, 1]], axis=1) for i in range(2)], axis=0
    )


def piece_panels_kernel(rolled, place, tiles_ref, lead_ref, diag_ref, out_ref):
    group = tiles_ref.shape[1]
    lead = dot(deep(square(lead_ref)), stacked(diag_ref[0]))
    small = [deep(diag_ref[0].T), deep(lead), deep(diag_ref[1].T)]
    columns = []
    for c in range(4):
        at = lax.rem(place[0] + 4 - c, 4) if rolled else c
        columns.append(jnp.concatenate([tiles_ref[at, t] for t in range(group)], axis=1))
    for i, panel in enumerate(two_panels_across(columns, small)):
        for j in range(2):
            for t in range(group):
                out_ref[2 * i + j, t] = panel[
                    j * TILE : (j + 1) * TILE, t * TILE : (t + 1) * TILE
                ]


def piece_panels(piece, lead, diag, place, rolled):
    return pl.pallas_call(
        functools.partial(piece_panels_kernel, rolled),
        in_specs=[pl.BlockSpec(memory_space=pltpu.SMEM)]
        + [pl.BlockSpec(memory_space=pltpu.VMEM)] * 3,
        out_specs=pl.BlockSpec(memory_space=pltpu.VMEM),
        out_shape=jax.ShapeDtypeStruct(piece.shape, jnp.float32),
        compiler_params=pltpu.CompilerParams(vmem_limit_bytes=VMEM),
        name="piece_panels",
    )(place, piece, lead, diag)


def row_panels_kernel(
    place, slot_in, t0, t1, t2, t3, lead_ref, diag_ref, pair_ref, out_ref, order, starts,
    small_ref, tiles_ref, cursor,
):
    step = pl.program_id(0)
    cols = starts.shape[0] - 1
    my_row, my_col = place[0], place[1]
    group = t0.shape[0]
    height = group * TILE

    @pl.when(step == 0)
    def _():
        small_ref[0] = stacked(diag_ref[0])
        lead = dot(deep(square(lead_ref)), small_ref[0])
        small_ref[1] = stacked(lead.T)
        small_ref[2] = stacked(diag_ref[1])

        @pl.loop(0, cols + 1)
        def _(b):
            starts[b] = 0

        @pl.loop(0, slot_in.shape[0])
        def _(s):
            @pl.when(slot_in[s] >= 0)
            def _():
                b = lax.rem(slot_in[s], cols)
                starts[b + 1] = starts[b + 1] + 1

        @pl.loop(0, cols)
        def _(b):
            cursor[b] = starts[b]
            starts[b + 1] = starts[b + 1] + starts[b]

        @pl.loop(0, slot_in.shape[0])
        def _(s):
            @pl.when(slot_in[s] >= 0)
            def _():
                b = lax.rem(slot_in[s], cols)
                i = cursor[b]
                order[2 * i] = s
                order[2 * i + 1] = lax.div(slot_in[s], cols)
                cursor[b] = i + 1


    for i, tile_ref in enumerate((t0, t1, t2, t3)):
        tiles_ref[jnp.bitwise_xor(my_col, i)] = tile_ref[...]
    columns = [tiles_ref[c].reshape(height, TILE) for c in range(4)]
    tile_row = lax.broadcasted_iota(jnp.int32, (height, PANEL), 0) // TILE
    first = jnp.logical_and(step == 0, tile_row == 0)

    def mask(panels_above, value):
        above = jnp.logical_and(first, my_row < 2 * panels_above)
        return jnp.where(above, 0.0, value) if panels_above else value

    one, two = two_panels(columns, small_ref, mask)
    for i, panel in enumerate((mask(1, one), mask(2, two))):
        for k, half in enumerate(halves(panel)):
            pair_ref[:, k * WIDTH + i * PANEL : k * WIDTH + (i + 1) * PANEL] = half
    pieces = (one[:, :TILE], one[:, TILE:], two[:, :TILE], two[:, TILE:])
    for c in range(4):

        @pl.when(my_col == c)
        def _():
            out_ref[:, 0, 0, 0] = pieces[c].reshape(group, TILE, TILE)


def row_panels(mine, others, lead, diag, place, slot_in, front):
    rows = front.shape[0]
    cols = front.shape[2]
    group = rows // 3
    height = group * TILE
    out_shape = [
        pltpu.HBM((rows * TILE, 2 * WIDTH), jnp.bfloat16),
        jax.ShapeDtypeStruct(front.shape, jnp.float32),
        jax.ShapeDtypeStruct((2 * slot_in.shape[0],), jnp.int32),
        jax.ShapeDtypeStruct((cols + 1,), jnp.int32),
    ]
    strip = pl.BlockSpec((group, TILE, TILE), lambda i, *_: (i, 0, 0))
    return pl.pallas_call(
        row_panels_kernel,
        grid_spec=pltpu.PrefetchScalarGridSpec(
            num_scalar_prefetch=2,
            grid=(3,),
            in_specs=[strip] * 4 + [whole_spec(lead), whole_spec(diag)],
            out_specs=[
                pl.BlockSpec((height, 2 * WIDTH), lambda i, *_: (i, 0)),
                pl.BlockSpec((group, 1, 1, 1, TILE, TILE), lambda i, *_: (i, 0, 0, 0, 0, 0)),
                pl.BlockSpec(memory_space=pltpu.SMEM),
                pl.BlockSpec(memory_space=pltpu.SMEM),
            ],
            scratch_shapes=[
                pltpu.VMEM((3, 3 * PANEL, PANEL), jnp.bfloat16),
                pltpu.VMEM((4, group, TILE, TILE), jnp.float32),
                pltpu.SMEM((cols,), jnp.int32),
            ],
        ),
        out_shape=out_shape,
        compiler_params=pltpu.CompilerParams(vmem_limit_bytes=VMEM),
        name="row_panels",
    )(place, slot_in, mine, *others, lead, diag)


def trailing_kernel(
    first, n_held, halved, place, columns_table, order, starts, pair_ref, *rest
):
    piece_refs = rest[:n_held]
    front_ref, incoming_ref, _, out_ref, right_ref, taken, given, child_ref, *rest = rest[n_held:]
    take_sems, give_sems, child_sems, *joined = rest
    if halved:
        joined[0][:2] = piece_refs[0][...]
        joined[0][2:] = piece_refs[1][...]
        piece_refs = joined
    n_pieces = len(piece_refs)
    group = piece_refs[0].shape[1]
    count = n_pieces * group
    steps = (count + 1) // 2
    rows, cols = front_ref.shape[0], front_ref.shape[2]
    columns_base = place[0] * cols + first * group

    def columns_of(step):
        for j in range(2):
            index = jnp.minimum(2 * step, count - 2) + j
            b = columns_table[columns_base + index]
            wanted = b > 0
            if count % 2 and j == 0:
                wanted = jnp.logical_and(wanted, step < steps - 1)
            yield j, b, wanted

    def each_take(step, act):
        slot = lax.rem(step, 2)
        for j, b, wanted in columns_of(step):

            @pl.when(wanted)
            def _():
                act(
                    pltpu.make_async_copy(
                        front_ref.at[:, 0, b, 0], taken.at[slot, j], take_sems.at[slot, j]
                    )
                )

    def each_give(step, act):
        slot = lax.rem(step, 2)
        for j, b, wanted in columns_of(step):

            @pl.when(wanted)
            def _():
                act(
                    pltpu.make_async_copy(
                        given.at[slot, j], out_ref.at[:, 0, b, 0], give_sems.at[slot, j]
                    )
                )

    def each_child(step, act):
        for j, b, wanted in columns_of(step):

            @pl.when(wanted)
            def _():
                @pl.loop(starts[b], starts[b + 1])
                def _(i):
                    s = order[2 * i]
                    copy = pltpu.make_async_copy(
                        incoming_ref.at[s, pl.ds(0, TILE)], child_ref.at[s], child_sems.at[s]
                    )
                    act(copy, j, s, order[2 * i + 1])

    for step in range(min(steps, 2)):
        each_take(step, lambda copy: copy.start())
    for step in range(steps):
        each_child(step, lambda copy, *_: copy.start())

    for c in range(4):
        tiles = [piece[c, t] for piece in piece_refs for t in range(group)]
        high, low = halves(jnp.concatenate(tiles, axis=1))
        for k, half in enumerate((high, high, low)):
            right_ref[k * WIDTH + c * TILE : k * WIDTH + (c + 1) * TILE] = half

    @pl.loop(0, steps)
    def _(step):
        slot = lax.rem(step, 2)
        each_take(step, lambda copy: copy.wait())

        @pl.when(step >= 2)
        def _():
            each_give(step - 2, lambda copy: copy.wait())

        start = jnp.minimum(2 * step, count - 2)
        lanes = pl.ds(pl.multiple_of(start * TILE, TILE), 2 * TILE)
        update = dot(pair_ref[...], right_ref[: 2 * WIDTH, lanes])
        update = update + dot(pair_ref[:, :WIDTH], right_ref[2 * WIDTH :, lanes])
        for j in range(2):
            part = update[:, j * TILE : (j + 1) * TILE].reshape(rows, TILE, TILE)
            given[slot, j] = taken[slot, j] - part

        def add(copy, j, s, a):
            copy.wait()
            given[slot, j, a] = given[slot, j, a] + child_ref[s]

        each_child(step, add)
        each_give(step, lambda copy: copy.start())

        @pl.when(step + 2 < steps)
        def _():
            each_take(step + 2, lambda copy: copy.start())

    for step in range(max(steps - 2, 0), steps):
        each_give(step, lambda copy: copy.wait())


def trailing(front, pieces, first, place, table, panels, incoming):
    rows = front.shape[0]
    pair, out, order, starts = panels
    group = pieces[0].shape[1]
    halved = pieces[0].shape[0] == 2
    count = group if halved else len(pieces) * group
    scalars = [place, table, order, starts]
    held = [pair, *pieces]
    distant = [front, incoming, out]
    spec = lambda space, n: [pl.BlockSpec(memory_space=space)] * n
    height = rows * TILE
    devices = incoming.shape[0]
    return pl.pallas_call(
        functools.partial(trailing_kernel, first, len(pieces), halved),
        in_specs=spec(pltpu.SMEM, 4) + spec(pltpu.VMEM, len(held)) + spec(pltpu.HBM, 3),
        out_specs=pl.BlockSpec(memory_space=pltpu.HBM),
        scratch_shapes=[
            pltpu.VMEM((3 * WIDTH, count * TILE), jnp.bfloat16),
            pltpu.VMEM((2, 2, rows, TILE, TILE), jnp.float32),
            pltpu.VMEM((2, 2, rows, TILE, TILE), jnp.float32),
            pltpu.VMEM((devices, TILE, TILE), jnp.float32),
            pltpu.SemaphoreType.DMA((2, 2)),
            pltpu.SemaphoreType.DMA((2, 2)),
            pltpu.SemaphoreType.DMA((devices,)),
        ]
        + [pltpu.VMEM((4, group, TILE, TILE), jnp.float32)] * halved,
        out_shape=jax.ShapeDtypeStruct(front.shape, jnp.float32),
        input_output_aliases={len(held) + 6: 0},
        compiler_params=pltpu.CompilerParams(vmem_limit_bytes=VMEM),
        cost_estimate=pl.CostEstimate(
            flops=8 * count * 2 * height * TILE * WIDTH,
            bytes_accessed=count * 2 * height * TILE * 4,
            transcendentals=0,
        ),
        name="trailing",
    )(*scalars, *held, *distant)


def body(front, child_tiles, tile_dest, tile_slot, tile_count, diag_inverses):
    n_row = lax.axis_size("row")
    n_col = lax.axis_size("col")
    my_row = lax.axis_index("row").astype(jnp.int32)
    my_col = lax.axis_index("col").astype(jnp.int32)
    rows_here, cols_here = (front.shape[0], front.shape[2])
    devices = n_row * n_col
    assert n_col == 4 and n_row % 4 == 0 and rows_here % 3 == 0
    owners = [r * n_col + c for r in (2, 3) for c in (0, 1)]
    place = jnp.stack([my_row, my_col, jnp.int32(cols_here), my_row * n_col + my_col])

    outgoing = pack(
        child_tiles, front, place, tile_dest[:, 0], tile_slot, tile_count, devices, owners
    )
    incoming = lax.all_to_all(outgoing, BOTH, split_axis=0, concat_axis=0, tiled=True)
    slot_in = lax.optimization_barrier(incoming[:, TILE, 0].astype(jnp.int32))

    ring = rows_here % n_col == 0
    mine, own, *parts = assemble_columns(front, incoming, place, slot_in, n_col if ring else 1)
    lead = lax.all_to_all(own, BOTH, split_axis=0, concat_axis=0, tiled=True)
    lead = lead[: lead_slices(devices)[0]].reshape(2, 2, TILE, TILE)

    def exchange(mine):
        near = lax.ppermute(mine, "col", [(c, c ^ 1) for c in range(n_col)])
        far = lax.ppermute(mine, "col", [(c, c ^ 2) for c in range(n_col)])
        return [near, far, lax.ppermute(far, "col", [(c, c ^ 1) for c in range(n_col)])]

    def own_panels(mine, lead):
        return row_panels(mine, exchange(mine), lead, diag_inverses, place, slot_in, front)

    sets = n_row // n_col
    circle = list(range(0, n_row, 2)) + list(range(n_row - 1, 0, -2))
    around = [0] + [sign * step for step in range(1, n_row // 2) for sign in (-1, 1)]
    shifts = around + [n_row // 2] if ring else list(range(sets))

    def described(row, shift):
        if not ring:
            return [a * sets + shift for a in range(rows_here)]
        origin = circle[(circle.index(row) + shift) % n_row]
        part, group = origin % n_col, rows_here // n_col
        return [(part * group + t) * sets + origin // n_col for t in range(group)]

    table = np.concatenate([described(row, shift) for row in range(n_row) for shift in shifts])
    table = jnp.asarray(table, jnp.int32)

    def updated(entries, panels, first):
        assert [shift for _, shift in entries] == shifts[first : first + len(entries)]
        pieces = [piece for piece, _ in entries]
        pieces = pieces[0] if isinstance(pieces[0], list) else pieces
        out = trailing(front, pieces, first, place, table, panels, incoming)
        return [panels[0], out, *panels[2:]]

    first = 0
    if ring:
        arrived = []
        for j, part in enumerate(parts):
            pairs = [
                (r * n_col + c, ((r // n_col) * n_col + (c + j) % n_col) * n_col + r % n_col)
                for r in range(n_row)
                for c in range(n_col)
            ]
            arrived.append(lax.ppermute(part, BOTH, pairs))
        arrived, mine, lead = lax.optimization_barrier((arrived, mine, lead))
        piece = piece_panels(jnp.stack(arrived), lead, diag_inverses, place, True)
        up = [(circle[i], circle[(i + 1) % n_row]) for i in range(n_row)]
        down = [(b, a) for a, b in up]
        rounds = [[(piece, 0)]]
        panels = own_panels(mine, lead)
        ahead = behind = piece
        for step in range(1, n_row // 2):
            ahead = lax.ppermute(ahead, "row", up)
            behind = lax.ppermute(behind, "row", down)
            if step == 2:
                panels = updated(rounds[0], panels, 0)
                ahead, behind, panels = lax.optimization_barrier((ahead, behind, panels))
            rounds.append([(ahead, -step), (behind, step)])
        last = [lax.ppermute(ahead[:2], "row", up), lax.ppermute(behind[2:], "row", down)]
        rounds = [*rounds[1:], [(last, n_row // 2)]]
        first = 1

    else:
        pairs = [
            (r * n_col + c, ((r // n_col) * n_col + c) * n_col + r % n_col)
            for r in range(n_row)
            for c in range(n_col)
        ]
        moved = lax.all_gather(lax.ppermute(parts[0], BOTH, pairs), "row", axis=0, tiled=False)
        raw = [moved[h * n_col : (h + 1) * n_col] for h in range(sets)]
        rounds = [
            [(piece_panels(piece, lead, diag_inverses, place, False), h)]
            for h, piece in enumerate(raw)
        ]
        panels = own_panels(mine, lead)

    for entries in rounds:
        panels = updated(entries, panels, first)
        first += len(entries)
    return panels[1]


def solution(mesh):
    return jax.shard_map(
        body,
        mesh=mesh,
        in_specs=(
            P(None, "row", None, "col", None, None),
            P(BOTH, None, None),
            P(BOTH, None),
            P(BOTH),
            P(BOTH),
            P(),
        ),
        out_specs=P(None, "row", None, "col", None, None),
        check_vma=False,
    )
```
